32 devices in a mesh: row: 4 (over y, core), seq: 8 (over z, x).
Axes of the slice: x: 2, y: 2, z: 4, core: 2. Of those that a mesh axis runs over, the one named last changes fastest.
Arguments:
- tokens: bfloat16 [4, 2048, 1536], P('row', 'seq'), may hold values from -6 to 6
- norm_gain: bfloat16 [1536], replicated, may hold values from 0.5 to 1.5
- input_weight: bfloat16 [1536, 6144], P('row'), may hold values from -0.15625 to 0.15625
- conv_weight: bfloat16 [4, 3072], replicated, may hold values from -3 to 3
- conv_bias: bfloat16 [3072], replicated, may hold values from -3 to 3
- select_weight: bfloat16 [3072, 128], replicated, may hold values from -0.109375 to 0.109375
- step_weight: bfloat16 [96, 3072], replicated, may hold values from -0.625 to 0.625
- step_bias: float32 [3072], replicated, may hold values from -13 to -3.5
- decay_log: bfloat16 [3072, 16], replicated, may hold values from 0 to 2.765625
- skip_scale: bfloat16 [3072], replicated, may hold values from 0.5 to 1.5
- output_weight: bfloat16 [3072, 1536], replicated, may hold values from -0.21875 to 0.21875
- attn_gain: bfloat16 [1536], replicated, may hold values from 0.5 to 1.5
- attn_weight: bfloat16 [1536, 4608], replicated, may hold values from -0.15625 to 0.15625
- attn_output: bfloat16 [1536, 1536], replicated, may hold values from -0.625 to 0.625
- mlp_gain: bfloat16 [2, 1536], replicated, may hold values from 0.5 to 1.5
- mlp_up_weight: bfloat16 [2, 1536, 8192], P(None, 'row'), may hold values from -0.15625 to 0.15625
- mlp_down_weight: bfloat16 [2, 4096, 1536], P(None, 'row'), may hold values from -0.1875 to 0.1875
- doc_lengths: int32 [4, 8], P('row'), may hold values from 1 to 1920, 2048 in all within a row
- cotangent: bfloat16 [4, 2048, 1536], P('row', 'seq'), may hold values from -6 to 6
Outputs:
- output: bfloat16 [4, 2048, 1536], P('row', 'seq')
- tokens_grad: bfloat16 [4, 2048, 1536], P('row', 'seq')
- norm_gain_grad: float32 [1536], P(('row', 'seq'))
- input_weight_grad: float32 [1536, 6144], P(None, ('row', 'seq'))
- conv_weight_grad: float32 [4, 3072], P(None, ('row', 'seq'))
- conv_bias_grad: float32 [3072], P(('row', 'seq'))
- select_weight_grad: float32 [3072, 128], P(('row', 'seq'))
- step_weight_grad: float32 [96, 3072], P(None, ('row', 'seq'))
- step_bias_grad: float32 [3072], P(('row', 'seq'))
- decay_log_grad: float32 [3072, 16], P(('row', 'seq'))
- skip_scale_grad: float32 [3072], P(('row', 'seq'))
- output_weight_grad: float32 [3072, 1536], P(('row', 'seq'))
- attn_gain_grad: float32 [1536], P(('row', 'seq'))
- attn_weight_grad: float32 [1536, 4608], P(None, ('row', 'seq'))
- attn_output_grad: float32 [1536, 1536], P(('row', 'seq'))
- mlp_gain_grad: float32 [2, 1536], P(None, ('row', 'seq'))
- mlp_up_weight_grad: float32 [2, 1536, 8192], P(None, None, ('row', 'seq'))
- mlp_down_weight_grad: float32 [2, 4096, 1536], P(None, ('row', 'seq'))
The draws below stay inside these ranges and needn't reach their ends.
All inputs are finite; a program needn't handle non-finite values.
Results may differ from the reference program's by a relative error of at most 0.028.
Values may be sent and summed in bfloat16 or wider, within the bound.
A program may use at most 512 MiB of HBM per device.

```python
import math
import jax
import jax.numpy as jnp
import numpy as np
from jax import lax

D = 1536
INNER = 3072
STATE = 16
CONV = 4
RANK = 96
HEADS = 12
HEAD_DIM = 128
WINDOW = 2048
FF = 4096
DOCS = 8
TOK_DEV = 256
LENGTH = 2048
HOPS = 7
ROWS = 4


def draw_step_bias(key, part):
    key = jax.random.fold_in(key, 5)
    return jax.random.uniform(key, (INNER,), jnp.float32, -12.0, -3.5)


def block_levels(own_key, extent, pieces, smallest, top_value):
    def one(position, shards_of):
        draws = jax.random.uniform(jax.random.fold_in(jax.random.fold_in(own_key, 6), position), (shards_of,), jnp.float32, smallest / len(pieces), top_value / len(pieces))
        return jnp.repeat(jnp.exp(draws), extent[position] // shards_of).reshape((-1,) + (1,) * (len(extent) - position - 1))

    gain = one(*pieces[0])
    for cut in pieces[1:]:
        gain = gain * one(*cut)
    return gain


def length_profile(amount, total, limit, skew):
    weights = [(1 << 20) // math.isqrt(grade ** skew) + 1 for grade in range(2, amount + 1)]
    surplus, holding = total - limit - (amount - 1), [1] * (amount - 1)
    while surplus > 0:
        candidates = [i for i in range(amount - 1) if holding[i] < limit]
        mass, remaining = sum([weights[i] for i in candidates]), surplus
        for i in candidates:
            more = min(limit - holding[i], max(1, remaining * weights[i] // mass), surplus)
            holding[i] = holding[i] + more
            surplus = surplus - more
    return np.array([limit] + holding)


def ragged(key, number_of, total, limit, skew):
    if number_of == 2:
        one = jax.random.randint(key, (), max(1, total - limit), min(limit, total - 1) + 1)
        return jnp.stack([one, total - one])
    sizes = jnp.asarray(length_profile(number_of, total, limit, skew), jnp.int32)
    twos = (number_of - 1) // 2
    source_of, taker = sizes[1:1 + 2 * twos:2], sizes[2:2 + 2 * twos:2]
    room = jnp.minimum(source_of - 1, limit - taker)
    shifted = jax.random.randint(jax.random.fold_in(key, 1), (twos,), 0, 1 << 20) % (room + 1)
    sizes = sizes.at[1:1 + 2 * twos:2].set(source_of - shifted).at[2:2 + 2 * twos:2].set(taker + shifted)
    return sizes[jax.random.permutation(jax.random.fold_in(key, 2), number_of)]


def normal_values(own_key, shape, spread, limit, shards=(), dtype=jnp.bfloat16):
    loudness = block_levels(own_key, shape, shards, -0.22, 0.18) if shards else 1.0
    array = jax.random.normal(own_key, shape, jnp.float32) * spread * loudness
    return jnp.minimum(jnp.maximum(array, -limit), limit).astype(dtype)


def setup_inputs(seed: int = 0) -> dict:
    streams_of = jax.random.split(jax.random.key(seed), 20)
    tokens = normal_values(streams_of[0], (ROWS, LENGTH, D), 1.0, 6.0, ((0, 4), (1, 8)))
    norm_gain = jnp.clip(1.0 + 0.1 * jax.random.normal(streams_of[1], (D,), jnp.float32), 0.5, 1.5).astype(jnp.bfloat16)
    input_weight = normal_values(streams_of[2], (D, 2 * INNER), D ** -0.5, 0.15625, ((0, 4),))
    conv_weight = normal_values(streams_of[3], (CONV, INNER), CONV ** -0.5, 3.0)
    conv_bias = normal_values(streams_of[4], (INNER,), 0.5, 3.0)
    select_weight = normal_values(streams_of[5], (INNER, RANK + 2 * STATE), INNER ** -0.5, 0.109375)
    step_weight = normal_values(streams_of[6], (RANK, INNER), RANK ** -0.5, 0.625)
    step_bias = draw_step_bias(jax.random.fold_in(streams_of[19], 71), 0)
    decay_log = jnp.clip(jax.random.uniform(streams_of[8], (INNER, STATE), jnp.float32, 0.0, 2.765625), 0.0, 2.765625).astype(jnp.bfloat16)
    skip_scale = jnp.clip(jax.random.uniform(streams_of[9], (INNER,), jnp.float32, 0.5, 1.5), 0.5, 1.5).astype(jnp.bfloat16)
    output_weight = normal_values(streams_of[10], (INNER, D), (INNER // 4) ** -0.5, 0.21875)
    attn_gain = jnp.clip(1.0 + 0.1 * jax.random.normal(streams_of[11], (D,), jnp.float32), 0.5, 1.5).astype(jnp.bfloat16)
    attn_weight = normal_values(streams_of[12], (D, 3 * D), D ** -0.5, 0.15625)
    attn_output = normal_values(streams_of[13], (D, D), (D // 16) ** -0.5, 0.625)
    mlp_gain = jnp.clip(1.0 + 0.1 * jax.random.normal(streams_of[14], (2, D), jnp.float32), 0.5, 1.5).astype(jnp.bfloat16)
    mlp_up_weight = normal_values(streams_of[15], (2, D, 2 * FF), D ** -0.5, 0.15625, ((1, 4),))
    mlp_down_weight = normal_values(streams_of[16], (2, FF, D), (FF // 4) ** -0.5, 0.1875, ((1, 4),))
    doc_lengths = jax.vmap(lambda own: ragged(own, DOCS, LENGTH, LENGTH - TOK_DEV // 2, 2))(jax.random.split(streams_of[17], ROWS)).reshape((ROWS, DOCS)).astype(jnp.int32)
    cotangent = normal_values(streams_of[18], (ROWS, LENGTH, D), 1.0, 6.0, ((0, 4), (1, 8)))
    return dict(tokens=tokens, norm_gain=norm_gain, input_weight=input_weight, conv_weight=conv_weight, conv_bias=conv_bias, select_weight=select_weight, step_weight=step_weight, step_bias=step_bias, decay_log=decay_log, skip_scale=skip_scale, output_weight=output_weight, attn_gain=attn_gain, attn_weight=attn_weight, attn_output=attn_output, mlp_gain=mlp_gain, mlp_up_weight=mlp_up_weight, mlp_down_weight=mlp_down_weight, doc_lengths=doc_lengths, cotangent=cotangent)


eps = 1e-05
rope_base = 10000.0

@jax.custom_vjp
def low(v):
    return lax.optimization_barrier(v.astype(jnp.bfloat16)).astype(jnp.float32)

@jax.custom_vjp
def low_back(v):
    return v

def low_keep(v):
    return (low(v), None)

def low_pass(kept, grad):
    return (grad,)

def back_keep(v):
    return (v, None)

def back_low(kept, grad):
    return (low(grad),)
low.defvjp(low_keep, low_pass)
low_back.defvjp(back_keep, back_low)

def hi_dot(left_op, right_op):
    return jnp.dot(left_op, right_op, precision=lax.Precision.HIGHEST, preferred_element_type=jnp.float32)

def rms_apply(values, gain_row):
    return values * lax.rsqrt(lax.optimization_barrier(jnp.mean(values * values, axis=-1, keepdims=True)) + eps) * gain_row

def doc_index(positions, lengths):
    ends_at = jnp.cumsum(lengths)
    return lax.optimization_barrier(jnp.sum((positions[:, None] >= ends_at[None, :]).astype(jnp.int32), axis=1))

def rotary(values, positions):
    half_dim = HEAD_DIM // 2
    frequency = jnp.power(rope_base, -2.0 * jnp.arange(half_dim).astype(jnp.float32) / HEAD_DIM)
    angles = positions.astype(jnp.float32)[:, None] * frequency[None, :]
    cosine = jnp.cos(angles)[:, None, :]
    sine_tab = jnp.sin(angles)[:, None, :]
    rows_here = values.shape[0]
    shaped = values.reshape(rows_here, HEADS, 2, half_dim)
    first_half = shaped[:, :, 0]
    second = shaped[:, :, 1]
    turned = jnp.stack([first_half * cosine - second * sine_tab, second * cosine + first_half * sine_tab], axis=2)
    return turned.reshape(rows_here, HEADS * HEAD_DIM)

def scan_blocks(start_hidden, step_size, activated, input_map, read_map, keep_flag, decays):
    rows_here = step_size.shape[0]
    block_len = min(64, rows_here)

    def one_step(hidden, entries):
        step_rate, drive_in, input_col, read_col, keep_one = entries
        hidden = jnp.exp(decays * step_rate[None, :]) * keep_one * hidden + input_col[:, None] * drive_in[None, :]
        return (hidden, lax.optimization_barrier(jnp.sum(read_col[:, None] * hidden, axis=0)))

    def one_block(hidden, entries):
        return lax.scan(one_step, hidden, entries, unroll=8)
    inputs = (step_size, step_size * activated, input_map, read_map, keep_flag)
    shaped = tuple((member.reshape((rows_here // block_len, block_len) + member.shape[1:]) for member in inputs))
    end_hidden, outputs = lax.scan(jax.checkpoint(one_block), start_hidden, shaped)
    return (outputs.reshape(rows_here, activated.shape[1]), end_hidden)

def mamba_layer(source, lengths, params):
    norm_gain, input_weight, conv_weight, conv_bias, select_weight, step_weight, step_bias, decay_log, skip_scale, output_weight = params
    positions = jnp.arange(LENGTH).astype(jnp.int32)
    normed = low(rms_apply(source, norm_gain))
    mixed_in = low_back(hi_dot(normed, input_weight))
    conv_input = mixed_in[:, :INNER]
    gate_input = mixed_in[:, INNER:]
    own_doc = doc_index(positions, lengths)
    padded = jnp.concatenate([jnp.zeros((CONV - 1, INNER), jnp.float32), conv_input], axis=0)
    conv_pre = conv_bias
    for tap_index in range(CONV):
        earlier = positions - (CONV - 1) + tap_index
        valid_tap = ((earlier >= 0) & (doc_index(earlier, lengths) == own_doc)).astype(jnp.float32)
        conv_pre = conv_pre + conv_weight[tap_index] * padded[tap_index:tap_index + LENGTH] * valid_tap[:, None]
    activated = low(jax.nn.silu(conv_pre))
    picked = low_back(hi_dot(activated, select_weight))
    step_pre = low_back(hi_dot(low(picked[:, :RANK]), step_weight)) + step_bias
    step_size = jax.nn.softplus(step_pre)
    input_map = picked[:, RANK:RANK + STATE]
    read_map = picked[:, RANK + STATE:]
    decays = -jnp.exp(decay_log).T
    keep_flag = ((positions > 0) & (own_doc == doc_index(positions - 1, lengths))).astype(jnp.float32)
    scanned, end_hidden = scan_blocks(jnp.zeros((STATE, INNER), jnp.float32), step_size, activated, input_map, read_map, keep_flag, decays)
    gated = low((scanned + skip_scale * activated) * jax.nn.silu(gate_input))
    return source + low_back(hi_dot(gated, output_weight))

def mlp_layer(source, gain_row, up_weight, down_weight):
    normed = low(rms_apply(source, gain_row))
    gate_up = low_back(hi_dot(normed, up_weight))
    hidden = low(jax.nn.silu(gate_up[:, :FF]) * gate_up[:, FF:])
    return source + low_back(hi_dot(hidden, down_weight))

def attention_layer(first_out, lengths, params):
    attn_gain, attn_weight, attn_output = params
    positions = jnp.arange(LENGTH).astype(jnp.int32)
    normed = low(rms_apply(first_out, attn_gain))
    triple = low_back(hi_dot(normed, attn_weight))
    query = low(rotary(triple[:, :D], positions))
    keys = low(rotary(triple[:, D:2 * D], positions))
    values = low(triple[:, 2 * D:])
    margin = HOPS * TOK_DEV
    key_pad = jnp.concatenate([jnp.zeros((margin, D), jnp.float32), keys], axis=0)
    value_pad = jnp.concatenate([jnp.zeros((margin, D), jnp.float32), values], axis=0)
    inv_scale = HEAD_DIM ** (-0.5)

    def one_block(block_index):
        row_start = (block_index * TOK_DEV).astype(jnp.int32)
        query_block = lax.dynamic_slice_in_dim(query, row_start, TOK_DEV, 0).reshape(TOK_DEV, HEADS, HEAD_DIM)
        key_block = lax.dynamic_slice_in_dim(key_pad, row_start, margin + TOK_DEV, 0).reshape(margin + TOK_DEV, HEADS, HEAD_DIM)
        value_block = lax.dynamic_slice_in_dim(value_pad, row_start, margin + TOK_DEV, 0).reshape(margin + TOK_DEV, HEADS, HEAD_DIM)
        query_pos = row_start + jnp.arange(TOK_DEV).astype(jnp.int32)
        key_pos = row_start - margin + jnp.arange(margin + TOK_DEV).astype(jnp.int32)
        query_doc = doc_index(query_pos, lengths)
        key_doc = doc_index(key_pos, lengths)
        allowed = (key_pos[None, :] <= query_pos[:, None]) & (key_pos[None, :] > query_pos[:, None] - WINDOW) & (key_pos[None, :] >= 0) & (key_doc[None, :] == query_doc[:, None])
        scores = low_back(jnp.einsum('qhd,khd->hqk', query_block, key_block, precision=lax.Precision.HIGHEST) * inv_scale)
        scores = jnp.where(allowed[None], scores, -1e+30)
        row_max = lax.optimization_barrier(jnp.max(scores, axis=-1, keepdims=True))
        exponent = jnp.where(allowed[None], jnp.exp(scores - row_max), 0.0)
        softmax = low(exponent / lax.optimization_barrier(jnp.sum(exponent, axis=-1, keepdims=True)))
        attended = jnp.einsum('hqk,khd->qhd', softmax, value_block, precision=lax.Precision.HIGHEST)
        return low(low_back(attended.reshape(TOK_DEV, D)))
    blocks_out = lax.map(jax.checkpoint(one_block), jnp.arange(LENGTH // TOK_DEV).astype(jnp.int32))
    return first_out + low_back(hi_dot(blocks_out.reshape(LENGTH, D), attn_output))

def reference(tokens, norm_gain, input_weight, conv_weight, conv_bias, select_weight, step_weight, step_bias, decay_log, skip_scale, output_weight, attn_gain, attn_weight, attn_output, mlp_gain, mlp_up_weight, mlp_down_weight, doc_lengths, cotangent):
    weights = tuple((member.astype(jnp.float32) for member in (norm_gain, input_weight, conv_weight, conv_bias, select_weight, step_weight, step_bias, decay_log, skip_scale, output_weight, attn_gain, attn_weight, attn_output, mlp_gain, mlp_up_weight, mlp_down_weight)))

    def forward(source, params):

        def one_row(entries):
            row_data, lengths = entries
            first_out = mamba_layer(row_data, lengths, params[:10])
            second_out = mlp_layer(first_out, params[13][0], params[14][0], params[15][0])
            third_out = attention_layer(second_out, lengths, params[10:13])
            return mlp_layer(third_out, params[13][1], params[14][1], params[15][1])
        return lax.map(jax.checkpoint(one_row), (source, doc_lengths))
    output, pullback = jax.vjp(forward, tokens.astype(jnp.float32), weights)
    d_tokens, d_weights = pullback(cotangent.astype(jnp.float32))
    return (output.astype(jnp.bfloat16), d_tokens.astype(jnp.bfloat16), d_weights[0], d_weights[1], d_weights[2], d_weights[3], d_weights[4], d_weights[5], d_weights[6], d_weights[7], d_weights[8], d_weights[9], d_weights[10], d_weights[11], d_weights[12], d_weights[13], d_weights[14], d_weights[15])
```

```python
import functools
import math

import jax
import jax.numpy as jnp
from jax import lax
from jax.experimental import pallas as pl
from jax.experimental.pallas import tpu as pltpu
from jax.sharding import PartitionSpec as P

LANES = 128
CHUNK = 32
RESET = 1e9
LOG2E = 1.4426950408889634
CONV = 4
HEADS = 12
HEAD_DIM = 128
WINDOW = 2048
GROUPS = 4
eps = 1e-05
rope_base = 10000.0


def from_behind(x, axis, by):
    length = lax.axis_size(axis)
    pairs = [(i, i + by) for i in range(length) if 0 <= i + by < length]
    return lax.ppermute(x, axis, pairs)


def product(left_op, right_op):
    return jnp.dot(left_op, right_op, preferred_element_type=jnp.float32)


def left_trans(left_op, right_op):
    return lax.dot_general(
        left_op, right_op, (((0,), (0,)), ((), ())), preferred_element_type=jnp.float32
    )


def right_trans(left_op, right_op):
    return lax.dot_general(
        left_op, right_op, (((1,), (1,)), ((), ())), preferred_element_type=jnp.float32
    )


def to_planes(tile_ref, value, group):
    for block in range(8):
        tile_ref[pl.ds(group * 64 + block * 8, 8), :] = value[:, block * LANES : (block + 1) * LANES]


def plane(tile_ref, index):
    return tile_ref[pl.ds((index // 8) * 64 + index % 8, 8, stride=8), :]


def tree_sum(terms):
    terms = list(terms)
    while len(terms) > 1:
        terms = [
            terms[i] + terms[i + 1] if i + 1 < len(terms) else terms[i]
            for i in range(0, len(terms), 2)
        ]
    return terms[0]


def scan_forward_kernel(
    with_output, states, chunk, *refs
):
    if with_output:
        (start_ref, step_ref, act_ref, keep_ref, in_ref, read_ref, decay_ref,
         out_ref, marks_ref, hidden_ref, step_t, drive_t, out_t) = refs
    else:
        (step_ref, act_ref, keep_ref, in_ref, decay_ref,
         end_ref, hidden_ref, step_t, drive_t) = refs
    index = pl.program_id(0)
    groups = step_ref.shape[1] // (8 * LANES)

    @pl.when(index == 0)
    def _():
        if with_output:
            hidden_ref[...] = start_ref[...]
        else:
            hidden_ref[...] = jnp.zeros_like(hidden_ref)

    if with_output:
        marks_ref[0] = hidden_ref[...]
    for group in range(groups):
        cols = pl.ds(group * 8 * LANES, 8 * LANES)
        for block in range(chunk // 8):
            rows = pl.ds(block * 8, 8)
            rate = step_ref[rows, cols]
            keep = keep_ref[rows, :]
            gated = jnp.where(jnp.concatenate([keep] * 8, axis=1) > 0, rate, RESET)
            to_planes(step_t, gated, block)
            to_planes(drive_t, rate * act_ref[rows, cols].astype(jnp.float32), block)
        decay = [decay_ref[n, pl.ds(group * 8, 8), :] * LOG2E for n in range(states)]

        def eight(block, hidden):
            hidden = list(hidden)
            for r in range(8):
                pos = index * chunk + block * 8 + r
                rate = step_t[pl.ds(block * 64 + r, 8, stride=8), :]
                drive = drive_t[pl.ds(block * 64 + r, 8, stride=8), :]
                terms = []
                for n in range(states):
                    hidden[n] = jnp.exp2(decay[n] * rate) * hidden[n] + drive * in_ref[pos * states + n]
                    if with_output:
                        terms.append(hidden[n] * read_ref[pos * states + n])
                if with_output:
                    out_t[pl.ds(block * 64 + r, 8, stride=8), :] = tree_sum(terms)
            return tuple(hidden)

        hidden = tuple(hidden_ref[n, pl.ds(group * 8, 8), :] for n in range(states))
        hidden = lax.fori_loop(0, chunk // 8, eight, hidden)
        for n in range(states):
            hidden_ref[n, pl.ds(group * 8, 8), :] = hidden[n]
        if with_output:
            for block in range(chunk // 8):
                for lane_block in range(8):
                    out_ref[pl.ds(block * 8, 8), pl.ds(group * 1024 + lane_block * LANES, LANES)] = out_t[
                        pl.ds(block * 64 + lane_block * 8, 8), :
                    ]
    if not with_output:
        end_ref[...] = hidden_ref[...]


def smem():
    return pl.BlockSpec(memory_space=pltpu.SMEM)


def scan_end(step, act, keep_lanes, in_flat, decay):
    rows, inner = step.shape
    states, planes, _ = decay.shape
    chunk = CHUNK
    whole = pl.BlockSpec((states, planes, LANES), lambda i: (0, 0, 0))
    rowed = pl.BlockSpec((chunk, inner), lambda i: (i, 0))
    return pl.pallas_call(
        functools.partial(scan_forward_kernel, False, states, chunk),
        out_shape=jax.ShapeDtypeStruct(decay.shape, jnp.float32),
        grid=(rows // chunk,),
        in_specs=[rowed, rowed, pl.BlockSpec((chunk, LANES), lambda i: (i, 0)), smem(), whole],
        out_specs=whole,
        scratch_shapes=[pltpu.VMEM(decay.shape, jnp.float32)]
        + [pltpu.VMEM((chunk * 8, LANES), jnp.float32)] * 2,
        compiler_params=pltpu.CompilerParams(vmem_limit_bytes=32 << 20),
        name="scan_end",
    )(step, act, keep_lanes, in_flat, decay)


def scan_out(start, step, act, keep_lanes, in_flat, read_flat, decay):
    rows, inner = step.shape
    states, planes, _ = decay.shape
    chunk = CHUNK
    whole = pl.BlockSpec((states, planes, LANES), lambda i: (0, 0, 0))
    rowed = pl.BlockSpec((chunk, inner), lambda i: (i, 0))
    return pl.pallas_call(
        functools.partial(scan_forward_kernel, True, states, chunk),
        out_shape=(
            jax.ShapeDtypeStruct((rows, inner), jnp.float32),
            jax.ShapeDtypeStruct((rows // chunk,) + decay.shape, jnp.float32),
        ),
        grid=(rows // chunk,),
        in_specs=[whole, rowed, rowed, pl.BlockSpec((chunk, LANES), lambda i: (i, 0)), smem(), smem(), whole],
        out_specs=(rowed, pl.BlockSpec((1, states, planes, LANES), lambda i: (i, 0, 0, 0))),
        scratch_shapes=[pltpu.VMEM(decay.shape, jnp.float32)]
        + [pltpu.VMEM((chunk * 8, LANES), jnp.float32)] * 3,
        compiler_params=pltpu.CompilerParams(vmem_limit_bytes=32 << 20),
        name="scan_out",
    )(start, step, act, keep_lanes, in_flat, read_flat, decay)


def adjoint_end_kernel(states, chunk, step_ref, grad_ref, keep_ref, read_ref, decay_ref, end_ref, carry_ref, step_t, grad_t):
    index = pl.program_id(0)
    last = pl.num_programs(0) - 1
    groups = step_ref.shape[1] // (8 * LANES)

    @pl.when(index == 0)
    def _():
        carry_ref[...] = jnp.zeros_like(carry_ref)

    for group in range(groups):
        cols = pl.ds(group * 8 * LANES, 8 * LANES)
        for block in range(chunk // 8):
            rows = pl.ds(block * 8, 8)
            keep = keep_ref[rows, :]
            to_planes(step_t, jnp.where(jnp.concatenate([keep] * 8, axis=1) > 0, step_ref[rows, cols], RESET), block)
            to_planes(grad_t, grad_ref[rows, cols], block)
        decay = [decay_ref[n, pl.ds(group * 8, 8), :] * LOG2E for n in range(states)]

        def eight(turn, carry):
            carry = list(carry)
            block = chunk // 8 - 1 - turn
            for r in range(7, -1, -1):
                pos = (last - index) * chunk + block * 8 + r
                rate = step_t[pl.ds(block * 64 + r, 8, stride=8), :]
                grad = grad_t[pl.ds(block * 64 + r, 8, stride=8), :]
                for n in range(states):
                    carry[n] = jnp.exp2(decay[n] * rate) * (carry[n] + grad * read_ref[pos * states + n])
            return tuple(carry)

        carry = tuple(carry_ref[n, pl.ds(group * 8, 8), :] for n in range(states))
        carry = lax.fori_loop(0, chunk // 8, eight, carry)
        for n in range(states):
            carry_ref[n, pl.ds(group * 8, 8), :] = carry[n]
    end_ref[...] = carry_ref[...]


def adjoint_end(step, grad, keep_lanes, read_flat, decay):
    rows, inner = step.shape
    states, planes, _ = decay.shape
    chunk = CHUNK
    count = rows // chunk
    whole = pl.BlockSpec((states, planes, LANES), lambda i: (0, 0, 0))
    rowed = pl.BlockSpec((chunk, inner), lambda i: (count - 1 - i, 0))
    return pl.pallas_call(
        functools.partial(adjoint_end_kernel, states, chunk),
        out_shape=jax.ShapeDtypeStruct(decay.shape, jnp.float32),
        grid=(count,),
        in_specs=[rowed, rowed, pl.BlockSpec((chunk, LANES), lambda i: (count - 1 - i, 0)), smem(), whole],
        out_specs=whole,
        scratch_shapes=[pltpu.VMEM(decay.shape, jnp.float32)]
        + [pltpu.VMEM((chunk * 8, LANES), jnp.float32)] * 2,
        compiler_params=pltpu.CompilerParams(vmem_limit_bytes=32 << 20),
        name="adjoint_end",
    )(step, grad, keep_lanes, read_flat, decay)


def adjoint_full_kernel(
    states, chunk,
    end_ref, marks_ref, step_ref, act_ref, grad_ref, keep_ref, in_ref, read_ref, decay_ref,
    d_step_ref, d_act_ref, d_in_ref, d_read_ref, d_decay_ref,
    carry_ref, step_t, rate_t, act_t, grad_t, d_step_t, d_act_t, factor_t, held_t, in_t, read_t,
):
    index = pl.program_id(0)
    last = pl.num_programs(0) - 1
    groups = step_ref.shape[1] // (8 * LANES)

    @pl.when(index == 0)
    def _():
        carry_ref[...] = end_ref[...]
        d_decay_ref[...] = jnp.zeros_like(d_decay_ref)

    for group in range(groups):
        cols = pl.ds(group * 8 * LANES, 8 * LANES)
        for block in range(chunk // 8):
            rows = pl.ds(block * 8, 8)
            rate = step_ref[rows, cols]
            keep = keep_ref[rows, :]
            to_planes(step_t, jnp.where(jnp.concatenate([keep] * 8, axis=1) > 0, rate, RESET), block)
            to_planes(rate_t, rate, block)
            to_planes(act_t, act_ref[rows, cols].astype(jnp.float32), block)
            to_planes(grad_t, grad_ref[rows, cols], block)

        def replay(block, hidden):
            hidden = list(hidden)
            for r in range(8):
                local = block * 8 + r
                pos = (last - index) * chunk + local
                view = pl.ds(block * 64 + r, 8, stride=8)
                gated = step_t[view, :]
                drive = rate_t[view, :] * act_t[view, :]
                grad = grad_t[view, :]
                for n in range(states):
                    slot = pl.ds((local * states + n) * 8, 8)
                    factor = jnp.exp2(decay_ref[n, pl.ds(group * 8, 8), :] * LOG2E * gated)
                    held = factor * hidden[n]
                    hidden[n] = held + drive * in_ref[pos * states + n]
                    factor_t[slot, :] = factor
                    held_t[slot, :] = held
                    if group == 0:
                        read_t[slot, :] = grad * hidden[n]
                    else:
                        read_t[slot, :] += grad * hidden[n]
            return tuple(hidden)

        lax.fori_loop(
            0, chunk // 8, replay,
            tuple(marks_ref[0, n, pl.ds(group * 8, 8), :] for n in range(states)),
        )

        def back(turn, carried):
            carry, d_decay = list(carried[0]), list(carried[1])
            block = chunk // 8 - 1 - turn
            for r in range(7, -1, -1):
                local = block * 8 + r
                pos = (last - index) * chunk + local
                view = pl.ds(block * 64 + r, 8, stride=8)
                rate = rate_t[view, :]
                act = act_t[view, :]
                grad = grad_t[view, :]
                drive = rate * act
                inner_terms = []
                step_terms = []
                for n in range(states):
                    slot = pl.ds((local * states + n) * 8, 8)
                    adjoint = carry[n] + grad * read_ref[pos * states + n]
                    moved = adjoint * held_t[slot, :]
                    step_terms.append(moved * decay_ref[n, pl.ds(group * 8, 8), :])
                    d_decay[n] = d_decay[n] + moved * rate
                    inner_terms.append(adjoint * in_ref[pos * states + n])
                    if group == 0:
                        in_t[slot, :] = adjoint * drive
                    else:
                        in_t[slot, :] += adjoint * drive
                    carry[n] = adjoint * factor_t[slot, :]
                inner_sum = tree_sum(inner_terms)
                d_step_t[view, :] = tree_sum(step_terms) + act * inner_sum
                d_act_t[view, :] = rate * inner_sum
            return (tuple(carry), tuple(d_decay))

        carry, d_decay = lax.fori_loop(
            0, chunk // 8, back,
            (
                tuple(carry_ref[n, pl.ds(group * 8, 8), :] for n in range(states)),
                tuple(d_decay_ref[n, pl.ds(group * 8, 8), :] for n in range(states)),
            ),
        )
        for n in range(states):
            carry_ref[n, pl.ds(group * 8, 8), :] = carry[n]
            d_decay_ref[n, pl.ds(group * 8, 8), :] = d_decay[n]
        for block in range(chunk // 8):
            for lane_block in range(8):
                where = (pl.ds(block * 8, 8), pl.ds(group * 1024 + lane_block * LANES, LANES))
                tile = pl.ds(block * 64 + lane_block * 8, 8)
                d_step_ref[where] = d_step_t[tile, :]
                d_act_ref[where] = d_act_t[tile, :]

    def shrink(block, _):
        for source, target in ((in_t, d_in_ref), (read_t, d_read_ref)):
            total = source[pl.ds(block * 64, 8, stride=8), :]
            for s in range(1, 8):
                total = total + source[pl.ds(block * 64 + s, 8, stride=8), :]
            target[pl.ds(block * 8, 8), :] = total
        return 0

    lax.fori_loop(0, chunk * states // 8, shrink, 0, unroll=4)


def adjoint_full(end_grad, marks, step, act, grad, keep_lanes, in_flat, read_flat, decay):
    rows, inner = step.shape
    states, planes, _ = decay.shape
    chunk = CHUNK
    count = rows // chunk
    whole = pl.BlockSpec((states, planes, LANES), lambda i: (0, 0, 0))
    rowed = pl.BlockSpec((chunk, inner), lambda i: (count - 1 - i, 0))
    maps = pl.BlockSpec((chunk * states, LANES), lambda i: (count - 1 - i, 0))
    big = pltpu.VMEM((chunk * states * 8, LANES), jnp.float32)
    return pl.pallas_call(
        functools.partial(adjoint_full_kernel, states, chunk),
        out_shape=(
            jax.ShapeDtypeStruct((rows, inner), jnp.float32),
            jax.ShapeDtypeStruct((rows, inner), jnp.float32),
            jax.ShapeDtypeStruct((rows * states, LANES), jnp.float32),
            jax.ShapeDtypeStruct((rows * states, LANES), jnp.float32),
            jax.ShapeDtypeStruct(decay.shape, jnp.float32),
        ),
        grid=(count,),
        in_specs=[
            whole,
            pl.BlockSpec((1, states, planes, LANES), lambda i: (count - 1 - i, 0, 0, 0)),
            rowed, rowed, rowed,
            pl.BlockSpec((chunk, LANES), lambda i: (count - 1 - i, 0)),
            smem(), smem(), whole,
        ],
        out_specs=(rowed, rowed, maps, maps, whole),
        scratch_shapes=[pltpu.VMEM(decay.shape, jnp.float32)]
        + [pltpu.VMEM((chunk * 8, LANES), jnp.float32)] * 6
        + [big] * 4,
        compiler_params=pltpu.CompilerParams(vmem_limit_bytes=48 << 20),
        name="adjoint_full",
    )(end_grad, marks, step, act, grad, keep_lanes, in_flat, read_flat, decay)


KEYS = 512


def turn_half(values):
    return pltpu.roll(values, HEAD_DIM // 2, 1)


def project_kernel(rotated, ctx_ref, weight_ref, cos_ref, sin_ref, out_ref):
    cosine, sine = cos_ref[...], sin_ref[...]
    ctx = ctx_ref[...]
    step = 3 * HEAD_DIM
    for start in range(0, weight_ref.shape[1], step):
        triple = product(ctx, weight_ref[:, start : start + step])
        for head in range(0, step, HEAD_DIM):
            part = triple[:, head : head + HEAD_DIM]
            if start + head < rotated:
                part = part * cosine + turn_half(part) * sine
            out_ref[:, start + head : start + head + HEAD_DIM] = part.astype(jnp.bfloat16)


def project_heads(ctx, weight, cosine, sine, rotated):
    length, width = ctx.shape
    columns = weight.shape[1]
    rows = min(256, length)
    return pl.pallas_call(
        functools.partial(project_kernel, rotated),
        out_shape=jax.ShapeDtypeStruct((length, columns), jnp.bfloat16),
        grid=(length // rows,),
        in_specs=[
            pl.BlockSpec((rows, width), lambda i: (i, 0)),
            pl.BlockSpec((width, columns), lambda i: (0, 0)),
            pl.BlockSpec((rows, HEAD_DIM), lambda i: (i, 0)),
            pl.BlockSpec((rows, HEAD_DIM), lambda i: (i, 0)),
        ],
        out_specs=pl.BlockSpec((rows, columns), lambda i: (i, 0)),
        compiler_params=pltpu.CompilerParams(vmem_limit_bytes=40 << 20),
        cost_estimate=pl.CostEstimate(
            flops=2 * length * width * columns, bytes_accessed=2 * (length * width + width * columns), transcendentals=0
        ),
        name="project_heads",
    )(ctx, weight, cosine, sine)


def mask_keys(scores_shape, chunk, first_key, q_pos):
    key_pos = chunk * KEYS + lax.broadcasted_iota(jnp.int32, scores_shape, 1)
    return (key_pos >= first_key) & (key_pos <= q_pos)


def attend_kernel(
    n_x, heads, scale, x_ref, low_ref, q_ref, k_ref, v_ref, first_ref, out_ref, lse_ref, score_t
):
    block = pl.program_id(1)
    rows = q_ref.shape[0]
    base = (block * n_x + x_ref[0]) * rows
    low_chunk = low_ref[block] // KEYS
    high_chunk = (base + rows - 1) // KEYS + 1
    q_pos = base + lax.broadcasted_iota(jnp.int32, (rows, KEYS), 0)
    first_key = first_ref[...]
    query = q_ref[...]

    def scores_of(chunk, top):
        where = pl.ds(pl.multiple_of(chunk * KEYS, KEYS), KEYS)
        scores = right_trans(query, k_ref[where, :]) * scale
        scores = jnp.where(mask_keys(scores.shape, chunk, first_key, q_pos), scores, -1e30)
        score_t[:, where] = scores
        for part in range(0, KEYS, LANES):
            top = jnp.maximum(top, scores[:, part : part + LANES])
        return top

    top = lax.fori_loop(low_chunk, high_chunk, scores_of, jnp.full((rows, LANES), -1e30, jnp.float32))
    top = jnp.max(top, axis=1, keepdims=True)

    def weigh(chunk, carried):
        total, mixed = carried
        where = pl.ds(pl.multiple_of(chunk * KEYS, KEYS), KEYS)
        weights = jnp.exp2(score_t[:, where] - top)
        for part in range(0, KEYS, LANES):
            total = total + weights[:, part : part + LANES]
        return (total, mixed + product(weights.astype(jnp.bfloat16), v_ref[where, :]))

    total, mixed = lax.fori_loop(
        low_chunk,
        high_chunk,
        weigh,
        (jnp.zeros((rows, LANES), jnp.float32), jnp.zeros((rows, HEAD_DIM), jnp.float32)),
    )
    total = jnp.sum(total, axis=1, keepdims=True)
    out_ref[...] = (mixed / total).astype(jnp.bfloat16)
    lse_ref[0] = top + jnp.log2(total)


def attend(x_index, lows, triple, first_key, n_x, heads, rows):
    length = triple.shape[0]
    blocks = length // (rows * n_x)
    scale = HEAD_DIM ** (-0.5) * LOG2E
    return pl.pallas_call(
        functools.partial(attend_kernel, n_x, heads, scale),
        out_shape=(
            jax.ShapeDtypeStruct((blocks * rows, heads * HEAD_DIM), jnp.bfloat16),
            jax.ShapeDtypeStruct((heads, blocks * rows, 1), jnp.float32),
        ),
        grid_spec=pltpu.PrefetchScalarGridSpec(
            num_scalar_prefetch=2,
            grid=(heads, blocks),
            in_specs=[
                pl.BlockSpec((rows, HEAD_DIM), lambda h, b, x, low: (b * n_x + x[0], h)),
                pl.BlockSpec((length, HEAD_DIM), lambda h, b, x, low: (0, heads + h)),
                pl.BlockSpec((length, HEAD_DIM), lambda h, b, x, low: (0, 2 * heads + h)),
                pl.BlockSpec((rows, 1), lambda h, b, x, low: (b, 0)),
            ],
            out_specs=(
                pl.BlockSpec((rows, HEAD_DIM), lambda h, b, x, low: (b, h)),
                pl.BlockSpec((1, rows, 1), lambda h, b, x, low: (h, b, 0)),
            ),
            scratch_shapes=[pltpu.VMEM((rows, length), jnp.float32)],
        ),
        compiler_params=pltpu.CompilerParams(vmem_limit_bytes=40 << 20),
        cost_estimate=pl.CostEstimate(
            flops=2 * heads * blocks * rows * length * HEAD_DIM, bytes_accessed=4 * length * heads * HEAD_DIM, transcendentals=0
        ),
        name="attend",
    )(x_index, lows, triple, triple, triple, first_key)


def attend_back_kernel(
    n_x, heads, scale,
    x_ref, low_ref, q_ref, k_ref, v_ref, out_ref, d_ref, lse_ref, first_ref, cos_ref, sin_ref, cos_all, sin_all,
    dq_ref, dk_ref, dv_ref, dk_t, dv_t,
):
    block = pl.program_id(1)
    rows = q_ref.shape[0]
    base = (block * n_x + x_ref[0]) * rows
    low_chunk = low_ref[block] // KEYS
    high_chunk = (base + rows - 1) // KEYS + 1
    q_pos = base + lax.broadcasted_iota(jnp.int32, (rows, KEYS), 0)
    first_key = first_ref[...]
    query = q_ref[...]
    d_out = d_ref[...]
    log_total = lse_ref[0]
    center = jnp.sum(d_out.astype(jnp.float32) * out_ref[...].astype(jnp.float32), axis=1, keepdims=True)

    @pl.when(block == 0)
    def _():
        dk_t[...] = jnp.zeros_like(dk_t)
        dv_t[...] = jnp.zeros_like(dv_t)

    def one(chunk, d_query):
        where = pl.ds(pl.multiple_of(chunk * KEYS, KEYS), KEYS)
        keys = k_ref[where, :]
        scores = right_trans(query, keys) * scale
        allowed = mask_keys(scores.shape, chunk, first_key, q_pos)
        weights = jnp.where(allowed, jnp.exp2(scores - log_total), 0.0)
        d_soft = right_trans(d_out, v_ref[where, :])
        d_scores = (weights * (d_soft - center)).astype(jnp.bfloat16)
        dv_t[where, :] += left_trans(weights.astype(jnp.bfloat16), d_out)
        dk_t[where, :] += left_trans(d_scores, query)
        return d_query + product(d_scores, keys)

    d_query = lax.fori_loop(low_chunk, high_chunk, one, jnp.zeros((rows, HEAD_DIM), jnp.float32))
    inv_scale = HEAD_DIM ** (-0.5)
    d_query = d_query * inv_scale
    dq_ref[...] = (d_query * cos_ref[...] - turn_half(d_query) * sin_ref[...]).astype(jnp.bfloat16)

    @pl.when(block == pl.num_programs(1) - 1)
    def _():
        def finish(chunk, _):
            where = pl.ds(pl.multiple_of(chunk * KEYS, KEYS), KEYS)
            d_keys = dk_t[where, :] * inv_scale
            dk_ref[where, :] = (d_keys * cos_all[where, :] - turn_half(d_keys) * sin_all[where, :]).astype(jnp.bfloat16)
            dv_ref[where, :] = dv_t[where, :].astype(jnp.bfloat16)
            return 0

        lax.fori_loop(0, k_ref.shape[0] // KEYS, finish, 0)


def attend_back(x_index, lows, triple, attended, d_attended, lse, first_key, cosine, sine, n_x, heads, rows):
    length = triple.shape[0]
    blocks = length // (rows * n_x)
    scale = HEAD_DIM ** (-0.5) * LOG2E
    q_spec = pl.BlockSpec((rows, HEAD_DIM), lambda h, b, x, low: (b * n_x + x[0], h))
    own = pl.BlockSpec((rows, HEAD_DIM), lambda h, b, x, low: (b, h))
    table_q = pl.BlockSpec((rows, HEAD_DIM), lambda h, b, x, low: (b * n_x + x[0], 0))
    table = pl.BlockSpec((length, HEAD_DIM), lambda h, b, x, low: (0, 0))
    column = pl.BlockSpec((length, HEAD_DIM), lambda h, b, x, low: (0, h))
    return pl.pallas_call(
        functools.partial(attend_back_kernel, n_x, heads, scale),
        out_shape=(
            jax.ShapeDtypeStruct((blocks * rows, heads * HEAD_DIM), jnp.bfloat16),
            jax.ShapeDtypeStruct((length, heads * HEAD_DIM), jnp.bfloat16),
            jax.ShapeDtypeStruct((length, heads * HEAD_DIM), jnp.bfloat16),
        ),
        grid_spec=pltpu.PrefetchScalarGridSpec(
            num_scalar_prefetch=2,
            grid=(heads, blocks),
            in_specs=[
                q_spec,
                pl.BlockSpec((length, HEAD_DIM), lambda h, b, x, low: (0, heads + h)),
                pl.BlockSpec((length, HEAD_DIM), lambda h, b, x, low: (0, 2 * heads + h)),
                own,
                own,
                pl.BlockSpec((1, rows, 1), lambda h, b, x, low: (h, b, 0)),
                pl.BlockSpec((rows, 1), lambda h, b, x, low: (b, 0)),
                table_q,
                table_q,
                table,
                table,
            ],
            out_specs=(own, column, column),
            scratch_shapes=[pltpu.VMEM((length, HEAD_DIM), jnp.float32)] * 2,
        ),
        compiler_params=pltpu.CompilerParams(vmem_limit_bytes=40 << 20),
        cost_estimate=pl.CostEstimate(
            flops=5 * heads * blocks * rows * length * HEAD_DIM, bytes_accessed=8 * length * heads * HEAD_DIM, transcendentals=0
        ),
        name="attend_back",
    )(x_index, lows, triple, triple, triple, attended, d_attended, lse, first_key, cosine, sine, cosine, sine)


def line_groups():
    n_seq = lax.axis_size("seq")
    n_x = n_seq // GROUPS
    return [[z * n_x + x for z in range(GROUPS)] for x in range(n_x)]


def plane_groups():
    n_seq = lax.axis_size("seq")
    n_x = n_seq // GROUPS
    n_row = lax.axis_size("row")
    return [
        [r * n_seq + z * n_x + x for r in range(n_row) for x in range(n_x)] for z in range(GROUPS)
    ]


def gather_rows(block):
    return lax.all_gather(block, "row", axis=0, tiled=True)


def reduce_rows(partial):
    return lax.psum_scatter(partial, "row", scatter_dimension=0, tiled=True)


def gather_seq(block):
    return lax.all_gather(block, "seq", axis=0, tiled=True)


def reduce_seq(partial):
    return lax.psum_scatter(partial, "seq", scatter_dimension=0, tiled=True)


def weight_term(moving, whole_gathered, split_rows):
    n_row = lax.axis_size("row")
    n_seq = lax.axis_size("seq")
    rows_here = moving.shape[0]
    columns = moving.shape[1]
    owned = columns // (n_row * n_seq)
    shaped = moving.reshape(rows_here, n_row, n_seq, owned)
    spread = lax.all_to_all(shaped, "seq", split_axis=2, concat_axis=0, tiled=True).reshape(
        n_seq * rows_here, n_row, owned
    )
    if split_rows:
        return jnp.einsum("tgc,tb->gcb", spread, whole_gathered, preferred_element_type=jnp.float32)
    return jnp.einsum("ta,tgc->agc", whole_gathered, spread, preferred_element_type=jnp.float32)


def norm_apply(values, gain_row):
    factor = lax.rsqrt(jnp.mean(values * values, axis=-1, keepdims=True) + eps)
    return (values * factor * gain_row, factor)


def norm_back(values, factor, gain_row, upstream):
    normed = values * factor
    weighted = upstream * gain_row
    gain_grad = jnp.sum(upstream * normed, axis=0)
    value_grad = factor * (weighted - normed * jnp.mean(weighted * normed, axis=-1, keepdims=True))
    return (value_grad, gain_grad)


def doc_index(positions, lengths):
    ends_at = jnp.cumsum(lengths)
    return jnp.sum((positions[:, None] >= ends_at[None, :]).astype(jnp.int32), axis=1)


def first_allowed(positions, lengths):
    ends_at = jnp.cumsum(lengths)
    begins = jnp.max(jnp.where(positions[:, None] >= ends_at[None, :], ends_at[None, :], 0), axis=1)
    return jnp.maximum(begins, positions - (WINDOW - 1)).astype(jnp.int32)


def conv_masks(positions, lengths):
    own_doc = doc_index(positions, lengths)
    rows_out = []
    for tap_index in range(CONV):
        earlier = positions - (CONV - 1) + tap_index
        rows_out.append(
            ((earlier >= 0) & (doc_index(earlier, lengths) == own_doc)).astype(jnp.float32)
        )
    return jnp.stack(rows_out, axis=0)


def rotary_tables(positions):
    half_dim = HEAD_DIM // 2
    frequency = jnp.power(rope_base, -2.0 * jnp.arange(half_dim).astype(jnp.float32) / HEAD_DIM)
    angles = positions.astype(jnp.float32)[:, None] * frequency[None, :]
    cosine, sine_tab = (jnp.cos(angles), jnp.sin(angles))
    return (
        jnp.concatenate([cosine, cosine], axis=1),
        jnp.concatenate([-sine_tab, sine_tab], axis=1),
    )


def own_up_columns(up_local):
    n_row = lax.axis_size("row")
    row = lax.axis_index("row")
    depth, both = up_local.shape
    ff_dim = both // 2
    ff_row = ff_dim // n_row
    width = depth * n_row

    def slab(dest):
        odd = dest % 2
        first = lax.dynamic_slice(up_local, (0, odd * ff_dim + dest * ff_row), (depth, ff_row))
        second = lax.dynamic_slice(up_local, (0, (1 - odd) * ff_dim + dest * ff_row), (depth, ff_row))
        return jnp.concatenate([first, second], axis=1)

    whole = jnp.zeros((width, 2 * ff_row), up_local.dtype)
    for turn in range(n_row):
        other = row ^ turn
        piece = slab(other)
        if turn:
            piece = lax.ppermute(piece, "row", [(i, i ^ turn) for i in range(n_row)])
        whole = lax.dynamic_update_slice(whole, piece, (other * depth, 0))
    return whole


def mlp_forward(values, gain_row, up_own, down_own):
    odd = lax.axis_index("row") % 2 == 1
    ff_row = down_own.shape[0]
    normed, factor = norm_apply(values, gain_row)
    spread = gather_rows(normed.astype(jnp.bfloat16))
    gate_up = product(spread, up_own)
    first, second = (gate_up[:, :ff_row], gate_up[:, ff_row:])
    gate_part = jnp.where(odd, second, first)
    up_part = jnp.where(odd, first, second)
    hidden = (jax.nn.silu(gate_part) * up_part).astype(jnp.bfloat16)
    partial = product(hidden, down_own).astype(jnp.bfloat16)
    return (values + reduce_rows(partial).astype(jnp.float32), (factor, spread, gate_part, up_part, hidden))


def place_up_grad(grad):
    n_row = lax.axis_size("row")
    n_seq = lax.axis_size("seq")
    half = n_seq // 2
    pairs = []
    for r in range(n_row):
        for s in range(n_seq):
            if s // half == r % 2:
                owner = (r // 2, s)
            else:
                owner = (n_row // 2 + r // 2, (r % 2) * half + s % half)
            pairs.append((r * n_seq + s, owner[0] * n_seq + owner[1]))
    return lax.ppermute(grad, ("row", "seq"), pairs)


def mlp_backward(values, gain_row, up_own, down_own, kept, upstream, upstream_all):
    factor, spread, gate_part, up_part, hidden = kept
    odd = lax.axis_index("row") % 2 == 1
    g_down = reduce_seq(left_trans(hidden, upstream_all).astype(jnp.bfloat16)).astype(jnp.float32)
    d_hidden = right_trans(upstream_all, down_own)
    gate_sig = jax.nn.sigmoid(gate_part)
    d_gate = d_hidden * up_part * gate_sig * (1.0 + gate_part * (1.0 - gate_sig))
    d_up = d_hidden * gate_part * gate_sig
    d_gate_up = jnp.concatenate(
        [jnp.where(odd, d_up, d_gate), jnp.where(odd, d_gate, d_up)], axis=1
    ).astype(jnp.bfloat16)
    d_normed = reduce_rows(right_trans(d_gate_up, up_own).astype(jnp.bfloat16)).astype(jnp.float32)
    g_up = place_up_grad(reduce_seq(left_trans(d_gate_up, spread).astype(jnp.bfloat16)))
    d_norm, g_gain = norm_back(values, factor, gain_row, d_normed)
    return (upstream + d_norm, g_gain, g_up.astype(jnp.float32).T, g_down)


def matchings(edges, size):
    rounds = []
    left = list(range(len(edges)))
    while left:
        taken = {}

        def assign(source, seen):
            for e in left:
                if edges[e][0] == source and edges[e][1] not in seen:
                    seen.add(edges[e][1])
                    if edges[e][1] not in taken or assign(edges[taken[edges[e][1]]][0], seen):
                        taken[edges[e][1]] = e
                        return True
            return False

        for source in range(size):
            assign(source, set())
        chosen = sorted(taken.values())
        rounds.append(chosen)
        left = [e for e in left if e not in chosen]
    return rounds


def place_attn_grad(piece, width):
    n_row = lax.axis_size("row")
    n_seq = lax.axis_size("seq")
    n_x = n_seq // GROUPS
    size = n_row * n_seq
    me = lax.axis_index("row") * n_seq + lax.axis_index("seq")
    group_cols = width // GROUPS
    owned = piece.shape[0]
    unit = math.gcd(owned, group_cols)
    count = owned // unit
    edges, slots = [], []
    for r in range(n_row):
        for z in range(GROUPS):
            for x in range(n_x):
                for u in range(count):
                    local = (r * n_x + x) * owned + u * unit
                    column = (local // group_cols) * width + z * group_cols + local % group_cols
                    edges.append((r * n_seq + z * n_x + x, column // owned))
                    slots.append((u, column % owned // unit))
    result = jnp.zeros_like(piece)
    for chosen in matchings(edges, size):
        send_slot = [0] * size
        recv_slot = [0] * size
        for e in chosen:
            send_slot[edges[e][0]] = slots[e][0]
            recv_slot[edges[e][1]] = slots[e][1]
        taken = lax.dynamic_slice(
            piece, (jnp.array(send_slot, jnp.int32)[me] * unit, 0), (unit, piece.shape[1])
        )
        moved = lax.ppermute(taken, ("row", "seq"), [edges[e] for e in chosen])
        result = lax.dynamic_update_slice(
            result, moved, (jnp.array(recv_slot, jnp.int32)[me] * unit, 0)
        )
    return result


def place_out_grad(piece):
    n_row = lax.axis_size("row")
    n_seq = lax.axis_size("seq")
    n_x = n_seq // GROUPS
    pairs = []
    for r in range(n_row):
        for z in range(GROUPS):
            for x in range(n_x):
                pairs.append((r * n_seq + z * n_x + x, z * n_row * n_x + r * n_x + x))
    return lax.ppermute(piece, ("row", "seq"), pairs)


def exchange_states(through, end_state, forward):
    n_seq = lax.axis_size("seq")
    me = lax.axis_index("seq")
    both = lax.all_gather(
        jnp.stack([through, end_state]).astype(jnp.bfloat16), "seq", axis=0
    ).astype(jnp.float32)
    carried = jnp.zeros_like(end_state)
    order = range(n_seq) if forward else range(n_seq - 1, -1, -1)
    for other in order:
        used = other < me if forward else other > me
        carried = jnp.where(used, both[other, 0] * carried + both[other, 1], carried)
    return carried


def per_device(
    tokens,
    norm_gain,
    input_weight,
    conv_weight,
    conv_bias,
    select_weight,
    step_weight,
    step_bias,
    decay_log,
    skip_scale,
    output_weight,
    attn_gain,
    attn_weight,
    attn_output,
    mlp_gain,
    mlp_up_weight,
    mlp_down_weight,
    doc_lengths,
    cotangent,
):
    n_row = lax.axis_size("row")
    n_seq = lax.axis_size("seq")
    n_x = n_seq // GROUPS
    rows_here = tokens.shape[1]
    width = tokens.shape[2]
    inner_dim = skip_scale.shape[0]
    rank_dim = step_weight.shape[0]
    state_dim = decay_log.shape[1]
    head_count = HEADS // GROUPS
    group_cols = head_count * HEAD_DIM
    lengths = doc_lengths[0]
    seq_index = lax.axis_index("seq")
    z_index = seq_index // n_x
    x_index = seq_index % n_x
    positions = seq_index * rows_here + jnp.arange(rows_here, dtype=jnp.int32)
    gain_in = norm_gain.astype(jnp.float32)
    gain_attn = attn_gain.astype(jnp.float32)
    gains_mlp = mlp_gain.astype(jnp.float32)
    conv_taps = conv_weight.astype(jnp.float32)
    skip_row = skip_scale.astype(jnp.float32)
    decays = -jnp.exp(decay_log.astype(jnp.float32)).T
    decay_planes = decays.reshape(state_dim, inner_dim // LANES, LANES)
    source = tokens[0].astype(jnp.float32)
    own_doc = doc_index(positions, lengths)
    keep_flag = ((positions > 0) & (own_doc == doc_index(positions - 1, lengths))).astype(
        jnp.float32
    )
    keep_lanes = jnp.broadcast_to(keep_flag[:, None], (rows_here, LANES))
    tap_masks = conv_masks(positions, lengths)
    whole_in = lax.all_gather(input_weight, "row", axis=0, tiled=True)
    up_local, grad_start = lax.optimization_barrier((mlp_up_weight, whole_in))[0], None
    up_first = own_up_columns(up_local[0])
    up_last = own_up_columns(up_local[1])
    down_first, down_last = (mlp_down_weight[0], mlp_down_weight[1])
    normed_in, factor_in = norm_apply(source, gain_in)
    low_in = normed_in.astype(jnp.bfloat16)
    mixed_in = product(low_in, whole_in)
    conv_input = mixed_in[:, :inner_dim]
    gate_input = mixed_in[:, inner_dim:]
    halo_rows = from_behind(
        conv_input[rows_here - (CONV - 1) :].astype(jnp.bfloat16), "seq", 1
    ).astype(jnp.float32)
    padded = jnp.concatenate([halo_rows, conv_input], axis=0)
    conv_pre = conv_bias.astype(jnp.float32)
    for tap_index in range(CONV):
        conv_pre = (
            conv_pre
            + conv_taps[tap_index]
            * padded[tap_index : tap_index + rows_here]
            * tap_masks[tap_index][:, None]
        )
    activated_low = jax.nn.silu(conv_pre).astype(jnp.bfloat16)
    activated = activated_low.astype(jnp.float32)
    picked = product(activated_low, select_weight)
    step_low = picked[:, :rank_dim].astype(jnp.bfloat16)
    step_pre = product(step_low, step_weight) + step_bias
    step_size = jax.nn.softplus(step_pre)
    in_flat = picked[:, rank_dim : rank_dim + state_dim].reshape(-1)
    read_flat = picked[:, rank_dim + state_dim :].reshape(-1)
    local_end = scan_end(step_size, activated_low, keep_lanes, in_flat, decay_planes)
    through = (
        jnp.exp(decay_planes * jnp.sum(step_size, axis=0).reshape(1, -1, LANES))
        * jnp.min(keep_flag)
    )
    start_hidden = exchange_states(through, local_end, True)
    scanned, marks = scan_out(
        start_hidden, step_size, activated_low, keep_lanes, in_flat, read_flat, decay_planes
    )
    mamba_out = scanned + skip_row * activated
    gate_act = jax.nn.silu(gate_input)
    gated = (mamba_out * gate_act).astype(jnp.bfloat16)
    first_out = source + product(gated, output_weight)
    second_out, kept_first = mlp_forward(first_out, gains_mlp[0], up_first, down_first)
    normed_attn, factor_attn = norm_apply(second_out, gain_attn)
    context = gather_seq(normed_attn.astype(jnp.bfloat16))
    length = context.shape[0]
    head_weight = jnp.concatenate(
        [
            lax.dynamic_slice(
                attn_weight, (0, part * width + z_index * group_cols), (width, group_cols)
            )
            for part in range(3)
        ],
        axis=1,
    )
    output_rows = lax.dynamic_slice(attn_output, (z_index * group_cols, 0), (group_cols, width))
    cosine, sine_tab = rotary_tables(jnp.arange(length, dtype=jnp.int32))
    block_starts = (jnp.arange(GROUPS, dtype=jnp.int32) * n_x + x_index) * rows_here
    query_pos = (
        block_starts[:, None] + jnp.arange(rows_here, dtype=jnp.int32)[None, :]
    ).reshape(-1)
    first_key = first_allowed(query_pos, lengths)
    lows = jnp.min(first_key.reshape(GROUPS, rows_here), axis=1)
    x_array = x_index.reshape(1).astype(jnp.int32)
    triple = project_heads(context, head_weight, cosine, sine_tab, 2 * group_cols)
    attended, log_total = attend(
        x_array, lows, triple, first_key[:, None], n_x, head_count, rows_here
    )
    attended_own = lax.all_to_all(
        attended.reshape(GROUPS, rows_here, group_cols),
        "seq",
        split_axis=0,
        concat_axis=0,
        axis_index_groups=line_groups(),
        tiled=True,
    )
    attended_low = attended_own.transpose(1, 0, 2).reshape(rows_here, width)
    third_out = second_out + product(attended_low, attn_output)
    final_out, kept_last = mlp_forward(third_out, gains_mlp[1], up_last, down_last)
    output = final_out.astype(jnp.bfloat16)
    grad_low = cotangent[0]
    d_third, g_gain_last, g_up_last, g_down_last = mlp_backward(
        third_out,
        gains_mlp[1],
        up_last,
        down_last,
        kept_last,
        grad_low.astype(jnp.float32),
        gather_rows(grad_low),
    )
    d_third_low = d_third.astype(jnp.bfloat16)
    d_third_line = lax.all_gather(
        d_third_low, "seq", axis=0, tiled=True, axis_index_groups=line_groups()
    )
    d_attended = right_trans(d_third_line, output_rows).astype(jnp.bfloat16)
    g_attn_output = place_out_grad(
        lax.psum_scatter(
            left_trans(attended, d_third_line).astype(jnp.bfloat16),
            ("row", "seq"),
            scatter_dimension=0,
            tiled=True,
            axis_index_groups=plane_groups(),
        )
    ).astype(jnp.float32)
    d_query, d_keys, d_values = attend_back(
        x_array,
        lows,
        triple,
        attended,
        d_attended,
        log_total,
        first_key[:, None],
        cosine,
        sine_tab,
        n_x,
        head_count,
        rows_here,
    )
    own_x = (jnp.arange(n_x) == x_index)[None, :, None, None]
    d_query_full = jnp.where(
        own_x, d_query.reshape(GROUPS, 1, rows_here, group_cols), jnp.bfloat16(0)
    ).reshape(length, group_cols)
    d_triple = jnp.concatenate([d_query_full, d_keys, d_values], axis=1)
    d_attn_normed = reduce_seq(right_trans(d_triple, head_weight).astype(jnp.bfloat16))
    g_attn_weight = (
        place_attn_grad(
            lax.psum_scatter(
                left_trans(d_triple, context).astype(jnp.bfloat16),
                ("row", "seq"),
                scatter_dimension=0,
                tiled=True,
                axis_index_groups=plane_groups(),
            ),
            width,
        )
        .astype(jnp.float32)
        .T
    )
    d_attn_norm, g_attn_gain = norm_back(
        second_out, factor_attn, gain_attn, d_attn_normed.astype(jnp.float32)
    )
    d_second = d_third + d_attn_norm
    d_first, g_gain_first, g_up_first, g_down_first = mlp_backward(
        first_out,
        gains_mlp[0],
        up_first,
        down_first,
        kept_first,
        d_second,
        gather_rows(d_second.astype(jnp.bfloat16)),
    )
    d_first_low = d_first.astype(jnp.bfloat16)
    g_output_weight = weight_term(gated, gather_seq(d_first_low), True)
    d_gated = right_trans(d_first_low, output_weight)
    d_scanned = d_gated * gate_act
    gate_sig = jax.nn.sigmoid(gate_input)
    d_gate = d_gated * mamba_out * gate_sig * (1.0 + gate_input * (1.0 - gate_sig))
    g_skip_scale = jnp.sum(d_scanned * activated, axis=0)
    back_end = adjoint_end(step_size, d_scanned, keep_lanes, read_flat, decay_planes)
    end_grad = exchange_states(through, back_end, False)
    g_step, g_activated, in_lanes, read_lanes, g_decays = adjoint_full(
        end_grad, marks, step_size, activated_low, d_scanned, keep_lanes, in_flat, read_flat, decay_planes
    )
    g_input_map = jnp.sum(in_lanes.reshape(rows_here, state_dim, LANES), axis=2)
    g_read_map = jnp.sum(read_lanes.reshape(rows_here, state_dim, LANES), axis=2)
    g_decay_log = (g_decays.reshape(state_dim, inner_dim) * decays).T
    d_step_pre = g_step * jax.nn.sigmoid(step_pre)
    g_step_bias = jnp.sum(d_step_pre, axis=0)
    d_step_low = d_step_pre.astype(jnp.bfloat16)
    g_step_weight = left_trans(step_low, d_step_low)
    d_picked = jnp.concatenate(
        [right_trans(d_step_low, step_weight), g_input_map, g_read_map], axis=1
    ).astype(jnp.bfloat16)
    g_select_weight = left_trans(activated_low, d_picked)
    d_activated = d_scanned * skip_row + g_activated + right_trans(d_picked, select_weight)
    pre_sig = jax.nn.sigmoid(conv_pre)
    d_conv_pre = d_activated * pre_sig * (1.0 + conv_pre * (1.0 - pre_sig))
    g_conv_bias = jnp.sum(d_conv_pre, axis=0)
    tap_grads = []
    d_padded = jnp.zeros((rows_here + CONV - 1, inner_dim), jnp.float32)
    for tap_index in range(CONV):
        masked = d_conv_pre * tap_masks[tap_index][:, None]
        tap_grads.append(jnp.sum(masked * padded[tap_index : tap_index + rows_here], axis=0))
        d_padded = d_padded + jnp.pad(
            masked * conv_taps[tap_index], ((tap_index, CONV - 1 - tap_index), (0, 0))
        )
    g_conv_weight = jnp.stack(tap_grads, axis=0)
    back_rows = from_behind(d_padded[: CONV - 1].astype(jnp.bfloat16), "seq", -1)
    d_conv_input = d_padded[CONV - 1 :] + jnp.pad(back_rows, ((rows_here - (CONV - 1), 0), (0, 0)))
    d_mixed = jnp.concatenate([d_conv_input, d_gate], axis=1).astype(jnp.bfloat16)
    g_input_weight = weight_term(d_mixed, gather_seq(low_in), False)
    d_normed_in = right_trans(d_mixed, whole_in)
    d_source, g_norm_gain = norm_back(source, factor_in, gain_in, d_normed_in)
    tokens_grad = (d_first + d_source).astype(jnp.bfloat16)

    owners = n_row * n_seq
    small_parts = (
        g_select_weight,
        g_step_weight.T,
        g_decay_log,
        g_conv_weight.T,
        g_conv_bias[:, None],
        g_step_bias[:, None],
        g_skip_scale[:, None],
    )
    gain_parts = (g_norm_gain, g_attn_gain, g_gain_first, g_gain_last)
    packed = jnp.concatenate(
        [part.reshape(owners, -1) for part in small_parts + gain_parts], axis=1
    )
    summed = lax.psum_scatter(packed, ("row", "seq"), scatter_dimension=0, tiled=True)[0]
    small = []
    at = 0
    for part in small_parts + gain_parts:
        size = part.size // owners
        piece = summed[at : at + size]
        small.append(piece.reshape((-1,) + part.shape[1:]))
        at += size
    g_input_weight = lax.psum_scatter(
        g_input_weight.astype(jnp.bfloat16), "row", scatter_dimension=1, tiled=True
    ).astype(jnp.float32)
    g_output_weight = lax.psum_scatter(
        g_output_weight.astype(jnp.bfloat16), "row", scatter_dimension=0, tiled=True
    ).astype(jnp.float32)
    return (
        output[None],
        tokens_grad[None],
        small[7],
        g_input_weight[:, 0],
        small[3].T,
        small[4][:, 0],
        small[0],
        small[1].T,
        small[5][:, 0],
        small[2],
        small[6][:, 0],
        g_output_weight[0],
        small[8],
        g_attn_weight,
        g_attn_output,
        jnp.stack([small[9], small[10]], axis=0),
        jnp.stack([g_up_first, g_up_last], axis=0),
        jnp.stack([g_down_first, g_down_last], axis=0),
    )


def solution(mesh):
    return jax.shard_map(
        per_device,
        mesh=mesh,
        in_specs=(
            P("row", "seq", None),
            P(),
            P("row", None),
            P(),
            P(),
            P(),
            P(),
            P(),
            P(),
            P(),
            P(),
            P(),
            P(),
            P(),
            P(),
            P(None, "row", None),
            P(None, "row", None),
            P("row", None),
            P("row", "seq", None),
        ),
        out_specs=(
            P("row", "seq", None),
            P("row", "seq", None),
            P(("row", "seq")),
            P(None, ("row", "seq")),
            P(None, ("row", "seq")),
            P(("row", "seq")),
            P(("row", "seq"), None),
            P(None, ("row", "seq")),
            P(("row", "seq")),
            P(("row", "seq"), None),
            P(("row", "seq")),
            P(("row", "seq"), None),
            P(("row", "seq")),
            P(None, ("row", "seq")),
            P(("row", "seq"), None),
            P(None, ("row", "seq")),
            P(None, None, ("row", "seq")),
            P(None, ("row", "seq"), None),
        ),
        check_vma=False,
    )
```

```python
import functools
import math

import jax
import jax.numpy as jnp
from jax import lax
from jax.experimental import pallas as pl
from jax.experimental.pallas import tpu as pltpu
from jax.sharding import PartitionSpec as P

LANES = 128
CHUNK = 32
RESET = 1e9
LOG2E = 1.4426950408889634
CONV = 4
HEADS = 12
HEAD_DIM = 128
WINDOW = 2048
GROUPS = 4
eps = 1e-05
rope_base = 10000.0


def from_behind(x, axis, by):
    length = lax.axis_size(axis)
    pairs = [(i, i + by) for i in range(length) if 0 <= i + by < length]
    return lax.ppermute(x, axis, pairs)


def product(left_op, right_op):
    return jnp.dot(left_op, right_op, preferred_element_type=jnp.float32)


def left_trans(left_op, right_op):
    return lax.dot_general(
        left_op, right_op, (((0,), (0,)), ((), ())), preferred_element_type=jnp.float32
    )


def right_trans(left_op, right_op):
    return lax.dot_general(
        left_op, right_op, (((1,), (1,)), ((), ())), preferred_element_type=jnp.float32
    )


def to_planes(tile_ref, value, group):
    for block in range(8):
        tile_ref[pl.ds(group * 64 + block * 8, 8), :] = value[:, block * LANES : (block + 1) * LANES]


def plane(tile_ref, index):
    return tile_ref[pl.ds((index // 8) * 64 + index % 8, 8, stride=8), :]


def tree_sum(terms):
    terms = list(terms)
    while len(terms) > 1:
        terms = [
            terms[i] + terms[i + 1] if i + 1 < len(terms) else terms[i]
            for i in range(0, len(terms), 2)
        ]
    return terms[0]


def scan_forward_kernel(
    with_output, states, chunk, *refs
):
    if with_output:
        (start_ref, step_ref, act_ref, keep_ref, in_ref, read_ref, decay_ref,
         out_ref, marks_ref, hidden_ref, step_t, drive_t, out_t) = refs
    else:
        (step_ref, act_ref, keep_ref, in_ref, decay_ref,
         end_ref, hidden_ref, step_t, drive_t) = refs
    index = pl.program_id(0)
    groups = step_ref.shape[1] // (8 * LANES)

    @pl.when(index == 0)
    def _():
        if with_output:
            hidden_ref[...] = start_ref[...]
        else:
            hidden_ref[...] = jnp.zeros_like(hidden_ref)

    if with_output:
        marks_ref[0] = hidden_ref[...]
    for group in range(groups):
        cols = pl.ds(group * 8 * LANES, 8 * LANES)
        for block in range(chunk // 8):
            rows = pl.ds(block * 8, 8)
            rate = step_ref[rows, cols]
            keep = keep_ref[rows, :]
            gated = jnp.where(jnp.concatenate([keep] * 8, axis=1) > 0, rate, RESET)
            to_planes(step_t, gated, block)
            to_planes(drive_t, rate * act_ref[rows, cols].astype(jnp.float32), block)
        decay = [decay_ref[n, pl.ds(group * 8, 8), :] * LOG2E for n in range(states)]

        def eight(block, hidden):
            hidden = list(hidden)
            for r in range(8):
                pos = index * chunk + block * 8 + r
                rate = step_t[pl.ds(block * 64 + r, 8, stride=8), :]
                drive = drive_t[pl.ds(block * 64 + r, 8, stride=8), :]
                terms = []
                for n in range(states):
                    hidden[n] = jnp.exp2(decay[n] * rate) * hidden[n] + drive * in_ref[pos * states + n]
                    if with_output:
                        terms.append(hidden[n] * read_ref[pos * states + n])
                if with_output:
                    out_t[pl.ds(block * 64 + r, 8, stride=8), :] = tree_sum(terms)
            return tuple(hidden)

        hidden = tuple(hidden_ref[n, pl.ds(group * 8, 8), :] for n in range(states))
        hidden = lax.fori_loop(0, chunk // 8, eight, hidden)
        for n in range(states):
            hidden_ref[n, pl.ds(group * 8, 8), :] = hidden[n]
        if with_output:
            for block in range(chunk // 8):
                for lane_block in range(8):
                    out_ref[pl.ds(block * 8, 8), pl.ds(group * 1024 + lane_block * LANES, LANES)] = out_t[
                        pl.ds(block * 64 + lane_block * 8, 8), :
                    ]
    if not with_output:
        end_ref[...] = hidden_ref[...]


def smem():
    return pl.BlockSpec(memory_space=pltpu.SMEM)


def scan_end(step, act, keep_lanes, in_flat, decay):
    rows, inner = step.shape
    states, planes, _ = decay.shape
    chunk = CHUNK
    whole = pl.BlockSpec((states, planes, LANES), lambda i: (0, 0, 0))
    rowed = pl.BlockSpec((chunk, inner), lambda i: (i, 0))
    return pl.pallas_call(
        functools.partial(scan_forward_kernel, False, states, chunk),
        out_shape=jax.ShapeDtypeStruct(decay.shape, jnp.float32),
        grid=(rows // chunk,),
        in_specs=[rowed, rowed, pl.BlockSpec((chunk, LANES), lambda i: (i, 0)), smem(), whole],
        out_specs=whole,
        scratch_shapes=[pltpu.VMEM(decay.shape, jnp.float32)]
        + [pltpu.VMEM((chunk * 8, LANES), jnp.float32)] * 2,
        compiler_params=pltpu.CompilerParams(vmem_limit_bytes=32 << 20),
        name="scan_end",
    )(step, act, keep_lanes, in_flat, decay)


def scan_out(start, step, act, keep_lanes, in_flat, read_flat, decay):
    rows, inner = step.shape
    states, planes, _ = decay.shape
    chunk = CHUNK
    whole = pl.BlockSpec((states, planes, LANES), lambda i: (0, 0, 0))
    rowed = pl.BlockSpec((chunk, inner), lambda i: (i, 0))
    return pl.pallas_call(
        functools.partial(scan_forward_kernel, True, states, chunk),
        out_shape=(
            jax.ShapeDtypeStruct((rows, inner), jnp.float32),
            jax.ShapeDtypeStruct((rows // chunk,) + decay.shape, jnp.float32),
        ),
        grid=(rows // chunk,),
        in_specs=[whole, rowed, rowed, pl.BlockSpec((chunk, LANES), lambda i: (i, 0)), smem(), smem(), whole],
        out_specs=(rowed, pl.BlockSpec((1, states, planes, LANES), lambda i: (i, 0, 0, 0))),
        scratch_shapes=[pltpu.VMEM(decay.shape, jnp.float32)]
        + [pltpu.VMEM((chunk * 8, LANES), jnp.float32)] * 3,
        compiler_params=pltpu.CompilerParams(vmem_limit_bytes=32 << 20),
        name="scan_out",
    )(start, step, act, keep_lanes, in_flat, read_flat, decay)


def adjoint_end_kernel(states, chunk, step_ref, grad_ref, keep_ref, read_ref, decay_ref, end_ref, carry_ref, step_t, grad_t):
    index = pl.program_id(0)
    last = pl.num_programs(0) - 1
    groups = step_ref.shape[1] // (8 * LANES)

    @pl.when(index == 0)
    def _():
        carry_ref[...] = jnp.zeros_like(carry_ref)

    for group in range(groups):
        cols = pl.ds(group * 8 * LANES, 8 * LANES)
        for block in range(chunk // 8):
            rows = pl.ds(block * 8, 8)
            keep = keep_ref[rows, :]
            to_planes(step_t, jnp.where(jnp.concatenate([keep] * 8, axis=1) > 0, step_ref[rows, cols], RESET), block)
            to_planes(grad_t, grad_ref[rows, cols], block)
        decay = [decay_ref[n, pl.ds(group * 8, 8), :] * LOG2E for n in range(states)]

        def eight(turn, carry):
            carry = list(carry)
            block = chunk // 8 - 1 - turn
            for r in range(7, -1, -1):
                pos = (last - index) * chunk + block * 8 + r
                rate = step_t[pl.ds(block * 64 + r, 8, stride=8), :]
                grad = grad_t[pl.ds(block * 64 + r, 8, stride=8), :]
                for n in range(states):
                    carry[n] = jnp.exp2(decay[n] * rate) * (carry[n] + grad * read_ref[pos * states + n])
            return tuple(carry)

        carry = tuple(carry_ref[n, pl.ds(group * 8, 8), :] for n in range(states))
        carry = lax.fori_loop(0, chunk // 8, eight, carry)
        for n in range(states):
            carry_ref[n, pl.ds(group * 8, 8), :] = carry[n]
    end_ref[...] = carry_ref[...]


def adjoint_end(step, grad, keep_lanes, read_flat, decay):
    rows, inner = step.shape
    states, planes, _ = decay.shape
    chunk = CHUNK
    count = rows // chunk
    whole = pl.BlockSpec((states, planes, LANES), lambda i: (0, 0, 0))
    rowed = pl.BlockSpec((chunk, inner), lambda i: (count - 1 - i, 0))
    return pl.pallas_call(
        functools.partial(adjoint_end_kernel, states, chunk),
        out_shape=jax.ShapeDtypeStruct(decay.shape, jnp.float32),
        grid=(count,),
        in_specs=[rowed, rowed, pl.BlockSpec((chunk, LANES), lambda i: (count - 1 - i, 0)), smem(), whole],
        out_specs=whole,
        scratch_shapes=[pltpu.VMEM(decay.shape, jnp.float32)]
        + [pltpu.VMEM((chunk * 8, LANES), jnp.float32)] * 2,
        compiler_params=pltpu.CompilerParams(vmem_limit_bytes=32 << 20),
        name="adjoint_end",
    )(step, grad, keep_lanes, read_flat, decay)


def adjoint_full_kernel(
    states, chunk,
    end_ref, marks_ref, step_ref, act_ref, grad_ref, keep_ref, in_ref, read_ref, decay_ref,
    d_step_ref, d_act_ref, d_in_ref, d_read_ref, d_decay_ref,
    carry_ref, step_t, rate_t, act_t, grad_t, d_step_t, d_act_t, factor_t, held_t, in_t, read_t,
):
    index = pl.program_id(0)
    last = pl.num_programs(0) - 1
    groups = step_ref.shape[1] // (8 * LANES)

    @pl.when(index == 0)
    def _():
        carry_ref[...] = end_ref[...]
        d_decay_ref[...] = jnp.zeros_like(d_decay_ref)

    for group in range(groups):
        cols = pl.ds(group * 8 * LANES, 8 * LANES)
        for block in range(chunk // 8):
            rows = pl.ds(block * 8, 8)
            rate = step_ref[rows, cols]
            keep = keep_ref[rows, :]
            to_planes(step_t, jnp.where(jnp.concatenate([keep] * 8, axis=1) > 0, rate, RESET), block)
            to_planes(rate_t, rate, block)
            to_planes(act_t, act_ref[rows, cols].astype(jnp.float32), block)
            to_planes(grad_t, grad_ref[rows, cols], block)

        def replay(block, hidden):
            hidden = list(hidden)
            for r in range(8):
                local = block * 8 + r
                pos = (last - index) * chunk + local
                view = pl.ds(block * 64 + r, 8, stride=8)
                gated = step_t[view, :]
                drive = rate_t[view, :] * act_t[view, :]
                grad = grad_t[view, :]
                for n in range(states):
                    slot = pl.ds((local * states + n) * 8, 8)
                    factor = jnp.exp2(decay_ref[n, pl.ds(group * 8, 8), :] * LOG2E * gated)
                    held = factor * hidden[n]
                    hidden[n] = held + drive * in_ref[pos * states + n]
                    factor_t[slot, :] = factor
                    held_t[slot, :] = held
                    if group == 0:
                        read_t[slot, :] = grad * hidden[n]
                    else:
                        read_t[slot, :] += grad * hidden[n]
            return tuple(hidden)

        lax.fori_loop(
            0, chunk // 8, replay,
            tuple(marks_ref[0, n, pl.ds(group * 8, 8), :] for n in range(states)),
        )

        def back(turn, carried):
            carry, d_decay = list(carried[0]), list(carried[1])
            block = chunk // 8 - 1 - turn
            for r in range(7, -1, -1):
                local = block * 8 + r
                pos = (last - index) * chunk + local
                view = pl.ds(block * 64 + r, 8, stride=8)
                rate = rate_t[view, :]
                act = act_t[view, :]
                grad = grad_t[view, :]
                drive = rate * act
                inner_terms = []
                step_terms = []
                for n in range(states):
                    slot = pl.ds((local * states + n) * 8, 8)
                    adjoint = carry[n] + grad * read_ref[pos * states + n]
                    moved = adjoint * held_t[slot, :]
                    step_terms.append(moved * decay_ref[n, pl.ds(group * 8, 8), :])
                    d_decay[n] = d_decay[n] + moved * rate
                    inner_terms.append(adjoint * in_ref[pos * states + n])
                    if group == 0:
                        in_t[slot, :] = adjoint * drive
                    else:
                        in_t[slot, :] += adjoint * drive
                    carry[n] = adjoint * factor_t[slot, :]
                inner_sum = tree_sum(inner_terms)
                d_step_t[view, :] = tree_sum(step_terms) + act * inner_sum
                d_act_t[view, :] = rate * inner_sum
            return (tuple(carry), tuple(d_decay))

        carry, d_decay = lax.fori_loop(
            0, chunk // 8, back,
            (
                tuple(carry_ref[n, pl.ds(group * 8, 8), :] for n in range(states)),
                tuple(d_decay_ref[n, pl.ds(group * 8, 8), :] for n in range(states)),
            ),
        )
        for n in range(states):
            carry_ref[n, pl.ds(group * 8, 8), :] = carry[n]
            d_decay_ref[n, pl.ds(group * 8, 8), :] = d_decay[n]
        for block in range(chunk // 8):
            for lane_block in range(8):
                where = (pl.ds(block * 8, 8), pl.ds(group * 1024 + lane_block * LANES, LANES))
                tile = pl.ds(block * 64 + lane_block * 8, 8)
                d_step_ref[where] = d_step_t[tile, :]
                d_act_ref[where] = d_act_t[tile, :]

    def shrink(block, _):
        for source, target in ((in_t, d_in_ref), (read_t, d_read_ref)):
            total = source[pl.ds(block * 64, 8, stride=8), :]
            for s in range(1, 8):
                total = total + source[pl.ds(block * 64 + s, 8, stride=8), :]
            target[pl.ds(block * 8, 8), :] = total
        return 0

    lax.fori_loop(0, chunk * states // 8, shrink, 0, unroll=4)


def adjoint_full(end_grad, marks, step, act, grad, keep_lanes, in_flat, read_flat, decay):
    rows, inner = step.shape
    states, planes, _ = decay.shape
    chunk = CHUNK
    count = rows // chunk
    whole = pl.BlockSpec((states, planes, LANES), lambda i: (0, 0, 0))
    rowed = pl.BlockSpec((chunk, inner), lambda i: (count - 1 - i, 0))
    maps = pl.BlockSpec((chunk * states, LANES), lambda i: (count - 1 - i, 0))
    big = pltpu.VMEM((chunk * states * 8, LANES), jnp.float32)
    return pl.pallas_call(
        functools.partial(adjoint_full_kernel, states, chunk),
        out_shape=(
            jax.ShapeDtypeStruct((rows, inner), jnp.float32),
            jax.ShapeDtypeStruct((rows, inner), jnp.float32),
            jax.ShapeDtypeStruct((rows * states, LANES), jnp.float32),
            jax.ShapeDtypeStruct((rows * states, LANES), jnp.float32),
            jax.ShapeDtypeStruct(decay.shape, jnp.float32),
        ),
        grid=(count,),
        in_specs=[
            whole,
            pl.BlockSpec((1, states, planes, LANES), lambda i: (count - 1 - i, 0, 0, 0)),
            rowed, rowed, rowed,
            pl.BlockSpec((chunk, LANES), lambda i: (count - 1 - i, 0)),
            smem(), smem(), whole,
        ],
        out_specs=(rowed, rowed, maps, maps, whole),
        scratch_shapes=[pltpu.VMEM(decay.shape, jnp.float32)]
        + [pltpu.VMEM((chunk * 8, LANES), jnp.float32)] * 6
        + [big] * 4,
        compiler_params=pltpu.CompilerParams(vmem_limit_bytes=48 << 20),
        name="adjoint_full",
    )(end_grad, marks, step, act, grad, keep_lanes, in_flat, read_flat, decay)


KEYS = 512


def turn_half(values):
    return pltpu.roll(values, HEAD_DIM // 2, 1)


def project_kernel(rotated, ctx_ref, weight_ref, cos_ref, sin_ref, out_ref):
    cosine, sine = cos_ref[...], sin_ref[...]
    ctx = ctx_ref[...]
    step = 3 * HEAD_DIM
    for start in range(0, weight_ref.shape[1], step):
        triple = product(ctx, weight_ref[:, start : start + step])
        for head in range(0, step, HEAD_DIM):
            part = triple[:, head : head + HEAD_DIM]
            if start + head < rotated:
                part = part * cosine + turn_half(part) * sine
            out_ref[:, start + head : start + head + HEAD_DIM] = part.astype(jnp.bfloat16)


def project_heads(ctx, weight, cosine, sine, rotated):
    length, width = ctx.shape
    columns = weight.shape[1]
    rows = min(256, length)
    return pl.pallas_call(
        functools.partial(project_kernel, rotated),
        out_shape=jax.ShapeDtypeStruct((length, columns), jnp.bfloat16),
        grid=(length // rows,),
        in_specs=[
            pl.BlockSpec((rows, width), lambda i: (i, 0)),
            pl.BlockSpec((width, columns), lambda i: (0, 0)),
            pl.BlockSpec((rows, HEAD_DIM), lambda i: (i, 0)),
            pl.BlockSpec((rows, HEAD_DIM), lambda i: (i, 0)),
        ],
        out_specs=pl.BlockSpec((rows, columns), lambda i: (i, 0)),
        compiler_params=pltpu.CompilerParams(vmem_limit_bytes=40 << 20),
        cost_estimate=pl.CostEstimate(
            flops=2 * length * width * columns, bytes_accessed=2 * (length * width + width * columns), transcendentals=0
        ),
        name="project_heads",
    )(ctx, weight, cosine, sine)


def mask_keys(scores_shape, chunk, first_key, q_pos):
    key_pos = chunk * KEYS + lax.broadcasted_iota(jnp.int32, scores_shape, 1)
    return (key_pos >= first_key) & (key_pos <= q_pos)


def attend_kernel(
    n_x, heads, scale, x_ref, low_ref, q_ref, k_ref, v_ref, first_ref, out_ref, lse_ref, score_t
):
    block = pl.program_id(1)
    rows = q_ref.shape[0]
    base = (block * n_x + x_ref[0]) * rows
    low_chunk = low_ref[block] // KEYS
    high_chunk = (base + rows - 1) // KEYS + 1
    q_pos = base + lax.broadcasted_iota(jnp.int32, (rows, KEYS), 0)
    first_key = first_ref[...]
    query = q_ref[...]

    def scores_of(chunk, top):
        where = pl.ds(pl.multiple_of(chunk * KEYS, KEYS), KEYS)
        scores = right_trans(query, k_ref[where, :]) * scale
        scores = jnp.where(mask_keys(scores.shape, chunk, first_key, q_pos), scores, -1e30)
        score_t[:, where] = scores
        for part in range(0, KEYS, LANES):
            top = jnp.maximum(top, scores[:, part : part + LANES])
        return top

    top = lax.fori_loop(low_chunk, high_chunk, scores_of, jnp.full((rows, LANES), -1e30, jnp.float32))
    top = jnp.max(top, axis=1, keepdims=True)

    def weigh(chunk, carried):
        total, mixed = carried
        where = pl.ds(pl.multiple_of(chunk * KEYS, KEYS), KEYS)
        weights = jnp.exp2(score_t[:, where] - top)
        for part in range(0, KEYS, LANES):
            total = total + weights[:, part : part + LANES]
        return (total, mixed + product(weights.astype(jnp.bfloat16), v_ref[where, :]))

    total, mixed = lax.fori_loop(
        low_chunk,
        high_chunk,
        weigh,
        (jnp.zeros((rows, LANES), jnp.float32), jnp.zeros((rows, HEAD_DIM), jnp.float32)),
    )
    total = jnp.sum(total, axis=1, keepdims=True)
    out_ref[...] = (mixed / total).astype(jnp.bfloat16)
    lse_ref[0] = top + jnp.log2(total)


def attend(x_index, lows, triple, first_key, n_x, heads, rows):
    length = triple.shape[0]
    blocks = length // (rows * n_x)
    scale = HEAD_DIM ** (-0.5) * LOG2E
    return pl.pallas_call(
        functools.partial(attend_kernel, n_x, heads, scale),
        out_shape=(
            jax.ShapeDtypeStruct((blocks * rows, heads * HEAD_DIM), jnp.bfloat16),
            jax.ShapeDtypeStruct((heads, blocks * rows, 1), jnp.float32),
        ),
        grid_spec=pltpu.PrefetchScalarGridSpec(
            num_scalar_prefetch=2,
            grid=(heads, blocks),
            in_specs=[
                pl.BlockSpec((rows, HEAD_DIM), lambda h, b, x, low: (b * n_x + x[0], h)),
                pl.BlockSpec((length, HEAD_DIM), lambda h, b, x, low: (0, heads + h)),
                pl.BlockSpec((length, HEAD_DIM), lambda h, b, x, low: (0, 2 * heads + h)),
                pl.BlockSpec((rows, 1), lambda h, b, x, low: (b, 0)),
            ],
            out_specs=(
                pl.BlockSpec((rows, HEAD_DIM), lambda h, b, x, low: (b, h)),
                pl.BlockSpec((1, rows, 1), lambda h, b, x, low: (h, b, 0)),
            ),
            scratch_shapes=[pltpu.VMEM((rows, length), jnp.float32)],
        ),
        compiler_params=pltpu.CompilerParams(vmem_limit_bytes=40 << 20),
        cost_estimate=pl.CostEstimate(
            flops=2 * heads * blocks * rows * length * HEAD_DIM, bytes_accessed=4 * length * heads * HEAD_DIM, transcendentals=0
        ),
        name="attend",
    )(x_index, lows, triple, triple, triple, first_key)


def attend_back_kernel(
    n_x, heads, scale,
    x_ref, low_ref, q_ref, k_ref, v_ref, out_ref, d_ref, lse_ref, first_ref, cos_ref, sin_ref, cos_all, sin_all,
    dq_ref, dk_ref, dv_ref, dk_t, dv_t,
):
    block = pl.program_id(1)
    rows = q_ref.shape[0]
    base = (block * n_x + x_ref[0]) * rows
    low_chunk = low_ref[block] // KEYS
    high_chunk = (base + rows - 1) // KEYS + 1
    q_pos = base + lax.broadcasted_iota(jnp.int32, (rows, KEYS), 0)
    first_key = first_ref[...]
    query = q_ref[...]
    d_out = d_ref[...]
    log_total = lse_ref[0]
    center = jnp.sum(d_out.astype(jnp.float32) * out_ref[...].astype(jnp.float32), axis=1, keepdims=True)

    @pl.when(block == 0)
    def _():
        dk_t[...] = jnp.zeros_like(dk_t)
        dv_t[...] = jnp.zeros_like(dv_t)

    def one(chunk, d_query):
        where = pl.ds(pl.multiple_of(chunk * KEYS, KEYS), KEYS)
        keys = k_ref[where, :]
        scores = right_trans(query, keys) * scale
        allowed = mask_keys(scores.shape, chunk, first_key, q_pos)
        weights = jnp.where(allowed, jnp.exp2(scores - log_total), 0.0)
        d_soft = right_trans(d_out, v_ref[where, :])
        d_scores = (weights * (d_soft - center)).astype(jnp.bfloat16)
        dv_t[where, :] += left_trans(weights.astype(jnp.bfloat16), d_out)
        dk_t[where, :] += left_trans(d_scores, query)
        return d_query + product(d_scores, keys)

    d_query = lax.fori_loop(low_chunk, high_chunk, one, jnp.zeros((rows, HEAD_DIM), jnp.float32))
    inv_scale = HEAD_DIM ** (-0.5)
    d_query = d_query * inv_scale
    dq_ref[...] = (d_query * cos_ref[...] - turn_half(d_query) * sin_ref[...]).astype(jnp.bfloat16)

    @pl.when(block == pl.num_programs(1) - 1)
    def _():
        def finish(chunk, _):
            where = pl.ds(pl.multiple_of(chunk * KEYS, KEYS), KEYS)
            d_keys = dk_t[where, :] * inv_scale
            dk_ref[where, :] = (d_keys * cos_all[where, :] - turn_half(d_keys) * sin_all[where, :]).astype(jnp.bfloat16)
            dv_ref[where, :] = dv_t[where, :].astype(jnp.bfloat16)
            return 0

        lax.fori_loop(0, k_ref.shape[0] // KEYS, finish, 0)


def attend_back(x_index, lows, triple, attended, d_attended, lse, first_key, cosine, sine, n_x, heads, rows):
    length = triple.shape[0]
    blocks = length // (rows * n_x)
    scale = HEAD_DIM ** (-0.5) * LOG2E
    q_spec = pl.BlockSpec((rows, HEAD_DIM), lambda h, b, x, low: (b * n_x + x[0], h))
    own = pl.BlockSpec((rows, HEAD_DIM), lambda h, b, x, low: (b, h))
    table_q = pl.BlockSpec((rows, HEAD_DIM), lambda h, b, x, low: (b * n_x + x[0], 0))
    table = pl.BlockSpec((length, HEAD_DIM), lambda h, b, x, low: (0, 0))
    column = pl.BlockSpec((length, HEAD_DIM), lambda h, b, x, low: (0, h))
    return pl.pallas_call(
        functools.partial(attend_back_kernel, n_x, heads, scale),
        out_shape=(
            jax.ShapeDtypeStruct((blocks * rows, heads * HEAD_DIM), jnp.bfloat16),
            jax.ShapeDtypeStruct((length, heads * HEAD_DIM), jnp.bfloat16),
            jax.ShapeDtypeStruct((length, heads * HEAD_DIM), jnp.bfloat16),
        ),
        grid_spec=pltpu.PrefetchScalarGridSpec(
            num_scalar_prefetch=2,
            grid=(heads, blocks),
            in_specs=[
                q_spec,
                pl.BlockSpec((length, HEAD_DIM), lambda h, b, x, low: (0, heads + h)),
                pl.BlockSpec((length, HEAD_DIM), lambda h, b, x, low: (0, 2 * heads + h)),
                own,
                own,
                pl.BlockSpec((1, rows, 1), lambda h, b, x, low: (h, b, 0)),
                pl.BlockSpec((rows, 1), lambda h, b, x, low: (b, 0)),
                table_q,
                table_q,
                table,
                table,
            ],
            out_specs=(own, column, column),
            scratch_shapes=[pltpu.VMEM((length, HEAD_DIM), jnp.float32)] * 2,
        ),
        compiler_params=pltpu.CompilerParams(vmem_limit_bytes=40 << 20),
        cost_estimate=pl.CostEstimate(
            flops=5 * heads * blocks * rows * length * HEAD_DIM, bytes_accessed=8 * length * heads * HEAD_DIM, transcendentals=0
        ),
        name="attend_back",
    )(x_index, lows, triple, triple, triple, attended, d_attended, lse, first_key, cosine, sine, cosine, sine)


MESH = pl.DeviceIdType.MESH


def greet(peers):
    barrier = pltpu.get_barrier_semaphore()
    for peer in peers:
        pl.semaphore_signal(barrier, inc=1, device_id=peer, device_id_type=MESH)
    pl.semaphore_wait(barrier, len(peers))


def send(source, target, send_sem, recv_sem, peer):
    return pltpu.make_async_remote_copy(
        src_ref=source,
        dst_ref=target,
        send_sem=send_sem,
        recv_sem=recv_sem,
        device_id=peer,
        device_id_type=MESH,
    )


def span(start, size):
    return pl.ds(pl.multiple_of(start, 16), size)


def ring_place(seq, n_x):
    z, x = seq // n_x, lax.rem(seq, n_x)
    side = lax.min(x, 1)
    turn = GROUPS - 1 - z
    odd = lax.rem(turn, 2)
    back = GROUPS + turn * (n_x - 1) + (1 - odd) * (x - 1) + odd * (n_x - 1 - x)
    return (1 - side) * z + side * back


def ring_member(place, n_x):
    side = lax.min(place // GROUPS, 1)
    late = lax.max(place - GROUPS, 0)
    turn = late // (n_x - 1)
    step = lax.rem(late, n_x - 1)
    odd = lax.rem(turn, 2)
    x = (1 - odd) * (1 + step) + odd * (n_x - 1 - step)
    return (1 - side) * place * n_x + side * ((GROUPS - 1 - turn) * n_x + x)


def remote_params(collective, limit):
    return pltpu.CompilerParams(
        collective_id=collective, has_side_effects=True, vmem_limit_bytes=limit << 20
    )


def vmem():
    return pl.BlockSpec(memory_space=pltpu.VMEM)


def gather_rows_kernel(n_row, parts, x_ref, out_ref, send_y, recv_y, send_f, recv_f, own_sem):
    row, seq = lax.axis_index("row"), lax.axis_index("seq")
    y, core = row // 2, lax.rem(row, 2)
    n_y = n_row // 2
    rows = x_ref.shape[0]
    piece = rows // parts
    sibling = (y * 2 + 1 - core, seq)
    across = [(lax.rem(y + d, n_y) * 2 + core, seq) for d in range(1, n_y)]
    greet([sibling] + across)
    pending = []
    for d in range(n_y - 1):
        for c in range(parts):
            copy = send(
                x_ref.at[pl.ds(c * piece, piece)],
                out_ref.at[span(row * rows + c * piece, piece)],
                send_y.at[d, c],
                recv_y.at[d, c],
                across[d],
            )
            copy.start()
            pending.append(copy)
    own = send(x_ref, out_ref.at[span(row * rows, rows)], own_sem.at[0], own_sem.at[1], sibling)
    own.start()
    out_ref[span(row * rows, rows), :] = x_ref[...]
    forwards = []
    for d in range(n_y - 1):
        origin = lax.rem(y + n_y - 1 - d, n_y) * 2 + core
        for c in range(parts):
            pending[d * parts + c].wait_recv()
            where = out_ref.at[span(origin * rows + c * piece, piece)]
            copy = send(where, where, send_f.at[d, c], recv_f.at[d, c], sibling)
            copy.start()
            forwards.append(copy)
    own.wait()
    for copy in pending:
        copy.wait_send()
    for copy in forwards:
        copy.wait()


def gather_rows(block, collective=1):
    n_row = lax.axis_size("row")
    rows, width = block.shape
    parts = 4 if rows % 64 == 0 else 1
    n_y = n_row // 2
    return pl.pallas_call(
        functools.partial(gather_rows_kernel, n_row, parts),
        out_shape=jax.ShapeDtypeStruct((n_row * rows, width), block.dtype),
        in_specs=[vmem()],
        out_specs=vmem(),
        scratch_shapes=[pltpu.SemaphoreType.DMA((n_y - 1, parts))] * 4
        + [pltpu.SemaphoreType.DMA((2,))],
        compiler_params=remote_params(collective, 40),
        name="gather_rows",
    )(block)


def reduce_rows_kernel(
    n_row, parts, x_ref, out_ref, near, stage, far, send_c, recv_c, send_y, recv_y
):
    row, seq = lax.axis_index("row"), lax.axis_index("seq")
    y, core = row // 2, lax.rem(row, 2)
    n_y = n_row // 2
    rows = out_ref.shape[0]
    piece = rows // parts
    other = 1 - core
    sibling = (y * 2 + other, seq)
    across = [(lax.rem(y + d, n_y) * 2 + core, seq) for d in range(1, n_y)]
    greet([sibling] + across)
    order = [(d + 1) % n_y for d in range(n_y)]
    crossing = {}
    for d in order:
        block = lax.rem(y + d, n_y)
        for c in range(parts):
            copy = send(
                x_ref.at[span((block * 2 + other) * rows + c * piece, piece)],
                near.at[d, pl.ds(c * piece, piece)],
                send_c.at[d, c],
                recv_c.at[d, c],
                sibling,
            )
            copy.start()
            crossing[d, c] = copy
    sent = {}
    for d in order[:-1]:
        block = lax.rem(y + d, n_y)
        for c in range(parts):
            crossing[d, c].wait_recv()
            where = pl.ds(c * piece, piece)
            total = x_ref[span((block * 2 + core) * rows + c * piece, piece), :].astype(
                jnp.float32
            ) + near[d, where, :].astype(jnp.float32)
            stage[d - 1, where, :] = total.astype(stage.dtype)
            copy = send(
                stage.at[d - 1, where],
                far.at[d - 1, where],
                send_y.at[d - 1, c],
                recv_y.at[d - 1, c],
                across[d - 1],
            )
            copy.start()
            sent[d, c] = copy
    for c in range(parts):
        where = pl.ds(c * piece, piece)
        crossing[0, c].wait_recv()
        total = x_ref[span(row * rows + c * piece, piece), :].astype(jnp.float32) + near[
            0, where, :
        ].astype(jnp.float32)
        for d in order[:-1]:
            sent[d, c].wait_recv()
            total = total + far[d - 1, where, :].astype(jnp.float32)
        out_ref[where, :] = total.astype(out_ref.dtype)
    for copy in crossing.values():
        copy.wait_send()
    for copy in sent.values():
        copy.wait_send()


def reduce_rows(partial, collective=2, dtype=jnp.float32):
    n_row = lax.axis_size("row")
    n_y = n_row // 2
    rows, width = partial.shape[0] // n_row, partial.shape[1]
    parts = 4 if rows % 64 == 0 else 2 if rows % 32 == 0 else 1
    buffer = (rows, width)
    return pl.pallas_call(
        functools.partial(reduce_rows_kernel, n_row, parts),
        out_shape=jax.ShapeDtypeStruct(buffer, dtype),
        in_specs=[vmem()],
        out_specs=vmem(),
        scratch_shapes=[
            pltpu.VMEM((n_y,) + buffer, partial.dtype),
            pltpu.VMEM((n_y - 1,) + buffer, partial.dtype),
            pltpu.VMEM((n_y - 1,) + buffer, partial.dtype),
        ]
        + [pltpu.SemaphoreType.DMA((n_y, parts))] * 2
        + [pltpu.SemaphoreType.DMA((n_y - 1, parts))] * 2,
        compiler_params=remote_params(collective, 40),
        name="reduce_rows",
    )(partial)


def ring_neighbours(n_seq):
    n_x = n_seq // GROUPS
    row, seq = lax.axis_index("row"), lax.axis_index("seq")
    place = ring_place(seq, n_x)
    after = (row, ring_member(lax.rem(place + 1, n_seq), n_x))
    before = (row, ring_member(lax.rem(place + n_seq - 1, n_seq), n_x))
    return row, seq, place, after, before


def ring_gather(n_seq, parts, rows, out_ref, send_sem, recv_sem, place, after, before):
    n_x = n_seq // GROUPS
    half = rows // 2
    piece = half // parts
    sent = {}
    for step in range(n_seq - 1):
        for c in range(parts):
            for way in range(2):
                if step:
                    sent[step - 1, c, way].wait_recv()
                shift = n_seq - step if way == 0 else step
                member = ring_member(lax.rem(place + shift, n_seq), n_x)
                where = out_ref.at[span(member * rows + way * half + c * piece, piece)]
                copy = send(
                    where,
                    where,
                    send_sem.at[way, step, c],
                    recv_sem.at[way, step, c],
                    after if way == 0 else before,
                )
                copy.start()
                sent[step, c, way] = copy
    for c in range(parts):
        for way in range(2):
            sent[n_seq - 2, c, way].wait_recv()
    for copy in sent.values():
        copy.wait_send()


def gather_seq_kernel(n_seq, parts, x_ref, out_ref, send_sem, recv_sem):
    _, seq, place, after, before = ring_neighbours(n_seq)
    rows = x_ref.shape[0]
    greet([after, before])
    out_ref[span(seq * rows, rows), :] = x_ref[...]
    ring_gather(n_seq, parts, rows, out_ref, send_sem, recv_sem, place, after, before)


def gather_seq(block, collective=3):
    n_seq = lax.axis_size("seq")
    rows, width = block.shape
    parts = 2 if rows % 64 == 0 else 1
    return pl.pallas_call(
        functools.partial(gather_seq_kernel, n_seq, parts),
        out_shape=jax.ShapeDtypeStruct((n_seq * rows, width), block.dtype),
        in_specs=[vmem()],
        out_specs=vmem(),
        scratch_shapes=[pltpu.SemaphoreType.DMA((2, n_seq - 1, parts))] * 2,
        compiler_params=remote_params(collective, 48),
        name="gather_seq",
    )(block)


def reduce_seq_kernel(n_seq, parts, x_ref, out_ref, held, send_sem, recv_sem):
    n_x = n_seq // GROUPS
    _, seq, place, after, before = ring_neighbours(n_seq)
    rows = out_ref.shape[0]
    half = rows // 2
    piece = half // parts
    greet([after, before])
    sent = {}
    for step in range(n_seq - 1):
        for c in range(parts):
            for way in range(2):
                shift = 2 * n_seq - 1 - step if way == 0 else 1 + step
                member = ring_member(lax.rem(place + shift, n_seq), n_x)
                own = span(member * rows + way * half + c * piece, piece)
                where = pl.ds(c * piece, piece)
                if step:
                    sent[step - 1, c, way].wait_recv()
                    held[way, step - 1, where, :] = (
                        held[way, step - 1, where, :].astype(jnp.float32)
                        + x_ref[own, :].astype(jnp.float32)
                    ).astype(held.dtype)
                    source = held.at[way, step - 1, where]
                else:
                    source = x_ref.at[own]
                copy = send(
                    source,
                    held.at[way, step, where],
                    send_sem.at[way, step, c],
                    recv_sem.at[way, step, c],
                    after if way == 0 else before,
                )
                copy.start()
                sent[step, c, way] = copy
    for c in range(parts):
        for way in range(2):
            sent[n_seq - 2, c, way].wait_recv()
            where = pl.ds(c * piece, piece)
            start = way * half + c * piece
            out_ref[pl.ds(start, piece), :] = (
                held[way, n_seq - 2, where, :].astype(jnp.float32)
                + x_ref[span(seq * rows + start, piece), :].astype(jnp.float32)
            ).astype(out_ref.dtype)
    for copy in sent.values():
        copy.wait_send()


def reduce_seq(partial, collective=4, dtype=jnp.float32):
    n_seq = lax.axis_size("seq")
    rows, width = partial.shape[0] // n_seq, partial.shape[1]
    if rows % 32:
        return lax.psum_scatter(partial, "seq", scatter_dimension=0, tiled=True).astype(dtype)
    parts = 2 if rows % 64 == 0 else 1
    return pl.pallas_call(
        functools.partial(reduce_seq_kernel, n_seq, parts),
        out_shape=jax.ShapeDtypeStruct((rows, width), dtype),
        in_specs=[vmem()],
        out_specs=vmem(),
        scratch_shapes=[pltpu.VMEM((2, n_seq - 1, rows // 2, width), partial.dtype)]
        + [pltpu.SemaphoreType.DMA((2, n_seq - 1, parts))] * 2,
        compiler_params=remote_params(collective, 48),
        name="reduce_seq",
    )(partial)


def exchange_kernel(n_seq, forward, x_ref, decay_ref, out_ref, all_ref, send_sem, recv_sem):
    _, seq, place, after, before = ring_neighbours(n_seq)
    rows = x_ref.shape[0]
    states, planes, _ = decay_ref.shape
    greet([after, before])
    all_ref[span(seq * rows, rows), :] = x_ref[...]
    ring_gather(n_seq, 1, rows, all_ref, send_sem, recv_sem, place, after, before)
    out_ref[...] = jnp.zeros_like(out_ref)

    def take(turn, _):
        other = turn if forward else n_seq - 1 - turn
        used = other < seq if forward else other > seq
        block = all_ref[span(other * rows, rows), :].astype(jnp.float32)
        base = states * planes
        summed = block[base : base + planes] + block[base + planes : base + 2 * planes]
        for n in range(states):
            kept = jnp.exp(decay_ref[n] * summed) * out_ref[n]
            ended = block[n * planes : (n + 1) * planes]
            out_ref[n] = jnp.where(used, kept + ended, out_ref[n])
        return 0

    lax.fori_loop(0, n_seq, take, 0)


def exchange_states(summed, end_state, decay, forward, collective):
    n_seq = lax.axis_size("seq")
    states, planes, _ = decay.shape
    high = summed.astype(jnp.bfloat16)
    lower = (summed - high.astype(jnp.float32)).astype(jnp.bfloat16)
    rows = -(-(states + 2) * planes // 32) * 32
    payload = jnp.concatenate(
        [
            end_state.astype(jnp.bfloat16).reshape(states * planes, LANES),
            high,
            lower,
            jnp.zeros((rows - (states + 2) * planes, LANES), jnp.bfloat16),
        ],
        axis=0,
    )
    return pl.pallas_call(
        functools.partial(exchange_kernel, n_seq, forward),
        out_shape=jax.ShapeDtypeStruct(decay.shape, jnp.float32),
        in_specs=[vmem(), vmem()],
        out_specs=vmem(),
        scratch_shapes=[pltpu.VMEM((n_seq * rows, LANES), jnp.bfloat16)]
        + [pltpu.SemaphoreType.DMA((2, n_seq - 1, 1))] * 2,
        compiler_params=remote_params(collective, 32),
        name="exchange_states",
    )(payload, decay)


def collect_heads_kernel(n_x, x_ref, out_ref, send_sem, recv_sem):
    row, seq = lax.axis_index("row"), lax.axis_index("seq")
    z, x = seq // n_x, lax.rem(seq, n_x)
    rows, cols = out_ref.shape[0], x_ref.shape[1]
    peers = [lax.rem(z + d, GROUPS) for d in range(1, GROUPS)]
    greet([(row, peer * n_x + x) for peer in peers])
    mine = pl.ds(pl.multiple_of(z * cols, LANES), cols)
    sent = []
    for d, peer in enumerate(peers):
        copy = send(
            x_ref.at[span(peer * rows, rows)],
            out_ref.at[:, mine],
            send_sem.at[d],
            recv_sem.at[d],
            (row, peer * n_x + x),
        )
        copy.start()
        sent.append(copy)
    out_ref[:, mine] = x_ref[span(z * rows, rows), :]
    for copy in sent:
        copy.wait()


def spread_heads_kernel(n_x, x_ref, out_ref, send_sem, recv_sem):
    row, seq = lax.axis_index("row"), lax.axis_index("seq")
    z, x = seq // n_x, lax.rem(seq, n_x)
    rows, cols = x_ref.shape[0], out_ref.shape[1]
    peers = [lax.rem(z + d, GROUPS) for d in range(1, GROUPS)]
    greet([(row, peer * n_x + x) for peer in peers])
    mine = span(z * rows, rows)
    sent = []
    for d, peer in enumerate(peers):
        copy = send(
            x_ref.at[:, pl.ds(pl.multiple_of(peer * cols, LANES), cols)],
            out_ref.at[mine],
            send_sem.at[d],
            recv_sem.at[d],
            (row, peer * n_x + x),
        )
        copy.start()
        sent.append(copy)
    out_ref[mine, :] = x_ref[:, pl.ds(pl.multiple_of(z * cols, LANES), cols)]
    for copy in sent:
        copy.wait()


def swap_heads(values, collect, collective):
    n_x = lax.axis_size("seq") // GROUPS
    rows, cols = values.shape
    shape = (rows // GROUPS, cols * GROUPS) if collect else (rows * GROUPS, cols // GROUPS)
    return pl.pallas_call(
        functools.partial(collect_heads_kernel if collect else spread_heads_kernel, n_x),
        out_shape=jax.ShapeDtypeStruct(shape, values.dtype),
        in_specs=[vmem()],
        out_specs=vmem(),
        scratch_shapes=[pltpu.SemaphoreType.DMA((GROUPS - 1,))] * 2,
        compiler_params=remote_params(collective, 32),
        name="collect_heads" if collect else "spread_heads",
    )(values)


def swap_seq_kernel(n_seq, x_ref, out_ref, send_sem, recv_sem):
    row, seq = lax.axis_index("row"), lax.axis_index("seq")
    peers = [lax.rem(seq + d, n_seq) for d in range(1, n_seq)]
    greet([(row, peer) for peer in peers])
    sent = []
    for d, peer in enumerate(peers):
        copy = send(x_ref.at[peer], out_ref.at[seq], send_sem.at[d], recv_sem.at[d], (row, peer))
        copy.start()
        sent.append(copy)
    out_ref[seq] = x_ref[seq]
    for copy in sent:
        copy.wait()


def swap_seq(blocks, collective):
    n_seq = lax.axis_size("seq")
    return pl.pallas_call(
        functools.partial(swap_seq_kernel, n_seq),
        out_shape=jax.ShapeDtypeStruct(blocks.shape, blocks.dtype),
        in_specs=[vmem()],
        out_specs=vmem(),
        scratch_shapes=[pltpu.SemaphoreType.DMA((n_seq - 1,))] * 2,
        compiler_params=remote_params(collective, 32),
        name="swap_seq",
    )(blocks)


def gather_input_kernel(
    parts, x_ref, out_ref, local_sem, own_sem, send_y, recv_y, send_f, recv_f, send_x, recv_x, send_g, recv_g
):
    row, seq = lax.axis_index("row"), lax.axis_index("seq")
    y, core = row // 2, lax.rem(row, 2)
    z, x = seq // 2, lax.rem(seq, 2)
    rows = x_ref.shape[0]
    half = rows // 2
    piece = half // parts
    sibling = (y * 2 + 1 - core, seq)
    over_y = ((1 - y) * 2 + core, seq)
    over_x = (row, z * 2 + 1 - x)
    greet([sibling, over_y, over_x])
    origin = (1 - y) * 2 + core
    first = []
    for c in range(parts):
        copy = send(
            x_ref.at[span(x * half + c * piece, piece)],
            out_ref.at[span(row * rows + x * half + c * piece, piece)],
            send_y.at[c],
            recv_y.at[c],
            over_y,
        )
        copy.start()
        first.append(copy)
    own = send(x_ref, out_ref.at[span(row * rows, rows)], own_sem.at[0], own_sem.at[1], sibling)
    own.start()
    local = pltpu.make_async_copy(x_ref, out_ref.at[span(row * rows, rows)], local_sem)
    local.start()
    rest = []
    side = []
    for c in range(parts):
        first[c].wait_recv()
        where = out_ref.at[span(origin * rows + x * half + c * piece, piece)]
        copy = send(where, where, send_x.at[c], recv_x.at[c], over_x)
        copy.start()
        side.append(copy)
        copy = send(where, where, send_f.at[c], recv_f.at[c], sibling)
        copy.start()
        rest.append(copy)
    for c in range(parts):
        side[c].wait_recv()
        where = out_ref.at[span(origin * rows + (1 - x) * half + c * piece, piece)]
        copy = send(where, where, send_g.at[c], recv_g.at[c], sibling)
        copy.start()
        rest.append(copy)
    local.wait()
    own.wait()
    for copy in first + side:
        copy.wait_send()
    for copy in rest:
        copy.wait()


def gather_input(shard, collective):
    n_row, n_seq = lax.axis_size("row"), lax.axis_size("seq")
    if n_row != 4 or n_seq != 2 * GROUPS:
        return lax.all_gather(shard, "row", axis=0, tiled=True)
    parts = 4
    sem = pltpu.SemaphoreType.DMA
    return pl.pallas_call(
        functools.partial(gather_input_kernel, parts),
        out_shape=jax.ShapeDtypeStruct((n_row * shard.shape[0], shard.shape[1]), shard.dtype),
        in_specs=[pl.BlockSpec(memory_space=pl.ANY)],
        out_specs=pl.BlockSpec(memory_space=pl.ANY),
        scratch_shapes=[sem, sem((2,))] + [sem((parts,))] * 8,
        compiler_params=remote_params(collective, 16),
        name="gather_input",
    )(shard)


def plane_groups():
    n_seq = lax.axis_size("seq")
    n_x = n_seq // GROUPS
    n_row = lax.axis_size("row")
    return [
        [r * n_seq + z * n_x + x for r in range(n_row) for x in range(n_x)] for z in range(GROUPS)
    ]


def swap_rows(values):
    n_row = lax.axis_size("row")
    row = lax.axis_index("row")
    rows, columns = values.shape
    owned = columns // n_row
    whole = jnp.zeros((n_row * rows, owned), values.dtype)
    for turn in range(n_row):
        other = row ^ turn
        piece = lax.dynamic_slice(values, (0, other * owned), (rows, owned))
        if turn:
            piece = lax.ppermute(piece, "row", [(i, i ^ turn) for i in range(n_row)])
        whole = lax.dynamic_update_slice(whole, piece, (other * rows, 0))
    return whole


def reduce_background(parts):
    n_seq = lax.axis_size("seq")
    shaped = [part.astype(jnp.bfloat16).reshape(n_seq, -1, part.shape[1]) for part in parts]
    merged = jnp.concatenate(shaped, axis=1)
    merged = merged.reshape(-1, merged.shape[2])
    summed = lax.psum_scatter(merged, "seq", scatter_dimension=0, tiled=True)
    pieces = []
    at = 0
    for part in shaped:
        pieces.append(summed[at : at + part.shape[1]])
        at += part.shape[1]
    return pieces


def owner_blocks(half):
    n_row, n_seq = lax.axis_size("row"), lax.axis_size("seq")
    rows, columns = half.shape
    owned = columns // (n_row // 2 * n_seq)
    shaped = half.reshape(rows, n_row // 2, n_seq, owned).transpose(2, 0, 1, 3)
    return shaped.reshape(n_seq, rows, n_row // 2 * owned)


def input_term(spread, gathered):
    flat = spread.reshape(-1, spread.shape[2])
    return left_trans(flat, gathered).astype(jnp.bfloat16)


def swap_seq_async(blocks):
    n_seq = lax.axis_size("seq")
    seq = lax.axis_index("seq")
    whole = jnp.zeros_like(blocks)
    for turn in range(n_seq):
        other = seq ^ turn
        piece = lax.dynamic_index_in_dim(blocks, other, 0)
        if turn:
            piece = lax.ppermute(piece, "seq", [(i, i ^ turn) for i in range(n_seq)])
        whole = lax.dynamic_update_slice(whole, piece, (other, 0, 0))
    return whole


def norm_apply(values, gain_row):
    factor = lax.rsqrt(jnp.mean(values * values, axis=-1, keepdims=True) + eps)
    return (values * factor * gain_row, factor)


def norm_back(values, factor, gain_row, upstream):
    normed = values * factor
    weighted = upstream * gain_row
    gain_grad = jnp.sum(upstream * normed, axis=0)
    value_grad = factor * (weighted - normed * jnp.mean(weighted * normed, axis=-1, keepdims=True))
    return (value_grad, gain_grad)


def doc_index(positions, lengths):
    ends_at = jnp.cumsum(lengths)
    return jnp.sum((positions[:, None] >= ends_at[None, :]).astype(jnp.int32), axis=1)


def first_allowed(positions, lengths):
    ends_at = jnp.cumsum(lengths)
    begins = jnp.max(jnp.where(positions[:, None] >= ends_at[None, :], ends_at[None, :], 0), axis=1)
    return jnp.maximum(begins, positions - (WINDOW - 1)).astype(jnp.int32)


def conv_masks(positions, lengths):
    own_doc = doc_index(positions, lengths)
    rows_out = []
    for tap_index in range(CONV):
        earlier = positions - (CONV - 1) + tap_index
        rows_out.append(
            ((earlier >= 0) & (doc_index(earlier, lengths) == own_doc)).astype(jnp.float32)
        )
    return jnp.stack(rows_out, axis=0)


def rotary_tables(positions):
    half_dim = HEAD_DIM // 2
    frequency = jnp.power(rope_base, -2.0 * jnp.arange(half_dim).astype(jnp.float32) / HEAD_DIM)
    angles = positions.astype(jnp.float32)[:, None] * frequency[None, :]
    cosine, sine_tab = (jnp.cos(angles), jnp.sin(angles))
    return (
        jnp.concatenate([cosine, cosine], axis=1),
        jnp.concatenate([-sine_tab, sine_tab], axis=1),
    )


def own_up_columns(up_local):
    n_row = lax.axis_size("row")
    row = lax.axis_index("row")
    depth, both = up_local.shape
    ff_dim = both // 2
    ff_row = ff_dim // n_row
    width = depth * n_row

    def slab(dest):
        odd = dest % 2
        first = lax.dynamic_slice(up_local, (0, odd * ff_dim + dest * ff_row), (depth, ff_row))
        second = lax.dynamic_slice(up_local, (0, (1 - odd) * ff_dim + dest * ff_row), (depth, ff_row))
        return jnp.concatenate([first, second], axis=1)

    whole = jnp.zeros((width, 2 * ff_row), up_local.dtype)
    for turn in range(n_row):
        other = row ^ turn
        piece = slab(other)
        if turn:
            piece = lax.ppermute(piece, "row", [(i, i ^ turn) for i in range(n_row)])
        whole = lax.dynamic_update_slice(whole, piece, (other * depth, 0))
    return whole


def mlp_forward(values, gain_row, up_own, down_own):
    odd = lax.axis_index("row") % 2 == 1
    ff_row = down_own.shape[0]
    normed, factor = norm_apply(values, gain_row)
    spread = gather_rows(normed.astype(jnp.bfloat16))
    gate_up = product(spread, up_own)
    first, second = (gate_up[:, :ff_row], gate_up[:, ff_row:])
    gate_part = jnp.where(odd, second, first)
    up_part = jnp.where(odd, first, second)
    hidden = (jax.nn.silu(gate_part) * up_part).astype(jnp.bfloat16)
    partial = product(hidden, down_own).astype(jnp.bfloat16)
    return (values + reduce_rows(partial), (factor, spread, gate_part, up_part, hidden))


def place_up_grad(grad):
    n_row = lax.axis_size("row")
    n_seq = lax.axis_size("seq")
    half = n_seq // 2
    pairs = []
    for r in range(n_row):
        for s in range(n_seq):
            if s // half == r % 2:
                owner = (r // 2, s)
            else:
                owner = (n_row // 2 + r // 2, (r % 2) * half + s % half)
            pairs.append((r * n_seq + s, owner[0] * n_seq + owner[1]))
    return lax.ppermute(grad, ("row", "seq"), pairs)


def mlp_backward(values, gain_row, up_own, down_own, kept, upstream, upstream_all):
    factor, spread, gate_part, up_part, hidden = kept
    odd = lax.axis_index("row") % 2 == 1
    g_down = left_trans(hidden, upstream_all)
    d_hidden = right_trans(upstream_all, down_own)
    gate_sig = jax.nn.sigmoid(gate_part)
    d_gate = d_hidden * up_part * gate_sig * (1.0 + gate_part * (1.0 - gate_sig))
    d_up = d_hidden * gate_part * gate_sig
    d_gate_up = jnp.concatenate(
        [jnp.where(odd, d_up, d_gate), jnp.where(odd, d_gate, d_up)], axis=1
    ).astype(jnp.bfloat16)
    d_normed = reduce_rows(right_trans(d_gate_up, up_own).astype(jnp.bfloat16))
    g_up = left_trans(d_gate_up, spread)
    d_norm, g_gain = norm_back(values, factor, gain_row, d_normed)
    return (upstream + d_norm, g_gain, g_up, g_down)


def matchings(edges, size):
    rounds = []
    left = list(range(len(edges)))
    while left:
        taken = {}

        def assign(source, seen):
            for e in left:
                if edges[e][0] == source and edges[e][1] not in seen:
                    seen.add(edges[e][1])
                    if edges[e][1] not in taken or assign(edges[taken[edges[e][1]]][0], seen):
                        taken[edges[e][1]] = e
                        return True
            return False

        for source in range(size):
            assign(source, set())
        chosen = sorted(taken.values())
        rounds.append(chosen)
        left = [e for e in left if e not in chosen]
    return rounds


def place_attn_grad(piece, width):
    n_row = lax.axis_size("row")
    n_seq = lax.axis_size("seq")
    n_x = n_seq // GROUPS
    size = n_row * n_seq
    me = lax.axis_index("row") * n_seq + lax.axis_index("seq")
    group_cols = width // GROUPS
    owned = piece.shape[0]
    unit = math.gcd(owned, group_cols)
    count = owned // unit
    edges, slots = [], []
    for r in range(n_row):
        for z in range(GROUPS):
            for x in range(n_x):
                for u in range(count):
                    local = (r * n_x + x) * owned + u * unit
                    column = (local // group_cols) * width + z * group_cols + local % group_cols
                    edges.append((r * n_seq + z * n_x + x, column // owned))
                    slots.append((u, column % owned // unit))
    result = jnp.zeros_like(piece)
    for chosen in matchings(edges, size):
        send_slot = [0] * size
        recv_slot = [0] * size
        for e in chosen:
            send_slot[edges[e][0]] = slots[e][0]
            recv_slot[edges[e][1]] = slots[e][1]
        taken = lax.dynamic_slice(
            piece, (jnp.array(send_slot, jnp.int32)[me] * unit, 0), (unit, piece.shape[1])
        )
        moved = lax.ppermute(taken, ("row", "seq"), [edges[e] for e in chosen])
        result = lax.dynamic_update_slice(
            result, moved, (jnp.array(recv_slot, jnp.int32)[me] * unit, 0)
        )
    return result


def place_out_grad(piece):
    n_row = lax.axis_size("row")
    n_seq = lax.axis_size("seq")
    n_x = n_seq // GROUPS
    pairs = []
    for r in range(n_row):
        for z in range(GROUPS):
            for x in range(n_x):
                pairs.append((r * n_seq + z * n_x + x, z * n_row * n_x + r * n_x + x))
    return lax.ppermute(piece, ("row", "seq"), pairs)


def per_device(
    tokens,
    norm_gain,
    input_weight,
    conv_weight,
    conv_bias,
    select_weight,
    step_weight,
    step_bias,
    decay_log,
    skip_scale,
    output_weight,
    attn_gain,
    attn_weight,
    attn_output,
    mlp_gain,
    mlp_up_weight,
    mlp_down_weight,
    doc_lengths,
    cotangent,
):
    n_row = lax.axis_size("row")
    n_seq = lax.axis_size("seq")
    n_x = n_seq // GROUPS
    rows_here = tokens.shape[1]
    width = tokens.shape[2]
    inner_dim = skip_scale.shape[0]
    rank_dim = step_weight.shape[0]
    state_dim = decay_log.shape[1]
    head_count = HEADS // GROUPS
    group_cols = head_count * HEAD_DIM
    lengths = doc_lengths[0]
    seq_index = lax.axis_index("seq")
    z_index = seq_index // n_x
    x_index = seq_index % n_x
    positions = seq_index * rows_here + jnp.arange(rows_here, dtype=jnp.int32)
    gain_in = norm_gain.astype(jnp.float32)
    gain_attn = attn_gain.astype(jnp.float32)
    gains_mlp = mlp_gain.astype(jnp.float32)
    conv_taps = conv_weight.astype(jnp.float32)
    skip_row = skip_scale.astype(jnp.float32)
    decays = -jnp.exp(decay_log.astype(jnp.float32)).T
    decay_planes = decays.reshape(state_dim, inner_dim // LANES, LANES)
    source = tokens[0].astype(jnp.float32)
    own_doc = doc_index(positions, lengths)
    keep_flag = ((positions > 0) & (own_doc == doc_index(positions - 1, lengths))).astype(
        jnp.float32
    )
    keep_lanes = jnp.broadcast_to(keep_flag[:, None], (rows_here, LANES))
    tap_masks = conv_masks(positions, lengths)
    whole_in = gather_input(input_weight, 10)
    up_local = lax.optimization_barrier((mlp_up_weight, whole_in))[0]
    up_first = own_up_columns(up_local[0])
    up_last = own_up_columns(up_local[1])
    down_first, down_last = (mlp_down_weight[0], mlp_down_weight[1])
    normed_in, factor_in = norm_apply(source, gain_in)
    low_in = normed_in.astype(jnp.bfloat16)
    gathered_in = lax.all_gather(low_in, "seq", axis=0, tiled=True)
    gathered_grad = lax.all_gather(cotangent[0], "row", axis=0, tiled=True)
    mixed_in = product(low_in, whole_in)
    conv_input = mixed_in[:, :inner_dim]
    gate_input = mixed_in[:, inner_dim:]
    halo_rows = from_behind(
        conv_input[rows_here - (CONV - 1) :].astype(jnp.bfloat16), "seq", 1
    ).astype(jnp.float32)
    padded = jnp.concatenate([halo_rows, conv_input], axis=0)
    conv_pre = conv_bias.astype(jnp.float32)
    for tap_index in range(CONV):
        conv_pre = (
            conv_pre
            + conv_taps[tap_index]
            * padded[tap_index : tap_index + rows_here]
            * tap_masks[tap_index][:, None]
        )
    activated_low = jax.nn.silu(conv_pre).astype(jnp.bfloat16)
    activated = activated_low.astype(jnp.float32)
    picked = product(activated_low, select_weight)
    step_low = picked[:, :rank_dim].astype(jnp.bfloat16)
    step_pre = product(step_low, step_weight) + step_bias
    step_size = jax.nn.softplus(step_pre)
    in_flat = picked[:, rank_dim : rank_dim + state_dim].reshape(-1)
    read_flat = picked[:, rank_dim + state_dim :].reshape(-1)
    local_end = scan_end(step_size, activated_low, keep_lanes, in_flat, decay_planes)
    summed_steps = jnp.where(
        jnp.min(keep_flag) > 0, jnp.sum(step_size, axis=0), RESET
    ).reshape(-1, LANES)
    start_hidden = exchange_states(summed_steps, local_end, decay_planes, True, 5)
    scanned, marks = scan_out(
        start_hidden, step_size, activated_low, keep_lanes, in_flat, read_flat, decay_planes
    )
    mamba_out = scanned + skip_row * activated
    gate_act = jax.nn.silu(gate_input)
    gated = (mamba_out * gate_act).astype(jnp.bfloat16)
    gated_rows = swap_rows(gated)
    first_out = source + product(gated, output_weight)
    second_out, kept_first = mlp_forward(first_out, gains_mlp[0], up_first, down_first)
    normed_attn, factor_attn = norm_apply(second_out, gain_attn)
    context = gather_seq(normed_attn.astype(jnp.bfloat16))
    length = context.shape[0]
    head_weight = jnp.concatenate(
        [
            lax.dynamic_slice(
                attn_weight, (0, part * width + z_index * group_cols), (width, group_cols)
            )
            for part in range(3)
        ],
        axis=1,
    )
    cosine, sine_tab = rotary_tables(jnp.arange(length, dtype=jnp.int32))
    block_starts = (jnp.arange(GROUPS, dtype=jnp.int32) * n_x + x_index) * rows_here
    query_pos = (
        block_starts[:, None] + jnp.arange(rows_here, dtype=jnp.int32)[None, :]
    ).reshape(-1)
    first_key = first_allowed(query_pos, lengths)
    lows = jnp.min(first_key.reshape(GROUPS, rows_here), axis=1)
    x_array = x_index.reshape(1).astype(jnp.int32)
    triple = project_heads(context, head_weight, cosine, sine_tab, 2 * group_cols)
    attended, log_total = attend(
        x_array, lows, triple, first_key[:, None], n_x, head_count, rows_here
    )
    attended_low = swap_heads(attended, True, 7)
    attended_rows = swap_rows(attended_low)
    third_out = second_out + product(attended_low, attn_output)
    final_out, kept_last = mlp_forward(third_out, gains_mlp[1], up_last, down_last)
    output = final_out.astype(jnp.bfloat16)
    grad_low = cotangent[0]
    d_third, g_gain_last, g_up_last, g_down_last = mlp_backward(
        third_out,
        gains_mlp[1],
        up_last,
        down_last,
        kept_last,
        grad_low.astype(jnp.float32),
        gathered_grad,
    )
    d_third_low = d_third.astype(jnp.bfloat16)
    d_third_rows = lax.all_gather(d_third_low, "row", axis=0, tiled=True)
    d_attended = swap_heads(right_trans(d_third_low, attn_output).astype(jnp.bfloat16), False, 8)
    up_piece, down_piece = reduce_background([g_up_last, g_down_last])
    g_up_last = place_up_grad(up_piece).astype(jnp.float32).T
    g_down_last = down_piece.astype(jnp.float32)
    d_query, d_keys, d_values = attend_back(
        x_array,
        lows,
        triple,
        attended,
        d_attended,
        log_total,
        first_key[:, None],
        cosine,
        sine_tab,
        n_x,
        head_count,
        rows_here,
    )
    own_x = (jnp.arange(n_x) == x_index)[None, :, None, None]
    d_query_full = jnp.where(
        own_x, d_query.reshape(GROUPS, 1, rows_here, group_cols), jnp.bfloat16(0)
    ).reshape(length, group_cols)
    d_triple = jnp.concatenate([d_query_full, d_keys, d_values], axis=1)
    d_attn_normed = reduce_seq(right_trans(d_triple, head_weight).astype(jnp.bfloat16))
    g_attn_weight = (
        place_attn_grad(
            lax.psum_scatter(
                left_trans(d_triple, context).astype(jnp.bfloat16),
                ("row", "seq"),
                scatter_dimension=0,
                tiled=True,
                axis_index_groups=plane_groups(),
            ),
            width,
        )
        .astype(jnp.float32)
        .T
    )
    d_attn_norm, g_attn_gain = norm_back(
        second_out, factor_attn, gain_attn, d_attn_normed
    )
    d_second = d_third + d_attn_norm
    d_first, g_gain_first, g_up_first, g_down_first = mlp_backward(
        first_out,
        gains_mlp[0],
        up_first,
        down_first,
        kept_first,
        d_second,
        gather_rows(d_second.astype(jnp.bfloat16)),
    )
    d_first_low = d_first.astype(jnp.bfloat16)
    d_first_rows = gather_rows(d_first_low)
    up_piece, down_piece, output_piece, attn_piece = reduce_background(
        [
            g_up_first,
            g_down_first,
            left_trans(gated_rows, d_first_rows),
            left_trans(attended_rows, d_third_rows),
        ]
    )
    g_up_first = place_up_grad(up_piece).astype(jnp.float32).T
    g_down_first = down_piece.astype(jnp.float32)
    g_output_weight = output_piece.astype(jnp.float32)
    g_attn_output = attn_piece.astype(jnp.float32)
    d_gated = right_trans(d_first_low, output_weight)
    d_scanned = d_gated * gate_act
    gate_sig = jax.nn.sigmoid(gate_input)
    d_gate = d_gated * mamba_out * gate_sig * (1.0 + gate_input * (1.0 - gate_sig))
    d_gate_low = d_gate.astype(jnp.bfloat16)
    g_input_gate = input_term(swap_seq_async(owner_blocks(d_gate_low)), gathered_in)
    g_skip_scale = jnp.sum(d_scanned * activated, axis=0)
    back_end = adjoint_end(step_size, d_scanned, keep_lanes, read_flat, decay_planes)
    end_grad = exchange_states(summed_steps, back_end, decay_planes, False, 6)
    g_step, g_activated, in_lanes, read_lanes, g_decays = adjoint_full(
        end_grad, marks, step_size, activated_low, d_scanned, keep_lanes, in_flat, read_flat, decay_planes
    )
    g_input_map = jnp.sum(in_lanes.reshape(rows_here, state_dim, LANES), axis=2)
    g_read_map = jnp.sum(read_lanes.reshape(rows_here, state_dim, LANES), axis=2)
    g_decay_log = (g_decays.reshape(state_dim, inner_dim) * decays).T
    d_step_pre = g_step * jax.nn.sigmoid(step_pre)
    g_step_bias = jnp.sum(d_step_pre, axis=0)
    d_step_low = d_step_pre.astype(jnp.bfloat16)
    d_picked = jnp.concatenate(
        [right_trans(d_step_low, step_weight), g_input_map, g_read_map], axis=1
    ).astype(jnp.bfloat16)
    g_select_weight = left_trans(activated_low, d_picked)
    d_activated = d_scanned * skip_row + g_activated + right_trans(d_picked, select_weight)
    pre_sig = jax.nn.sigmoid(conv_pre)
    d_conv_pre = d_activated * pre_sig * (1.0 + conv_pre * (1.0 - pre_sig))
    g_conv_bias = jnp.sum(d_conv_pre, axis=0)
    tap_grads = []
    d_padded = jnp.zeros((rows_here + CONV - 1, inner_dim), jnp.float32)
    for tap_index in range(CONV):
        masked = d_conv_pre * tap_masks[tap_index][:, None]
        tap_grads.append(jnp.sum(masked * padded[tap_index : tap_index + rows_here], axis=0))
        d_padded = d_padded + jnp.pad(
            masked * conv_taps[tap_index], ((tap_index, CONV - 1 - tap_index), (0, 0))
        )
    g_conv_weight = jnp.stack(tap_grads, axis=0)
    back_rows = from_behind(d_padded[: CONV - 1].astype(jnp.bfloat16), "seq", -1)
    d_conv_input = d_padded[CONV - 1 :] + jnp.pad(back_rows, ((rows_here - (CONV - 1), 0), (0, 0)))
    d_conv_low = d_conv_input.astype(jnp.bfloat16)
    g_input_conv = input_term(swap_seq(owner_blocks(d_conv_low), 9), gathered_in)
    d_mixed = jnp.concatenate([d_conv_low, d_gate_low], axis=1)
    d_normed_in = right_trans(d_mixed, whole_in)
    d_source, g_norm_gain = norm_back(source, factor_in, gain_in, d_normed_in)
    tokens_grad = (d_first + d_source).astype(jnp.bfloat16)

    owners = n_row * n_seq
    g_input_weight = (
        reduce_rows(jnp.concatenate([g_input_conv, g_input_gate], axis=0), 13).T
    )
    gains = jnp.stack([g_norm_gain, g_attn_gain, g_gain_first, g_gain_last], axis=0)
    gain_cols = gains.size // inner_dim
    columns = [
        g_select_weight,
        left_trans(d_step_low, step_low),
        g_decay_log,
        g_conv_weight.T,
        g_conv_bias[:, None],
        g_step_bias[:, None],
        g_skip_scale[:, None],
        gains.reshape(4, owners, -1).transpose(1, 0, 2).reshape(inner_dim, gain_cols),
    ]
    used = sum(part.shape[1] for part in columns)
    packed = jnp.concatenate(
        [part.astype(jnp.bfloat16) for part in columns]
        + [jnp.zeros((inner_dim, -used % LANES), jnp.bfloat16)],
        axis=1,
    )
    summed = reduce_seq(reduce_rows(packed, 11, jnp.bfloat16), 12)
    small = []
    at = 0
    for part in columns:
        small.append(summed[:, at : at + part.shape[1]])
        at += part.shape[1]
    gain_sums = small[7].reshape(4, -1)
    return (
        output[None],
        tokens_grad[None],
        gain_sums[0],
        g_input_weight,
        small[3].T,
        small[4][:, 0],
        small[0],
        small[1].T,
        small[5][:, 0],
        small[2],
        small[6][:, 0],
        g_output_weight,
        gain_sums[1],
        g_attn_weight,
        g_attn_output,
        gain_sums[2:],
        jnp.stack([g_up_first, g_up_last], axis=0),
        jnp.stack([g_down_first, g_down_last], axis=0),
    )


def solution(mesh):
    return jax.shard_map(
        per_device,
        mesh=mesh,
        in_specs=(
            P("row", "seq", None),
            P(),
            P("row", None),
            P(),
            P(),
            P(),
            P(),
            P(),
            P(),
            P(),
            P(),
            P(),
            P(),
            P(),
            P(),
            P(None, "row", None),
            P(None, "row", None),
            P("row", None),
            P("row", "seq", None),
        ),
        out_specs=(
            P("row", "seq", None),
            P("row", "seq", None),
            P(("row", "seq")),
            P(None, ("row", "seq")),
            P(None, ("row", "seq")),
            P(("row", "seq")),
            P(("row", "seq"), None),
            P(None, ("row", "seq")),
            P(("row", "seq")),
            P(("row", "seq"), None),
            P(("row", "seq")),
            P(("row", "seq"), None),
            P(("row", "seq")),
            P(None, ("row", "seq")),
            P(("row", "seq"), None),
            P(None, ("row", "seq")),
            P(None, None, ("row", "seq")),
            P(None, ("row", "seq"), None),
        ),
        check_vma=False,
    )
```

```python
import functools
import math

import jax
import jax.numpy as jnp
from jax import lax
from jax.experimental import pallas as pl
from jax.experimental.pallas import tpu as pltpu
from jax.sharding import PartitionSpec as P

LANES = 128
CHUNK = 32
RESET = 1e9
LOG2E = 1.4426950408889634
CONV = 4
HEADS = 12
HEAD_DIM = 128
WINDOW = 2048
GROUPS = 4
eps = 1e-05
rope_base = 10000.0


def from_behind(x, axis, by):
    length = lax.axis_size(axis)
    pairs = [(i, i + by) for i in range(length) if 0 <= i + by < length]
    return lax.ppermute(x, axis, pairs)


def product(left_op, right_op):
    return jnp.dot(left_op, right_op, preferred_element_type=jnp.float32)


def left_trans(left_op, right_op):
    return lax.dot_general(
        left_op, right_op, (((0,), (0,)), ((), ())), preferred_element_type=jnp.float32
    )


def right_trans(left_op, right_op):
    return lax.dot_general(
        left_op, right_op, (((1,), (1,)), ((), ())), preferred_element_type=jnp.float32
    )


def to_planes(tile_ref, value, group):
    for block in range(8):
        tile_ref[pl.ds(group * 64 + block * 8, 8), :] = value[:, block * LANES : (block + 1) * LANES]


def plane(tile_ref, index):
    return tile_ref[pl.ds((index // 8) * 64 + index % 8, 8, stride=8), :]


def tree_sum(terms):
    terms = list(terms)
    while len(terms) > 1:
        terms = [
            terms[i] + terms[i + 1] if i + 1 < len(terms) else terms[i]
            for i in range(0, len(terms), 2)
        ]
    return terms[0]


def scan_forward_kernel(
    with_output, states, chunk, *refs
):
    if with_output:
        (start_ref, step_ref, act_ref, keep_ref, in_ref, read_ref, decay_ref,
         out_ref, marks_ref, hidden_ref, step_t, drive_t, out_t) = refs
    else:
        (step_ref, act_ref, keep_ref, in_ref, decay_ref,
         end_ref, hidden_ref, step_t, drive_t) = refs
    index = pl.program_id(0)
    groups = step_ref.shape[1] // (8 * LANES)

    @pl.when(index == 0)
    def _():
        if with_output:
            hidden_ref[...] = start_ref[...]
        else:
            hidden_ref[...] = jnp.zeros_like(hidden_ref)

    if with_output:
        marks_ref[0] = hidden_ref[...]
    for group in range(groups):
        cols = pl.ds(group * 8 * LANES, 8 * LANES)
        for block in range(chunk // 8):
            rows = pl.ds(block * 8, 8)
            rate = step_ref[rows, cols]
            keep = keep_ref[rows, :]
            gated = jnp.where(jnp.concatenate([keep] * 8, axis=1) > 0, rate, RESET)
            to_planes(step_t, gated, block)
            to_planes(drive_t, rate * act_ref[rows, cols].astype(jnp.float32), block)
        decay = [decay_ref[n, pl.ds(group * 8, 8), :] * LOG2E for n in range(states)]

        def eight(block, hidden):
            hidden = list(hidden)
            for r in range(8):
                pos = index * chunk + block * 8 + r
                rate = step_t[pl.ds(block * 64 + r, 8, stride=8), :]
                drive = drive_t[pl.ds(block * 64 + r, 8, stride=8), :]
                terms = []
                for n in range(states):
                    hidden[n] = jnp.exp2(decay[n] * rate) * hidden[n] + drive * in_ref[pos * states + n]
                    if with_output:
                        terms.append(hidden[n] * read_ref[pos * states + n])
                if with_output:
                    out_t[pl.ds(block * 64 + r, 8, stride=8), :] = tree_sum(terms)
            return tuple(hidden)

        hidden = tuple(hidden_ref[n, pl.ds(group * 8, 8), :] for n in range(states))
        hidden = lax.fori_loop(0, chunk // 8, eight, hidden)
        for n in range(states):
            hidden_ref[n, pl.ds(group * 8, 8), :] = hidden[n]
        if with_output:
            for block in range(chunk // 8):
                for lane_block in range(8):
                    out_ref[pl.ds(block * 8, 8), pl.ds(group * 1024 + lane_block * LANES, LANES)] = out_t[
                        pl.ds(block * 64 + lane_block * 8, 8), :
                    ]
    if not with_output:
        end_ref[...] = hidden_ref[...]


def smem():
    return pl.BlockSpec(memory_space=pltpu.SMEM)


def scan_end(step, act, keep_lanes, in_flat, decay):
    rows, inner = step.shape
    states, planes, _ = decay.shape
    chunk = CHUNK
    whole = pl.BlockSpec((states, planes, LANES), lambda i: (0, 0, 0))
    rowed = pl.BlockSpec((chunk, inner), lambda i: (i, 0))
    return pl.pallas_call(
        functools.partial(scan_forward_kernel, False, states, chunk),
        out_shape=jax.ShapeDtypeStruct(decay.shape, jnp.float32),
        grid=(rows // chunk,),
        in_specs=[rowed, rowed, pl.BlockSpec((chunk, LANES), lambda i: (i, 0)), smem(), whole],
        out_specs=whole,
        scratch_shapes=[pltpu.VMEM(decay.shape, jnp.float32)]
        + [pltpu.VMEM((chunk * 8, LANES), jnp.float32)] * 2,
        compiler_params=pltpu.CompilerParams(vmem_limit_bytes=32 << 20),
        name="scan_end",
    )(step, act, keep_lanes, in_flat, decay)


def scan_out(start, step, act, keep_lanes, in_flat, read_flat, decay):
    rows, inner = step.shape
    states, planes, _ = decay.shape
    chunk = CHUNK
    whole = pl.BlockSpec((states, planes, LANES), lambda i: (0, 0, 0))
    rowed = pl.BlockSpec((chunk, inner), lambda i: (i, 0))
    return pl.pallas_call(
        functools.partial(scan_forward_kernel, True, states, chunk),
        out_shape=(
            jax.ShapeDtypeStruct((rows, inner), jnp.float32),
            jax.ShapeDtypeStruct((rows // chunk,) + decay.shape, jnp.float32),
        ),
        grid=(rows // chunk,),
        in_specs=[whole, rowed, rowed, pl.BlockSpec((chunk, LANES), lambda i: (i, 0)), smem(), smem(), whole],
        out_specs=(rowed, pl.BlockSpec((1, states, planes, LANES), lambda i: (i, 0, 0, 0))),
        scratch_shapes=[pltpu.VMEM(decay.shape, jnp.float32)]
        + [pltpu.VMEM((chunk * 8, LANES), jnp.float32)] * 3,
        compiler_params=pltpu.CompilerParams(vmem_limit_bytes=32 << 20),
        name="scan_out",
    )(start, step, act, keep_lanes, in_flat, read_flat, decay)


def adjoint_end_kernel(states, chunk, step_ref, grad_ref, keep_ref, read_ref, decay_ref, *refs):
    end_ref, carry_ref, step_t, grad_t = refs[-4:]
    index = pl.program_id(0)
    last = pl.num_programs(0) - 1
    groups = step_ref.shape[1] // (8 * LANES)

    @pl.when(index == 0)
    def _():
        carry_ref[...] = jnp.zeros_like(carry_ref)

    for group in range(groups):
        cols = pl.ds(group * 8 * LANES, 8 * LANES)
        for block in range(chunk // 8):
            rows = pl.ds(block * 8, 8)
            keep = keep_ref[rows, :]
            to_planes(step_t, jnp.where(jnp.concatenate([keep] * 8, axis=1) > 0, step_ref[rows, cols], RESET), block)
            to_planes(grad_t, grad_ref[rows, cols], block)
        decay = [decay_ref[n, pl.ds(group * 8, 8), :] * LOG2E for n in range(states)]

        def eight(turn, carry):
            carry = list(carry)
            block = chunk // 8 - 1 - turn
            for r in range(7, -1, -1):
                pos = (last - index) * chunk + block * 8 + r
                rate = step_t[pl.ds(block * 64 + r, 8, stride=8), :]
                grad = grad_t[pl.ds(block * 64 + r, 8, stride=8), :]
                for n in range(states):
                    carry[n] = jnp.exp2(decay[n] * rate) * (carry[n] + grad * read_ref[pos * states + n])
            return tuple(carry)

        carry = tuple(carry_ref[n, pl.ds(group * 8, 8), :] for n in range(states))
        carry = lax.fori_loop(0, chunk // 8, eight, carry)
        for n in range(states):
            carry_ref[n, pl.ds(group * 8, 8), :] = carry[n]
    end_ref[...] = carry_ref[...]


def adjoint_end(step, grad, keep_lanes, read_flat, decay, after=()):
    rows, inner = step.shape
    states, planes, _ = decay.shape
    chunk = CHUNK
    count = rows // chunk
    whole = pl.BlockSpec((states, planes, LANES), lambda i: (0, 0, 0))
    rowed = pl.BlockSpec((chunk, inner), lambda i: (count - 1 - i, 0))
    return pl.pallas_call(
        functools.partial(adjoint_end_kernel, states, chunk),
        out_shape=jax.ShapeDtypeStruct(decay.shape, jnp.float32),
        grid=(count,),
        in_specs=[rowed, rowed, pl.BlockSpec((chunk, LANES), lambda i: (count - 1 - i, 0)), smem(), whole]
        + [pl.BlockSpec(memory_space=pl.ANY)] * len(after),
        out_specs=whole,
        scratch_shapes=[pltpu.VMEM(decay.shape, jnp.float32)]
        + [pltpu.VMEM((chunk * 8, LANES), jnp.float32)] * 2,
        compiler_params=pltpu.CompilerParams(vmem_limit_bytes=32 << 20),
        name="adjoint_end",
    )(step, grad, keep_lanes, read_flat, decay, *after)


def adjoint_full_kernel(
    states, chunk,
    end_ref, marks_ref, step_ref, act_ref, grad_ref, keep_ref, in_ref, read_ref, decay_ref,
    d_step_ref, d_act_ref, d_in_ref, d_read_ref, d_decay_ref,
    carry_ref, step_t, rate_t, act_t, grad_t, d_step_t, d_act_t, factor_t, held_t, in_t, read_t,
):
    index = pl.program_id(0)
    last = pl.num_programs(0) - 1
    groups = step_ref.shape[1] // (8 * LANES)

    @pl.when(index == 0)
    def _():
        carry_ref[...] = end_ref[...]
        d_decay_ref[...] = jnp.zeros_like(d_decay_ref)

    for group in range(groups):
        cols = pl.ds(group * 8 * LANES, 8 * LANES)
        for block in range(chunk // 8):
            rows = pl.ds(block * 8, 8)
            rate = step_ref[rows, cols]
            keep = keep_ref[rows, :]
            to_planes(step_t, jnp.where(jnp.concatenate([keep] * 8, axis=1) > 0, rate, RESET), block)
            to_planes(rate_t, rate, block)
            to_planes(act_t, act_ref[rows, cols].astype(jnp.float32), block)
            to_planes(grad_t, grad_ref[rows, cols], block)

        def replay(block, hidden):
            hidden = list(hidden)
            for r in range(8):
                local = block * 8 + r
                pos = (last - index) * chunk + local
                view = pl.ds(block * 64 + r, 8, stride=8)
                gated = step_t[view, :]
                drive = rate_t[view, :] * act_t[view, :]
                grad = grad_t[view, :]
                for n in range(states):
                    slot = pl.ds((local * states + n) * 8, 8)
                    factor = jnp.exp2(decay_ref[n, pl.ds(group * 8, 8), :] * LOG2E * gated)
                    held = factor * hidden[n]
                    hidden[n] = held + drive * in_ref[pos * states + n]
                    factor_t[slot, :] = factor
                    held_t[slot, :] = held
                    if group == 0:
                        read_t[slot, :] = grad * hidden[n]
                    else:
                        read_t[slot, :] += grad * hidden[n]
            return tuple(hidden)

        lax.fori_loop(
            0, chunk // 8, replay,
            tuple(marks_ref[0, n, pl.ds(group * 8, 8), :] for n in range(states)),
        )

        def back(turn, carried):
            carry, d_decay = list(carried[0]), list(carried[1])
            block = chunk // 8 - 1 - turn
            for r in range(7, -1, -1):
                local = block * 8 + r
                pos = (last - index) * chunk + local
                view = pl.ds(block * 64 + r, 8, stride=8)
                rate = rate_t[view, :]
                act = act_t[view, :]
                grad = grad_t[view, :]
                drive = rate * act
                inner_terms = []
                step_terms = []
                for n in range(states):
                    slot = pl.ds((local * states + n) * 8, 8)
                    adjoint = carry[n] + grad * read_ref[pos * states + n]
                    moved = adjoint * held_t[slot, :]
                    step_terms.append(moved * decay_ref[n, pl.ds(group * 8, 8), :])
                    d_decay[n] = d_decay[n] + moved * rate
                    inner_terms.append(adjoint * in_ref[pos * states + n])
                    if group == 0:
                        in_t[slot, :] = adjoint * drive
                    else:
                        in_t[slot, :] += adjoint * drive
                    carry[n] = adjoint * factor_t[slot, :]
                inner_sum = tree_sum(inner_terms)
                d_step_t[view, :] = tree_sum(step_terms) + act * inner_sum
                d_act_t[view, :] = rate * inner_sum
            return (tuple(carry), tuple(d_decay))

        carry, d_decay = lax.fori_loop(
            0, chunk // 8, back,
            (
                tuple(carry_ref[n, pl.ds(group * 8, 8), :] for n in range(states)),
                tuple(d_decay_ref[n, pl.ds(group * 8, 8), :] for n in range(states)),
            ),
        )
        for n in range(states):
            carry_ref[n, pl.ds(group * 8, 8), :] = carry[n]
            d_decay_ref[n, pl.ds(group * 8, 8), :] = d_decay[n]
        for block in range(chunk // 8):
            for lane_block in range(8):
                where = (pl.ds(block * 8, 8), pl.ds(group * 1024 + lane_block * LANES, LANES))
                tile = pl.ds(block * 64 + lane_block * 8, 8)
                d_step_ref[where] = d_step_t[tile, :]
                d_act_ref[where] = d_act_t[tile, :]

    def shrink(block, _):
        for source, target in ((in_t, d_in_ref), (read_t, d_read_ref)):
            total = source[pl.ds(block * 64, 8, stride=8), :]
            for s in range(1, 8):
                total = total + source[pl.ds(block * 64 + s, 8, stride=8), :]
            target[pl.ds(block * 8, 8), :] = total
        return 0

    lax.fori_loop(0, chunk * states // 8, shrink, 0, unroll=4)


def adjoint_full(end_grad, marks, step, act, grad, keep_lanes, in_flat, read_flat, decay):
    rows, inner = step.shape
    states, planes, _ = decay.shape
    chunk = CHUNK
    count = rows // chunk
    whole = pl.BlockSpec((states, planes, LANES), lambda i: (0, 0, 0))
    rowed = pl.BlockSpec((chunk, inner), lambda i: (count - 1 - i, 0))
    maps = pl.BlockSpec((chunk * states, LANES), lambda i: (count - 1 - i, 0))
    big = pltpu.VMEM((chunk * states * 8, LANES), jnp.float32)
    return pl.pallas_call(
        functools.partial(adjoint_full_kernel, states, chunk),
        out_shape=(
            jax.ShapeDtypeStruct((rows, inner), jnp.float32),
            jax.ShapeDtypeStruct((rows, inner), jnp.float32),
            jax.ShapeDtypeStruct((rows * states, LANES), jnp.float32),
            jax.ShapeDtypeStruct((rows * states, LANES), jnp.float32),
            jax.ShapeDtypeStruct(decay.shape, jnp.float32),
        ),
        grid=(count,),
        in_specs=[
            whole,
            pl.BlockSpec((1, states, planes, LANES), lambda i: (count - 1 - i, 0, 0, 0)),
            rowed, rowed, rowed,
            pl.BlockSpec((chunk, LANES), lambda i: (count - 1 - i, 0)),
            smem(), smem(), whole,
        ],
        out_specs=(rowed, rowed, maps, maps, whole),
        scratch_shapes=[pltpu.VMEM(decay.shape, jnp.float32)]
        + [pltpu.VMEM((chunk * 8, LANES), jnp.float32)] * 6
        + [big] * 4,
        compiler_params=pltpu.CompilerParams(vmem_limit_bytes=48 << 20),
        name="adjoint_full",
    )(end_grad, marks, step, act, grad, keep_lanes, in_flat, read_flat, decay)


KEYS = 512


def turn_half(values):
    return pltpu.roll(values, HEAD_DIM // 2, 1)


def project_kernel(rotated, ctx_ref, weight_ref, cos_ref, sin_ref, out_ref):
    cosine, sine = cos_ref[...], sin_ref[...]
    ctx = ctx_ref[...]
    step = 3 * HEAD_DIM
    for start in range(0, weight_ref.shape[1], step):
        triple = product(ctx, weight_ref[:, start : start + step])
        for head in range(0, step, HEAD_DIM):
            part = triple[:, head : head + HEAD_DIM]
            if start + head < rotated:
                part = part * cosine + turn_half(part) * sine
            out_ref[:, start + head : start + head + HEAD_DIM] = part.astype(jnp.bfloat16)


def project_heads(ctx, weight, cosine, sine, rotated):
    length, width = ctx.shape
    columns = weight.shape[1]
    rows = min(256, length)
    return pl.pallas_call(
        functools.partial(project_kernel, rotated),
        out_shape=jax.ShapeDtypeStruct((length, columns), jnp.bfloat16),
        grid=(length // rows,),
        in_specs=[
            pl.BlockSpec((rows, width), lambda i: (i, 0)),
            pl.BlockSpec((width, columns), lambda i: (0, 0)),
            pl.BlockSpec((rows, HEAD_DIM), lambda i: (i, 0)),
            pl.BlockSpec((rows, HEAD_DIM), lambda i: (i, 0)),
        ],
        out_specs=pl.BlockSpec((rows, columns), lambda i: (i, 0)),
        compiler_params=pltpu.CompilerParams(vmem_limit_bytes=40 << 20),
        cost_estimate=pl.CostEstimate(
            flops=2 * length * width * columns, bytes_accessed=2 * (length * width + width * columns), transcendentals=0
        ),
        name="project_heads",
    )(ctx, weight, cosine, sine)


def mask_keys(scores_shape, chunk, first_key, q_pos):
    key_pos = chunk * KEYS + lax.broadcasted_iota(jnp.int32, scores_shape, 1)
    return (key_pos >= first_key) & (key_pos <= q_pos)


def attend_kernel(
    n_x, heads, scale, x_ref, low_ref, q_ref, k_ref, v_ref, first_ref, out_ref, lse_ref, score_t
):
    block = pl.program_id(1)
    rows = q_ref.shape[0]
    base = (block * n_x + x_ref[0]) * rows
    low_chunk = low_ref[block] // KEYS
    high_chunk = (base + rows - 1) // KEYS + 1
    q_pos = base + lax.broadcasted_iota(jnp.int32, (rows, KEYS), 0)
    first_key = first_ref[...]
    query = q_ref[...]

    def scores_of(chunk, top):
        where = pl.ds(pl.multiple_of(chunk * KEYS, KEYS), KEYS)
        scores = right_trans(query, k_ref[where, :]) * scale
        scores = jnp.where(mask_keys(scores.shape, chunk, first_key, q_pos), scores, -1e30)
        score_t[:, where] = scores
        for part in range(0, KEYS, LANES):
            top = jnp.maximum(top, scores[:, part : part + LANES])
        return top

    top = lax.fori_loop(low_chunk, high_chunk, scores_of, jnp.full((rows, LANES), -1e30, jnp.float32))
    top = jnp.max(top, axis=1, keepdims=True)

    def weigh(chunk, carried):
        total, mixed = carried
        where = pl.ds(pl.multiple_of(chunk * KEYS, KEYS), KEYS)
        weights = jnp.exp2(score_t[:, where] - top)
        for part in range(0, KEYS, LANES):
            total = total + weights[:, part : part + LANES]
        return (total, mixed + product(weights.astype(jnp.bfloat16), v_ref[where, :]))

    total, mixed = lax.fori_loop(
        low_chunk,
        high_chunk,
        weigh,
        (jnp.zeros((rows, LANES), jnp.float32), jnp.zeros((rows, HEAD_DIM), jnp.float32)),
    )
    total = jnp.sum(total, axis=1, keepdims=True)
    out_ref[...] = (mixed / total).astype(jnp.bfloat16)
    lse_ref[0] = top + jnp.log2(total)


def attend(x_index, lows, triple, first_key, n_x, heads, rows):
    length = triple.shape[0]
    blocks = length // (rows * n_x)
    scale = HEAD_DIM ** (-0.5) * LOG2E
    return pl.pallas_call(
        functools.partial(attend_kernel, n_x, heads, scale),
        out_shape=(
            jax.ShapeDtypeStruct((blocks * rows, heads * HEAD_DIM), jnp.bfloat16),
            jax.ShapeDtypeStruct((heads, blocks * rows, 1), jnp.float32),
        ),
        grid_spec=pltpu.PrefetchScalarGridSpec(
            num_scalar_prefetch=2,
            grid=(heads, blocks),
            in_specs=[
                pl.BlockSpec((rows, HEAD_DIM), lambda h, b, x, low: (b * n_x + x[0], h)),
                pl.BlockSpec((length, HEAD_DIM), lambda h, b, x, low: (0, heads + h)),
                pl.BlockSpec((length, HEAD_DIM), lambda h, b, x, low: (0, 2 * heads + h)),
                pl.BlockSpec((rows, 1), lambda h, b, x, low: (b, 0)),
            ],
            out_specs=(
                pl.BlockSpec((rows, HEAD_DIM), lambda h, b, x, low: (b, h)),
                pl.BlockSpec((1, rows, 1), lambda h, b, x, low: (h, b, 0)),
            ),
            scratch_shapes=[pltpu.VMEM((rows, length), jnp.float32)],
        ),
        compiler_params=pltpu.CompilerParams(vmem_limit_bytes=40 << 20),
        cost_estimate=pl.CostEstimate(
            flops=2 * heads * blocks * rows * length * HEAD_DIM, bytes_accessed=4 * length * heads * HEAD_DIM, transcendentals=0
        ),
        name="attend",
    )(x_index, lows, triple, triple, triple, first_key)


def attend_back_kernel(
    n_x, heads, scale,
    x_ref, low_ref, q_ref, k_ref, v_ref, out_ref, d_ref, lse_ref, first_ref, cos_ref, sin_ref, cos_all, sin_all,
    dq_ref, dk_ref, dv_ref, dk_t, dv_t,
):
    block = pl.program_id(1)
    rows = q_ref.shape[0]
    base = (block * n_x + x_ref[0]) * rows
    low_chunk = low_ref[block] // KEYS
    high_chunk = (base + rows - 1) // KEYS + 1
    q_pos = base + lax.broadcasted_iota(jnp.int32, (rows, KEYS), 0)
    first_key = first_ref[...]
    query = q_ref[...]
    d_out = d_ref[...]
    log_total = lse_ref[0]
    center = jnp.sum(d_out.astype(jnp.float32) * out_ref[...].astype(jnp.float32), axis=1, keepdims=True)

    @pl.when(block == 0)
    def _():
        dk_t[...] = jnp.zeros_like(dk_t)
        dv_t[...] = jnp.zeros_like(dv_t)

    def one(chunk, d_query):
        where = pl.ds(pl.multiple_of(chunk * KEYS, KEYS), KEYS)
        keys = k_ref[where, :]
        scores = right_trans(query, keys) * scale
        allowed = mask_keys(scores.shape, chunk, first_key, q_pos)
        weights = jnp.where(allowed, jnp.exp2(scores - log_total), 0.0)
        d_soft = right_trans(d_out, v_ref[where, :])
        d_scores = (weights * (d_soft - center)).astype(jnp.bfloat16)
        dv_t[where, :] += left_trans(weights.astype(jnp.bfloat16), d_out)
        dk_t[where, :] += left_trans(d_scores, query)
        return d_query + product(d_scores, keys)

    d_query = lax.fori_loop(low_chunk, high_chunk, one, jnp.zeros((rows, HEAD_DIM), jnp.float32))
    inv_scale = HEAD_DIM ** (-0.5)
    d_query = d_query * inv_scale
    dq_ref[...] = (d_query * cos_ref[...] - turn_half(d_query) * sin_ref[...]).astype(jnp.bfloat16)

    @pl.when(block == pl.num_programs(1) - 1)
    def _():
        def finish(chunk, _):
            where = pl.ds(pl.multiple_of(chunk * KEYS, KEYS), KEYS)
            d_keys = dk_t[where, :] * inv_scale
            dk_ref[where, :] = (d_keys * cos_all[where, :] - turn_half(d_keys) * sin_all[where, :]).astype(jnp.bfloat16)
            dv_ref[where, :] = dv_t[where, :].astype(jnp.bfloat16)
            return 0

        lax.fori_loop(0, k_ref.shape[0] // KEYS, finish, 0)


def attend_back(x_index, lows, triple, attended, d_attended, lse, first_key, cosine, sine, n_x, heads, rows):
    length = triple.shape[0]
    blocks = length // (rows * n_x)
    scale = HEAD_DIM ** (-0.5) * LOG2E
    q_spec = pl.BlockSpec((rows, HEAD_DIM), lambda h, b, x, low: (b * n_x + x[0], h))
    own = pl.BlockSpec((rows, HEAD_DIM), lambda h, b, x, low: (b, h))
    table_q = pl.BlockSpec((rows, HEAD_DIM), lambda h, b, x, low: (b * n_x + x[0], 0))
    table = pl.BlockSpec((length, HEAD_DIM), lambda h, b, x, low: (0, 0))
    column = pl.BlockSpec((length, HEAD_DIM), lambda h, b, x, low: (0, h))
    return pl.pallas_call(
        functools.partial(attend_back_kernel, n_x, heads, scale),
        out_shape=(
            jax.ShapeDtypeStruct((blocks * rows, heads * HEAD_DIM), jnp.bfloat16),
            jax.ShapeDtypeStruct((length, heads * HEAD_DIM), jnp.bfloat16),
            jax.ShapeDtypeStruct((length, heads * HEAD_DIM), jnp.bfloat16),
        ),
        grid_spec=pltpu.PrefetchScalarGridSpec(
            num_scalar_prefetch=2,
            grid=(heads, blocks),
            in_specs=[
                q_spec,
                pl.BlockSpec((length, HEAD_DIM), lambda h, b, x, low: (0, heads + h)),
                pl.BlockSpec((length, HEAD_DIM), lambda h, b, x, low: (0, 2 * heads + h)),
                own,
                own,
                pl.BlockSpec((1, rows, 1), lambda h, b, x, low: (h, b, 0)),
                pl.BlockSpec((rows, 1), lambda h, b, x, low: (b, 0)),
                table_q,
                table_q,
                table,
                table,
            ],
            out_specs=(own, column, column),
            scratch_shapes=[pltpu.VMEM((length, HEAD_DIM), jnp.float32)] * 2,
        ),
        compiler_params=pltpu.CompilerParams(vmem_limit_bytes=40 << 20),
        cost_estimate=pl.CostEstimate(
            flops=5 * heads * blocks * rows * length * HEAD_DIM, bytes_accessed=8 * length * heads * HEAD_DIM, transcendentals=0
        ),
        name="attend_back",
    )(x_index, lows, triple, triple, triple, attended, d_attended, lse, first_key, cosine, sine, cosine, sine)


MESH = pl.DeviceIdType.MESH


def greet(peers):
    barrier = pltpu.get_barrier_semaphore()
    for peer in peers:
        pl.semaphore_signal(barrier, inc=1, device_id=peer, device_id_type=MESH)
    pl.semaphore_wait(barrier, len(peers))


def send(source, target, send_sem, recv_sem, peer):
    return pltpu.make_async_remote_copy(
        src_ref=source,
        dst_ref=target,
        send_sem=send_sem,
        recv_sem=recv_sem,
        device_id=peer,
        device_id_type=MESH,
    )


def span(start, size):
    return pl.ds(pl.multiple_of(start, 16), size)


def ring_place(seq, n_x):
    z, x = seq // n_x, lax.rem(seq, n_x)
    side = lax.min(x, 1)
    turn = GROUPS - 1 - z
    odd = lax.rem(turn, 2)
    back = GROUPS + turn * (n_x - 1) + (1 - odd) * (x - 1) + odd * (n_x - 1 - x)
    return (1 - side) * z + side * back


def ring_member(place, n_x):
    side = lax.min(place // GROUPS, 1)
    late = lax.max(place - GROUPS, 0)
    turn = late // (n_x - 1)
    step = lax.rem(late, n_x - 1)
    odd = lax.rem(turn, 2)
    x = (1 - odd) * (1 + step) + odd * (n_x - 1 - step)
    return (1 - side) * place * n_x + side * ((GROUPS - 1 - turn) * n_x + x)


def remote_params(collective, limit):
    return pltpu.CompilerParams(
        collective_id=collective, has_side_effects=True, vmem_limit_bytes=limit << 20
    )


def anywhere():
    return pl.BlockSpec(memory_space=pl.ANY)


def vmem():
    return pl.BlockSpec(memory_space=pltpu.VMEM)


def gather_rows_kernel(n_row, parts, x_ref, *refs):
    sibling, across = row_peers(n_row)
    greet([sibling] + across)
    finish_gather_rows(start_gather_rows(n_row, parts, x_ref, *refs[-6:]))


def start_gather_rows(n_row, parts, x_ref, out_ref, send_y, recv_y, send_f, recv_f, own_sem):
    row, seq = lax.axis_index("row"), lax.axis_index("seq")
    y, core = row // 2, lax.rem(row, 2)
    n_y = n_row // 2
    rows = x_ref.shape[0]
    piece = rows // parts
    sibling, across = row_peers(n_row)
    pending = []
    for d in range(n_y - 1):
        for c in range(parts):
            copy = send(
                x_ref.at[pl.ds(c * piece, piece)],
                out_ref.at[span(row * rows + c * piece, piece)],
                send_y.at[d, c],
                recv_y.at[d, c],
                across[d],
            )
            copy.start()
            pending.append(copy)
    own = send(x_ref, out_ref.at[span(row * rows, rows)], own_sem.at[0], own_sem.at[1], sibling)
    own.start()
    out_ref[span(row * rows, rows), :] = x_ref[...]
    return (n_row, parts, out_ref, piece, rows, pending, own, send_f, recv_f)


def finish_gather_rows(started):
    n_row, parts, out_ref, piece, rows, pending, own, send_f, recv_f = started
    row = lax.axis_index("row")
    y, core = row // 2, lax.rem(row, 2)
    n_y = n_row // 2
    sibling = row_peers(n_row)[0]
    forwards = []
    for d in range(n_y - 1):
        origin = lax.rem(y + n_y - 1 - d, n_y) * 2 + core
        for c in range(parts):
            pending[d * parts + c].wait_recv()
            where = out_ref.at[span(origin * rows + c * piece, piece)]
            copy = send(where, where, send_f.at[d, c], recv_f.at[d, c], sibling)
            copy.start()
            forwards.append(copy)
    own.wait()
    for copy in pending:
        copy.wait_send()
    for copy in forwards:
        copy.wait()


def gather_rows_scratch(n_y, parts):
    return [pltpu.SemaphoreType.DMA((n_y - 1, parts))] * 4 + [pltpu.SemaphoreType.DMA((2,))]


def gather_rows(block, after=(), collective=1):
    n_row = lax.axis_size("row")
    rows, width = block.shape
    parts = 4 if rows % 64 == 0 else 1
    n_y = n_row // 2
    return pl.pallas_call(
        functools.partial(gather_rows_kernel, n_row, parts),
        out_shape=jax.ShapeDtypeStruct((n_row * rows, width), block.dtype),
        in_specs=[vmem()] + [anywhere()] * len(after),
        out_specs=vmem(),
        scratch_shapes=gather_rows_scratch(n_y, parts),
        compiler_params=remote_params(collective + len(after), 40),
        name="gather_rows",
    )(block, *after)


def row_peers(n_row):
    row, seq = lax.axis_index("row"), lax.axis_index("seq")
    y, core = row // 2, lax.rem(row, 2)
    n_y = n_row // 2
    sibling = (y * 2 + 1 - core, seq)
    across = [(lax.rem(y + d, n_y) * 2 + core, seq) for d in range(1, n_y)]
    return sibling, across


def reduce_rows_kernel(n_row, parts, x_ref, out_ref, *scratch):
    sibling, across = row_peers(n_row)
    greet([sibling] + across)
    reduce_rows_body(n_row, parts, x_ref, out_ref, *scratch)


def reduce_rows_body(
    n_row, parts, x_ref, out_ref, near, stage, far, send_c, recv_c, send_y, recv_y
):
    row = lax.axis_index("row")
    sibling, across = row_peers(n_row)
    y, core = row // 2, lax.rem(row, 2)
    n_y = n_row // 2
    rows = out_ref.shape[0]
    piece = rows // parts
    other = 1 - core
    order = [(d + 1) % n_y for d in range(n_y)]
    crossing = {}
    for d in order:
        block = lax.rem(y + d, n_y)
        for c in range(parts):
            copy = send(
                x_ref.at[span((block * 2 + other) * rows + c * piece, piece)],
                near.at[d, pl.ds(c * piece, piece)],
                send_c.at[d, c],
                recv_c.at[d, c],
                sibling,
            )
            copy.start()
            crossing[d, c] = copy
    sent = {}
    for d in order[:-1]:
        block = lax.rem(y + d, n_y)
        for c in range(parts):
            crossing[d, c].wait_recv()
            where = pl.ds(c * piece, piece)
            total = x_ref[span((block * 2 + core) * rows + c * piece, piece), :].astype(
                jnp.float32
            ) + near[d, where, :].astype(jnp.float32)
            stage[d - 1, where, :] = total.astype(stage.dtype)
            copy = send(
                stage.at[d - 1, where],
                far.at[d - 1, where],
                send_y.at[d - 1, c],
                recv_y.at[d - 1, c],
                across[d - 1],
            )
            copy.start()
            sent[d, c] = copy
    for c in range(parts):
        where = pl.ds(c * piece, piece)
        crossing[0, c].wait_recv()
        total = x_ref[span(row * rows + c * piece, piece), :].astype(jnp.float32) + near[
            0, where, :
        ].astype(jnp.float32)
        for d in order[:-1]:
            sent[d, c].wait_recv()
            total = total + far[d - 1, where, :].astype(jnp.float32)
        out_ref[where, :] = total.astype(out_ref.dtype)
    for copy in crossing.values():
        copy.wait_send()
    for copy in sent.values():
        copy.wait_send()


def reduce_rows_scratch(n_y, parts, buffer, dtype):
    return (
        [
            pltpu.VMEM((n_y,) + buffer, dtype),
            pltpu.VMEM((n_y - 1,) + buffer, dtype),
            pltpu.VMEM((n_y - 1,) + buffer, dtype),
        ]
        + [pltpu.SemaphoreType.DMA((n_y, parts))] * 2
        + [pltpu.SemaphoreType.DMA((n_y - 1, parts))] * 2
    )


def reduce_rows(partial, collective=14, dtype=jnp.float32):
    n_row = lax.axis_size("row")
    n_y = n_row // 2
    rows, width = partial.shape[0] // n_row, partial.shape[1]
    parts = 4 if rows % 64 == 0 else 2 if rows % 32 == 0 else 1
    buffer = (rows, width)
    return pl.pallas_call(
        functools.partial(reduce_rows_kernel, n_row, parts),
        out_shape=jax.ShapeDtypeStruct(buffer, dtype),
        in_specs=[vmem()],
        out_specs=vmem(),
        scratch_shapes=reduce_rows_scratch(n_y, parts, buffer, partial.dtype),
        compiler_params=remote_params(collective, 40),
        name="reduce_rows",
    )(partial)


def ring_neighbours(n_seq):
    n_x = n_seq // GROUPS
    row, seq = lax.axis_index("row"), lax.axis_index("seq")
    place = ring_place(seq, n_x)
    after = (row, ring_member(lax.rem(place + 1, n_seq), n_x))
    before = (row, ring_member(lax.rem(place + n_seq - 1, n_seq), n_x))
    return row, seq, place, after, before


def ring_gather(n_seq, parts, rows, out_ref, send_sem, recv_sem, place, after, before):
    n_x = n_seq // GROUPS
    half = rows // 2
    piece = half // parts
    sent = {}
    for step in range(n_seq - 1):
        for c in range(parts):
            for way in range(2):
                if step:
                    sent[step - 1, c, way].wait_recv()
                shift = n_seq - step if way == 0 else step
                member = ring_member(lax.rem(place + shift, n_seq), n_x)
                where = out_ref.at[span(member * rows + way * half + c * piece, piece)]
                copy = send(
                    where,
                    where,
                    send_sem.at[way, step, c],
                    recv_sem.at[way, step, c],
                    after if way == 0 else before,
                )
                copy.start()
                sent[step, c, way] = copy
    for c in range(parts):
        for way in range(2):
            sent[n_seq - 2, c, way].wait_recv()
    for copy in sent.values():
        copy.wait_send()


def gather_seq_kernel(
    n_row, n_seq, parts, x_ref, up_ref, *refs
):
    out_ref, own_ref, send_sem, recv_sem, send_w, recv_w, local_sem = refs[-7:]
    row, seq, place, after, before = ring_neighbours(n_seq)
    rows = x_ref.shape[0]
    depth, both = up_ref.shape[1:]
    ff_dim = both // 2
    ff_row = ff_dim // n_row
    others = [lax.rem(row + d, n_row) for d in range(1, n_row)]
    greet([after, before] + [(other, seq) for other in others])

    def slabs(dest):
        odd = lax.rem(dest, 2)
        for part in range(2):
            column = part * ff_dim + dest * ff_row
            slot = part * (1 - odd) + (1 - part) * odd
            yield part, (
                up_ref.at[1, :, pl.ds(pl.multiple_of(column, LANES), ff_row)],
                own_ref.at[span(row * depth, depth), pl.ds(pl.multiple_of(slot * ff_row, LANES), ff_row)],
            )

    moved = []
    for d, other in enumerate(others):
        for part, (source, target) in slabs(other):
            copy = send(source, target, send_w.at[d, part], recv_w.at[d, part], (other, seq))
            copy.start()
            moved.append(copy)
    local = []
    for part, (source, target) in slabs(row):
        copy = pltpu.make_async_copy(source, target, local_sem.at[part])
        copy.start()
        local.append(copy)
    out_ref[span(seq * rows, rows), :] = x_ref[...]
    ring_gather(n_seq, parts, rows, out_ref, send_sem, recv_sem, place, after, before)
    for copy in moved + local:
        copy.wait()


def gather_seq(block, up_weight, after=(), collective=3):
    n_row, n_seq = lax.axis_size("row"), lax.axis_size("seq")
    rows, width = block.shape
    parts = 2 if rows % 64 == 0 else 1
    depth, both = up_weight.shape[1:]
    return pl.pallas_call(
        functools.partial(gather_seq_kernel, n_row, n_seq, parts),
        out_shape=(
            jax.ShapeDtypeStruct((n_seq * rows, width), block.dtype),
            jax.ShapeDtypeStruct((depth * n_row, both // n_row), up_weight.dtype),
        ),
        in_specs=[vmem(), anywhere()] + [anywhere()] * len(after),
        out_specs=(vmem(), anywhere()),
        scratch_shapes=[pltpu.SemaphoreType.DMA((2, n_seq - 1, parts))] * 2
        + [pltpu.SemaphoreType.DMA((n_row - 1, 2))] * 2
        + [pltpu.SemaphoreType.DMA((2,))],
        compiler_params=remote_params(collective, 48),
        name="gather_seq",
    )(block, up_weight, *after)


def reduce_seq_kernel(n_seq, parts, x_ref, *refs):
    out_ref, held, send_sem, recv_sem = refs[-4:]
    _, _, _, after, before = ring_neighbours(n_seq)
    greet([after, before])
    reduce_seq_body(n_seq, parts, x_ref, out_ref, held, send_sem, recv_sem)


def reduce_seq_body(n_seq, parts, x_ref, out_ref, held, send_sem, recv_sem):
    n_x = n_seq // GROUPS
    _, seq, place, after, before = ring_neighbours(n_seq)
    rows = out_ref.shape[0]
    half = rows // 2
    piece = half // parts
    sent = {}
    for step in range(n_seq - 1):
        for c in range(parts):
            for way in range(2):
                shift = 2 * n_seq - 1 - step if way == 0 else 1 + step
                member = ring_member(lax.rem(place + shift, n_seq), n_x)
                own = span(member * rows + way * half + c * piece, piece)
                where = pl.ds(c * piece, piece)
                if step:
                    sent[step - 1, c, way].wait_recv()
                    held[way, step - 1, where, :] = (
                        held[way, step - 1, where, :].astype(jnp.float32)
                        + x_ref[own, :].astype(jnp.float32)
                    ).astype(held.dtype)
                    source = held.at[way, step - 1, where]
                else:
                    source = x_ref.at[own]
                copy = send(
                    source,
                    held.at[way, step, where],
                    send_sem.at[way, step, c],
                    recv_sem.at[way, step, c],
                    after if way == 0 else before,
                )
                copy.start()
                sent[step, c, way] = copy
    for c in range(parts):
        for way in range(2):
            sent[n_seq - 2, c, way].wait_recv()
            where = pl.ds(c * piece, piece)
            start = way * half + c * piece
            out_ref[pl.ds(start, piece), :] = (
                held[way, n_seq - 2, where, :].astype(jnp.float32)
                + x_ref[span(seq * rows + start, piece), :].astype(jnp.float32)
            ).astype(out_ref.dtype)
    for copy in sent.values():
        copy.wait_send()


def reduce_seq(partial, after=(), collective=4, dtype=jnp.float32):
    n_seq = lax.axis_size("seq")
    rows, width = partial.shape[0] // n_seq, partial.shape[1]
    if rows % 32:
        return lax.psum_scatter(partial, "seq", scatter_dimension=0, tiled=True).astype(dtype)
    parts = 2 if rows % 64 == 0 else 1
    return pl.pallas_call(
        functools.partial(reduce_seq_kernel, n_seq, parts),
        out_shape=jax.ShapeDtypeStruct((rows, width), dtype),
        in_specs=[vmem()] + [anywhere()] * len(after),
        out_specs=vmem(),
        scratch_shapes=[pltpu.VMEM((2, n_seq - 1, rows // 2, width), partial.dtype)]
        + [pltpu.SemaphoreType.DMA((2, n_seq - 1, parts))] * 2,
        compiler_params=remote_params(collective, 48),
        name="reduce_seq",
    )(partial, *after)


def exchange_kernel(n_row, n_seq, forward, x_ref, decay_ref, *refs):
    if forward:
        out_ref, all_ref, send_sem, recv_sem = refs[-4:]
    else:
        blocks_ref, low_ref = refs[:2]
        out_ref, spread_ref, rows_ref, all_ref, send_sem, recv_sem, send_b, recv_b = refs[-13:-5]
    row, seq, place, after, before = ring_neighbours(n_seq)
    rows = x_ref.shape[0]
    states, planes, _ = decay_ref.shape
    if forward:
        greet([after, before])
    else:
        sibling, across = row_peers(n_row)
        greet([sibling] + across + [(row, lax.rem(seq + d, n_seq)) for d in range(1, n_seq)])
        riding = start_gather_rows(n_row, 4, low_ref, rows_ref, *refs[-5:])
    all_ref[span(seq * rows, rows), :] = x_ref[...]
    ring_gather(n_seq, 1, rows, all_ref, send_sem, recv_sem, place, after, before)
    swapped = [] if forward else start_swap(n_seq, blocks_ref, spread_ref, send_b, recv_b)
    out_ref[...] = jnp.zeros_like(out_ref)

    def take(turn, _):
        other = turn if forward else n_seq - 1 - turn
        used = other < seq if forward else other > seq
        block = all_ref[span(other * rows, rows), :].astype(jnp.float32)
        base = states * planes
        summed = block[base : base + planes] + block[base + planes : base + 2 * planes]
        for n in range(states):
            kept = jnp.exp(decay_ref[n] * summed) * out_ref[n]
            ended = block[n * planes : (n + 1) * planes]
            out_ref[n] = jnp.where(used, kept + ended, out_ref[n])
        return 0

    lax.fori_loop(0, n_seq, take, 0)
    if not forward:
        finish_gather_rows(riding)
    for copy in swapped:
        copy.wait()


def exchange_states(summed, end_state, decay, collective, blocks=None, rider=None, after=()):
    n_row, n_seq = lax.axis_size("row"), lax.axis_size("seq")
    states, planes, _ = decay.shape
    high = summed.astype(jnp.bfloat16)
    lower = (summed - high.astype(jnp.float32)).astype(jnp.bfloat16)
    rows = -(-(states + 2) * planes // 32) * 32
    payload = jnp.concatenate(
        [
            end_state.astype(jnp.bfloat16).reshape(states * planes, LANES),
            high,
            lower,
            jnp.zeros((rows - (states + 2) * planes, LANES), jnp.bfloat16),
        ],
        axis=0,
    )
    ring = [pltpu.VMEM((n_seq * rows, LANES), jnp.bfloat16)] + [
        pltpu.SemaphoreType.DMA((2, n_seq - 1, 1))
    ] * 2
    entering = jax.ShapeDtypeStruct(decay.shape, jnp.float32)
    if blocks is None:
        return pl.pallas_call(
            functools.partial(exchange_kernel, n_row, n_seq, True),
            out_shape=entering,
            in_specs=[vmem(), vmem()] + [anywhere()] * len(after),
            out_specs=vmem(),
            scratch_shapes=ring,
            compiler_params=remote_params(collective, 32),
            name="exchange_states",
        )(payload, decay, *after)
    return pl.pallas_call(
        functools.partial(exchange_kernel, n_row, n_seq, False),
        out_shape=(
            entering,
            jax.ShapeDtypeStruct(blocks.shape, blocks.dtype),
            jax.ShapeDtypeStruct((n_row * rider.shape[0], rider.shape[1]), rider.dtype),
        ),
        in_specs=[vmem()] * 4 + [anywhere()] * len(after),
        out_specs=(vmem(),) * 3,
        scratch_shapes=ring
        + [pltpu.SemaphoreType.DMA((n_seq - 1,))] * 2
        + gather_rows_scratch(n_row // 2, 4),
        compiler_params=remote_params(collective, 40),
        name="exchange_states_back",
    )(payload, decay, blocks, rider, *after)


def start_row_swap(n_row, x_ref, out_ref, send_sem, recv_sem, local_sem):
    row, seq = lax.axis_index("row"), lax.axis_index("seq")
    rows, cols = x_ref.shape[0], out_ref.shape[1]
    mine = out_ref.at[span(row * rows, rows)]
    moved = []
    for d in range(1, n_row):
        other = lax.rem(row + d, n_row)
        copy = send(
            x_ref.at[:, pl.ds(pl.multiple_of(other * cols, LANES), cols)],
            mine,
            send_sem.at[d - 1],
            recv_sem.at[d - 1],
            (other, seq),
        )
        copy.start()
        moved.append(copy)
    own = pltpu.make_async_copy(
        x_ref.at[:, pl.ds(pl.multiple_of(row * cols, LANES), cols)], mine, local_sem
    )
    own.start()
    return moved + [own]


def swap_heads_kernel(
    n_row, n_x, collect, x_ref, rider_ref, *refs
):
    if collect:
        out_ref, rode_ref, send_sem, recv_sem, send_r, recv_r, local_sem = refs
    else:
        part_ref, out_ref, rode_ref, sum_ref, send_sem, recv_sem, send_r, recv_r, local_sem, *scratch = refs
    row, seq = lax.axis_index("row"), lax.axis_index("seq")
    z, x = seq // n_x, lax.rem(seq, n_x)
    peers = [lax.rem(z + d, GROUPS) for d in range(1, GROUPS)]
    greet(
        [(row, peer * n_x + x) for peer in peers]
        + [(lax.rem(row + d, n_row), seq) for d in range(1, n_row)]
    )

    def block(ref, place, wide):
        if wide:
            cols = ref.shape[1] // GROUPS
            return ref.at[:, pl.ds(pl.multiple_of(place * cols, LANES), cols)]
        rows = ref.shape[0] // GROUPS
        return ref.at[span(place * rows, rows)]

    sent = []
    for d, peer in enumerate(peers):
        copy = send(
            block(x_ref, peer, not collect),
            block(out_ref, z, collect),
            send_sem.at[d],
            recv_sem.at[d],
            (row, peer * n_x + x),
        )
        copy.start()
        sent.append(copy)
    riding = start_row_swap(n_row, rider_ref, rode_ref, send_r, recv_r, local_sem)
    block(out_ref, z, collect)[...] = block(x_ref, z, not collect)[...]
    if not collect:
        reduce_rows_body(n_row, 4, part_ref, sum_ref, *scratch)
    for copy in sent + riding:
        copy.wait()


def swap_heads(values, rider, collect, collective, partial=None):
    n_row, n_x = lax.axis_size("row"), lax.axis_size("seq") // GROUPS
    rows, cols = values.shape
    shape = (rows // GROUPS, cols * GROUPS) if collect else (rows * GROUPS, cols // GROUPS)
    narrow = rider.shape[1] // n_row % LANES
    if narrow:
        swapped = lax.all_to_all(rider, "row", split_axis=1, concat_axis=0, tiled=True)
        rider = jnp.zeros((16, n_row * LANES), rider.dtype)
    rode = (rider.shape[0] * n_row, rider.shape[1] // n_row)
    sem = pltpu.SemaphoreType.DMA
    operands = [values, rider]
    outputs = [
        jax.ShapeDtypeStruct(shape, values.dtype),
        jax.ShapeDtypeStruct(rode, rider.dtype),
    ]
    scratch = [sem((GROUPS - 1,))] * 2 + [sem((n_row - 1,))] * 2 + [sem]
    if not collect:
        buffer = (partial.shape[0] // n_row, partial.shape[1])
        operands.append(partial)
        outputs.append(jax.ShapeDtypeStruct(buffer, jnp.float32))
        scratch += reduce_rows_scratch(n_row // 2, 4, buffer, partial.dtype)
    results = pl.pallas_call(
        functools.partial(swap_heads_kernel, n_row, n_x, collect),
        out_shape=tuple(outputs),
        in_specs=[vmem()] * len(operands),
        out_specs=(vmem(),) * len(outputs),
        scratch_shapes=scratch,
        compiler_params=remote_params(collective, 40),
        name="collect_heads" if collect else "spread_heads",
    )(*operands)
    if narrow:
        return (results[0], swapped) + tuple(results[2:])
    return results


def start_swap(n_seq, x_ref, out_ref, send_sem, recv_sem):
    row, seq = lax.axis_index("row"), lax.axis_index("seq")
    place = ring_place(seq, n_seq // GROUPS)
    sent = []
    for d in range(1, n_seq):
        peer = lax.rem(seq + d, n_seq)
        copy = send(
            x_ref.at[peer], out_ref.at[place], send_sem.at[d - 1], recv_sem.at[d - 1], (row, peer)
        )
        copy.start()
        sent.append(copy)
    out_ref[place] = x_ref[seq]
    return sent


def swap_seq_kernel(n_seq, x_ref, out_ref, send_sem, recv_sem):
    row, seq = lax.axis_index("row"), lax.axis_index("seq")
    greet([(row, lax.rem(seq + d, n_seq)) for d in range(1, n_seq)])
    for copy in start_swap(n_seq, x_ref, out_ref, send_sem, recv_sem):
        copy.wait()


def finish_kernel(
    n_row, n_seq, parts, anchors, blocks_ref, packed_ref, *refs
):
    spread_ref, out_ref, send_b, recv_b, rowed, held, send_s, recv_s, *scratch = refs[anchors:]
    row, seq = lax.axis_index("row"), lax.axis_index("seq")
    sibling, across = row_peers(n_row)
    greet([sibling] + across + [(row, lax.rem(seq + d, n_seq)) for d in range(1, n_seq)])
    swapped = start_swap(n_seq, blocks_ref, spread_ref, send_b, recv_b)
    reduce_rows_body(n_row, parts, packed_ref, rowed, *scratch)
    reduce_seq_body(n_seq, 1, rowed, out_ref, held, send_s, recv_s)
    for copy in swapped:
        copy.wait()


def swap_and_reduce(blocks, packed, collective, after=()):
    n_row, n_seq = lax.axis_size("row"), lax.axis_size("seq")
    rows, width = packed.shape[0] // (n_row * n_seq), packed.shape[1]
    if rows % 32:
        summed = lax.psum_scatter(packed, ("row", "seq"), scatter_dimension=0, tiled=True)
        return swap_seq(blocks, collective), summed.astype(jnp.float32)
    buffer = (n_seq * rows, width)
    parts = 4
    sem = pltpu.SemaphoreType.DMA
    return pl.pallas_call(
        functools.partial(finish_kernel, n_row, n_seq, parts, len(after)),
        out_shape=(
            jax.ShapeDtypeStruct(blocks.shape, blocks.dtype),
            jax.ShapeDtypeStruct((rows, width), jnp.float32),
        ),
        in_specs=[vmem()] * 2 + [anywhere()] * len(after),
        out_specs=(vmem(), vmem()),
        scratch_shapes=[sem((n_seq - 1,))] * 2
        + [
            pltpu.VMEM(buffer, packed.dtype),
            pltpu.VMEM((2, n_seq - 1, rows // 2, width), packed.dtype),
        ]
        + [sem((2, n_seq - 1, 1))] * 2
        + reduce_rows_scratch(n_row // 2, parts, buffer, packed.dtype),
        compiler_params=remote_params(collective, 32),
        name="swap_and_reduce",
    )(blocks, packed, *after)


def swap_seq(blocks, collective):
    n_seq = lax.axis_size("seq")
    return pl.pallas_call(
        functools.partial(swap_seq_kernel, n_seq),
        out_shape=jax.ShapeDtypeStruct(blocks.shape, blocks.dtype),
        in_specs=[vmem()],
        out_specs=vmem(),
        scratch_shapes=[pltpu.SemaphoreType.DMA((n_seq - 1,))] * 2,
        compiler_params=remote_params(collective, 32),
        name="swap_seq",
    )(blocks)


def gather_input_kernel(
    parts, x_ref, out_ref, local_sem, own_sem, send_y, recv_y, send_f, recv_f, send_x, recv_x, send_g, recv_g
):
    row, seq = lax.axis_index("row"), lax.axis_index("seq")
    y, core = row // 2, lax.rem(row, 2)
    z, x = seq // 2, lax.rem(seq, 2)
    rows = x_ref.shape[0]
    half = rows // 2
    piece = half // parts
    sibling = (y * 2 + 1 - core, seq)
    over_y = ((1 - y) * 2 + core, seq)
    over_x = (row, z * 2 + 1 - x)
    greet([sibling, over_y, over_x])
    origin = (1 - y) * 2 + core
    first = []
    for c in range(parts):
        copy = send(
            x_ref.at[span(x * half + c * piece, piece)],
            out_ref.at[span(row * rows + x * half + c * piece, piece)],
            send_y.at[c],
            recv_y.at[c],
            over_y,
        )
        copy.start()
        first.append(copy)
    own = send(x_ref, out_ref.at[span(row * rows, rows)], own_sem.at[0], own_sem.at[1], sibling)
    own.start()
    local = pltpu.make_async_copy(x_ref, out_ref.at[span(row * rows, rows)], local_sem)
    local.start()
    rest = []
    side = []
    for c in range(parts):
        first[c].wait_recv()
        where = out_ref.at[span(origin * rows + x * half + c * piece, piece)]
        copy = send(where, where, send_x.at[c], recv_x.at[c], over_x)
        copy.start()
        side.append(copy)
        copy = send(where, where, send_f.at[c], recv_f.at[c], sibling)
        copy.start()
        rest.append(copy)
    for c in range(parts):
        side[c].wait_recv()
        where = out_ref.at[span(origin * rows + (1 - x) * half + c * piece, piece)]
        copy = send(where, where, send_g.at[c], recv_g.at[c], sibling)
        copy.start()
        rest.append(copy)
    local.wait()
    own.wait()
    for copy in first + side:
        copy.wait_send()
    for copy in rest:
        copy.wait()


def gather_input(shard, collective):
    n_row, n_seq = lax.axis_size("row"), lax.axis_size("seq")
    if n_row != 4 or n_seq != 2 * GROUPS:
        return lax.all_gather(shard, "row", axis=0, tiled=True)
    parts = 4
    sem = pltpu.SemaphoreType.DMA
    return pl.pallas_call(
        functools.partial(gather_input_kernel, parts),
        out_shape=jax.ShapeDtypeStruct((n_row * shard.shape[0], shard.shape[1]), shard.dtype),
        in_specs=[pl.BlockSpec(memory_space=pltpu.HBM)],
        out_specs=pl.BlockSpec(memory_space=pltpu.HBM),
        scratch_shapes=[sem, sem((2,))] + [sem((parts,))] * 8,
        compiler_params=remote_params(collective, 16),
        name="gather_input",
    )(shard)


def grad_blocks_kernel(up_rows, d_ref, x_ref, h_ref, u_ref, out_ref):
    out_ref[:up_rows, :] = left_trans(d_ref[...], x_ref[...]).astype(out_ref.dtype)
    out_ref[up_rows:, :] = left_trans(h_ref[...], u_ref[...]).astype(out_ref.dtype)


def grad_blocks(d_gate_up, spread, hidden, upstream):
    n_seq = lax.axis_size("seq")
    n_x = n_seq // GROUPS
    tokens, width = spread.shape
    up_rows, down_rows = d_gate_up.shape[1] // n_seq, hidden.shape[1] // n_seq
    whole = pl.BlockSpec((tokens, width), lambda k: (0, 0))
    return pl.pallas_call(
        functools.partial(grad_blocks_kernel, up_rows),
        out_shape=jax.ShapeDtypeStruct((n_seq * (up_rows + down_rows), width), jnp.bfloat16),
        grid=(n_seq,),
        in_specs=[
            pl.BlockSpec((tokens, up_rows), lambda k: (0, ring_member(k, n_x))),
            whole,
            pl.BlockSpec((tokens, down_rows), lambda k: (0, ring_member(k, n_x))),
            whole,
        ],
        out_specs=pl.BlockSpec((up_rows + down_rows, width), lambda k: (k, 0)),
        compiler_params=pltpu.CompilerParams(vmem_limit_bytes=40 << 20),
        name="grad_blocks",
    )(d_gate_up, spread, hidden, upstream)


def cycle(depth, breadth):
    order = [(z, 0) for z in range(depth)]
    for turn in range(depth):
        across = range(1, breadth) if turn % 2 == 0 else range(breadth - 1, 0, -1)
        order += [(depth - 1 - turn, x) for x in across]
    return order


def seq_order():
    n_x = lax.axis_size("seq") // GROUPS
    return [z * n_x + x for z, x in cycle(GROUPS, n_x)]


def plane_order():
    n_x = lax.axis_size("seq") // GROUPS
    order = []
    for y, x in cycle(lax.axis_size("row") // 2, n_x):
        cores = (0, 1) if len(order) // 2 % 2 == 0 else (1, 0)
        order += [(2 * y + core, x) for core in cores]
    return order


def plane_groups():
    n_seq = lax.axis_size("seq")
    n_x = n_seq // GROUPS
    return [[r * n_seq + z * n_x + x for r, x in plane_order()] for z in range(GROUPS)]


def reduce_background(parts):
    n_seq = lax.axis_size("seq")
    shaped = [part.astype(jnp.bfloat16).reshape(n_seq, -1, part.shape[1]) for part in parts]
    merged = jnp.concatenate(shaped, axis=1)
    merged = merged.reshape(-1, merged.shape[2])
    summed = lax.psum_scatter(merged, "seq", scatter_dimension=0, tiled=True)
    pieces = []
    at = 0
    for part in shaped:
        pieces.append(summed[at : at + part.shape[1]])
        at += part.shape[1]
    return pieces


def owner_blocks(half):
    n_row, n_seq = lax.axis_size("row"), lax.axis_size("seq")
    rows, columns = half.shape
    owned = columns // (n_row // 2 * n_seq)
    shaped = half.reshape(rows, n_row // 2, n_seq, owned).transpose(2, 0, 1, 3)
    return shaped.reshape(n_seq, rows, n_row // 2 * owned)


def input_term(spread, gathered):
    flat = spread.reshape(-1, spread.shape[2])
    return left_trans(flat, gathered).astype(jnp.bfloat16)


def norm_apply(values, gain_row):
    factor = lax.rsqrt(jnp.mean(values * values, axis=-1, keepdims=True) + eps)
    return (values * factor * gain_row, factor)


def norm_back(values, factor, gain_row, upstream):
    normed = values * factor
    weighted = upstream * gain_row
    gain_grad = jnp.sum(upstream * normed, axis=0)
    value_grad = factor * (weighted - normed * jnp.mean(weighted * normed, axis=-1, keepdims=True))
    return (value_grad, gain_grad)


def doc_index(positions, lengths):
    ends_at = jnp.cumsum(lengths)
    return jnp.sum((positions[:, None] >= ends_at[None, :]).astype(jnp.int32), axis=1)


def first_allowed(positions, lengths):
    ends_at = jnp.cumsum(lengths)
    begins = jnp.max(jnp.where(positions[:, None] >= ends_at[None, :], ends_at[None, :], 0), axis=1)
    return jnp.maximum(begins, positions - (WINDOW - 1)).astype(jnp.int32)


def conv_masks(positions, lengths):
    own_doc = doc_index(positions, lengths)
    rows_out = []
    for tap_index in range(CONV):
        earlier = positions - (CONV - 1) + tap_index
        rows_out.append(
            ((earlier >= 0) & (doc_index(earlier, lengths) == own_doc)).astype(jnp.float32)
        )
    return jnp.stack(rows_out, axis=0)


def rotary_tables(positions):
    half_dim = HEAD_DIM // 2
    frequency = jnp.power(rope_base, -2.0 * jnp.arange(half_dim).astype(jnp.float32) / HEAD_DIM)
    angles = positions.astype(jnp.float32)[:, None] * frequency[None, :]
    cosine, sine_tab = (jnp.cos(angles), jnp.sin(angles))
    return (
        jnp.concatenate([cosine, cosine], axis=1),
        jnp.concatenate([-sine_tab, sine_tab], axis=1),
    )


def own_up_columns(up_local, number):
    n_row = lax.axis_size("row")
    row = lax.axis_index("row")
    depth, both = up_local.shape[1:]
    ff_dim = both // 2
    ff_row = ff_dim // n_row
    width = depth * n_row

    def slab(dest):
        odd = dest % 2
        halves = [
            lax.dynamic_slice(
                up_local, (number, 0, half * ff_dim + dest * ff_row), (1, depth, ff_row)
            )[0]
            for half in (odd, 1 - odd)
        ]
        return jnp.concatenate(halves, axis=1)

    whole = jnp.zeros((width, 2 * ff_row), up_local.dtype)
    for turn in range(n_row):
        other = row ^ turn
        piece = slab(other)
        if turn:
            piece = lax.ppermute(piece, "row", [(i, i ^ turn) for i in range(n_row)])
        whole = lax.dynamic_update_slice(whole, piece, (other * depth, 0))
    return whole


def mlp_forward(values, gain_row, up_own, down_own, after=()):
    odd = lax.axis_index("row") % 2 == 1
    ff_row = down_own.shape[0]
    normed, factor = norm_apply(values, gain_row)
    spread = gather_rows(normed.astype(jnp.bfloat16), after)
    gate_up = product(spread, up_own)
    first, second = (gate_up[:, :ff_row], gate_up[:, ff_row:])
    gate_part = jnp.where(odd, second, first)
    up_part = jnp.where(odd, first, second)
    hidden = (jax.nn.silu(gate_part) * up_part).astype(jnp.bfloat16)
    partial = product(hidden, down_own).astype(jnp.bfloat16)
    return (partial, (factor, spread, gate_part, up_part, hidden))


def place_up_grad(grad):
    n_row = lax.axis_size("row")
    n_seq = lax.axis_size("seq")
    half = n_seq // 2
    pairs = []
    for r in range(n_row):
        for s in range(n_seq):
            if s // half == r % 2:
                owner = (r // 2, s)
            else:
                owner = (n_row // 2 + r // 2, (r % 2) * half + s % half)
            pairs.append((r * n_seq + s, owner[0] * n_seq + owner[1]))
    return lax.ppermute(grad, ("row", "seq"), pairs)


def mlp_backward(values, gain_row, up_own, down_own, kept, upstream, upstream_all, sums_before=()):
    factor, spread, gate_part, up_part, hidden = kept
    odd = lax.axis_index("row") % 2 == 1
    d_hidden = right_trans(upstream_all, down_own)
    gate_sig = jax.nn.sigmoid(gate_part)
    d_gate = d_hidden * up_part * gate_sig * (1.0 + gate_part * (1.0 - gate_sig))
    d_up = d_hidden * gate_part * gate_sig
    d_gate_up = jnp.concatenate(
        [jnp.where(odd, d_up, d_gate), jnp.where(odd, d_gate, d_up)], axis=1
    ).astype(jnp.bfloat16)
    n_seq = lax.axis_size("seq")
    up_rows = d_gate_up.shape[1] // n_seq
    if up_rows % (2 * LANES):
        merged = jnp.concatenate(
            [
                left_trans(d_gate_up, spread).reshape(n_seq, up_rows, -1)[jnp.array(seq_order())],
                left_trans(hidden, upstream_all).reshape(n_seq, up_rows // 2, -1)[jnp.array(seq_order())],
            ],
            axis=1,
        )
        merged = merged.reshape(-1, merged.shape[2]).astype(jnp.bfloat16)
    else:
        merged = grad_blocks(d_gate_up, spread, hidden, upstream_all)
    d_gate_up, merged = lax.optimization_barrier((d_gate_up, merged))
    merged = lax.optimization_barrier((merged,) + sums_before)[0]
    summed = lax.psum_scatter(
        merged, "seq", scatter_dimension=0, tiled=True, axis_index_groups=[seq_order()]
    )
    summed = (summed[:up_rows], summed[up_rows:])
    d_normed = reduce_rows(right_trans(d_gate_up, up_own).astype(jnp.bfloat16))
    d_norm, g_gain = norm_back(values, factor, gain_row, d_normed)
    return (upstream + d_norm, g_gain, summed)


def matchings(edges, size):
    rounds = []
    left = list(range(len(edges)))
    while left:
        taken = {}

        def assign(source, seen):
            for e in left:
                if edges[e][0] == source and edges[e][1] not in seen:
                    seen.add(edges[e][1])
                    if edges[e][1] not in taken or assign(edges[taken[edges[e][1]]][0], seen):
                        taken[edges[e][1]] = e
                        return True
            return False

        for source in range(size):
            assign(source, set())
        chosen = sorted(taken.values())
        rounds.append(chosen)
        left = [e for e in left if e not in chosen]
    return rounds


def place_attn_grad(piece, width):
    n_row = lax.axis_size("row")
    n_seq = lax.axis_size("seq")
    n_x = n_seq // GROUPS
    size = n_row * n_seq
    me = lax.axis_index("row") * n_seq + lax.axis_index("seq")
    group_cols = width // GROUPS
    owned = piece.shape[0]
    unit = math.gcd(owned, group_cols)
    count = owned // unit
    edges, slots = [], []
    for member, (r, x) in enumerate(plane_order()):
        for z in range(GROUPS):
            for u in range(count):
                local = member * owned + u * unit
                column = (local // group_cols) * width + z * group_cols + local % group_cols
                edges.append((r * n_seq + z * n_x + x, column // owned))
                slots.append((u, column % owned // unit))
    result = jnp.zeros_like(piece)
    for chosen in matchings(edges, size):
        send_slot = [0] * size
        recv_slot = [0] * size
        for e in chosen:
            send_slot[edges[e][0]] = slots[e][0]
            recv_slot[edges[e][1]] = slots[e][1]
        taken = lax.dynamic_slice(
            piece, (jnp.array(send_slot, jnp.int32)[me] * unit, 0), (unit, piece.shape[1])
        )
        moved = lax.ppermute(taken, ("row", "seq"), [edges[e] for e in chosen])
        result = lax.dynamic_update_slice(
            result, moved, (jnp.array(recv_slot, jnp.int32)[me] * unit, 0)
        )
    return result


def per_device(
    tokens,
    norm_gain,
    input_weight,
    conv_weight,
    conv_bias,
    select_weight,
    step_weight,
    step_bias,
    decay_log,
    skip_scale,
    output_weight,
    attn_gain,
    attn_weight,
    attn_output,
    mlp_gain,
    mlp_up_weight,
    mlp_down_weight,
    doc_lengths,
    cotangent,
):
    n_row = lax.axis_size("row")
    n_seq = lax.axis_size("seq")
    n_x = n_seq // GROUPS
    rows_here = tokens.shape[1]
    width = tokens.shape[2]
    inner_dim = skip_scale.shape[0]
    rank_dim = step_weight.shape[0]
    state_dim = decay_log.shape[1]
    head_count = HEADS // GROUPS
    group_cols = head_count * HEAD_DIM
    lengths = doc_lengths[0]
    seq_index = lax.axis_index("seq")
    z_index = seq_index // n_x
    x_index = seq_index % n_x
    positions = seq_index * rows_here + jnp.arange(rows_here, dtype=jnp.int32)
    gain_in = norm_gain.astype(jnp.float32)
    gain_attn = attn_gain.astype(jnp.float32)
    gains_mlp = mlp_gain.astype(jnp.float32)
    conv_taps = conv_weight.astype(jnp.float32)
    skip_row = skip_scale.astype(jnp.float32)
    decays = -jnp.exp(decay_log.astype(jnp.float32)).T
    decay_planes = decays.reshape(state_dim, inner_dim // LANES, LANES)
    source = tokens[0].astype(jnp.float32)
    own_doc = doc_index(positions, lengths)
    keep_flag = ((positions > 0) & (own_doc == doc_index(positions - 1, lengths))).astype(
        jnp.float32
    )
    keep_lanes = jnp.broadcast_to(keep_flag[:, None], (rows_here, LANES))
    tap_masks = conv_masks(positions, lengths)
    whole_in = gather_input(input_weight, 10)
    up_local = lax.optimization_barrier((mlp_up_weight, whole_in))[0]
    up_first = own_up_columns(up_local, 0)
    down_first, down_last = (mlp_down_weight[0], mlp_down_weight[1])
    normed_in, factor_in = norm_apply(source, gain_in)
    low_in = normed_in.astype(jnp.bfloat16)
    low_sent, grad_sent = lax.optimization_barrier((low_in, cotangent[0], whole_in))[:2]
    gathered_in = lax.all_gather(
        low_sent, "seq", axis=0, tiled=True, axis_index_groups=[seq_order()]
    )
    gathered_grad = lax.all_gather(grad_sent, "row", axis=0, tiled=True)
    mixed_in = product(low_in, whole_in)
    conv_input = mixed_in[:, :inner_dim]
    gate_input = mixed_in[:, inner_dim:]
    halo_rows = from_behind(
        conv_input[rows_here - (CONV - 1) :].astype(jnp.bfloat16), "seq", 1
    ).astype(jnp.float32)
    padded = jnp.concatenate([halo_rows, conv_input], axis=0)
    conv_pre = conv_bias.astype(jnp.float32)
    for tap_index in range(CONV):
        conv_pre = (
            conv_pre
            + conv_taps[tap_index]
            * padded[tap_index : tap_index + rows_here]
            * tap_masks[tap_index][:, None]
        )
    activated_low = jax.nn.silu(conv_pre).astype(jnp.bfloat16)
    activated = activated_low.astype(jnp.float32)
    picked = product(activated_low, select_weight)
    step_low = picked[:, :rank_dim].astype(jnp.bfloat16)
    step_pre = product(step_low, step_weight) + step_bias
    step_size = jax.nn.softplus(step_pre)
    in_flat = picked[:, rank_dim : rank_dim + state_dim].reshape(-1)
    read_flat = picked[:, rank_dim + state_dim :].reshape(-1)
    local_end = scan_end(step_size, activated_low, keep_lanes, in_flat, decay_planes)
    summed_steps = jnp.where(
        jnp.min(keep_flag) > 0, jnp.sum(step_size, axis=0), RESET
    ).reshape(-1, LANES)
    start_hidden = exchange_states(
        summed_steps, local_end, decay_planes, 5
    )
    scanned, marks = scan_out(
        start_hidden, step_size, activated_low, keep_lanes, in_flat, read_flat, decay_planes
    )
    mamba_out = scanned + skip_row * activated
    gate_act = jax.nn.silu(gate_input)
    gated = (mamba_out * gate_act).astype(jnp.bfloat16)
    first_out = source + product(gated, output_weight)
    second_partial, kept_first = mlp_forward(first_out, gains_mlp[0], up_first, down_first)
    second_out = first_out + reduce_rows(second_partial)
    normed_attn, factor_attn = norm_apply(second_out, gain_attn)
    context, up_last = gather_seq(normed_attn.astype(jnp.bfloat16), mlp_up_weight, (gathered_in,))
    length = context.shape[0]
    head_weight = jnp.concatenate(
        [
            lax.dynamic_slice(
                attn_weight, (0, part * width + z_index * group_cols), (width, group_cols)
            )
            for part in range(3)
        ],
        axis=1,
    )
    cosine, sine_tab = rotary_tables(jnp.arange(length, dtype=jnp.int32))
    block_starts = (jnp.arange(GROUPS, dtype=jnp.int32) * n_x + x_index) * rows_here
    query_pos = (
        block_starts[:, None] + jnp.arange(rows_here, dtype=jnp.int32)[None, :]
    ).reshape(-1)
    first_key = first_allowed(query_pos, lengths)
    lows = jnp.min(first_key.reshape(GROUPS, rows_here), axis=1)
    x_array = x_index.reshape(1).astype(jnp.int32)
    triple = project_heads(context, head_weight, cosine, sine_tab, 2 * group_cols)
    attended, log_total = attend(
        x_array, lows, triple, first_key[:, None], n_x, head_count, rows_here
    )
    attended_low, gated_rows = swap_heads(attended, gated, True, 7)
    third_out = second_out + product(attended_low, attn_output)
    final_partial, kept_last = mlp_forward(
        third_out, gains_mlp[1], up_last, down_last, (gathered_grad,)
    )
    grad_low = cotangent[0]
    d_third, g_gain_last, summed_last = mlp_backward(
        third_out,
        gains_mlp[1],
        up_last,
        down_last,
        kept_last,
        grad_low.astype(jnp.float32),
        gathered_grad,
    )
    d_third_low = d_third.astype(jnp.bfloat16)
    d_third_rows = lax.all_gather(d_third_low, "row", axis=0, tiled=True)
    d_attended, attended_rows, final_sum = swap_heads(
        right_trans(d_third_low, attn_output).astype(jnp.bfloat16),
        attended_low,
        False,
        8,
        final_partial,
    )
    output = (third_out + final_sum).astype(jnp.bfloat16)
    g_down_last = summed_last[1].astype(jnp.float32)
    d_query, d_keys, d_values = attend_back(
        x_array,
        lows,
        triple,
        attended,
        d_attended,
        log_total,
        first_key[:, None],
        cosine,
        sine_tab,
        n_x,
        head_count,
        rows_here,
    )
    own_x = (jnp.arange(n_x) == x_index)[None, :, None, None]
    d_query_full = jnp.where(
        own_x, d_query.reshape(GROUPS, 1, rows_here, group_cols), jnp.bfloat16(0)
    ).reshape(length, group_cols)
    d_triple = jnp.concatenate([d_query_full, d_keys, d_values], axis=1)
    d_attn_normed = reduce_seq(
        right_trans(d_triple, head_weight).astype(jnp.bfloat16), tuple(summed_last)
    )
    g_attn_weight = lax.psum_scatter(
        left_trans(d_triple, context).astype(jnp.bfloat16),
        ("row", "seq"),
        scatter_dimension=0,
        tiled=True,
        axis_index_groups=plane_groups(),
    )
    d_attn_norm, g_attn_gain = norm_back(
        second_out, factor_attn, gain_attn, d_attn_normed
    )
    d_second = d_third + d_attn_norm
    d_first, g_gain_first, summed_first = mlp_backward(
        first_out,
        gains_mlp[0],
        up_first,
        down_first,
        kept_first,
        d_second,
        gather_rows(d_second.astype(jnp.bfloat16), (d_third_rows,)),
        (g_attn_weight,),
    )
    d_first_low = d_first.astype(jnp.bfloat16)
    g_down_first = summed_first[1].astype(jnp.float32)
    d_gated = right_trans(d_first_low, output_weight)
    d_scanned = d_gated * gate_act
    gate_sig = jax.nn.sigmoid(gate_input)
    d_gate = d_gated * mamba_out * gate_sig * (1.0 + gate_input * (1.0 - gate_sig))
    d_gate_low = d_gate.astype(jnp.bfloat16)
    g_skip_scale = jnp.sum(d_scanned * activated, axis=0)
    back_end = adjoint_end(
        step_size, d_scanned, keep_lanes, read_flat, decay_planes
    )
    end_grad, gate_spread, d_first_rows = exchange_states(
        summed_steps, back_end, decay_planes, 6, owner_blocks(d_gate_low), d_first_low, tuple(summed_first)
    )
    sums = [
        left_trans(gated_rows, d_first_rows).astype(jnp.bfloat16),
        left_trans(attended_rows, d_third_rows).astype(jnp.bfloat16),
    ]
    sums = lax.optimization_barrier(tuple(sums) + tuple(summed_first))[:2]
    output_piece, attn_piece = reduce_background(sums)
    g_output_weight = output_piece.astype(jnp.float32)
    g_attn_output = attn_piece.astype(jnp.float32)
    late = lax.optimization_barrier((summed_last[0], summed_first[0], g_attn_weight, end_grad))
    g_up_last, g_up_first = [place_up_grad(piece).astype(jnp.float32).T for piece in late[:2]]
    g_attn_weight = place_attn_grad(late[2], width).astype(jnp.float32).T
    g_step, g_activated, in_lanes, read_lanes, g_decays = adjoint_full(
        end_grad, marks, step_size, activated_low, d_scanned, keep_lanes, in_flat, read_flat, decay_planes
    )
    g_input_map = jnp.sum(in_lanes.reshape(rows_here, state_dim, LANES), axis=2)
    g_read_map = jnp.sum(read_lanes.reshape(rows_here, state_dim, LANES), axis=2)
    g_decay_log = g_decays.reshape(state_dim, inner_dim) * decays
    d_step_pre = g_step * jax.nn.sigmoid(step_pre)
    g_step_bias = jnp.sum(d_step_pre, axis=0)
    d_step_low = d_step_pre.astype(jnp.bfloat16)
    d_picked = jnp.concatenate(
        [right_trans(d_step_low, step_weight), g_input_map, g_read_map], axis=1
    ).astype(jnp.bfloat16)
    g_select_weight = left_trans(activated_low, d_picked)
    d_activated = d_scanned * skip_row + g_activated + right_trans(d_picked, select_weight)
    pre_sig = jax.nn.sigmoid(conv_pre)
    d_conv_pre = d_activated * pre_sig * (1.0 + conv_pre * (1.0 - pre_sig))
    g_conv_bias = jnp.sum(d_conv_pre, axis=0)
    tap_grads = []
    d_padded = jnp.zeros((rows_here + CONV - 1, inner_dim), jnp.float32)
    for tap_index in range(CONV):
        masked = d_conv_pre * tap_masks[tap_index][:, None]
        tap_grads.append(jnp.sum(masked * padded[tap_index : tap_index + rows_here], axis=0))
        d_padded = d_padded + jnp.pad(
            masked * conv_taps[tap_index], ((tap_index, CONV - 1 - tap_index), (0, 0))
        )
    g_conv_weight = jnp.stack(tap_grads, axis=0)
    back_rows = from_behind(d_padded[: CONV - 1].astype(jnp.bfloat16), "seq", -1)
    d_conv_input = d_padded[CONV - 1 :] + jnp.pad(back_rows, ((rows_here - (CONV - 1), 0), (0, 0)))
    d_conv_low = d_conv_input.astype(jnp.bfloat16)
    d_mixed = jnp.concatenate([d_conv_low, d_gate_low], axis=1)
    d_normed_in = right_trans(d_mixed, whole_in)
    d_source, g_norm_gain = norm_back(source, factor_in, gain_in, d_normed_in)
    tokens_grad = (d_first + d_source).astype(jnp.bfloat16)

    owners = n_row * n_seq
    gains = jnp.stack([g_norm_gain, g_attn_gain, g_gain_first, g_gain_last], axis=0)
    gain_rows = gains.size // inner_dim
    lines = [
        g_decay_log,
        g_conv_weight,
        g_conv_bias[None],
        g_step_bias[None],
        g_skip_scale[None],
        gains.reshape(gain_rows, -1, owners, width // owners)
        .transpose(0, 2, 1, 3)
        .reshape(gain_rows, inner_dim),
    ]
    used = sum(part.shape[0] for part in lines)
    columns = [g_select_weight, left_trans(d_step_low, step_low)]
    spare = -(used + sum(part.shape[1] for part in columns)) % LANES
    lines.append(jnp.zeros((spare, inner_dim), jnp.float32))
    packed = jnp.concatenate(columns + [jnp.concatenate(lines, axis=0).T], axis=1)
    conv_spread, summed = swap_and_reduce(
        owner_blocks(d_conv_low), packed.astype(jnp.bfloat16), 11, (output_piece, attn_piece)
    )
    g_input_weight = reduce_rows(
        jnp.concatenate(
            [input_term(conv_spread, gathered_in), input_term(gate_spread, gathered_in)], axis=0
        ),
        13,
    ).T
    at = columns[0].shape[1]
    small_select = summed[:, :at]
    small_step = summed[:, at : at + rank_dim].T
    tail = summed[:, at + rank_dim :]
    small_lines = tail.T
    small = []
    at = 0
    for part in lines[:-1]:
        small.append(small_lines[at : at + part.shape[0]])
        at += part.shape[0]
    gain_sums = (
        small[5].reshape(gain_rows, -1, width // owners).reshape(4, width // owners)
    )
    return (
        output[None],
        tokens_grad[None],
        gain_sums[0],
        g_input_weight,
        small[1],
        small[2][0],
        small_select,
        small_step,
        small[3][0],
        tail[:, :state_dim],
        small[4][0],
        g_output_weight,
        gain_sums[1],
        g_attn_weight,
        g_attn_output,
        gain_sums[2:],
        jnp.stack([g_up_first, g_up_last], axis=0),
        jnp.stack([g_down_first, g_down_last], axis=0),
    )


def solution(mesh):
    return jax.shard_map(
        per_device,
        mesh=mesh,
        in_specs=(
            P("row", "seq", None),
            P(),
            P("row", None),
            P(),
            P(),
            P(),
            P(),
            P(),
            P(),
            P(),
            P(),
            P(),
            P(),
            P(),
            P(),
            P(None, "row", None),
            P(None, "row", None),
            P("row", None),
            P("row", "seq", None),
        ),
        out_specs=(
            P("row", "seq", None),
            P("row", "seq", None),
            P(("row", "seq")),
            P(None, ("row", "seq")),
            P(None, ("row", "seq")),
            P(("row", "seq")),
            P(("row", "seq"), None),
            P(None, ("row", "seq")),
            P(("row", "seq")),
            P(("row", "seq"), None),
            P(("row", "seq")),
            P(("row", "seq"), None),
            P(("row", "seq")),
            P(None, ("row", "seq")),
            P(("row", "seq"), None),
            P(None, ("row", "seq")),
            P(None, None, ("row", "seq")),
            P(None, ("row", "seq"), None),
        ),
        check_vma=False,
    )
```

```python
import functools
import math

import jax
import jax.numpy as jnp
from jax import lax
from jax.experimental import pallas as pl
from jax.experimental.pallas import tpu as pltpu
from jax.sharding import PartitionSpec as P

LANES = 128
CHUNK = 32
RESET = 1e9
LOG2E = 1.4426950408889634
CONV = 4
HEADS = 12
HEAD_DIM = 128
WINDOW = 2048
GROUPS = 4
eps = 1e-05
rope_base = 10000.0


def from_behind(x, axis, by):
    length = lax.axis_size(axis)
    pairs = [(i, i + by) for i in range(length) if 0 <= i + by < length]
    return lax.ppermute(x, axis, pairs)


def product(left_op, right_op):
    return jnp.dot(left_op, right_op, preferred_element_type=jnp.float32)


def left_trans(left_op, right_op):
    return lax.dot_general(
        left_op, right_op, (((0,), (0,)), ((), ())), preferred_element_type=jnp.float32
    )


def right_trans(left_op, right_op):
    return lax.dot_general(
        left_op, right_op, (((1,), (1,)), ((), ())), preferred_element_type=jnp.float32
    )


def to_planes(tile_ref, value, group):
    for block in range(8):
        tile_ref[pl.ds(group * 64 + block * 8, 8), :] = value[:, block * LANES : (block + 1) * LANES]


def plane(tile_ref, index):
    return tile_ref[pl.ds((index // 8) * 64 + index % 8, 8, stride=8), :]


def tree_sum(terms):
    terms = list(terms)
    while len(terms) > 1:
        terms = [
            terms[i] + terms[i + 1] if i + 1 < len(terms) else terms[i]
            for i in range(0, len(terms), 2)
        ]
    return terms[0]


def scan_forward_kernel(
    with_output, states, chunk, *refs
):
    if with_output:
        (start_ref, step_ref, act_ref, keep_ref, in_ref, read_ref, decay_ref,
         out_ref, marks_ref, hidden_ref, step_t, drive_t, out_t) = refs
    else:
        (step_ref, act_ref, keep_ref, in_ref, decay_ref,
         end_ref, hidden_ref, step_t, drive_t) = refs
    index = pl.program_id(0)
    groups = step_ref.shape[1] // (8 * LANES)

    @pl.when(index == 0)
    def _():
        if with_output:
            hidden_ref[...] = start_ref[...]
        else:
            hidden_ref[...] = jnp.zeros_like(hidden_ref)

    if with_output:
        marks_ref[0] = hidden_ref[...]
    for group in range(groups):
        cols = pl.ds(group * 8 * LANES, 8 * LANES)
        for block in range(chunk // 8):
            rows = pl.ds(block * 8, 8)
            rate = step_ref[rows, cols]
            keep = keep_ref[rows, :]
            gated = jnp.where(jnp.concatenate([keep] * 8, axis=1) > 0, rate, RESET)
            to_planes(step_t, gated, block)
            to_planes(drive_t, rate * act_ref[rows, cols].astype(jnp.float32), block)
        decay = [decay_ref[n, pl.ds(group * 8, 8), :] * LOG2E for n in range(states)]

        def eight(block, hidden):
            hidden = list(hidden)
            for r in range(8):
                pos = index * chunk + block * 8 + r
                rate = step_t[pl.ds(block * 64 + r, 8, stride=8), :]
                drive = drive_t[pl.ds(block * 64 + r, 8, stride=8), :]
                terms = []
                for n in range(states):
                    hidden[n] = jnp.exp2(decay[n] * rate) * hidden[n] + drive * in_ref[pos * states + n]
                    if with_output:
                        terms.append(hidden[n] * read_ref[pos * states + n])
                if with_output:
                    out_t[pl.ds(block * 64 + r, 8, stride=8), :] = tree_sum(terms)
            return tuple(hidden)

        hidden = tuple(hidden_ref[n, pl.ds(group * 8, 8), :] for n in range(states))
        hidden = lax.fori_loop(0, chunk // 8, eight, hidden)
        for n in range(states):
            hidden_ref[n, pl.ds(group * 8, 8), :] = hidden[n]
        if with_output:
            for block in range(chunk // 8):
                for lane_block in range(8):
                    out_ref[pl.ds(block * 8, 8), pl.ds(group * 1024 + lane_block * LANES, LANES)] = out_t[
                        pl.ds(block * 64 + lane_block * 8, 8), :
                    ]
    if not with_output:
        end_ref[...] = hidden_ref[...]


def smem():
    return pl.BlockSpec(memory_space=pltpu.SMEM)


def scan_end(step, act, keep_lanes, in_flat, decay):
    rows, inner = step.shape
    states, planes, _ = decay.shape
    chunk = CHUNK
    whole = pl.BlockSpec((states, planes, LANES), lambda i: (0, 0, 0))
    rowed = pl.BlockSpec((chunk, inner), lambda i: (i, 0))
    return pl.pallas_call(
        functools.partial(scan_forward_kernel, False, states, chunk),
        out_shape=jax.ShapeDtypeStruct(decay.shape, jnp.float32),
        grid=(rows // chunk,),
        in_specs=[rowed, rowed, pl.BlockSpec((chunk, LANES), lambda i: (i, 0)), smem(), whole],
        out_specs=whole,
        scratch_shapes=[pltpu.VMEM(decay.shape, jnp.float32)]
        + [pltpu.VMEM((chunk * 8, LANES), jnp.float32)] * 2,
        compiler_params=pltpu.CompilerParams(vmem_limit_bytes=32 << 20),
        name="scan_end",
    )(step, act, keep_lanes, in_flat, decay)


def scan_out(start, step, act, keep_lanes, in_flat, read_flat, decay):
    rows, inner = step.shape
    states, planes, _ = decay.shape
    chunk = CHUNK
    whole = pl.BlockSpec((states, planes, LANES), lambda i: (0, 0, 0))
    rowed = pl.BlockSpec((chunk, inner), lambda i: (i, 0))
    return pl.pallas_call(
        functools.partial(scan_forward_kernel, True, states, chunk),
        out_shape=(
            jax.ShapeDtypeStruct((rows, inner), jnp.float32),
            jax.ShapeDtypeStruct((rows // chunk,) + decay.shape, jnp.float32),
        ),
        grid=(rows // chunk,),
        in_specs=[whole, rowed, rowed, pl.BlockSpec((chunk, LANES), lambda i: (i, 0)), smem(), smem(), whole],
        out_specs=(rowed, pl.BlockSpec((1, states, planes, LANES), lambda i: (i, 0, 0, 0))),
        scratch_shapes=[pltpu.VMEM(decay.shape, jnp.float32)]
        + [pltpu.VMEM((chunk * 8, LANES), jnp.float32)] * 3,
        compiler_params=pltpu.CompilerParams(vmem_limit_bytes=32 << 20),
        name="scan_out",
    )(start, step, act, keep_lanes, in_flat, read_flat, decay)


def adjoint_end_kernel(states, chunk, step_ref, grad_ref, keep_ref, read_ref, decay_ref, *refs):
    end_ref, carry_ref, step_t, grad_t = refs[-4:]
    index = pl.program_id(0)
    last = pl.num_programs(0) - 1
    groups = step_ref.shape[1] // (8 * LANES)

    @pl.when(index == 0)
    def _():
        carry_ref[...] = jnp.zeros_like(carry_ref)

    for group in range(groups):
        cols = pl.ds(group * 8 * LANES, 8 * LANES)
        for block in range(chunk // 8):
            rows = pl.ds(block * 8, 8)
            keep = keep_ref[rows, :]
            to_planes(step_t, jnp.where(jnp.concatenate([keep] * 8, axis=1) > 0, step_ref[rows, cols], RESET), block)
            to_planes(grad_t, grad_ref[rows, cols], block)
        decay = [decay_ref[n, pl.ds(group * 8, 8), :] * LOG2E for n in range(states)]

        def eight(turn, carry):
            carry = list(carry)
            block = chunk // 8 - 1 - turn
            for r in range(7, -1, -1):
                pos = (last - index) * chunk + block * 8 + r
                rate = step_t[pl.ds(block * 64 + r, 8, stride=8), :]
                grad = grad_t[pl.ds(block * 64 + r, 8, stride=8), :]
                for n in range(states):
                    carry[n] = jnp.exp2(decay[n] * rate) * (carry[n] + grad * read_ref[pos * states + n])
            return tuple(carry)

        carry = tuple(carry_ref[n, pl.ds(group * 8, 8), :] for n in range(states))
        carry = lax.fori_loop(0, chunk // 8, eight, carry)
        for n in range(states):
            carry_ref[n, pl.ds(group * 8, 8), :] = carry[n]
    end_ref[...] = carry_ref[...]


def adjoint_end(step, grad, keep_lanes, read_flat, decay, after=()):
    rows, inner = step.shape
    states, planes, _ = decay.shape
    chunk = CHUNK
    count = rows // chunk
    whole = pl.BlockSpec((states, planes, LANES), lambda i: (0, 0, 0))
    rowed = pl.BlockSpec((chunk, inner), lambda i: (count - 1 - i, 0))
    return pl.pallas_call(
        functools.partial(adjoint_end_kernel, states, chunk),
        out_shape=jax.ShapeDtypeStruct(decay.shape, jnp.float32),
        grid=(count,),
        in_specs=[rowed, rowed, pl.BlockSpec((chunk, LANES), lambda i: (count - 1 - i, 0)), smem(), whole]
        + [pl.BlockSpec(memory_space=pl.ANY)] * len(after),
        out_specs=whole,
        scratch_shapes=[pltpu.VMEM(decay.shape, jnp.float32)]
        + [pltpu.VMEM((chunk * 8, LANES), jnp.float32)] * 2,
        compiler_params=pltpu.CompilerParams(vmem_limit_bytes=32 << 20),
        name="adjoint_end",
    )(step, grad, keep_lanes, read_flat, decay, *after)


def adjoint_full_kernel(
    states, chunk, anchors,
    end_ref, marks_ref, step_ref, act_ref, grad_ref, keep_ref, in_ref, read_ref, decay_ref, *refs
):
    (
    d_step_ref, d_act_ref, d_in_ref, d_read_ref, d_decay_ref,
    carry_ref, step_t, rate_t, act_t, grad_t, d_step_t, d_act_t, factor_t, held_t, in_t, read_t,
    ) = refs[anchors:]
    index = pl.program_id(0)
    last = pl.num_programs(0) - 1
    groups = step_ref.shape[1] // (8 * LANES)

    @pl.when(index == 0)
    def _():
        carry_ref[...] = end_ref[...]
        d_decay_ref[...] = jnp.zeros_like(d_decay_ref)

    for group in range(groups):
        cols = pl.ds(group * 8 * LANES, 8 * LANES)
        for block in range(chunk // 8):
            rows = pl.ds(block * 8, 8)
            rate = step_ref[rows, cols]
            keep = keep_ref[rows, :]
            to_planes(step_t, jnp.where(jnp.concatenate([keep] * 8, axis=1) > 0, rate, RESET), block)
            to_planes(rate_t, rate, block)
            to_planes(act_t, act_ref[rows, cols].astype(jnp.float32), block)
            to_planes(grad_t, grad_ref[rows, cols], block)

        def replay(block, hidden):
            hidden = list(hidden)
            for r in range(8):
                local = block * 8 + r
                pos = (last - index) * chunk + local
                view = pl.ds(block * 64 + r, 8, stride=8)
                gated = step_t[view, :]
                drive = rate_t[view, :] * act_t[view, :]
                grad = grad_t[view, :]
                for n in range(states):
                    slot = pl.ds((local * states + n) * 8, 8)
                    factor = jnp.exp2(decay_ref[n, pl.ds(group * 8, 8), :] * LOG2E * gated)
                    held = factor * hidden[n]
                    hidden[n] = held + drive * in_ref[pos * states + n]
                    factor_t[slot, :] = factor
                    held_t[slot, :] = held
                    if group == 0:
                        read_t[slot, :] = grad * hidden[n]
                    else:
                        read_t[slot, :] += grad * hidden[n]
            return tuple(hidden)

        lax.fori_loop(
            0, chunk // 8, replay,
            tuple(marks_ref[0, n, pl.ds(group * 8, 8), :] for n in range(states)),
        )

        def back(turn, carried):
            carry, d_decay = list(carried[0]), list(carried[1])
            block = chunk // 8 - 1 - turn
            for r in range(7, -1, -1):
                local = block * 8 + r
                pos = (last - index) * chunk + local
                view = pl.ds(block * 64 + r, 8, stride=8)
                rate = rate_t[view, :]
                act = act_t[view, :]
                grad = grad_t[view, :]
                drive = rate * act
                inner_terms = []
                step_terms = []
                for n in range(states):
                    slot = pl.ds((local * states + n) * 8, 8)
                    adjoint = carry[n] + grad * read_ref[pos * states + n]
                    moved = adjoint * held_t[slot, :]
                    step_terms.append(moved * decay_ref[n, pl.ds(group * 8, 8), :])
                    d_decay[n] = d_decay[n] + moved * rate
                    inner_terms.append(adjoint * in_ref[pos * states + n])
                    if group == 0:
                        in_t[slot, :] = adjoint * drive
                    else:
                        in_t[slot, :] += adjoint * drive
                    carry[n] = adjoint * factor_t[slot, :]
                inner_sum = tree_sum(inner_terms)
                d_step_t[view, :] = tree_sum(step_terms) + act * inner_sum
                d_act_t[view, :] = rate * inner_sum
            return (tuple(carry), tuple(d_decay))

        carry, d_decay = lax.fori_loop(
            0, chunk // 8, back,
            (
                tuple(carry_ref[n, pl.ds(group * 8, 8), :] for n in range(states)),
                tuple(d_decay_ref[n, pl.ds(group * 8, 8), :] for n in range(states)),
            ),
        )
        for n in range(states):
            carry_ref[n, pl.ds(group * 8, 8), :] = carry[n]
            d_decay_ref[n, pl.ds(group * 8, 8), :] = d_decay[n]
        for block in range(chunk // 8):
            for lane_block in range(8):
                where = (pl.ds(block * 8, 8), pl.ds(group * 1024 + lane_block * LANES, LANES))
                tile = pl.ds(block * 64 + lane_block * 8, 8)
                d_step_ref[where] = d_step_t[tile, :]
                d_act_ref[where] = d_act_t[tile, :]

    def shrink(block, _):
        for source, target in ((in_t, d_in_ref), (read_t, d_read_ref)):
            total = source[pl.ds(block * 64, 8, stride=8), :]
            for s in range(1, 8):
                total = total + source[pl.ds(block * 64 + s, 8, stride=8), :]
            target[pl.ds(block * 8, 8), :] = total
        return 0

    lax.fori_loop(0, chunk * states // 8, shrink, 0, unroll=4)


def adjoint_full(end_grad, marks, step, act, grad, keep_lanes, in_flat, read_flat, decay, after=()):
    rows, inner = step.shape
    states, planes, _ = decay.shape
    chunk = CHUNK
    count = rows // chunk
    whole = pl.BlockSpec((states, planes, LANES), lambda i: (0, 0, 0))
    rowed = pl.BlockSpec((chunk, inner), lambda i: (count - 1 - i, 0))
    maps = pl.BlockSpec((chunk * states, LANES), lambda i: (count - 1 - i, 0))
    big = pltpu.VMEM((chunk * states * 8, LANES), jnp.float32)
    return pl.pallas_call(
        functools.partial(adjoint_full_kernel, states, chunk, len(after)),
        out_shape=(
            jax.ShapeDtypeStruct((rows, inner), jnp.float32),
            jax.ShapeDtypeStruct((rows, inner), jnp.float32),
            jax.ShapeDtypeStruct((rows * states, LANES), jnp.float32),
            jax.ShapeDtypeStruct((rows * states, LANES), jnp.float32),
            jax.ShapeDtypeStruct(decay.shape, jnp.float32),
        ),
        grid=(count,),
        in_specs=[
            whole,
            pl.BlockSpec((1, states, planes, LANES), lambda i: (count - 1 - i, 0, 0, 0)),
            rowed, rowed, rowed,
            pl.BlockSpec((chunk, LANES), lambda i: (count - 1 - i, 0)),
            smem(), smem(), whole,
        ]
        + [pl.BlockSpec(memory_space=pl.ANY)] * len(after),
        out_specs=(rowed, rowed, maps, maps, whole),
        scratch_shapes=[pltpu.VMEM(decay.shape, jnp.float32)]
        + [pltpu.VMEM((chunk * 8, LANES), jnp.float32)] * 6
        + [big] * 4,
        compiler_params=pltpu.CompilerParams(vmem_limit_bytes=48 << 20),
        name="adjoint_full",
    )(end_grad, marks, step, act, grad, keep_lanes, in_flat, read_flat, decay, *after)


KEYS = 512


def turn_half(values):
    return pltpu.roll(values, HEAD_DIM // 2, 1)


def project_kernel(rotated, ctx_ref, weight_ref, cos_ref, sin_ref, out_ref):
    cosine, sine = cos_ref[...], sin_ref[...]
    ctx = ctx_ref[...]
    step = 3 * HEAD_DIM
    for start in range(0, weight_ref.shape[1], step):
        triple = product(ctx, weight_ref[:, start : start + step])
        for head in range(0, step, HEAD_DIM):
            part = triple[:, head : head + HEAD_DIM]
            if start + head < rotated:
                part = part * cosine + turn_half(part) * sine
            out_ref[:, start + head : start + head + HEAD_DIM] = part.astype(jnp.bfloat16)


def project_heads(ctx, weight, cosine, sine, rotated):
    length, width = ctx.shape
    columns = weight.shape[1]
    rows = min(256, length)
    return pl.pallas_call(
        functools.partial(project_kernel, rotated),
        out_shape=jax.ShapeDtypeStruct((length, columns), jnp.bfloat16),
        grid=(length // rows,),
        in_specs=[
            pl.BlockSpec((rows, width), lambda i: (i, 0)),
            pl.BlockSpec((width, columns), lambda i: (0, 0)),
            pl.BlockSpec((rows, HEAD_DIM), lambda i: (i, 0)),
            pl.BlockSpec((rows, HEAD_DIM), lambda i: (i, 0)),
        ],
        out_specs=pl.BlockSpec((rows, columns), lambda i: (i, 0)),
        compiler_params=pltpu.CompilerParams(vmem_limit_bytes=40 << 20),
        cost_estimate=pl.CostEstimate(
            flops=2 * length * width * columns, bytes_accessed=2 * (length * width + width * columns), transcendentals=0
        ),
        name="project_heads",
    )(ctx, weight, cosine, sine)


def mask_keys(scores_shape, chunk, first_key, q_pos):
    key_pos = chunk * KEYS + lax.broadcasted_iota(jnp.int32, scores_shape, 1)
    return (key_pos >= first_key) & (key_pos <= q_pos)


def attend_kernel(
    n_x, heads, scale, x_ref, low_ref, q_ref, k_ref, v_ref, first_ref, out_ref, lse_ref, score_t
):
    block = pl.program_id(1)
    rows = q_ref.shape[0]
    base = (block * n_x + x_ref[0]) * rows
    low_chunk = low_ref[block] // KEYS
    high_chunk = (base + rows - 1) // KEYS + 1
    q_pos = base + lax.broadcasted_iota(jnp.int32, (rows, KEYS), 0)
    first_key = first_ref[...]
    query = q_ref[...]

    def scores_of(chunk, top):
        where = pl.ds(pl.multiple_of(chunk * KEYS, KEYS), KEYS)
        scores = right_trans(query, k_ref[where, :]) * scale
        scores = jnp.where(mask_keys(scores.shape, chunk, first_key, q_pos), scores, -1e30)
        score_t[:, where] = scores
        for part in range(0, KEYS, LANES):
            top = jnp.maximum(top, scores[:, part : part + LANES])
        return top

    top = lax.fori_loop(low_chunk, high_chunk, scores_of, jnp.full((rows, LANES), -1e30, jnp.float32))
    top = jnp.max(top, axis=1, keepdims=True)

    def weigh(chunk, carried):
        total, mixed = carried
        where = pl.ds(pl.multiple_of(chunk * KEYS, KEYS), KEYS)
        weights = jnp.exp2(score_t[:, where] - top)
        for part in range(0, KEYS, LANES):
            total = total + weights[:, part : part + LANES]
        return (total, mixed + product(weights.astype(jnp.bfloat16), v_ref[where, :]))

    total, mixed = lax.fori_loop(
        low_chunk,
        high_chunk,
        weigh,
        (jnp.zeros((rows, LANES), jnp.float32), jnp.zeros((rows, HEAD_DIM), jnp.float32)),
    )
    total = jnp.sum(total, axis=1, keepdims=True)
    out_ref[...] = (mixed / total).astype(jnp.bfloat16)
    lse_ref[0] = top + jnp.log2(total)


def attend(x_index, lows, triple, first_key, n_x, heads, rows):
    length = triple.shape[0]
    blocks = length // (rows * n_x)
    scale = HEAD_DIM ** (-0.5) * LOG2E
    return pl.pallas_call(
        functools.partial(attend_kernel, n_x, heads, scale),
        out_shape=(
            jax.ShapeDtypeStruct((blocks * rows, heads * HEAD_DIM), jnp.bfloat16),
            jax.ShapeDtypeStruct((heads, blocks * rows, 1), jnp.float32),
        ),
        grid_spec=pltpu.PrefetchScalarGridSpec(
            num_scalar_prefetch=2,
            grid=(heads, blocks),
            in_specs=[
                pl.BlockSpec((rows, HEAD_DIM), lambda h, b, x, low: (b * n_x + x[0], h)),
                pl.BlockSpec((length, HEAD_DIM), lambda h, b, x, low: (0, heads + h)),
                pl.BlockSpec((length, HEAD_DIM), lambda h, b, x, low: (0, 2 * heads + h)),
                pl.BlockSpec((rows, 1), lambda h, b, x, low: (b, 0)),
            ],
            out_specs=(
                pl.BlockSpec((rows, HEAD_DIM), lambda h, b, x, low: (b, h)),
                pl.BlockSpec((1, rows, 1), lambda h, b, x, low: (h, b, 0)),
            ),
            scratch_shapes=[pltpu.VMEM((rows, length), jnp.float32)],
        ),
        compiler_params=pltpu.CompilerParams(vmem_limit_bytes=40 << 20),
        cost_estimate=pl.CostEstimate(
            flops=2 * heads * blocks * rows * length * HEAD_DIM, bytes_accessed=4 * length * heads * HEAD_DIM, transcendentals=0
        ),
        name="attend",
    )(x_index, lows, triple, triple, triple, first_key)


def attend_back_kernel(
    n_x, heads, scale,
    x_ref, low_ref, q_ref, k_ref, v_ref, out_ref, d_ref, lse_ref, first_ref, cos_ref, sin_ref, cos_all, sin_all,
    dq_ref, dk_ref, dv_ref, dk_t, dv_t,
):
    block = pl.program_id(1)
    rows = q_ref.shape[0]
    base = (block * n_x + x_ref[0]) * rows
    low_chunk = low_ref[block] // KEYS
    high_chunk = (base + rows - 1) // KEYS + 1
    q_pos = base + lax.broadcasted_iota(jnp.int32, (rows, KEYS), 0)
    first_key = first_ref[...]
    query = q_ref[...]
    d_out = d_ref[...]
    log_total = lse_ref[0]
    center = jnp.sum(d_out.astype(jnp.float32) * out_ref[...].astype(jnp.float32), axis=1, keepdims=True)

    @pl.when(block == 0)
    def _():
        dk_t[...] = jnp.zeros_like(dk_t)
        dv_t[...] = jnp.zeros_like(dv_t)

    def one(chunk, d_query):
        where = pl.ds(pl.multiple_of(chunk * KEYS, KEYS), KEYS)
        keys = k_ref[where, :]
        scores = right_trans(query, keys) * scale
        allowed = mask_keys(scores.shape, chunk, first_key, q_pos)
        weights = jnp.where(allowed, jnp.exp2(scores - log_total), 0.0)
        d_soft = right_trans(d_out, v_ref[where, :])
        d_scores = (weights * (d_soft - center)).astype(jnp.bfloat16)
        dv_t[where, :] += left_trans(weights.astype(jnp.bfloat16), d_out)
        dk_t[where, :] += left_trans(d_scores, query)
        return d_query + product(d_scores, keys)

    d_query = lax.fori_loop(low_chunk, high_chunk, one, jnp.zeros((rows, HEAD_DIM), jnp.float32))
    inv_scale = HEAD_DIM ** (-0.5)
    d_query = d_query * inv_scale
    dq_ref[...] = (d_query * cos_ref[...] - turn_half(d_query) * sin_ref[...]).astype(jnp.bfloat16)

    @pl.when(block == pl.num_programs(1) - 1)
    def _():
        def finish(chunk, _):
            where = pl.ds(pl.multiple_of(chunk * KEYS, KEYS), KEYS)
            d_keys = dk_t[where, :] * inv_scale
            dk_ref[where, :] = (d_keys * cos_all[where, :] - turn_half(d_keys) * sin_all[where, :]).astype(jnp.bfloat16)
            dv_ref[where, :] = dv_t[where, :].astype(jnp.bfloat16)
            return 0

        lax.fori_loop(0, k_ref.shape[0] // KEYS, finish, 0)


def attend_back(x_index, lows, triple, attended, d_attended, lse, first_key, cosine, sine, n_x, heads, rows):
    length = triple.shape[0]
    blocks = length // (rows * n_x)
    scale = HEAD_DIM ** (-0.5) * LOG2E
    q_spec = pl.BlockSpec((rows, HEAD_DIM), lambda h, b, x, low: (b * n_x + x[0], h))
    own = pl.BlockSpec((rows, HEAD_DIM), lambda h, b, x, low: (b, h))
    table_q = pl.BlockSpec((rows, HEAD_DIM), lambda h, b, x, low: (b * n_x + x[0], 0))
    table = pl.BlockSpec((length, HEAD_DIM), lambda h, b, x, low: (0, 0))
    column = pl.BlockSpec((length, HEAD_DIM), lambda h, b, x, low: (0, h))
    return pl.pallas_call(
        functools.partial(attend_back_kernel, n_x, heads, scale),
        out_shape=(
            jax.ShapeDtypeStruct((blocks * rows, heads * HEAD_DIM), jnp.bfloat16),
            jax.ShapeDtypeStruct((length, heads * HEAD_DIM), jnp.bfloat16),
            jax.ShapeDtypeStruct((length, heads * HEAD_DIM), jnp.bfloat16),
        ),
        grid_spec=pltpu.PrefetchScalarGridSpec(
            num_scalar_prefetch=2,
            grid=(heads, blocks),
            in_specs=[
                q_spec,
                pl.BlockSpec((length, HEAD_DIM), lambda h, b, x, low: (0, heads + h)),
                pl.BlockSpec((length, HEAD_DIM), lambda h, b, x, low: (0, 2 * heads + h)),
                own,
                own,
                pl.BlockSpec((1, rows, 1), lambda h, b, x, low: (h, b, 0)),
                pl.BlockSpec((rows, 1), lambda h, b, x, low: (b, 0)),
                table_q,
                table_q,
                table,
                table,
            ],
            out_specs=(own, column, column),
            scratch_shapes=[pltpu.VMEM((length, HEAD_DIM), jnp.float32)] * 2,
        ),
        compiler_params=pltpu.CompilerParams(vmem_limit_bytes=40 << 20),
        cost_estimate=pl.CostEstimate(
            flops=5 * heads * blocks * rows * length * HEAD_DIM, bytes_accessed=8 * length * heads * HEAD_DIM, transcendentals=0
        ),
        name="attend_back",
    )(x_index, lows, triple, triple, triple, attended, d_attended, lse, first_key, cosine, sine, cosine, sine)


MESH = pl.DeviceIdType.MESH


def greet(peers):
    barrier = pltpu.get_barrier_semaphore()
    for peer in peers:
        pl.semaphore_signal(barrier, inc=1, device_id=peer, device_id_type=MESH)
    pl.semaphore_wait(barrier, len(peers))


def send(source, target, send_sem, recv_sem, peer):
    return pltpu.make_async_remote_copy(
        src_ref=source,
        dst_ref=target,
        send_sem=send_sem,
        recv_sem=recv_sem,
        device_id=peer,
        device_id_type=MESH,
    )


def span(start, size):
    return pl.ds(pl.multiple_of(start, 16), size)


def ring_place(seq, n_x):
    z, x = seq // n_x, lax.rem(seq, n_x)
    side = lax.min(x, 1)
    turn = GROUPS - 1 - z
    odd = lax.rem(turn, 2)
    back = GROUPS + turn * (n_x - 1) + (1 - odd) * (x - 1) + odd * (n_x - 1 - x)
    return (1 - side) * z + side * back


def ring_member(place, n_x):
    side = lax.min(place // GROUPS, 1)
    late = lax.max(place - GROUPS, 0)
    turn = late // (n_x - 1)
    step = lax.rem(late, n_x - 1)
    odd = lax.rem(turn, 2)
    x = (1 - odd) * (1 + step) + odd * (n_x - 1 - step)
    return (1 - side) * place * n_x + side * ((GROUPS - 1 - turn) * n_x + x)


def remote_params(collective, limit):
    return pltpu.CompilerParams(
        collective_id=collective, has_side_effects=True, vmem_limit_bytes=limit << 20
    )


def anywhere():
    return pl.BlockSpec(memory_space=pl.ANY)


def vmem():
    return pl.BlockSpec(memory_space=pltpu.VMEM)


def start_gather_rows(n_row, parts, x_ref, out_ref, send_y, recv_y, send_f, recv_f, own_sem):
    row, seq = lax.axis_index("row"), lax.axis_index("seq")
    y, core = row // 2, lax.rem(row, 2)
    n_y = n_row // 2
    rows = x_ref.shape[0]
    piece = rows // parts
    sibling, across = row_peers(n_row)
    pending = []
    for d in range(n_y - 1):
        for c in range(parts):
            copy = send(
                x_ref.at[pl.ds(c * piece, piece)],
                out_ref.at[span(row * rows + c * piece, piece)],
                send_y.at[d, c],
                recv_y.at[d, c],
                across[d],
            )
            copy.start()
            pending.append(copy)
    own = send(x_ref, out_ref.at[span(row * rows, rows)], own_sem.at[0], own_sem.at[1], sibling)
    own.start()
    out_ref[span(row * rows, rows), :] = x_ref[...]
    return (n_row, parts, out_ref, piece, rows, pending, own, send_f, recv_f)


def finish_gather_rows(started):
    n_row, parts, out_ref, piece, rows, pending, own, send_f, recv_f = started
    row = lax.axis_index("row")
    y, core = row // 2, lax.rem(row, 2)
    n_y = n_row // 2
    sibling = row_peers(n_row)[0]
    forwards = []
    for d in range(n_y - 1):
        origin = lax.rem(y + n_y - 1 - d, n_y) * 2 + core
        for c in range(parts):
            pending[d * parts + c].wait_recv()
            where = out_ref.at[span(origin * rows + c * piece, piece)]
            copy = send(where, where, send_f.at[d, c], recv_f.at[d, c], sibling)
            copy.start()
            forwards.append(copy)
    own.wait()
    for copy in pending:
        copy.wait_send()
    for copy in forwards:
        copy.wait()


def gather_rows_scratch(n_y, parts):
    return [pltpu.SemaphoreType.DMA((n_y - 1, parts))] * 4 + [pltpu.SemaphoreType.DMA((2,))]


def owner_of(row, seq, n_row, n_seq):
    half = n_seq // 2
    late, odd = seq // half, lax.rem(row, 2)
    moved = late + odd - 2 * late * odd
    owner_seq = (1 - moved) * seq + moved * (odd * half + lax.rem(seq, half))
    return moved * (n_row // 2) + row // 2, owner_seq


def holder_of(row, seq, n_row, n_seq):
    half = n_seq // 2
    raised, late = row // (n_row // 2), seq // half
    holder_seq = (1 - raised) * seq + raised * ((1 - late) * half + lax.rem(seq, half))
    return 2 * (row - raised * (n_row // 2)) + late, holder_seq


def greet_riders(peers, n_row, n_seq):
    row, seq = lax.axis_index("row"), lax.axis_index("seq")
    target, source = owner_of(row, seq, n_row, n_seq), holder_of(row, seq, n_row, n_seq)
    staying = jnp.logical_and(target[0] == row, target[1] == seq)
    barrier = pltpu.get_barrier_semaphore()
    for peer in peers:
        pl.semaphore_signal(barrier, inc=1, device_id=peer, device_id_type=MESH)

    @pl.when(jnp.logical_not(staying))
    def _():
        pl.semaphore_signal(barrier, inc=1, device_id=source, device_id_type=MESH)

    pl.semaphore_wait(barrier, len(peers) + 1 - staying.astype(jnp.int32))


def start_ride(n_row, n_seq, ride_ref, rode_ref, ride_sem):
    row, seq = lax.axis_index("row"), lax.axis_index("seq")
    target = owner_of(row, seq, n_row, n_seq)
    staying = jnp.logical_and(target[0] == row, target[1] == seq)
    ride = send(ride_ref, rode_ref, ride_sem.at[0], ride_sem.at[1], target)
    keep = pltpu.make_async_copy(ride_ref, rode_ref, ride_sem.at[2])

    @pl.when(jnp.logical_not(staying))
    def _():
        ride.start()

    @pl.when(staying)
    def _():
        keep.start()

    return staying, ride, keep


def finish_ride(started):
    staying, ride, keep = started

    @pl.when(jnp.logical_not(staying))
    def _():
        ride.wait()

    @pl.when(staying)
    def _():
        keep.wait()


def row_peers(n_row):
    row, seq = lax.axis_index("row"), lax.axis_index("seq")
    y, core = row // 2, lax.rem(row, 2)
    n_y = n_row // 2
    sibling = (y * 2 + 1 - core, seq)
    across = [(lax.rem(y + d, n_y) * 2 + core, seq) for d in range(1, n_y)]
    return sibling, across


def reduce_rows_kernel(n_row, n_seq, parts, x_ref, ride_ref, out_ref, rode_ref, ride_sem, *scratch):
    sibling, across = row_peers(n_row)
    greet_riders([sibling] + across, n_row, n_seq)
    ridden = start_ride(n_row, n_seq, ride_ref, rode_ref, ride_sem)
    reduce_rows_body(n_row, parts, x_ref, out_ref, *scratch)
    finish_ride(ridden)


def reduce_rows_body(
    n_row, parts, x_ref, out_ref, near, stage, far, send_c, recv_c, send_y, recv_y
):
    row = lax.axis_index("row")
    sibling, across = row_peers(n_row)
    y, core = row // 2, lax.rem(row, 2)
    n_y = n_row // 2
    rows = out_ref.shape[0]
    piece = rows // parts
    other = 1 - core
    order = [(d + 1) % n_y for d in range(n_y)]
    crossing = {}
    for d in order:
        block = lax.rem(y + d, n_y)
        for c in range(parts):
            copy = send(
                x_ref.at[span((block * 2 + other) * rows + c * piece, piece)],
                near.at[d, pl.ds(c * piece, piece)],
                send_c.at[d, c],
                recv_c.at[d, c],
                sibling,
            )
            copy.start()
            crossing[d, c] = copy
    sent = {}
    for d in order[:-1]:
        block = lax.rem(y + d, n_y)
        for c in range(parts):
            crossing[d, c].wait_recv()
            where = pl.ds(c * piece, piece)
            total = x_ref[span((block * 2 + core) * rows + c * piece, piece), :].astype(
                jnp.float32
            ) + near[d, where, :].astype(jnp.float32)
            stage[d - 1, where, :] = total.astype(stage.dtype)
            copy = send(
                stage.at[d - 1, where],
                far.at[d - 1, where],
                send_y.at[d - 1, c],
                recv_y.at[d - 1, c],
                across[d - 1],
            )
            copy.start()
            sent[d, c] = copy
    for c in range(parts):
        where = pl.ds(c * piece, piece)
        crossing[0, c].wait_recv()
        total = x_ref[span(row * rows + c * piece, piece), :].astype(jnp.float32) + near[
            0, where, :
        ].astype(jnp.float32)
        for d in order[:-1]:
            sent[d, c].wait_recv()
            total = total + far[d - 1, where, :].astype(jnp.float32)
        out_ref[where, :] = total.astype(out_ref.dtype)
    for copy in crossing.values():
        copy.wait_send()
    for copy in sent.values():
        copy.wait_send()


def reduce_rows_scratch(n_y, parts, buffer, dtype):
    return (
        [
            pltpu.VMEM((n_y,) + buffer, dtype),
            pltpu.VMEM((n_y - 1,) + buffer, dtype),
            pltpu.VMEM((n_y - 1,) + buffer, dtype),
        ]
        + [pltpu.SemaphoreType.DMA((n_y, parts))] * 2
        + [pltpu.SemaphoreType.DMA((n_y - 1, parts))] * 2
    )


def reduce_rows(partial, ride, collective):
    n_row, n_seq = lax.axis_size("row"), lax.axis_size("seq")
    rows, width = partial.shape[0] // n_row, partial.shape[1]
    parts = 4 if rows % 64 == 0 else 2 if rows % 32 == 0 else 1
    buffer = (rows, width)
    return pl.pallas_call(
        functools.partial(reduce_rows_kernel, n_row, n_seq, parts),
        out_shape=(
            jax.ShapeDtypeStruct(buffer, jnp.float32),
            jax.ShapeDtypeStruct(ride.shape, ride.dtype),
        ),
        in_specs=[vmem(), anywhere()],
        out_specs=(vmem(), anywhere()),
        scratch_shapes=[pltpu.SemaphoreType.DMA((3,))]
        + reduce_rows_scratch(n_row // 2, parts, buffer, partial.dtype),
        compiler_params=remote_params(collective, 40),
        name="reduce_rows",
    )(partial, ride)


def ring_neighbours(n_seq):
    n_x = n_seq // GROUPS
    row, seq = lax.axis_index("row"), lax.axis_index("seq")
    place = ring_place(seq, n_x)
    after = (row, ring_member(lax.rem(place + 1, n_seq), n_x))
    before = (row, ring_member(lax.rem(place + n_seq - 1, n_seq), n_x))
    return row, seq, place, after, before


def ring_gather(n_seq, parts, rows, out_ref, send_sem, recv_sem, place, after, before):
    n_x = n_seq // GROUPS
    half = rows // 2
    piece = half // parts
    sent = {}
    for step in range(n_seq - 1):
        for c in range(parts):
            for way in range(2):
                if step:
                    sent[step - 1, c, way].wait_recv()
                shift = n_seq - step if way == 0 else step
                member = ring_member(lax.rem(place + shift, n_seq), n_x)
                where = out_ref.at[span(member * rows + way * half + c * piece, piece)]
                copy = send(
                    where,
                    where,
                    send_sem.at[way, step, c],
                    recv_sem.at[way, step, c],
                    after if way == 0 else before,
                )
                copy.start()
                sent[step, c, way] = copy
    for c in range(parts):
        for way in range(2):
            sent[n_seq - 2, c, way].wait_recv()
    for copy in sent.values():
        copy.wait_send()


def gather_seq_kernel(
    n_row, n_seq, parts, x_ref, up_ref, *refs
):
    out_ref, own_ref, send_sem, recv_sem, send_w, recv_w, local_sem = refs[-7:]
    row, seq, place, after, before = ring_neighbours(n_seq)
    rows = x_ref.shape[0]
    depth, both = up_ref.shape[1:]
    ff_dim = both // 2
    ff_row = ff_dim // n_row
    others = [lax.rem(row + d, n_row) for d in range(1, n_row)]
    greet([after, before] + [(other, seq) for other in others])

    def slabs(dest):
        odd = lax.rem(dest, 2)
        for part in range(2):
            column = part * ff_dim + dest * ff_row
            slot = part * (1 - odd) + (1 - part) * odd
            yield part, (
                up_ref.at[1, :, pl.ds(pl.multiple_of(column, LANES), ff_row)],
                own_ref.at[span(row * depth, depth), pl.ds(pl.multiple_of(slot * ff_row, LANES), ff_row)],
            )

    moved = []
    for d, other in enumerate(others):
        for part, (source, target) in slabs(other):
            copy = send(source, target, send_w.at[d, part], recv_w.at[d, part], (other, seq))
            copy.start()
            moved.append(copy)
    local = []
    for part, (source, target) in slabs(row):
        copy = pltpu.make_async_copy(source, target, local_sem.at[part])
        copy.start()
        local.append(copy)
    out_ref[span(seq * rows, rows), :] = x_ref[...]
    ring_gather(n_seq, parts, rows, out_ref, send_sem, recv_sem, place, after, before)
    for copy in moved + local:
        copy.wait()


def gather_seq(block, up_weight, after=(), collective=15):
    n_row, n_seq = lax.axis_size("row"), lax.axis_size("seq")
    rows, width = block.shape
    parts = 2 if rows % 64 == 0 else 1
    depth, both = up_weight.shape[1:]
    return pl.pallas_call(
        functools.partial(gather_seq_kernel, n_row, n_seq, parts),
        out_shape=(
            jax.ShapeDtypeStruct((n_seq * rows, width), block.dtype),
            jax.ShapeDtypeStruct((depth * n_row, both // n_row), up_weight.dtype),
        ),
        in_specs=[vmem(), anywhere()] + [anywhere()] * len(after),
        out_specs=(vmem(), anywhere()),
        scratch_shapes=[pltpu.SemaphoreType.DMA((2, n_seq - 1, parts))] * 2
        + [pltpu.SemaphoreType.DMA((n_row - 1, 2))] * 2
        + [pltpu.SemaphoreType.DMA((2,))],
        compiler_params=remote_params(collective, 48),
        name="gather_seq",
    )(block, up_weight, *after)


def reduce_seq_kernel(n_seq, parts, x_ref, *refs):
    out_ref, held, send_sem, recv_sem = refs[-4:]
    _, _, _, after, before = ring_neighbours(n_seq)
    greet([after, before])
    reduce_seq_body(n_seq, parts, x_ref, out_ref, held, send_sem, recv_sem)


def reduce_seq_body(n_seq, parts, x_ref, out_ref, held, send_sem, recv_sem):
    n_x = n_seq // GROUPS
    _, seq, place, after, before = ring_neighbours(n_seq)
    rows = out_ref.shape[0]
    half = rows // 2
    piece = half // parts
    sent = {}
    for step in range(n_seq - 1):
        for c in range(parts):
            for way in range(2):
                shift = 2 * n_seq - 1 - step if way == 0 else 1 + step
                member = ring_member(lax.rem(place + shift, n_seq), n_x)
                own = span(member * rows + way * half + c * piece, piece)
                where = pl.ds(c * piece, piece)
                if step:
                    sent[step - 1, c, way].wait_recv()
                    held[way, step - 1, where, :] = (
                        held[way, step - 1, where, :].astype(jnp.float32)
                        + x_ref[own, :].astype(jnp.float32)
                    ).astype(held.dtype)
                    source = held.at[way, step - 1, where]
                else:
                    source = x_ref.at[own]
                copy = send(
                    source,
                    held.at[way, step, where],
                    send_sem.at[way, step, c],
                    recv_sem.at[way, step, c],
                    after if way == 0 else before,
                )
                copy.start()
                sent[step, c, way] = copy
    for c in range(parts):
        for way in range(2):
            sent[n_seq - 2, c, way].wait_recv()
            where = pl.ds(c * piece, piece)
            start = way * half + c * piece
            out_ref[pl.ds(start, piece), :] = (
                held[way, n_seq - 2, where, :].astype(jnp.float32)
                + x_ref[span(seq * rows + start, piece), :].astype(jnp.float32)
            ).astype(out_ref.dtype)
    for copy in sent.values():
        copy.wait_send()


def reduce_seq(partial, after=(), collective=4, dtype=jnp.float32):
    n_seq = lax.axis_size("seq")
    rows, width = partial.shape[0] // n_seq, partial.shape[1]
    if rows % 32:
        return lax.psum_scatter(partial, "seq", scatter_dimension=0, tiled=True).astype(dtype)
    parts = 2 if rows % 64 == 0 else 1
    return pl.pallas_call(
        functools.partial(reduce_seq_kernel, n_seq, parts),
        out_shape=jax.ShapeDtypeStruct((rows, width), dtype),
        in_specs=[vmem()] + [anywhere()] * len(after),
        out_specs=vmem(),
        scratch_shapes=[pltpu.VMEM((2, n_seq - 1, rows // 2, width), partial.dtype)]
        + [pltpu.SemaphoreType.DMA((2, n_seq - 1, parts))] * 2,
        compiler_params=remote_params(collective, 48),
        name="reduce_seq",
    )(partial, *after)


def exchange_kernel(n_row, n_seq, forward, x_ref, decay_ref, *refs):
    if forward:
        out_ref, all_ref, send_sem, recv_sem = refs[-4:]
    else:
        blocks_ref, low_ref = refs[:2]
        out_ref, spread_ref, rows_ref, all_ref, send_sem, recv_sem, send_b, recv_b = refs[-13:-5]
    row, seq, place, after, before = ring_neighbours(n_seq)
    rows = x_ref.shape[0]
    states, planes, _ = decay_ref.shape
    if forward:
        greet([after, before])
    else:
        sibling, across = row_peers(n_row)
        greet([sibling] + across + [(row, lax.rem(seq + d, n_seq)) for d in range(1, n_seq)])
        riding = start_gather_rows(n_row, 4, low_ref, rows_ref, *refs[-5:])
    all_ref[span(seq * rows, rows), :] = x_ref[...]
    ring_gather(n_seq, 1, rows, all_ref, send_sem, recv_sem, place, after, before)
    swapped = [] if forward else start_swap(n_seq, blocks_ref, spread_ref, send_b, recv_b)
    out_ref[...] = jnp.zeros_like(out_ref)

    def take(turn, _):
        other = turn if forward else n_seq - 1 - turn
        used = other < seq if forward else other > seq
        block = all_ref[span(other * rows, rows), :].astype(jnp.float32)
        base = states * planes
        summed = block[base : base + planes] + block[base + planes : base + 2 * planes]
        for n in range(states):
            kept = jnp.exp(decay_ref[n] * summed) * out_ref[n]
            ended = block[n * planes : (n + 1) * planes]
            out_ref[n] = jnp.where(used, kept + ended, out_ref[n])
        return 0

    lax.fori_loop(0, n_seq, take, 0)
    if not forward:
        finish_gather_rows(riding)
    for copy in swapped:
        copy.wait()


def exchange_states(summed, end_state, decay, collective, blocks=None, rider=None, after=()):
    n_row, n_seq = lax.axis_size("row"), lax.axis_size("seq")
    states, planes, _ = decay.shape
    high = summed.astype(jnp.bfloat16)
    lower = (summed - high.astype(jnp.float32)).astype(jnp.bfloat16)
    rows = -(-(states + 2) * planes // 32) * 32
    payload = jnp.concatenate(
        [
            end_state.astype(jnp.bfloat16).reshape(states * planes, LANES),
            high,
            lower,
            jnp.zeros((rows - (states + 2) * planes, LANES), jnp.bfloat16),
        ],
        axis=0,
    )
    ring = [pltpu.VMEM((n_seq * rows, LANES), jnp.bfloat16)] + [
        pltpu.SemaphoreType.DMA((2, n_seq - 1, 1))
    ] * 2
    entering = jax.ShapeDtypeStruct(decay.shape, jnp.float32)
    if blocks is None:
        return pl.pallas_call(
            functools.partial(exchange_kernel, n_row, n_seq, True),
            out_shape=entering,
            in_specs=[vmem(), vmem()] + [anywhere()] * len(after),
            out_specs=vmem(),
            scratch_shapes=ring,
            compiler_params=remote_params(collective, 32),
            name="exchange_states",
        )(payload, decay, *after)
    return pl.pallas_call(
        functools.partial(exchange_kernel, n_row, n_seq, False),
        out_shape=(
            entering,
            jax.ShapeDtypeStruct(blocks.shape, blocks.dtype),
            jax.ShapeDtypeStruct((n_row * rider.shape[0], rider.shape[1]), rider.dtype),
        ),
        in_specs=[vmem()] * 4 + [anywhere()] * len(after),
        out_specs=(vmem(),) * 3,
        scratch_shapes=ring
        + [pltpu.SemaphoreType.DMA((n_seq - 1,))] * 2
        + gather_rows_scratch(n_row // 2, 4),
        compiler_params=remote_params(collective, 40),
        name="exchange_states_back",
    )(payload, decay, blocks, rider, *after)


def start_row_swap(n_row, x_ref, out_ref, send_sem, recv_sem, local_sem):
    row, seq = lax.axis_index("row"), lax.axis_index("seq")
    rows, cols = x_ref.shape[0], out_ref.shape[1]
    mine = out_ref.at[span(row * rows, rows)]
    moved = []
    for d in range(1, n_row):
        other = lax.rem(row + d, n_row)
        copy = send(
            x_ref.at[:, pl.ds(pl.multiple_of(other * cols, LANES), cols)],
            mine,
            send_sem.at[d - 1],
            recv_sem.at[d - 1],
            (other, seq),
        )
        copy.start()
        moved.append(copy)
    own = pltpu.make_async_copy(
        x_ref.at[:, pl.ds(pl.multiple_of(row * cols, LANES), cols)], mine, local_sem
    )
    own.start()
    return moved + [own]


def swap_heads_kernel(
    n_row, n_x, collect, x_ref, rider_ref, *refs
):
    if collect:
        out_ref, rode_ref, send_sem, recv_sem, send_r, recv_r, local_sem = refs
    else:
        part_ref, out_ref, rode_ref, sum_ref, send_sem, recv_sem, send_r, recv_r, local_sem, *scratch = refs
    row, seq = lax.axis_index("row"), lax.axis_index("seq")
    z, x = seq // n_x, lax.rem(seq, n_x)
    peers = [lax.rem(z + d, GROUPS) for d in range(1, GROUPS)]
    greet(
        [(row, peer * n_x + x) for peer in peers]
        + [(lax.rem(row + d, n_row), seq) for d in range(1, n_row)]
    )

    def block(ref, place, wide):
        if wide:
            cols = ref.shape[1] // GROUPS
            return ref.at[:, pl.ds(pl.multiple_of(place * cols, LANES), cols)]
        rows = ref.shape[0] // GROUPS
        return ref.at[span(place * rows, rows)]

    sent = []
    for d, peer in enumerate(peers):
        copy = send(
            block(x_ref, peer, not collect),
            block(out_ref, z, collect),
            send_sem.at[d],
            recv_sem.at[d],
            (row, peer * n_x + x),
        )
        copy.start()
        sent.append(copy)
    riding = start_row_swap(n_row, rider_ref, rode_ref, send_r, recv_r, local_sem)
    block(out_ref, z, collect)[...] = block(x_ref, z, not collect)[...]
    if not collect:
        reduce_rows_body(n_row, 4, part_ref, sum_ref, *scratch)
    for copy in sent + riding:
        copy.wait()


def swap_heads(values, rider, collect, collective, partial=None):
    n_row, n_x = lax.axis_size("row"), lax.axis_size("seq") // GROUPS
    rows, cols = values.shape
    shape = (rows // GROUPS, cols * GROUPS) if collect else (rows * GROUPS, cols // GROUPS)
    narrow = rider.shape[1] // n_row % LANES
    if narrow:
        swapped = lax.all_to_all(rider, "row", split_axis=1, concat_axis=0, tiled=True)
        rider = jnp.zeros((16, n_row * LANES), rider.dtype)
    rode = (rider.shape[0] * n_row, rider.shape[1] // n_row)
    sem = pltpu.SemaphoreType.DMA
    operands = [values, rider]
    outputs = [
        jax.ShapeDtypeStruct(shape, values.dtype),
        jax.ShapeDtypeStruct(rode, rider.dtype),
    ]
    scratch = [sem((GROUPS - 1,))] * 2 + [sem((n_row - 1,))] * 2 + [sem]
    if not collect:
        buffer = (partial.shape[0] // n_row, partial.shape[1])
        operands.append(partial)
        outputs.append(jax.ShapeDtypeStruct(buffer, jnp.float32))
        scratch += reduce_rows_scratch(n_row // 2, 4, buffer, partial.dtype)
    results = pl.pallas_call(
        functools.partial(swap_heads_kernel, n_row, n_x, collect),
        out_shape=tuple(outputs),
        in_specs=[vmem()] * len(operands),
        out_specs=(vmem(),) * len(outputs),
        scratch_shapes=scratch,
        compiler_params=remote_params(collective, 40),
        name="collect_heads" if collect else "spread_heads",
    )(*operands)
    if narrow:
        return (results[0], swapped) + tuple(results[2:])
    return results


def start_swap(n_seq, x_ref, out_ref, send_sem, recv_sem):
    row, seq = lax.axis_index("row"), lax.axis_index("seq")
    place = ring_place(seq, n_seq // GROUPS)
    sent = []
    for d in range(1, n_seq):
        peer = lax.rem(seq + d, n_seq)
        copy = send(
            x_ref.at[peer], out_ref.at[place], send_sem.at[d - 1], recv_sem.at[d - 1], (row, peer)
        )
        copy.start()
        sent.append(copy)
    out_ref[place] = x_ref[seq]
    return sent


def swap_seq_kernel(n_seq, x_ref, out_ref, send_sem, recv_sem):
    row, seq = lax.axis_index("row"), lax.axis_index("seq")
    greet([(row, lax.rem(seq + d, n_seq)) for d in range(1, n_seq)])
    for copy in start_swap(n_seq, x_ref, out_ref, send_sem, recv_sem):
        copy.wait()


def finish_kernel(
    n_row, n_seq, parts, anchors, blocks_ref, packed_ref, *refs
):
    spread_ref, out_ref, send_b, recv_b, rowed, held, send_s, recv_s, *scratch = refs[anchors:]
    rows = out_ref.shape[0]
    row, seq = lax.axis_index("row"), lax.axis_index("seq")
    sibling, across = row_peers(n_row)
    greet([sibling] + across + [(row, lax.rem(seq + d, n_seq)) for d in range(1, n_seq)])
    swapped = start_swap(n_seq, blocks_ref, spread_ref, send_b, recv_b)
    reduce_rows_body(n_row, parts, packed_ref, rowed, *scratch)
    spread = []
    for d in range(1, n_seq):
        peer = lax.rem(seq + d, n_seq)
        copy = send(
            rowed.at[span(peer * rows, rows)], held.at[d - 1], send_s.at[d - 1], recv_s.at[d - 1], (row, peer)
        )
        copy.start()
        spread.append(copy)
    total = rowed[span(seq * rows, rows), :].astype(jnp.float32)
    for d, copy in enumerate(spread):
        copy.wait_recv()
        total = total + held[d].astype(jnp.float32)
    out_ref[...] = total
    for copy in spread:
        copy.wait_send()
    for copy in swapped:
        copy.wait()


def swap_and_reduce(blocks, packed, collective, after=()):
    n_row, n_seq = lax.axis_size("row"), lax.axis_size("seq")
    rows, width = packed.shape[0] // (n_row * n_seq), packed.shape[1]
    if rows % 16:
        summed = lax.psum_scatter(packed, ("row", "seq"), scatter_dimension=0, tiled=True)
        return swap_seq(blocks, collective), summed.astype(jnp.float32)
    buffer = (n_seq * rows, width)
    parts = 4
    sem = pltpu.SemaphoreType.DMA
    return pl.pallas_call(
        functools.partial(finish_kernel, n_row, n_seq, parts, len(after)),
        out_shape=(
            jax.ShapeDtypeStruct(blocks.shape, blocks.dtype),
            jax.ShapeDtypeStruct((rows, width), jnp.float32),
        ),
        in_specs=[vmem()] * 2 + [anywhere()] * len(after),
        out_specs=(vmem(), vmem()),
        scratch_shapes=[sem((n_seq - 1,))] * 2
        + [
            pltpu.VMEM(buffer, packed.dtype),
            pltpu.VMEM((n_seq - 1, rows, width), packed.dtype),
        ]
        + [sem((n_seq - 1,))] * 2
        + reduce_rows_scratch(n_row // 2, parts, buffer, packed.dtype),
        compiler_params=remote_params(collective, 32),
        name="swap_and_reduce",
    )(blocks, packed, *after)


def swap_seq(blocks, collective):
    n_seq = lax.axis_size("seq")
    return pl.pallas_call(
        functools.partial(swap_seq_kernel, n_seq),
        out_shape=jax.ShapeDtypeStruct(blocks.shape, blocks.dtype),
        in_specs=[vmem()],
        out_specs=vmem(),
        scratch_shapes=[pltpu.SemaphoreType.DMA((n_seq - 1,))] * 2,
        compiler_params=remote_params(collective, 32),
        name="swap_seq",
    )(blocks)


def gather_input_kernel(
    parts, x_ref, out_ref, local_sem, own_sem, send_y, recv_y, send_f, recv_f, send_x, recv_x, send_g, recv_g
):
    row, seq = lax.axis_index("row"), lax.axis_index("seq")
    y, core = row // 2, lax.rem(row, 2)
    z, x = seq // 2, lax.rem(seq, 2)
    rows = x_ref.shape[0]
    half = rows // 2
    piece = half // parts
    sibling = (y * 2 + 1 - core, seq)
    over_y = ((1 - y) * 2 + core, seq)
    over_x = (row, z * 2 + 1 - x)
    greet([sibling, over_y, over_x])
    origin = (1 - y) * 2 + core
    first = []
    for c in range(parts):
        copy = send(
            x_ref.at[span(x * half + c * piece, piece)],
            out_ref.at[span(row * rows + x * half + c * piece, piece)],
            send_y.at[c],
            recv_y.at[c],
            over_y,
        )
        copy.start()
        first.append(copy)
    own = send(x_ref, out_ref.at[span(row * rows, rows)], own_sem.at[0], own_sem.at[1], sibling)
    own.start()
    local = pltpu.make_async_copy(x_ref, out_ref.at[span(row * rows, rows)], local_sem)
    local.start()
    rest = []
    side = []
    for c in range(parts):
        first[c].wait_recv()
        where = out_ref.at[span(origin * rows + x * half + c * piece, piece)]
        copy = send(where, where, send_x.at[c], recv_x.at[c], over_x)
        copy.start()
        side.append(copy)
        copy = send(where, where, send_f.at[c], recv_f.at[c], sibling)
        copy.start()
        rest.append(copy)
    for c in range(parts):
        side[c].wait_recv()
        where = out_ref.at[span(origin * rows + (1 - x) * half + c * piece, piece)]
        copy = send(where, where, send_g.at[c], recv_g.at[c], sibling)
        copy.start()
        rest.append(copy)
    local.wait()
    own.wait()
    for copy in first + side:
        copy.wait_send()
    for copy in rest:
        copy.wait()


def gather_input(shard, collective):
    n_row, n_seq = lax.axis_size("row"), lax.axis_size("seq")
    if n_row != 4 or n_seq != 2 * GROUPS:
        return lax.all_gather(shard, "row", axis=0, tiled=True)
    parts = 4
    sem = pltpu.SemaphoreType.DMA
    return pl.pallas_call(
        functools.partial(gather_input_kernel, parts),
        out_shape=jax.ShapeDtypeStruct((n_row * shard.shape[0], shard.shape[1]), shard.dtype),
        in_specs=[pl.BlockSpec(memory_space=pltpu.HBM)],
        out_specs=pl.BlockSpec(memory_space=pltpu.HBM),
        scratch_shapes=[sem, sem((2,))] + [sem((parts,))] * 8,
        compiler_params=remote_params(collective, 16),
        name="gather_input",
    )(shard)


def grad_blocks_kernel(up_rows, down_rows, d_ref, x_ref, h_ref, u_ref, *refs):
    out_ref = refs[-1]
    both = up_rows + down_rows
    out_ref[:up_rows, :] = left_trans(d_ref[...], x_ref[...]).astype(out_ref.dtype)
    out_ref[up_rows:both, :] = left_trans(h_ref[...], u_ref[...]).astype(out_ref.dtype)
    if len(refs) > 1:
        out_ref[both:, :] = refs[0][0]


def grad_blocks(d_gate_up, spread, hidden, upstream, extra=()):
    n_seq = lax.axis_size("seq")
    n_x = n_seq // GROUPS
    tokens, width = spread.shape
    up_rows, down_rows = d_gate_up.shape[1] // n_seq, hidden.shape[1] // n_seq
    rows = up_rows + down_rows + sum(part.shape[1] for part in extra)
    whole = pl.BlockSpec((tokens, width), lambda k: (0, 0))
    return pl.pallas_call(
        functools.partial(grad_blocks_kernel, up_rows, down_rows),
        out_shape=jax.ShapeDtypeStruct((n_seq * rows, width), jnp.bfloat16),
        grid=(n_seq,),
        in_specs=[
            pl.BlockSpec((tokens, up_rows), lambda k: (0, ring_member(k, n_x))),
            whole,
            pl.BlockSpec((tokens, down_rows), lambda k: (0, ring_member(k, n_x))),
            whole,
        ]
        + [
            pl.BlockSpec((1,) + part.shape[1:], lambda k: (ring_member(k, n_x), 0, 0))
            for part in extra
        ],
        out_specs=pl.BlockSpec((rows, width), lambda k: (k, 0)),
        compiler_params=pltpu.CompilerParams(vmem_limit_bytes=44 << 20),
        name="grad_blocks",
    )(d_gate_up, spread, hidden, upstream, *extra)


UNITS = 256
COLUMNS = 512


def mlp_kernel(mode, n_row, n_seq, parts, anchors, *refs):
    forward, both = mode == "forward", mode == "both"
    refs = list(refs)

    def take(count):
        taken = refs[:count]
        del refs[:count]
        return taken

    block_ref, up_ref, down_ref = take(3)
    if both:
        (back_ref,) = take(1)
    elif not forward:
        gate_ref, raise_ref, ride_ref = take(3)
    take(anchors)
    if forward:
        all_ref, sum_ref, hidden_ref, gate_ref, raise_ref = take(5)
    elif both:
        all_ref, sum_ref, hidden_ref, slope_ref, out_ref = take(5)
    else:
        all_ref, sum_ref, slope_ref, rode_ref = take(4)
        back_ref = all_ref
    up, down, local_sem, part, near, stage, far, values_t, back_t, unit_t = take(10)
    send_c, recv_c, send_t, recv_t = take(4)
    gather_scratch = take(5)
    send_y, recv_y, send_f, recv_f, _ = gather_scratch
    riding = not forward and not both
    if riding:
        (ride_sem,) = take(1)

    row, seq = lax.axis_index("row"), lax.axis_index("seq")
    y, core = row // 2, lax.rem(row, 2)
    n_y = n_row // 2
    rows = block_ref.shape[0]
    piece = rows // parts
    width = block_ref.shape[1]
    units = down.shape[0]
    sibling, across = row_peers(n_row)
    beside = y * 2 + 1 - core
    if riding:
        greet_riders([sibling] + across, n_row, n_seq)
    else:
        greet([sibling] + across)
    if riding:
        ridden = start_ride(n_row, n_seq, ride_ref, rode_ref, ride_sem)
    loads = [
        pltpu.make_async_copy(up_ref, up, local_sem.at[0]),
        pltpu.make_async_copy(down_ref, down, local_sem.at[1]),
    ]
    for load in loads:
        load.start()
    started = start_gather_rows(n_row, parts, block_ref, all_ref, *gather_scratch)
    pending, own = started[5], started[6]
    for load in loads:
        load.wait()

    def work(offsets, size):
        spans = [span(offset, size) for offset in offsets]
        many = len(offsets) * size
        used = pl.ds(0, many)

        def joined(ref, cols):
            return jnp.concatenate([ref[here, cols] for here in spans], axis=0)

        def divided(ref, cols, value):
            for i, here in enumerate(spans):
                ref[here, cols] = value[i * size : (i + 1) * size]

        for i, here in enumerate(spans):
            values_t[pl.ds(i * size, size), :] = all_ref[here, :]
            if both:
                back_t[pl.ds(i * size, size), :] = back_ref[here, :]
        back = back_t if both else values_t

        def unit(j, _):
            at = pl.multiple_of(j * UNITS, UNITS)
            low = pl.ds(at, UNITS)
            gate_cols = pl.ds(pl.multiple_of(core * units + at, UNITS), UNITS)
            up_cols = pl.ds(pl.multiple_of((1 - core) * units + at, UNITS), UNITS)
            if forward or both:
                gate = product(values_t[used, :], up[:, gate_cols])
                raised = product(values_t[used, :], up[:, up_cols])
            else:
                gate, raised = joined(gate_ref, low), joined(raise_ref, low)
            share = 1.0 / (1.0 + jnp.exp(-gate))
            active = gate * share
            if forward or both:
                hidden = (active * raised).astype(hidden_ref.dtype)
                divided(hidden_ref, low, hidden)
            if forward:
                unit_t[used, low] = hidden
                divided(gate_ref, low, gate)
                divided(raise_ref, low, raised)
            else:
                d_hidden = right_trans(back[used, :], down[low, :])
                d_gate = d_hidden * raised * share * (1.0 + gate * (1.0 - share))
                d_gate = d_gate.astype(slope_ref.dtype)
                d_raised = (d_hidden * active).astype(slope_ref.dtype)
                unit_t[used, gate_cols] = d_gate
                unit_t[used, up_cols] = d_raised
                divided(slope_ref, gate_cols, d_gate)
                divided(slope_ref, up_cols, d_raised)
            return 0

        lax.fori_loop(0, units // UNITS, unit, 0)

        def column(j, _):
            cols = pl.ds(pl.multiple_of(j * COLUMNS, COLUMNS), COLUMNS)
            if forward:
                total = product(unit_t[used, :], down[:, cols])
            else:
                total = right_trans(unit_t[used, :], up[cols, :])
            divided(part, cols, total.astype(part.dtype))
            return 0

        lax.fori_loop(0, width // COLUMNS, column, 0)

    def to_sibling(d, block, c):
        return send(
            part.at[span(block * rows + c * piece, piece)],
            near.at[d, span(c * piece, piece)],
            send_c.at[d, c],
            recv_c.at[d, c],
            sibling,
        )

    def to_far(d, c):
        where = span(c * piece, piece)
        return send(
            stage.at[d - 1, where],
            far.at[d - 1, where],
            send_t.at[d - 1, c],
            recv_t.at[d - 1, c],
            across[d - 1],
        )

    def forwarded(d, block, c):
        where = all_ref.at[span(block * rows + c * piece, piece)]
        return send(where, where, send_f.at[d, c], recv_f.at[d, c], sibling)

    def arriving(d, c):
        return send(
            block_ref.at[span(c * piece, piece)],
            all_ref.at[span(row * rows + c * piece, piece)],
            send_y.at[d, c],
            recv_y.at[d, c],
            across[d],
        )

    own.wait_recv()
    work([row * rows, beside * rows], rows)
    for c in range(parts):
        to_sibling(0, beside, c).start()
    for d in range(n_y - 1):
        shift = n_y - 1 - d
        there = lax.rem(y + shift, n_y) * 2

        def far_step(c, _, d=d, shift=shift, there=there):
            arriving(d, c).wait_recv()
            forwarded(d, there + core, c).start()
            forwarded(d, there + core, c).wait_recv()
            work([(there + core) * rows + c * piece, (there + 1 - core) * rows + c * piece], piece)
            to_sibling(shift, there + 1 - core, c).start()
            to_sibling(shift, there + 1 - core, c).wait_recv()
            where = span(c * piece, piece)
            total = part[span((there + core) * rows + c * piece, piece), :].astype(
                jnp.float32
            ) + near[shift, where, :].astype(jnp.float32)
            stage[shift - 1, where, :] = total.astype(stage.dtype)
            to_far(shift, c).start()
            return 0

        lax.fori_loop(0, parts, far_step, 0)

    if both:

        def result(i, _):
            here = span(i * rows, rows)

            def column(j, _):
                cols = pl.ds(pl.multiple_of(j * COLUMNS, COLUMNS), COLUMNS)
                out_ref[here, cols] = product(hidden_ref[here, :], down[:, cols]).astype(
                    out_ref.dtype
                )
                return 0

            lax.fori_loop(0, width // COLUMNS, column, 0)
            return 0

        lax.fori_loop(0, n_row, result, 0)

    def last(c, _):
        where = span(c * piece, piece)
        to_sibling(0, beside, c).wait()
        total = part[span(row * rows + c * piece, piece), :].astype(jnp.float32) + near[
            0, where, :
        ].astype(jnp.float32)
        for d in range(n_y - 1):
            to_far(d + 1, c).wait()
            total = total + far[d, where, :].astype(jnp.float32)
        sum_ref[where, :] = total
        for d in range(n_y - 1):
            shift = n_y - 1 - d
            there = lax.rem(y + shift, n_y) * 2
            to_sibling(shift, there + 1 - core, c).wait_send()
            forwarded(d, there + core, c).wait_send()
            arriving(d, c).wait_send()
        return 0

    lax.fori_loop(0, parts, last, 0)
    own.wait_send()
    if riding:
        finish_ride(ridden)


def mlp_fused(mode, block, up_own, down_own, extra, after, collective, ride=()):
    n_row, n_seq = lax.axis_size("row"), lax.axis_size("seq")
    n_y = n_row // 2
    rows, width = block.shape
    units = down_own.shape[0]
    parts = 2
    total = n_row * rows
    low, high = jnp.bfloat16, jnp.float32
    shapes = [((total, width), low), ((rows, width), high)]
    if mode == "forward":
        shapes += [((total, units), low), ((total, units), high), ((total, units), high)]
    elif mode == "both":
        shapes += [((total, units), low), ((total, 2 * units), low), ((total, width), low)]
    else:
        shapes += [((total, 2 * units), low)]
    shapes += [(rider.shape, rider.dtype) for rider in ride]
    sem = pltpu.SemaphoreType.DMA
    buffer = (rows, width)
    return pl.pallas_call(
        functools.partial(mlp_kernel, mode, n_row, n_seq, parts, len(after)),
        out_shape=tuple(jax.ShapeDtypeStruct(*shape) for shape in shapes),
        in_specs=[vmem(), anywhere(), anywhere()]
        + [vmem()] * len(extra)
        + [anywhere()] * (len(ride) + len(after)),
        out_specs=(vmem(),) * (len(shapes) - len(ride)) + (anywhere(),) * len(ride),
        scratch_shapes=[
            pltpu.VMEM(up_own.shape, low),
            pltpu.VMEM(down_own.shape, low),
            sem((2,)),
            pltpu.VMEM((total, width), low),
            pltpu.VMEM((n_y,) + buffer, low),
            pltpu.VMEM((n_y - 1,) + buffer, low),
            pltpu.VMEM((n_y - 1,) + buffer, low),
            pltpu.VMEM((2 * rows, width), low),
            pltpu.VMEM((2 * rows, width) if mode == "both" else (16, LANES), low),
            pltpu.VMEM((2 * rows, units if mode == "forward" else 2 * units), low),
        ]
        + [sem((n_y, parts))] * 2
        + [sem((n_y - 1, parts))] * 2
        + gather_rows_scratch(n_y, parts)
        + [sem((3,))] * len(ride),
        compiler_params=remote_params(collective, 56),
        name="mlp_" + mode,
    )(block, up_own, down_own, *extra, *ride, *after)


def cycle(depth, breadth):
    order = [(z, 0) for z in range(depth)]
    for turn in range(depth):
        across = range(1, breadth) if turn % 2 == 0 else range(breadth - 1, 0, -1)
        order += [(depth - 1 - turn, x) for x in across]
    return order


def seq_order():
    n_x = lax.axis_size("seq") // GROUPS
    return [z * n_x + x for z, x in cycle(GROUPS, n_x)]


def plane_order():
    n_x = lax.axis_size("seq") // GROUPS
    order = []
    for y, x in cycle(lax.axis_size("row") // 2, n_x):
        cores = (0, 1) if len(order) // 2 % 2 == 0 else (1, 0)
        order += [(2 * y + core, x) for core in cores]
    return order


def plane_groups():
    n_seq = lax.axis_size("seq")
    n_x = n_seq // GROUPS
    return [[r * n_seq + z * n_x + x for r, x in plane_order()] for z in range(GROUPS)]


def owner_blocks(half):
    n_row, n_seq = lax.axis_size("row"), lax.axis_size("seq")
    rows, columns = half.shape
    owned = columns // (n_row // 2 * n_seq)
    shaped = half.reshape(rows, n_row // 2, n_seq, owned).transpose(2, 0, 1, 3)
    return shaped.reshape(n_seq, rows, n_row // 2 * owned)


def input_term(spread, gathered):
    flat = spread.reshape(-1, spread.shape[2])
    return left_trans(flat, gathered).astype(jnp.bfloat16)


def norm_apply(values, gain_row):
    factor = lax.rsqrt(jnp.mean(values * values, axis=-1, keepdims=True) + eps)
    return (values * factor * gain_row, factor)


def norm_back(values, factor, gain_row, upstream):
    normed = values * factor
    weighted = upstream * gain_row
    gain_grad = jnp.sum(upstream * normed, axis=0)
    value_grad = factor * (weighted - normed * jnp.mean(weighted * normed, axis=-1, keepdims=True))
    return (value_grad, gain_grad)


def doc_index(positions, lengths):
    ends_at = jnp.cumsum(lengths)
    return jnp.sum((positions[:, None] >= ends_at[None, :]).astype(jnp.int32), axis=1)


def first_allowed(positions, lengths):
    ends_at = jnp.cumsum(lengths)
    begins = jnp.max(jnp.where(positions[:, None] >= ends_at[None, :], ends_at[None, :], 0), axis=1)
    return jnp.maximum(begins, positions - (WINDOW - 1)).astype(jnp.int32)


def conv_masks(positions, lengths):
    own_doc = doc_index(positions, lengths)
    rows_out = []
    for tap_index in range(CONV):
        earlier = positions - (CONV - 1) + tap_index
        rows_out.append(
            ((earlier >= 0) & (doc_index(earlier, lengths) == own_doc)).astype(jnp.float32)
        )
    return jnp.stack(rows_out, axis=0)


def rotary_tables(positions):
    half_dim = HEAD_DIM // 2
    frequency = jnp.power(rope_base, -2.0 * jnp.arange(half_dim).astype(jnp.float32) / HEAD_DIM)
    angles = positions.astype(jnp.float32)[:, None] * frequency[None, :]
    cosine, sine_tab = (jnp.cos(angles), jnp.sin(angles))
    return (
        jnp.concatenate([cosine, cosine], axis=1),
        jnp.concatenate([-sine_tab, sine_tab], axis=1),
    )


def own_up_columns(up_local, number):
    n_row = lax.axis_size("row")
    row = lax.axis_index("row")
    depth, both = up_local.shape[1:]
    ff_dim = both // 2
    ff_row = ff_dim // n_row
    width = depth * n_row

    def slab(dest):
        odd = dest % 2
        halves = [
            lax.dynamic_slice(
                up_local, (number, 0, half * ff_dim + dest * ff_row), (1, depth, ff_row)
            )[0]
            for half in (odd, 1 - odd)
        ]
        return jnp.concatenate(halves, axis=1)

    whole = jnp.zeros((width, 2 * ff_row), up_local.dtype)
    for turn in range(n_row):
        other = row ^ turn
        piece = slab(other)
        if turn:
            piece = lax.ppermute(piece, "row", [(i, i ^ turn) for i in range(n_row)])
        whole = lax.dynamic_update_slice(whole, piece, (other * depth, 0))
    return whole


def mlp_gradients(spread, hidden, d_gate_up, upstream_all, extra=(), before=()):
    n_seq = lax.axis_size("seq")
    width = spread.shape[1]
    up_rows = d_gate_up.shape[1] // n_seq
    if extra:
        extra = [part.astype(jnp.bfloat16).reshape(n_seq, -1, width) for part in extra]
        extra = [jnp.concatenate(extra, axis=1)]
    if up_rows % (2 * LANES) or (extra and extra[0].shape[1] % 16):
        parts = [left_trans(d_gate_up, spread), left_trans(hidden, upstream_all)]
        parts = [part.astype(jnp.bfloat16).reshape(n_seq, -1, width) for part in parts]
        merged = jnp.concatenate(parts + list(extra), axis=1)[jnp.array(seq_order())]
        merged = merged.reshape(-1, width)
    else:
        merged = grad_blocks(d_gate_up, spread, hidden, upstream_all, extra)
    merged = lax.optimization_barrier((merged,) + before)[0]
    summed = lax.psum_scatter(
        merged, "seq", scatter_dimension=0, tiled=True, axis_index_groups=[seq_order()]
    )
    down_end = up_rows + up_rows // 2
    return (merged, summed[:up_rows], summed[up_rows:down_end], summed[down_end:])


def matchings(edges, size):
    rounds = []
    left = list(range(len(edges)))
    while left:
        taken = {}

        def assign(source, seen):
            for e in left:
                if edges[e][0] == source and edges[e][1] not in seen:
                    seen.add(edges[e][1])
                    if edges[e][1] not in taken or assign(edges[taken[edges[e][1]]][0], seen):
                        taken[edges[e][1]] = e
                        return True
            return False

        for source in range(size):
            assign(source, set())
        chosen = sorted(taken.values())
        rounds.append(chosen)
        left = [e for e in left if e not in chosen]
    return rounds


def place_attn_grad(piece, width):
    n_row = lax.axis_size("row")
    n_seq = lax.axis_size("seq")
    n_x = n_seq // GROUPS
    size = n_row * n_seq
    me = lax.axis_index("row") * n_seq + lax.axis_index("seq")
    group_cols = width // GROUPS
    owned = piece.shape[0]
    unit = math.gcd(owned, group_cols)
    count = owned // unit
    edges, slots = [], []
    for member, (r, x) in enumerate(plane_order()):
        for z in range(GROUPS):
            for u in range(count):
                local = member * owned + u * unit
                column = (local // group_cols) * width + z * group_cols + local % group_cols
                edges.append((r * n_seq + z * n_x + x, column // owned))
                slots.append((u, column % owned // unit))
    result = jnp.zeros_like(piece)
    for chosen in matchings(edges, size):
        send_slot = [0] * size
        recv_slot = [0] * size
        for e in chosen:
            send_slot[edges[e][0]] = slots[e][0]
            recv_slot[edges[e][1]] = slots[e][1]
        taken = lax.dynamic_slice(
            piece, (jnp.array(send_slot, jnp.int32)[me] * unit, 0), (unit, piece.shape[1])
        )
        moved = lax.ppermute(taken, ("row", "seq"), [edges[e] for e in chosen])
        result = lax.dynamic_update_slice(
            result, moved, (jnp.array(recv_slot, jnp.int32)[me] * unit, 0)
        )
    return result


def per_device(
    tokens,
    norm_gain,
    input_weight,
    conv_weight,
    conv_bias,
    select_weight,
    step_weight,
    step_bias,
    decay_log,
    skip_scale,
    output_weight,
    attn_gain,
    attn_weight,
    attn_output,
    mlp_gain,
    mlp_up_weight,
    mlp_down_weight,
    doc_lengths,
    cotangent,
):
    n_row = lax.axis_size("row")
    n_seq = lax.axis_size("seq")
    n_x = n_seq // GROUPS
    rows_here = tokens.shape[1]
    width = tokens.shape[2]
    inner_dim = skip_scale.shape[0]
    rank_dim = step_weight.shape[0]
    state_dim = decay_log.shape[1]
    head_count = HEADS // GROUPS
    group_cols = head_count * HEAD_DIM
    lengths = doc_lengths[0]
    seq_index = lax.axis_index("seq")
    z_index = seq_index // n_x
    x_index = seq_index % n_x
    positions = seq_index * rows_here + jnp.arange(rows_here, dtype=jnp.int32)
    gain_in = norm_gain.astype(jnp.float32)
    gain_attn = attn_gain.astype(jnp.float32)
    gains_mlp = mlp_gain.astype(jnp.float32)
    conv_taps = conv_weight.astype(jnp.float32)
    skip_row = skip_scale.astype(jnp.float32)
    decays = -jnp.exp(decay_log.astype(jnp.float32)).T
    decay_planes = decays.reshape(state_dim, inner_dim // LANES, LANES)
    source = tokens[0].astype(jnp.float32)
    own_doc = doc_index(positions, lengths)
    keep_flag = ((positions > 0) & (own_doc == doc_index(positions - 1, lengths))).astype(
        jnp.float32
    )
    keep_lanes = jnp.broadcast_to(keep_flag[:, None], (rows_here, LANES))
    tap_masks = conv_masks(positions, lengths)
    whole_in = gather_input(input_weight, 10)
    up_local = lax.optimization_barrier((mlp_up_weight, whole_in))[0]
    up_first = own_up_columns(up_local, 0)
    down_first, down_last = (mlp_down_weight[0], mlp_down_weight[1])
    normed_in, factor_in = norm_apply(source, gain_in)
    low_in = normed_in.astype(jnp.bfloat16)
    low_sent, grad_sent = lax.optimization_barrier((low_in, cotangent[0], whole_in))[:2]
    gathered_in = lax.all_gather(
        low_sent, "seq", axis=0, tiled=True, axis_index_groups=[seq_order()]
    )
    gathered_grad = lax.all_gather(grad_sent, "row", axis=0, tiled=True)
    mixed_in = product(low_in, whole_in)
    conv_input = mixed_in[:, :inner_dim]
    gate_input = mixed_in[:, inner_dim:]
    halo_rows = from_behind(
        conv_input[rows_here - (CONV - 1) :].astype(jnp.bfloat16), "seq", 1
    ).astype(jnp.float32)
    padded = jnp.concatenate([halo_rows, conv_input], axis=0)
    conv_pre = conv_bias.astype(jnp.float32)
    for tap_index in range(CONV):
        conv_pre = (
            conv_pre
            + conv_taps[tap_index]
            * padded[tap_index : tap_index + rows_here]
            * tap_masks[tap_index][:, None]
        )
    activated_low = jax.nn.silu(conv_pre).astype(jnp.bfloat16)
    activated = activated_low.astype(jnp.float32)
    picked = product(activated_low, select_weight)
    step_low = picked[:, :rank_dim].astype(jnp.bfloat16)
    step_pre = product(step_low, step_weight) + step_bias
    step_size = jax.nn.softplus(step_pre)
    in_flat = picked[:, rank_dim : rank_dim + state_dim].reshape(-1)
    read_flat = picked[:, rank_dim + state_dim :].reshape(-1)
    local_end = scan_end(step_size, activated_low, keep_lanes, in_flat, decay_planes)
    summed_steps = jnp.where(
        jnp.min(keep_flag) > 0, jnp.sum(step_size, axis=0), RESET
    ).reshape(-1, LANES)
    start_hidden = exchange_states(
        summed_steps, local_end, decay_planes, 5
    )
    scanned, marks = scan_out(
        start_hidden, step_size, activated_low, keep_lanes, in_flat, read_flat, decay_planes
    )
    mamba_out = scanned + skip_row * activated
    gate_act = jax.nn.silu(gate_input)
    gated = (mamba_out * gate_act).astype(jnp.bfloat16)
    first_out = source + product(gated, output_weight)
    normed_first, factor_first = norm_apply(first_out, gains_mlp[0])
    spread_first, second_sum, hidden_first, gate_first, raise_first = mlp_fused(
        "forward", normed_first.astype(jnp.bfloat16), up_first, down_first, (), (), 1
    )
    second_out = first_out + second_sum
    normed_attn, factor_attn = norm_apply(second_out, gain_attn)
    context, up_last = gather_seq(normed_attn.astype(jnp.bfloat16), mlp_up_weight, (gathered_in,))
    length = context.shape[0]
    head_weight = jnp.concatenate(
        [
            lax.dynamic_slice(
                attn_weight, (0, part * width + z_index * group_cols), (width, group_cols)
            )
            for part in range(3)
        ],
        axis=1,
    )
    cosine, sine_tab = rotary_tables(jnp.arange(length, dtype=jnp.int32))
    block_starts = (jnp.arange(GROUPS, dtype=jnp.int32) * n_x + x_index) * rows_here
    query_pos = (
        block_starts[:, None] + jnp.arange(rows_here, dtype=jnp.int32)[None, :]
    ).reshape(-1)
    first_key = first_allowed(query_pos, lengths)
    lows = jnp.min(first_key.reshape(GROUPS, rows_here), axis=1)
    x_array = x_index.reshape(1).astype(jnp.int32)
    triple = project_heads(context, head_weight, cosine, sine_tab, 2 * group_cols)
    attended, log_total = attend(
        x_array, lows, triple, first_key[:, None], n_x, head_count, rows_here
    )
    attended_low, gated_rows = swap_heads(attended, gated, True, 7)
    third_out = second_out + product(attended_low, attn_output)
    normed_last, factor_last = norm_apply(third_out, gains_mlp[1])
    spread_last, d_normed_last, hidden_last, slope_last, final_partial = mlp_fused(
        "both", normed_last.astype(jnp.bfloat16), up_last, down_last, (gathered_grad,), (), 2
    )
    summed_last = mlp_gradients(spread_last, hidden_last, slope_last, gathered_grad)[1:3]
    d_norm_last, g_gain_last = norm_back(third_out, factor_last, gains_mlp[1], d_normed_last)
    d_third = cotangent[0].astype(jnp.float32) + d_norm_last
    d_third_low = d_third.astype(jnp.bfloat16)
    d_third_rows = lax.all_gather(d_third_low, "row", axis=0, tiled=True)
    d_attended, attended_rows, final_sum = swap_heads(
        right_trans(d_third_low, attn_output).astype(jnp.bfloat16),
        attended_low,
        False,
        8,
        final_partial,
    )
    output = (third_out + final_sum).astype(jnp.bfloat16)
    g_down_last = summed_last[1].astype(jnp.float32)
    d_query, d_keys, d_values = attend_back(
        x_array,
        lows,
        triple,
        attended,
        d_attended,
        log_total,
        first_key[:, None],
        cosine,
        sine_tab,
        n_x,
        head_count,
        rows_here,
    )
    own_x = (jnp.arange(n_x) == x_index)[None, :, None, None]
    d_query_full = jnp.where(
        own_x, d_query.reshape(GROUPS, 1, rows_here, group_cols), jnp.bfloat16(0)
    ).reshape(length, group_cols)
    d_triple = jnp.concatenate([d_query_full, d_keys, d_values], axis=1)
    d_attn_normed = reduce_seq(
        right_trans(d_triple, head_weight).astype(jnp.bfloat16), tuple(summed_last)
    )
    g_attn_local = left_trans(d_triple, context).astype(jnp.bfloat16)
    g_attn_local = lax.optimization_barrier((g_attn_local, d_attn_normed))[0]
    g_attn_weight = lax.psum_scatter(
        g_attn_local,
        ("row", "seq"),
        scatter_dimension=0,
        tiled=True,
        axis_index_groups=plane_groups(),
    )
    d_attn_norm, g_attn_gain = norm_back(
        second_out, factor_attn, gain_attn, d_attn_normed
    )
    d_second = d_third + d_attn_norm
    second_rows, d_normed_first, slope_first, up_placed = mlp_fused(
        "backward",
        d_second.astype(jnp.bfloat16),
        up_first,
        down_first,
        (gate_first, raise_first),
        (d_third_rows,),
        3,
        (summed_last[0],),
    )
    d_norm_first, g_gain_first = norm_back(first_out, factor_first, gains_mlp[0], d_normed_first)
    d_first = d_second + d_norm_first
    d_first_low = d_first.astype(jnp.bfloat16)
    d_gated = right_trans(d_first_low, output_weight)
    d_scanned = d_gated * gate_act
    gate_sig = jax.nn.sigmoid(gate_input)
    d_gate = d_gated * mamba_out * gate_sig * (1.0 + gate_input * (1.0 - gate_sig))
    d_gate_low = d_gate.astype(jnp.bfloat16)
    g_skip_scale = jnp.sum(d_scanned * activated, axis=0)
    back_end = adjoint_end(
        step_size, d_scanned, keep_lanes, read_flat, decay_planes
    )
    end_grad, gate_spread, d_first_rows = exchange_states(
        summed_steps, back_end, decay_planes, 6, owner_blocks(d_gate_low), d_first_low
    )
    merged_first, up_first_sum, g_down_first, tail_sum = mlp_gradients(
        spread_first,
        hidden_first,
        slope_first,
        second_rows,
        (left_trans(gated_rows, d_first_rows), left_trans(attended_rows, d_third_rows)),
        (g_attn_weight, end_grad),
    )
    g_step, g_activated, in_lanes, read_lanes, g_decays = adjoint_full(
        end_grad,
        marks,
        step_size,
        activated_low,
        d_scanned,
        keep_lanes,
        in_flat,
        read_flat,
        decay_planes,
        (merged_first,),
    )
    g_up_last = up_placed.astype(jnp.float32).T
    g_attn_weight = lax.optimization_barrier((g_attn_weight, end_grad))[0]
    attn_placed = place_attn_grad(g_attn_weight, width)
    g_attn_weight = attn_placed.astype(jnp.float32).T
    g_down_first = g_down_first.astype(jnp.float32)
    output_rows = inner_dim // (n_row * n_seq)
    g_output_weight = tail_sum[:output_rows].astype(jnp.float32)
    g_attn_output = tail_sum[output_rows:].astype(jnp.float32)
    g_input_map = jnp.sum(in_lanes.reshape(rows_here, state_dim, LANES), axis=2)
    g_read_map = jnp.sum(read_lanes.reshape(rows_here, state_dim, LANES), axis=2)
    g_decay_log = g_decays.reshape(state_dim, inner_dim) * decays
    d_step_pre = g_step * jax.nn.sigmoid(step_pre)
    g_step_bias = jnp.sum(d_step_pre, axis=0)
    d_step_low = d_step_pre.astype(jnp.bfloat16)
    d_picked = jnp.concatenate(
        [right_trans(d_step_low, step_weight), g_input_map, g_read_map], axis=1
    ).astype(jnp.bfloat16)
    g_select_weight = left_trans(activated_low, d_picked)
    d_activated = d_scanned * skip_row + g_activated + right_trans(d_picked, select_weight)
    pre_sig = jax.nn.sigmoid(conv_pre)
    d_conv_pre = d_activated * pre_sig * (1.0 + conv_pre * (1.0 - pre_sig))
    g_conv_bias = jnp.sum(d_conv_pre, axis=0)
    tap_grads = []
    d_padded = jnp.zeros((rows_here + CONV - 1, inner_dim), jnp.float32)
    for tap_index in range(CONV):
        masked = d_conv_pre * tap_masks[tap_index][:, None]
        tap_grads.append(jnp.sum(masked * padded[tap_index : tap_index + rows_here], axis=0))
        d_padded = d_padded + jnp.pad(
            masked * conv_taps[tap_index], ((tap_index, CONV - 1 - tap_index), (0, 0))
        )
    g_conv_weight = jnp.stack(tap_grads, axis=0)
    back_rows = from_behind(d_padded[: CONV - 1].astype(jnp.bfloat16), "seq", -1)
    d_conv_input = d_padded[CONV - 1 :] + jnp.pad(back_rows, ((rows_here - (CONV - 1), 0), (0, 0)))
    d_conv_low = d_conv_input.astype(jnp.bfloat16)
    d_mixed = jnp.concatenate([d_conv_low, d_gate_low], axis=1)
    d_normed_in = right_trans(d_mixed, whole_in)
    d_source, g_norm_gain = norm_back(source, factor_in, gain_in, d_normed_in)
    tokens_grad = (d_first + d_source).astype(jnp.bfloat16)

    owners = n_row * n_seq
    gains = jnp.stack([g_norm_gain, g_attn_gain, g_gain_first, g_gain_last], axis=0)
    gain_rows = gains.size // inner_dim
    lines = [
        g_decay_log,
        g_conv_weight,
        g_conv_bias[None],
        g_step_bias[None],
        g_skip_scale[None],
        gains.reshape(gain_rows, -1, owners, width // owners)
        .transpose(0, 2, 1, 3)
        .reshape(gain_rows, inner_dim),
    ]
    used = sum(part.shape[0] for part in lines)
    columns = [g_select_weight, left_trans(d_step_low, step_low)]
    spare = -(used + sum(part.shape[1] for part in columns)) % LANES
    lines.append(jnp.zeros((spare, inner_dim), jnp.float32))
    packed = jnp.concatenate(columns + [jnp.concatenate(lines, axis=0).T], axis=1)
    conv_spread, summed = swap_and_reduce(
        owner_blocks(d_conv_low), packed.astype(jnp.bfloat16), 11, (attn_placed,)
    )
    g_input_weight, first_placed = reduce_rows(
        jnp.concatenate(
            [input_term(conv_spread, gathered_in), input_term(gate_spread, gathered_in)], axis=0
        ),
        up_first_sum,
        13,
    )
    g_input_weight = g_input_weight.T
    g_up_first = first_placed.astype(jnp.float32).T
    at = columns[0].shape[1]
    small_select = summed[:, :at]
    small_step = summed[:, at : at + rank_dim].T
    tail = summed[:, at + rank_dim :]
    small_lines = tail.T
    small = []
    at = 0
    for part in lines[:-1]:
        small.append(small_lines[at : at + part.shape[0]])
        at += part.shape[0]
    gain_sums = (
        small[5].reshape(gain_rows, -1, width // owners).reshape(4, width // owners)
    )
    return (
        output[None],
        tokens_grad[None],
        gain_sums[0],
        g_input_weight,
        small[1],
        small[2][0],
        small_select,
        small_step,
        small[3][0],
        tail[:, :state_dim],
        small[4][0],
        g_output_weight,
        gain_sums[1],
        g_attn_weight,
        g_attn_output,
        gain_sums[2:],
        jnp.stack([g_up_first, g_up_last], axis=0),
        jnp.stack([g_down_first, g_down_last], axis=0),
    )


def solution(mesh):
    return jax.shard_map(
        per_device,
        mesh=mesh,
        in_specs=(
            P("row", "seq", None),
            P(),
            P("row", None),
            P(),
            P(),
            P(),
            P(),
            P(),
            P(),
            P(),
            P(),
            P(),
            P(),
            P(),
            P(),
            P(None, "row", None),
            P(None, "row", None),
            P("row", None),
            P("row", "seq", None),
        ),
        out_specs=(
            P("row", "seq", None),
            P("row", "seq", None),
            P(("row", "seq")),
            P(None, ("row", "seq")),
            P(None, ("row", "seq")),
            P(("row", "seq")),
            P(("row", "seq"), None),
            P(None, ("row", "seq")),
            P(("row", "seq")),
            P(("row", "seq"), None),
            P(("row", "seq")),
            P(("row", "seq"), None),
            P(("row", "seq")),
            P(None, ("row", "seq")),
            P(("row", "seq"), None),
            P(None, ("row", "seq")),
            P(None, None, ("row", "seq")),
            P(None, ("row", "seq"), None),
        ),
        check_vma=False,
    )
```

```python
import functools
import math

import jax
import jax.numpy as jnp
from jax import lax
from jax.experimental import pallas as pl
from jax.experimental.pallas import tpu as pltpu
from jax.sharding import PartitionSpec as P

LANES = 128
CHUNK = 32
RESET = 1e9
LOG2E = 1.4426950408889634
CONV = 4
HEADS = 12
HEAD_DIM = 128
WINDOW = 2048
GROUPS = 4
eps = 1e-05
rope_base = 10000.0


def from_behind(x, axis, by):
    length = lax.axis_size(axis)
    pairs = [(i, i + by) for i in range(length) if 0 <= i + by < length]
    return lax.ppermute(x, axis, pairs)


def product(left_op, right_op):
    return jnp.dot(left_op, right_op, preferred_element_type=jnp.float32)


def left_trans(left_op, right_op):
    return lax.dot_general(
        left_op, right_op, (((0,), (0,)), ((), ())), preferred_element_type=jnp.float32
    )


def right_trans(left_op, right_op):
    return lax.dot_general(
        left_op, right_op, (((1,), (1,)), ((), ())), preferred_element_type=jnp.float32
    )


def to_planes(tile_ref, value, group):
    for block in range(8):
        tile_ref[pl.ds(group * 64 + block * 8, 8), :] = value[:, block * LANES : (block + 1) * LANES]


def plane(tile_ref, index):
    return tile_ref[pl.ds((index // 8) * 64 + index % 8, 8, stride=8), :]


def tree_sum(terms):
    terms = list(terms)
    while len(terms) > 1:
        terms = [
            terms[i] + terms[i + 1] if i + 1 < len(terms) else terms[i]
            for i in range(0, len(terms), 2)
        ]
    return terms[0]


def scan_forward_kernel(
    with_output, states, chunk, *refs
):
    if with_output:
        (start_ref, step_ref, act_ref, keep_ref, in_ref, read_ref, decay_ref,
         out_ref, marks_ref, hidden_ref, step_t, drive_t, out_t) = refs
    else:
        (step_ref, act_ref, keep_ref, in_ref, decay_ref,
         end_ref, hidden_ref, step_t, drive_t) = refs
    index = pl.program_id(0)
    groups = step_ref.shape[1] // (8 * LANES)

    @pl.when(index == 0)
    def _():
        if with_output:
            hidden_ref[...] = start_ref[...]
        else:
            hidden_ref[...] = jnp.zeros_like(hidden_ref)

    if with_output:
        marks_ref[0] = hidden_ref[...]
    for group in range(groups):
        cols = pl.ds(group * 8 * LANES, 8 * LANES)
        for block in range(chunk // 8):
            rows = pl.ds(block * 8, 8)
            rate = step_ref[rows, cols]
            keep = keep_ref[rows, :]
            gated = jnp.where(jnp.concatenate([keep] * 8, axis=1) > 0, rate, RESET)
            to_planes(step_t, gated, block)
            to_planes(drive_t, rate * act_ref[rows, cols].astype(jnp.float32), block)
        decay = [decay_ref[n, pl.ds(group * 8, 8), :] * LOG2E for n in range(states)]

        def eight(block, hidden):
            hidden = list(hidden)
            for r in range(8):
                pos = index * chunk + block * 8 + r
                rate = step_t[pl.ds(block * 64 + r, 8, stride=8), :]
                drive = drive_t[pl.ds(block * 64 + r, 8, stride=8), :]
                terms = []
                for n in range(states):
                    hidden[n] = jnp.exp2(decay[n] * rate) * hidden[n] + drive * in_ref[pos * states + n]
                    if with_output:
                        terms.append(hidden[n] * read_ref[pos * states + n])
                if with_output:
                    out_t[pl.ds(block * 64 + r, 8, stride=8), :] = tree_sum(terms)
            return tuple(hidden)

        hidden = tuple(hidden_ref[n, pl.ds(group * 8, 8), :] for n in range(states))
        hidden = lax.fori_loop(0, chunk // 8, eight, hidden)
        for n in range(states):
            hidden_ref[n, pl.ds(group * 8, 8), :] = hidden[n]
        if with_output:
            for block in range(chunk // 8):
                for lane_block in range(8):
                    out_ref[pl.ds(block * 8, 8), pl.ds(group * 1024 + lane_block * LANES, LANES)] = out_t[
                        pl.ds(block * 64 + lane_block * 8, 8), :
                    ]
    if not with_output:
        end_ref[...] = hidden_ref[...]


def smem():
    return pl.BlockSpec(memory_space=pltpu.SMEM)


def scan_end(step, act, keep_lanes, in_flat, decay):
    rows, inner = step.shape
    states, planes, _ = decay.shape
    chunk = CHUNK
    whole = pl.BlockSpec((states, planes, LANES), lambda i: (0, 0, 0))
    rowed = pl.BlockSpec((chunk, inner), lambda i: (i, 0))
    return pl.pallas_call(
        functools.partial(scan_forward_kernel, False, states, chunk),
        out_shape=jax.ShapeDtypeStruct(decay.shape, jnp.float32),
        grid=(rows // chunk,),
        in_specs=[rowed, rowed, pl.BlockSpec((chunk, LANES), lambda i: (i, 0)), smem(), whole],
        out_specs=whole,
        scratch_shapes=[pltpu.VMEM(decay.shape, jnp.float32)]
        + [pltpu.VMEM((chunk * 8, LANES), jnp.float32)] * 2,
        compiler_params=pltpu.CompilerParams(vmem_limit_bytes=32 << 20),
        name="scan_end",
    )(step, act, keep_lanes, in_flat, decay)


def scan_out(start, step, act, keep_lanes, in_flat, read_flat, decay):
    rows, inner = step.shape
    states, planes, _ = decay.shape
    chunk = CHUNK
    whole = pl.BlockSpec((states, planes, LANES), lambda i: (0, 0, 0))
    rowed = pl.BlockSpec((chunk, inner), lambda i: (i, 0))
    return pl.pallas_call(
        functools.partial(scan_forward_kernel, True, states, chunk),
        out_shape=(
            jax.ShapeDtypeStruct((rows, inner), jnp.float32),
            jax.ShapeDtypeStruct((rows // chunk,) + decay.shape, jnp.float32),
        ),
        grid=(rows // chunk,),
        in_specs=[whole, rowed, rowed, pl.BlockSpec((chunk, LANES), lambda i: (i, 0)), smem(), smem(), whole],
        out_specs=(rowed, pl.BlockSpec((1, states, planes, LANES), lambda i: (i, 0, 0, 0))),
        scratch_shapes=[pltpu.VMEM(decay.shape, jnp.float32)]
        + [pltpu.VMEM((chunk * 8, LANES), jnp.float32)] * 3,
        compiler_params=pltpu.CompilerParams(vmem_limit_bytes=32 << 20),
        name="scan_out",
    )(start, step, act, keep_lanes, in_flat, read_flat, decay)


def adjoint_end_kernel(states, chunk, step_ref, grad_ref, keep_ref, read_ref, decay_ref, *refs):
    end_ref, carry_ref, step_t, grad_t = refs[-4:]
    index = pl.program_id(0)
    last = pl.num_programs(0) - 1
    groups = step_ref.shape[1] // (8 * LANES)

    @pl.when(index == 0)
    def _():
        carry_ref[...] = jnp.zeros_like(carry_ref)

    for group in range(groups):
        cols = pl.ds(group * 8 * LANES, 8 * LANES)
        for block in range(chunk // 8):
            rows = pl.ds(block * 8, 8)
            keep = keep_ref[rows, :]
            to_planes(step_t, jnp.where(jnp.concatenate([keep] * 8, axis=1) > 0, step_ref[rows, cols], RESET), block)
            to_planes(grad_t, grad_ref[rows, cols], block)
        decay = [decay_ref[n, pl.ds(group * 8, 8), :] * LOG2E for n in range(states)]

        def eight(turn, carry):
            carry = list(carry)
            block = chunk // 8 - 1 - turn
            for r in range(7, -1, -1):
                pos = (last - index) * chunk + block * 8 + r
                rate = step_t[pl.ds(block * 64 + r, 8, stride=8), :]
                grad = grad_t[pl.ds(block * 64 + r, 8, stride=8), :]
                for n in range(states):
                    carry[n] = jnp.exp2(decay[n] * rate) * (carry[n] + grad * read_ref[pos * states + n])
            return tuple(carry)

        carry = tuple(carry_ref[n, pl.ds(group * 8, 8), :] for n in range(states))
        carry = lax.fori_loop(0, chunk // 8, eight, carry)
        for n in range(states):
            carry_ref[n, pl.ds(group * 8, 8), :] = carry[n]
    end_ref[...] = carry_ref[...]


def adjoint_end(step, grad, keep_lanes, read_flat, decay, after=()):
    rows, inner = step.shape
    states, planes, _ = decay.shape
    chunk = CHUNK
    count = rows // chunk
    whole = pl.BlockSpec((states, planes, LANES), lambda i: (0, 0, 0))
    rowed = pl.BlockSpec((chunk, inner), lambda i: (count - 1 - i, 0))
    return pl.pallas_call(
        functools.partial(adjoint_end_kernel, states, chunk),
        out_shape=jax.ShapeDtypeStruct(decay.shape, jnp.float32),
        grid=(count,),
        in_specs=[rowed, rowed, pl.BlockSpec((chunk, LANES), lambda i: (count - 1 - i, 0)), smem(), whole]
        + [pl.BlockSpec(memory_space=pl.ANY)] * len(after),
        out_specs=whole,
        scratch_shapes=[pltpu.VMEM(decay.shape, jnp.float32)]
        + [pltpu.VMEM((chunk * 8, LANES), jnp.float32)] * 2,
        compiler_params=pltpu.CompilerParams(vmem_limit_bytes=32 << 20),
        name="adjoint_end",
    )(step, grad, keep_lanes, read_flat, decay, *after)


def adjoint_full_kernel(
    states, chunk, anchors,
    end_ref, marks_ref, step_ref, act_ref, grad_ref, keep_ref, in_ref, read_ref, decay_ref, *refs
):
    (
    d_step_ref, d_act_ref, d_in_ref, d_read_ref, d_decay_ref,
    carry_ref, step_t, rate_t, act_t, grad_t, d_step_t, d_act_t, factor_t, held_t, in_t, read_t,
    ) = refs[anchors:]
    index = pl.program_id(0)
    last = pl.num_programs(0) - 1
    groups = step_ref.shape[1] // (8 * LANES)

    @pl.when(index == 0)
    def _():
        carry_ref[...] = end_ref[...]
        d_decay_ref[...] = jnp.zeros_like(d_decay_ref)

    for group in range(groups):
        cols = pl.ds(group * 8 * LANES, 8 * LANES)
        for block in range(chunk // 8):
            rows = pl.ds(block * 8, 8)
            rate = step_ref[rows, cols]
            keep = keep_ref[rows, :]
            to_planes(step_t, jnp.where(jnp.concatenate([keep] * 8, axis=1) > 0, rate, RESET), block)
            to_planes(rate_t, rate, block)
            to_planes(act_t, act_ref[rows, cols].astype(jnp.float32), block)
            to_planes(grad_t, grad_ref[rows, cols], block)

        def replay(block, hidden):
            hidden = list(hidden)
            for r in range(8):
                local = block * 8 + r
                pos = (last - index) * chunk + local
                view = pl.ds(block * 64 + r, 8, stride=8)
                gated = step_t[view, :]
                drive = rate_t[view, :] * act_t[view, :]
                grad = grad_t[view, :]
                for n in range(states):
                    slot = pl.ds((local * states + n) * 8, 8)
                    factor = jnp.exp2(decay_ref[n, pl.ds(group * 8, 8), :] * LOG2E * gated)
                    held = factor * hidden[n]
                    hidden[n] = held + drive * in_ref[pos * states + n]
                    factor_t[slot, :] = factor
                    held_t[slot, :] = held
                    if group == 0:
                        read_t[slot, :] = grad * hidden[n]
                    else:
                        read_t[slot, :] += grad * hidden[n]
            return tuple(hidden)

        lax.fori_loop(
            0, chunk // 8, replay,
            tuple(marks_ref[0, n, pl.ds(group * 8, 8), :] for n in range(states)),
        )

        def back(turn, carried):
            carry, d_decay = list(carried[0]), list(carried[1])
            block = chunk // 8 - 1 - turn
            for r in range(7, -1, -1):
                local = block * 8 + r
                pos = (last - index) * chunk + local
                view = pl.ds(block * 64 + r, 8, stride=8)
                rate = rate_t[view, :]
                act = act_t[view, :]
                grad = grad_t[view, :]
                drive = rate * act
                inner_terms = []
                step_terms = []
                for n in range(states):
                    slot = pl.ds((local * states + n) * 8, 8)
                    adjoint = carry[n] + grad * read_ref[pos * states + n]
                    moved = adjoint * held_t[slot, :]
                    step_terms.append(moved * decay_ref[n, pl.ds(group * 8, 8), :])
                    d_decay[n] = d_decay[n] + moved * rate
                    inner_terms.append(adjoint * in_ref[pos * states + n])
                    if group == 0:
                        in_t[slot, :] = adjoint * drive
                    else:
                        in_t[slot, :] += adjoint * drive
                    carry[n] = adjoint * factor_t[slot, :]
                inner_sum = tree_sum(inner_terms)
                d_step_t[view, :] = tree_sum(step_terms) + act * inner_sum
                d_act_t[view, :] = rate * inner_sum
            return (tuple(carry), tuple(d_decay))

        carry, d_decay = lax.fori_loop(
            0, chunk // 8, back,
            (
                tuple(carry_ref[n, pl.ds(group * 8, 8), :] for n in range(states)),
                tuple(d_decay_ref[n, pl.ds(group * 8, 8), :] for n in range(states)),
            ),
        )
        for n in range(states):
            carry_ref[n, pl.ds(group * 8, 8), :] = carry[n]
            d_decay_ref[n, pl.ds(group * 8, 8), :] = d_decay[n]
        for block in range(chunk // 8):
            for lane_block in range(8):
                where = (pl.ds(block * 8, 8), pl.ds(group * 1024 + lane_block * LANES, LANES))
                tile = pl.ds(block * 64 + lane_block * 8, 8)
                d_step_ref[where] = d_step_t[tile, :]
                d_act_ref[where] = d_act_t[tile, :]

    def shrink(block, _):
        for source, target in ((in_t, d_in_ref), (read_t, d_read_ref)):
            total = source[pl.ds(block * 64, 8, stride=8), :]
            for s in range(1, 8):
                total = total + source[pl.ds(block * 64 + s, 8, stride=8), :]
            target[pl.ds(block * 8, 8), :] = total
        return 0

    lax.fori_loop(0, chunk * states // 8, shrink, 0, unroll=4)


def adjoint_full(end_grad, marks, step, act, grad, keep_lanes, in_flat, read_flat, decay, after=()):
    rows, inner = step.shape
    states, planes, _ = decay.shape
    chunk = CHUNK
    count = rows // chunk
    whole = pl.BlockSpec((states, planes, LANES), lambda i: (0, 0, 0))
    rowed = pl.BlockSpec((chunk, inner), lambda i: (count - 1 - i, 0))
    maps = pl.BlockSpec((chunk * states, LANES), lambda i: (count - 1 - i, 0))
    big = pltpu.VMEM((chunk * states * 8, LANES), jnp.float32)
    return pl.pallas_call(
        functools.partial(adjoint_full_kernel, states, chunk, len(after)),
        out_shape=(
            jax.ShapeDtypeStruct((rows, inner), jnp.float32),
            jax.ShapeDtypeStruct((rows, inner), jnp.float32),
            jax.ShapeDtypeStruct((rows * states, LANES), jnp.float32),
            jax.ShapeDtypeStruct((rows * states, LANES), jnp.float32),
            jax.ShapeDtypeStruct(decay.shape, jnp.float32),
        ),
        grid=(count,),
        in_specs=[
            whole,
            pl.BlockSpec((1, states, planes, LANES), lambda i: (count - 1 - i, 0, 0, 0)),
            rowed, rowed, rowed,
            pl.BlockSpec((chunk, LANES), lambda i: (count - 1 - i, 0)),
            smem(), smem(), whole,
        ]
        + [pl.BlockSpec(memory_space=pl.ANY)] * len(after),
        out_specs=(rowed, rowed, maps, maps, whole),
        scratch_shapes=[pltpu.VMEM(decay.shape, jnp.float32)]
        + [pltpu.VMEM((chunk * 8, LANES), jnp.float32)] * 6
        + [big] * 4,
        compiler_params=pltpu.CompilerParams(vmem_limit_bytes=48 << 20),
        name="adjoint_full",
    )(end_grad, marks, step, act, grad, keep_lanes, in_flat, read_flat, decay, *after)


KEYS = 512


def turn_half(values):
    return pltpu.roll(values, HEAD_DIM // 2, 1)


def mask_keys(scores_shape, chunk, first_key, q_pos):
    key_pos = chunk * KEYS + lax.broadcasted_iota(jnp.int32, scores_shape, 1)
    return (key_pos >= first_key) & (key_pos <= q_pos)


def attend_kernel(
    n_x, heads, scale, x_ref, low_ref, q_ref, k_ref, v_ref, first_ref, out_ref, lse_ref, score_t
):
    block = pl.program_id(1)
    rows = q_ref.shape[0]
    base = (block * n_x + x_ref[0]) * rows
    low_chunk = low_ref[block] // KEYS
    high_chunk = (base + rows - 1) // KEYS + 1
    q_pos = base + lax.broadcasted_iota(jnp.int32, (rows, KEYS), 0)
    first_key = first_ref[...]
    query = q_ref[...]

    def scores_of(chunk, top):
        where = pl.ds(pl.multiple_of(chunk * KEYS, KEYS), KEYS)
        scores = right_trans(query, k_ref[where, :]) * scale
        scores = jnp.where(mask_keys(scores.shape, chunk, first_key, q_pos), scores, -1e30)
        score_t[:, where] = scores
        for part in range(0, KEYS, LANES):
            top = jnp.maximum(top, scores[:, part : part + LANES])
        return top

    top = lax.fori_loop(low_chunk, high_chunk, scores_of, jnp.full((rows, LANES), -1e30, jnp.float32))
    top = jnp.max(top, axis=1, keepdims=True)

    def weigh(chunk, carried):
        total, mixed = carried
        where = pl.ds(pl.multiple_of(chunk * KEYS, KEYS), KEYS)
        weights = jnp.exp2(score_t[:, where] - top)
        for part in range(0, KEYS, LANES):
            total = total + weights[:, part : part + LANES]
        return (total, mixed + product(weights.astype(jnp.bfloat16), v_ref[where, :]))

    total, mixed = lax.fori_loop(
        low_chunk,
        high_chunk,
        weigh,
        (jnp.zeros((rows, LANES), jnp.float32), jnp.zeros((rows, HEAD_DIM), jnp.float32)),
    )
    total = jnp.sum(total, axis=1, keepdims=True)
    out_ref[...] = (mixed / total).astype(jnp.bfloat16)
    lse_ref[0] = top + jnp.log2(total)


def attend(x_index, lows, triple, first_key, n_x, heads, rows):
    length = triple.shape[0]
    blocks = length // (rows * n_x)
    scale = HEAD_DIM ** (-0.5) * LOG2E
    return pl.pallas_call(
        functools.partial(attend_kernel, n_x, heads, scale),
        out_shape=(
            jax.ShapeDtypeStruct((blocks * rows, heads * HEAD_DIM), jnp.bfloat16),
            jax.ShapeDtypeStruct((heads, blocks * rows, 1), jnp.float32),
        ),
        grid_spec=pltpu.PrefetchScalarGridSpec(
            num_scalar_prefetch=2,
            grid=(heads, blocks),
            in_specs=[
                pl.BlockSpec((rows, HEAD_DIM), lambda h, b, x, low: (b * n_x + x[0], h)),
                pl.BlockSpec((length, HEAD_DIM), lambda h, b, x, low: (0, heads + h)),
                pl.BlockSpec((length, HEAD_DIM), lambda h, b, x, low: (0, 2 * heads + h)),
                pl.BlockSpec((rows, 1), lambda h, b, x, low: (b, 0)),
            ],
            out_specs=(
                pl.BlockSpec((rows, HEAD_DIM), lambda h, b, x, low: (b, h)),
                pl.BlockSpec((1, rows, 1), lambda h, b, x, low: (h, b, 0)),
            ),
            scratch_shapes=[pltpu.VMEM((rows, length), jnp.float32)],
        ),
        compiler_params=pltpu.CompilerParams(vmem_limit_bytes=40 << 20),
        cost_estimate=pl.CostEstimate(
            flops=2 * heads * blocks * rows * length * HEAD_DIM, bytes_accessed=4 * length * heads * HEAD_DIM, transcendentals=0
        ),
        name="attend",
    )(x_index, lows, triple, triple, triple, first_key)


def attend_back_kernel(
    n_x, heads, scale,
    x_ref, low_ref, q_ref, k_ref, v_ref, out_ref, d_ref, lse_ref, first_ref, cos_ref, sin_ref, cos_all, sin_all,
    dq_ref, dk_ref, dv_ref, dk_t, dv_t,
):
    block = pl.program_id(1)
    rows = q_ref.shape[0]
    base = (block * n_x + x_ref[0]) * rows
    low_chunk = low_ref[block] // KEYS
    high_chunk = (base + rows - 1) // KEYS + 1
    q_pos = base + lax.broadcasted_iota(jnp.int32, (rows, KEYS), 0)
    first_key = first_ref[...]
    query = q_ref[...]
    d_out = d_ref[...]
    log_total = lse_ref[0]
    center = jnp.sum(d_out.astype(jnp.float32) * out_ref[...].astype(jnp.float32), axis=1, keepdims=True)

    @pl.when(block == 0)
    def _():
        dk_t[...] = jnp.zeros_like(dk_t)
        dv_t[...] = jnp.zeros_like(dv_t)

    def one(chunk, d_query):
        where = pl.ds(pl.multiple_of(chunk * KEYS, KEYS), KEYS)
        keys = k_ref[where, :]
        scores = right_trans(query, keys) * scale
        allowed = mask_keys(scores.shape, chunk, first_key, q_pos)
        weights = jnp.where(allowed, jnp.exp2(scores - log_total), 0.0)
        d_soft = right_trans(d_out, v_ref[where, :])
        d_scores = (weights * (d_soft - center)).astype(jnp.bfloat16)
        dv_t[where, :] += left_trans(weights.astype(jnp.bfloat16), d_out)
        dk_t[where, :] += left_trans(d_scores, query)
        return d_query + product(d_scores, keys)

    d_query = lax.fori_loop(low_chunk, high_chunk, one, jnp.zeros((rows, HEAD_DIM), jnp.float32))
    inv_scale = HEAD_DIM ** (-0.5)
    d_query = d_query * inv_scale
    dq_ref[...] = (d_query * cos_ref[...] - turn_half(d_query) * sin_ref[...]).astype(jnp.bfloat16)

    @pl.when(block == pl.num_programs(1) - 1)
    def _():
        def finish(chunk, _):
            where = pl.ds(pl.multiple_of(chunk * KEYS, KEYS), KEYS)
            d_keys = dk_t[where, :] * inv_scale
            dk_ref[where, :] = (d_keys * cos_all[where, :] - turn_half(d_keys) * sin_all[where, :]).astype(jnp.bfloat16)
            dv_ref[where, :] = dv_t[where, :].astype(jnp.bfloat16)
            return 0

        lax.fori_loop(0, k_ref.shape[0] // KEYS, finish, 0)


def attend_back(x_index, lows, triple, attended, d_attended, lse, first_key, cosine, sine, n_x, heads, rows):
    length = triple.shape[0]
    blocks = length // (rows * n_x)
    scale = HEAD_DIM ** (-0.5) * LOG2E
    q_spec = pl.BlockSpec((rows, HEAD_DIM), lambda h, b, x, low: (b * n_x + x[0], h))
    own = pl.BlockSpec((rows, HEAD_DIM), lambda h, b, x, low: (b, h))
    table_q = pl.BlockSpec((rows, HEAD_DIM), lambda h, b, x, low: (b * n_x + x[0], 0))
    table = pl.BlockSpec((length, HEAD_DIM), lambda h, b, x, low: (0, 0))
    column = pl.BlockSpec((length, HEAD_DIM), lambda h, b, x, low: (0, h))
    return pl.pallas_call(
        functools.partial(attend_back_kernel, n_x, heads, scale),
        out_shape=(
            jax.ShapeDtypeStruct((blocks * rows, heads * HEAD_DIM), jnp.bfloat16),
            jax.ShapeDtypeStruct((length, heads * HEAD_DIM), jnp.bfloat16),
            jax.ShapeDtypeStruct((length, heads * HEAD_DIM), jnp.bfloat16),
        ),
        grid_spec=pltpu.PrefetchScalarGridSpec(
            num_scalar_prefetch=2,
            grid=(heads, blocks),
            in_specs=[
                q_spec,
                pl.BlockSpec((length, HEAD_DIM), lambda h, b, x, low: (0, heads + h)),
                pl.BlockSpec((length, HEAD_DIM), lambda h, b, x, low: (0, 2 * heads + h)),
                own,
                own,
                pl.BlockSpec((1, rows, 1), lambda h, b, x, low: (h, b, 0)),
                pl.BlockSpec((rows, 1), lambda h, b, x, low: (b, 0)),
                table_q,
                table_q,
                table,
                table,
            ],
            out_specs=(own, column, column),
            scratch_shapes=[pltpu.VMEM((length, HEAD_DIM), jnp.float32)] * 2,
        ),
        compiler_params=pltpu.CompilerParams(vmem_limit_bytes=40 << 20),
        cost_estimate=pl.CostEstimate(
            flops=5 * heads * blocks * rows * length * HEAD_DIM, bytes_accessed=8 * length * heads * HEAD_DIM, transcendentals=0
        ),
        name="attend_back",
    )(x_index, lows, triple, triple, triple, attended, d_attended, lse, first_key, cosine, sine, cosine, sine)


MESH = pl.DeviceIdType.MESH


def greet(peers):
    barrier = pltpu.get_barrier_semaphore()
    for peer in peers:
        pl.semaphore_signal(barrier, inc=1, device_id=peer, device_id_type=MESH)
    pl.semaphore_wait(barrier, len(peers))


def send(source, target, send_sem, recv_sem, peer):
    return pltpu.make_async_remote_copy(
        src_ref=source,
        dst_ref=target,
        send_sem=send_sem,
        recv_sem=recv_sem,
        device_id=peer,
        device_id_type=MESH,
    )


def span(start, size):
    return pl.ds(pl.multiple_of(start, 16), size)


def ring_place(seq, n_x):
    z, x = seq // n_x, lax.rem(seq, n_x)
    side = lax.min(x, 1)
    turn = GROUPS - 1 - z
    odd = lax.rem(turn, 2)
    back = GROUPS + turn * (n_x - 1) + (1 - odd) * (x - 1) + odd * (n_x - 1 - x)
    return (1 - side) * z + side * back


def ring_member(place, n_x):
    side = lax.min(place // GROUPS, 1)
    late = lax.max(place - GROUPS, 0)
    turn = late // (n_x - 1)
    step = lax.rem(late, n_x - 1)
    odd = lax.rem(turn, 2)
    x = (1 - odd) * (1 + step) + odd * (n_x - 1 - step)
    return (1 - side) * place * n_x + side * ((GROUPS - 1 - turn) * n_x + x)


def remote_params(collective, limit):
    return pltpu.CompilerParams(
        collective_id=collective, has_side_effects=True, vmem_limit_bytes=limit << 20
    )


def anywhere():
    return pl.BlockSpec(memory_space=pl.ANY)


def vmem():
    return pl.BlockSpec(memory_space=pltpu.VMEM)


def start_gather_rows(n_row, parts, x_ref, out_ref, send_y, recv_y, send_f, recv_f, own_sem):
    row, seq = lax.axis_index("row"), lax.axis_index("seq")
    y, core = row // 2, lax.rem(row, 2)
    n_y = n_row // 2
    rows = x_ref.shape[0]
    piece = rows // parts
    sibling, across = row_peers(n_row)
    pending = []
    for d in range(n_y - 1):
        for c in range(parts):
            copy = send(
                x_ref.at[pl.ds(c * piece, piece)],
                out_ref.at[span(row * rows + c * piece, piece)],
                send_y.at[d, c],
                recv_y.at[d, c],
                across[d],
            )
            copy.start()
            pending.append(copy)
    own = send(x_ref, out_ref.at[span(row * rows, rows)], own_sem.at[0], own_sem.at[1], sibling)
    own.start()
    out_ref[span(row * rows, rows), :] = x_ref[...]
    return (n_row, parts, out_ref, piece, rows, pending, own, send_f, recv_f)


def finish_gather_rows(started):
    n_row, parts, out_ref, piece, rows, pending, own, send_f, recv_f = started
    row = lax.axis_index("row")
    y, core = row // 2, lax.rem(row, 2)
    n_y = n_row // 2
    sibling = row_peers(n_row)[0]
    forwards = []
    for d in range(n_y - 1):
        origin = lax.rem(y + n_y - 1 - d, n_y) * 2 + core
        for c in range(parts):
            pending[d * parts + c].wait_recv()
            where = out_ref.at[span(origin * rows + c * piece, piece)]
            copy = send(where, where, send_f.at[d, c], recv_f.at[d, c], sibling)
            copy.start()
            forwards.append(copy)
    own.wait()
    for copy in pending:
        copy.wait_send()
    for copy in forwards:
        copy.wait()


def gather_rows_scratch(n_y, parts):
    return [pltpu.SemaphoreType.DMA((n_y - 1, parts))] * 4 + [pltpu.SemaphoreType.DMA((2,))]


def owner_of(row, seq, n_row, n_seq):
    half = n_seq // 2
    late, odd = seq // half, lax.rem(row, 2)
    moved = late + odd - 2 * late * odd
    owner_seq = (1 - moved) * seq + moved * (odd * half + lax.rem(seq, half))
    return moved * (n_row // 2) + row // 2, owner_seq


def holder_of(row, seq, n_row, n_seq):
    half = n_seq // 2
    raised, late = row // (n_row // 2), seq // half
    holder_seq = (1 - raised) * seq + raised * ((1 - late) * half + lax.rem(seq, half))
    return 2 * (row - raised * (n_row // 2)) + late, holder_seq


def greet_riders(peers, n_row, n_seq):
    row, seq = lax.axis_index("row"), lax.axis_index("seq")
    target, source = owner_of(row, seq, n_row, n_seq), holder_of(row, seq, n_row, n_seq)
    staying = jnp.logical_and(target[0] == row, target[1] == seq)
    barrier = pltpu.get_barrier_semaphore()
    for peer in peers:
        pl.semaphore_signal(barrier, inc=1, device_id=peer, device_id_type=MESH)

    @pl.when(jnp.logical_not(staying))
    def _():
        pl.semaphore_signal(barrier, inc=1, device_id=source, device_id_type=MESH)

    pl.semaphore_wait(barrier, len(peers) + 1 - staying.astype(jnp.int32))


def start_ride(n_row, n_seq, ride_ref, rode_ref, ride_sem):
    row, seq = lax.axis_index("row"), lax.axis_index("seq")
    target = owner_of(row, seq, n_row, n_seq)
    staying = jnp.logical_and(target[0] == row, target[1] == seq)
    ride = send(ride_ref, rode_ref, ride_sem.at[0], ride_sem.at[1], target)
    keep = pltpu.make_async_copy(ride_ref, rode_ref, ride_sem.at[2])

    @pl.when(jnp.logical_not(staying))
    def _():
        ride.start()

    @pl.when(staying)
    def _():
        keep.start()

    return staying, ride, keep


def finish_ride(started):
    staying, ride, keep = started

    @pl.when(jnp.logical_not(staying))
    def _():
        ride.wait()

    @pl.when(staying)
    def _():
        keep.wait()


def row_peers(n_row):
    row, seq = lax.axis_index("row"), lax.axis_index("seq")
    y, core = row // 2, lax.rem(row, 2)
    n_y = n_row // 2
    sibling = (y * 2 + 1 - core, seq)
    across = [(lax.rem(y + d, n_y) * 2 + core, seq) for d in range(1, n_y)]
    return sibling, across


def reduce_rows_kernel(n_row, n_seq, parts, x_ref, ride_ref, out_ref, rode_ref, ride_sem, *scratch):
    sibling, across = row_peers(n_row)
    greet_riders([sibling] + across, n_row, n_seq)
    ridden = start_ride(n_row, n_seq, ride_ref, rode_ref, ride_sem)
    reduce_rows_body(n_row, parts, x_ref, out_ref, *scratch)
    finish_ride(ridden)


def reduce_rows_body(
    n_row, parts, x_ref, out_ref, near, stage, far, send_c, recv_c, send_y, recv_y
):
    row = lax.axis_index("row")
    sibling, across = row_peers(n_row)
    y, core = row // 2, lax.rem(row, 2)
    n_y = n_row // 2
    rows = out_ref.shape[0]
    piece = rows // parts
    other = 1 - core
    order = [(d + 1) % n_y for d in range(n_y)]
    crossing = {}
    for d in order:
        block = lax.rem(y + d, n_y)
        for c in range(parts):
            copy = send(
                x_ref.at[span((block * 2 + other) * rows + c * piece, piece)],
                near.at[d, pl.ds(c * piece, piece)],
                send_c.at[d, c],
                recv_c.at[d, c],
                sibling,
            )
            copy.start()
            crossing[d, c] = copy
    sent = {}
    for d in order[:-1]:
        block = lax.rem(y + d, n_y)
        for c in range(parts):
            crossing[d, c].wait_recv()
            where = pl.ds(c * piece, piece)
            total = x_ref[span((block * 2 + core) * rows + c * piece, piece), :].astype(
                jnp.float32
            ) + near[d, where, :].astype(jnp.float32)
            stage[d - 1, where, :] = total.astype(stage.dtype)
            copy = send(
                stage.at[d - 1, where],
                far.at[d - 1, where],
                send_y.at[d - 1, c],
                recv_y.at[d - 1, c],
                across[d - 1],
            )
            copy.start()
            sent[d, c] = copy
    for c in range(parts):
        where = pl.ds(c * piece, piece)
        crossing[0, c].wait_recv()
        total = x_ref[span(row * rows + c * piece, piece), :].astype(jnp.float32) + near[
            0, where, :
        ].astype(jnp.float32)
        for d in order[:-1]:
            sent[d, c].wait_recv()
            total = total + far[d - 1, where, :].astype(jnp.float32)
        out_ref[where, :] = total.astype(out_ref.dtype)
    for copy in crossing.values():
        copy.wait_send()
    for copy in sent.values():
        copy.wait_send()


def reduce_rows_scratch(n_y, parts, buffer, dtype):
    return (
        [
            pltpu.VMEM((n_y,) + buffer, dtype),
            pltpu.VMEM((n_y - 1,) + buffer, dtype),
            pltpu.VMEM((n_y - 1,) + buffer, dtype),
        ]
        + [pltpu.SemaphoreType.DMA((n_y, parts))] * 2
        + [pltpu.SemaphoreType.DMA((n_y - 1, parts))] * 2
    )


def reduce_rows(partial, ride, collective):
    n_row, n_seq = lax.axis_size("row"), lax.axis_size("seq")
    rows, width = partial.shape[0] // n_row, partial.shape[1]
    parts = 4 if rows % 64 == 0 else 2 if rows % 32 == 0 else 1
    buffer = (rows, width)
    return pl.pallas_call(
        functools.partial(reduce_rows_kernel, n_row, n_seq, parts),
        out_shape=(
            jax.ShapeDtypeStruct(buffer, jnp.float32),
            jax.ShapeDtypeStruct(ride.shape, ride.dtype),
        ),
        in_specs=[vmem(), anywhere()],
        out_specs=(vmem(), anywhere()),
        scratch_shapes=[pltpu.SemaphoreType.DMA((3,))]
        + reduce_rows_scratch(n_row // 2, parts, buffer, partial.dtype),
        compiler_params=remote_params(collective, 40),
        name="reduce_rows",
    )(partial, ride)


def load_heads(weight_ref, weight, weight_sem, n_x):
    width = weight_ref.shape[0]
    cols = weight.shape[1] // 3
    z = lax.axis_index("seq") // n_x
    loads = []
    for part in range(3):
        column = pl.ds(pl.multiple_of(part * width + z * cols, LANES), cols)
        load = pltpu.make_async_copy(
            weight_ref.at[:, column],
            weight.at[:, pl.ds(part * cols, cols)],
            weight_sem.at[part],
        )
        load.start()
        loads.append(load)
    return loads


def ring_neighbours(n_seq):
    n_x = n_seq // GROUPS
    row, seq = lax.axis_index("row"), lax.axis_index("seq")
    place = ring_place(seq, n_x)
    after = (row, ring_member(lax.rem(place + 1, n_seq), n_x))
    before = (row, ring_member(lax.rem(place + n_seq - 1, n_seq), n_x))
    return row, seq, place, after, before


def ring_gather(
    n_seq, parts, rows, out_ref, send_sem, recv_sem, place, after, before, work=None
):
    n_x = n_seq // GROUPS
    half = rows // 2
    piece = half // parts
    sent = {}

    def start_of(step, way):
        shift = n_seq - step if way == 0 else step
        member = ring_member(lax.rem(place + shift, n_seq), n_x)
        return member * rows + way * half

    for step in range(n_seq - 1):
        for c in range(parts):
            for way in range(2):
                if step:
                    sent[step - 1, c, way].wait_recv()
                where = out_ref.at[span(start_of(step, way) + c * piece, piece)]
                copy = send(
                    where,
                    where,
                    send_sem.at[way, step, c],
                    recv_sem.at[way, step, c],
                    after if way == 0 else before,
                )
                copy.start()
                sent[step, c, way] = copy
        if work is not None:
            for way in range(2):
                work(start_of(step, way), half)
    for way in range(2):
        for c in range(parts):
            sent[n_seq - 2, c, way].wait_recv()
        if work is not None:
            work(start_of(n_seq - 1, way), half)
    for copy in sent.values():
        copy.wait_send()


def gather_seq_kernel(
    n_row, n_seq, parts, rotated, x_ref, up_ref, weight_ref, cos_ref, sin_ref, *refs
):
    (
        out_ref, triple_ref, own_ref, send_sem, recv_sem, send_w, recv_w, local_sem, weight, weight_sem,
    ) = refs[-10:]
    loads = load_heads(weight_ref, weight, weight_sem, n_seq // GROUPS)
    row, seq, place, after, before = ring_neighbours(n_seq)
    rows = x_ref.shape[0]
    depth, both = up_ref.shape[1:]
    ff_dim = both // 2
    ff_row = ff_dim // n_row
    others = [lax.rem(row + d, n_row) for d in range(1, n_row)]
    greet([after, before] + [(other, seq) for other in others])

    def slabs(dest):
        odd = lax.rem(dest, 2)
        for part in range(2):
            column = part * ff_dim + dest * ff_row
            slot = part * (1 - odd) + (1 - part) * odd
            yield part, (
                up_ref.at[1, :, pl.ds(pl.multiple_of(column, LANES), ff_row)],
                own_ref.at[span(row * depth, depth), pl.ds(pl.multiple_of(slot * ff_row, LANES), ff_row)],
            )

    moved = []
    for d, other in enumerate(others):
        for part, (source, target) in slabs(other):
            copy = send(source, target, send_w.at[d, part], recv_w.at[d, part], (other, seq))
            copy.start()
            moved.append(copy)
    local = []
    for part, (source, target) in slabs(row):
        copy = pltpu.make_async_copy(source, target, local_sem.at[part])
        copy.start()
        local.append(copy)
    def project(start, size):
        here = span(start, size)
        cosine, sine = cos_ref[here, :], sin_ref[here, :]
        step = 3 * HEAD_DIM
        for left in range(0, weight.shape[1], step):
            triple = product(out_ref[here, :], weight[:, left : left + step])
            for head in range(0, step, HEAD_DIM):
                value = triple[:, head : head + HEAD_DIM]
                if left + head < rotated:
                    value = value * cosine + turn_half(value) * sine
                triple_ref[here, left + head : left + head + HEAD_DIM] = value.astype(
                    triple_ref.dtype
                )

    out_ref[span(seq * rows, rows), :] = x_ref[...]
    for load in loads:
        load.wait()
    ring_gather(n_seq, parts, rows, out_ref, send_sem, recv_sem, place, after, before, project)
    for copy in moved + local:
        copy.wait()


def gather_seq(block, up_weight, weight, cosine, sine, rotated, after=(), collective=15):
    n_row, n_seq = lax.axis_size("row"), lax.axis_size("seq")
    rows, width = block.shape
    parts = 2 if rows % 64 == 0 else 1
    depth, both = up_weight.shape[1:]
    return pl.pallas_call(
        functools.partial(gather_seq_kernel, n_row, n_seq, parts, rotated),
        out_shape=(
            jax.ShapeDtypeStruct((n_seq * rows, width), block.dtype),
            jax.ShapeDtypeStruct((n_seq * rows, weight.shape[1] // GROUPS), block.dtype),
            jax.ShapeDtypeStruct((depth * n_row, both // n_row), up_weight.dtype),
        ),
        in_specs=[vmem()] + [anywhere()] * 2 + [vmem()] * 2 + [anywhere()] * len(after),
        out_specs=(vmem(), vmem(), anywhere()),
        scratch_shapes=[pltpu.SemaphoreType.DMA((2, n_seq - 1, parts))] * 2
        + [pltpu.SemaphoreType.DMA((n_row - 1, 2))] * 2
        + [pltpu.SemaphoreType.DMA((2,))]
        + [
            pltpu.VMEM((width, weight.shape[1] // GROUPS), weight.dtype),
            pltpu.SemaphoreType.DMA((3,)),
        ],
        compiler_params=remote_params(collective, 48),
        name="gather_seq",
    )(block, up_weight, weight, cosine, sine, *after)


def reduce_seq_kernel(n_row, n_seq, parts, x_ref, weight_ref, rider_ref, *refs):
    out_ref, rode_ref, held, made, send_sem, recv_sem, weight, weight_sem, *scratch = refs
    n_x = n_seq // GROUPS
    loads = load_heads(weight_ref, weight, weight_sem, n_x)
    _, seq, place, after, before = ring_neighbours(n_seq)
    rows, width = out_ref.shape
    half = rows // 2
    piece = half // parts
    sibling, across = row_peers(n_row)
    greet([after, before, sibling] + across)
    riding = start_gather_rows(n_row, 4, rider_ref, rode_ref, *scratch)
    for load in loads:
        load.wait()

    def make(step, way):
        shift = 2 * n_seq - 1 - step if way == 0 else 1 + step
        member = ring_member(lax.rem(place + shift, n_seq), n_x)
        here = span(member * rows + way * half, half)
        for left in range(0, width, COLUMNS):
            made[way, step % 2, :, left : left + COLUMNS] = right_trans(
                x_ref[here, :], weight[left : left + COLUMNS, :]
            ).astype(made.dtype)

    sent = {}
    for step in range(n_seq - 1):
        for way in range(2):
            if step == 0:
                make(step, way)
            for c in range(parts):
                where = pl.ds(c * piece, piece)
                if step:
                    sent[step - 1, c, way].wait_recv()
                    held[way, step - 1, where, :] = (
                        held[way, step - 1, where, :].astype(jnp.float32)
                        + made[way, step % 2, where, :].astype(jnp.float32)
                    ).astype(held.dtype)
                    source = held.at[way, step - 1, where]
                else:
                    source = made.at[way, 0, where]
                copy = send(
                    source,
                    held.at[way, step, where],
                    send_sem.at[way, step, c],
                    recv_sem.at[way, step, c],
                    after if way == 0 else before,
                )
                copy.start()
                sent[step, c, way] = copy
        for way in range(2):
            if step == 1:
                for c in range(parts):
                    sent[0, c, way].wait_send()
            make(step + 1, way)
    for way in range(2):
        for c in range(parts):
            sent[n_seq - 2, c, way].wait_recv()
            where = pl.ds(c * piece, piece)
            out_ref[pl.ds(way * half + c * piece, piece), :] = held[
                way, n_seq - 2, where, :
            ].astype(jnp.float32) + made[way, (n_seq - 1) % 2, where, :].astype(jnp.float32)
    for (step, _, _), copy in sent.items():
        if step:
            copy.wait_send()
    finish_gather_rows(riding)


def reduce_seq(values, weight, rider, collective=4):
    n_row, n_seq = lax.axis_size("row"), lax.axis_size("seq")
    rows, width = values.shape[0] // n_seq, weight.shape[0]
    parts = 2
    return pl.pallas_call(
        functools.partial(reduce_seq_kernel, n_row, n_seq, parts),
        out_shape=(
            jax.ShapeDtypeStruct((rows, width), jnp.float32),
            jax.ShapeDtypeStruct((n_row * rider.shape[0], rider.shape[1]), rider.dtype),
        ),
        in_specs=[vmem(), anywhere(), vmem()],
        out_specs=(vmem(), vmem()),
        scratch_shapes=[
            pltpu.VMEM((2, n_seq - 1, rows // 2, width), values.dtype),
            pltpu.VMEM((2, 2, rows // 2, width), values.dtype),
        ]
        + [pltpu.SemaphoreType.DMA((2, n_seq - 1, parts))] * 2
        + [
            pltpu.VMEM((width, values.shape[1]), weight.dtype),
            pltpu.SemaphoreType.DMA((3,)),
        ]
        + gather_rows_scratch(n_row // 2, 4),
        compiler_params=remote_params(collective, 48),
        name="reduce_seq",
    )(values, weight, rider)


def exchange_kernel(n_row, n_seq, forward, x_ref, decay_ref, *refs):
    if forward:
        out_ref, all_ref, send_sem, recv_sem = refs[-4:]
    else:
        blocks_ref, low_ref = refs[:2]
        out_ref, spread_ref, rows_ref, all_ref, send_sem, recv_sem, send_b, recv_b = refs[-13:-5]
    row, seq, place, after, before = ring_neighbours(n_seq)
    rows = x_ref.shape[0]
    states, planes, _ = decay_ref.shape
    if forward:
        greet([after, before])
    else:
        sibling, across = row_peers(n_row)
        greet([sibling] + across + [(row, lax.rem(seq + d, n_seq)) for d in range(1, n_seq)])
        riding = start_gather_rows(n_row, 4, low_ref, rows_ref, *refs[-5:])
    all_ref[span(seq * rows, rows), :] = x_ref[...]
    ring_gather(n_seq, 1, rows, all_ref, send_sem, recv_sem, place, after, before)
    swapped = [] if forward else start_swap(n_seq, blocks_ref, spread_ref, send_b, recv_b)
    out_ref[...] = jnp.zeros_like(out_ref)

    def take(turn, _):
        other = turn if forward else n_seq - 1 - turn
        used = other < seq if forward else other > seq
        block = all_ref[span(other * rows, rows), :].astype(jnp.float32)
        base = states * planes
        summed = block[base : base + planes] + block[base + planes : base + 2 * planes]
        for n in range(states):
            kept = jnp.exp(decay_ref[n] * summed) * out_ref[n]
            ended = block[n * planes : (n + 1) * planes]
            out_ref[n] = jnp.where(used, kept + ended, out_ref[n])
        return 0

    lax.fori_loop(0, n_seq, take, 0)
    if not forward:
        finish_gather_rows(riding)
    for copy in swapped:
        copy.wait()


def exchange_states(summed, end_state, decay, collective, blocks=None, rider=None, after=()):
    n_row, n_seq = lax.axis_size("row"), lax.axis_size("seq")
    states, planes, _ = decay.shape
    high = summed.astype(jnp.bfloat16)
    lower = (summed - high.astype(jnp.float32)).astype(jnp.bfloat16)
    rows = -(-(states + 2) * planes // 32) * 32
    payload = jnp.concatenate(
        [
            end_state.astype(jnp.bfloat16).reshape(states * planes, LANES),
            high,
            lower,
            jnp.zeros((rows - (states + 2) * planes, LANES), jnp.bfloat16),
        ],
        axis=0,
    )
    ring = [pltpu.VMEM((n_seq * rows, LANES), jnp.bfloat16)] + [
        pltpu.SemaphoreType.DMA((2, n_seq - 1, 1))
    ] * 2
    entering = jax.ShapeDtypeStruct(decay.shape, jnp.float32)
    if blocks is None:
        return pl.pallas_call(
            functools.partial(exchange_kernel, n_row, n_seq, True),
            out_shape=entering,
            in_specs=[vmem(), vmem()] + [anywhere()] * len(after),
            out_specs=vmem(),
            scratch_shapes=ring,
            compiler_params=remote_params(collective, 32),
            name="exchange_states",
        )(payload, decay, *after)
    return pl.pallas_call(
        functools.partial(exchange_kernel, n_row, n_seq, False),
        out_shape=(
            entering,
            jax.ShapeDtypeStruct(blocks.shape, blocks.dtype),
            jax.ShapeDtypeStruct((n_row * rider.shape[0], rider.shape[1]), rider.dtype),
        ),
        in_specs=[vmem()] * 4 + [anywhere()] * len(after),
        out_specs=(vmem(),) * 3,
        scratch_shapes=ring
        + [pltpu.SemaphoreType.DMA((n_seq - 1,))] * 2
        + gather_rows_scratch(n_row // 2, 4),
        compiler_params=remote_params(collective, 40),
        name="exchange_states_back",
    )(payload, decay, blocks, rider, *after)


def start_row_swap(n_row, x_ref, out_ref, send_sem, recv_sem, local_sem):
    row, seq = lax.axis_index("row"), lax.axis_index("seq")
    rows, cols = x_ref.shape[0], out_ref.shape[1]
    mine = out_ref.at[span(row * rows, rows)]
    moved = []
    for d in range(1, n_row):
        other = lax.rem(row + d, n_row)
        copy = send(
            x_ref.at[:, pl.ds(pl.multiple_of(other * cols, LANES), cols)],
            mine,
            send_sem.at[d - 1],
            recv_sem.at[d - 1],
            (other, seq),
        )
        copy.start()
        moved.append(copy)
    own = pltpu.make_async_copy(
        x_ref.at[:, pl.ds(pl.multiple_of(row * cols, LANES), cols)], mine, local_sem
    )
    own.start()
    return moved + [own]


def swap_heads_kernel(
    n_row, n_x, collect, x_ref, rider_ref, *refs
):
    if collect:
        out_ref, rode_ref, send_sem, recv_sem, send_r, recv_r, local_sem = refs
    else:
        part_ref, out_ref, rode_ref, sum_ref, send_sem, recv_sem, send_r, recv_r, local_sem, *scratch = refs
    row, seq = lax.axis_index("row"), lax.axis_index("seq")
    z, x = seq // n_x, lax.rem(seq, n_x)
    peers = [lax.rem(z + d, GROUPS) for d in range(1, GROUPS)]
    greet(
        [(row, peer * n_x + x) for peer in peers]
        + [(lax.rem(row + d, n_row), seq) for d in range(1, n_row)]
    )

    def block(ref, place, wide):
        if wide:
            cols = ref.shape[1] // GROUPS
            return ref.at[:, pl.ds(pl.multiple_of(place * cols, LANES), cols)]
        rows = ref.shape[0] // GROUPS
        return ref.at[span(place * rows, rows)]

    sent = []
    for d, peer in enumerate(peers):
        copy = send(
            block(x_ref, peer, not collect),
            block(out_ref, z, collect),
            send_sem.at[d],
            recv_sem.at[d],
            (row, peer * n_x + x),
        )
        copy.start()
        sent.append(copy)
    riding = start_row_swap(n_row, rider_ref, rode_ref, send_r, recv_r, local_sem)
    block(out_ref, z, collect)[...] = block(x_ref, z, not collect)[...]
    if not collect:
        reduce_rows_body(n_row, 4, part_ref, sum_ref, *scratch)
    for copy in sent + riding:
        copy.wait()


def swap_heads(values, rider, collect, collective, partial=None):
    n_row, n_x = lax.axis_size("row"), lax.axis_size("seq") // GROUPS
    rows, cols = values.shape
    shape = (rows // GROUPS, cols * GROUPS) if collect else (rows * GROUPS, cols // GROUPS)
    narrow = rider.shape[1] // n_row % LANES
    if narrow:
        swapped = lax.all_to_all(rider, "row", split_axis=1, concat_axis=0, tiled=True)
        rider = jnp.zeros((16, n_row * LANES), rider.dtype)
    rode = (rider.shape[0] * n_row, rider.shape[1] // n_row)
    sem = pltpu.SemaphoreType.DMA
    operands = [values, rider]
    outputs = [
        jax.ShapeDtypeStruct(shape, values.dtype),
        jax.ShapeDtypeStruct(rode, rider.dtype),
    ]
    scratch = [sem((GROUPS - 1,))] * 2 + [sem((n_row - 1,))] * 2 + [sem]
    if not collect:
        buffer = (partial.shape[0] // n_row, partial.shape[1])
        operands.append(partial)
        outputs.append(jax.ShapeDtypeStruct(buffer, jnp.float32))
        scratch += reduce_rows_scratch(n_row // 2, 4, buffer, partial.dtype)
    results = pl.pallas_call(
        functools.partial(swap_heads_kernel, n_row, n_x, collect),
        out_shape=tuple(outputs),
        in_specs=[vmem()] * len(operands),
        out_specs=(vmem(),) * len(outputs),
        scratch_shapes=scratch,
        compiler_params=remote_params(collective, 40),
        name="collect_heads" if collect else "spread_heads",
    )(*operands)
    if narrow:
        return (results[0], swapped) + tuple(results[2:])
    return results


def start_swap(n_seq, x_ref, out_ref, send_sem, recv_sem):
    row, seq = lax.axis_index("row"), lax.axis_index("seq")
    place = ring_place(seq, n_seq // GROUPS)
    sent = []
    for d in range(1, n_seq):
        peer = lax.rem(seq + d, n_seq)
        copy = send(
            x_ref.at[peer], out_ref.at[place], send_sem.at[d - 1], recv_sem.at[d - 1], (row, peer)
        )
        copy.start()
        sent.append(copy)
    out_ref[place] = x_ref[seq]
    return sent


def swap_seq_kernel(n_seq, x_ref, out_ref, send_sem, recv_sem):
    row, seq = lax.axis_index("row"), lax.axis_index("seq")
    greet([(row, lax.rem(seq + d, n_seq)) for d in range(1, n_seq)])
    for copy in start_swap(n_seq, x_ref, out_ref, send_sem, recv_sem):
        copy.wait()


def finish_kernel(
    n_row, n_seq, parts, anchors, blocks_ref, packed_ref, *refs
):
    spread_ref, out_ref, send_b, recv_b, rowed, held, send_s, recv_s, *scratch = refs[anchors:]
    rows = out_ref.shape[0]
    row, seq = lax.axis_index("row"), lax.axis_index("seq")
    sibling, across = row_peers(n_row)
    greet([sibling] + across + [(row, lax.rem(seq + d, n_seq)) for d in range(1, n_seq)])
    swapped = start_swap(n_seq, blocks_ref, spread_ref, send_b, recv_b)
    reduce_rows_body(n_row, parts, packed_ref, rowed, *scratch)
    spread = []
    for d in range(1, n_seq):
        peer = lax.rem(seq + d, n_seq)
        copy = send(
            rowed.at[span(peer * rows, rows)], held.at[d - 1], send_s.at[d - 1], recv_s.at[d - 1], (row, peer)
        )
        copy.start()
        spread.append(copy)
    total = rowed[span(seq * rows, rows), :].astype(jnp.float32)
    for d, copy in enumerate(spread):
        copy.wait_recv()
        total = total + held[d].astype(jnp.float32)
    out_ref[...] = total
    for copy in spread:
        copy.wait_send()
    for copy in swapped:
        copy.wait()


def swap_and_reduce(blocks, packed, collective, after=()):
    n_row, n_seq = lax.axis_size("row"), lax.axis_size("seq")
    rows, width = packed.shape[0] // (n_row * n_seq), packed.shape[1]
    if rows % 16:
        summed = lax.psum_scatter(packed, ("row", "seq"), scatter_dimension=0, tiled=True)
        return swap_seq(blocks, collective), summed.astype(jnp.float32)
    buffer = (n_seq * rows, width)
    parts = 4
    sem = pltpu.SemaphoreType.DMA
    return pl.pallas_call(
        functools.partial(finish_kernel, n_row, n_seq, parts, len(after)),
        out_shape=(
            jax.ShapeDtypeStruct(blocks.shape, blocks.dtype),
            jax.ShapeDtypeStruct((rows, width), jnp.float32),
        ),
        in_specs=[vmem()] * 2 + [anywhere()] * len(after),
        out_specs=(vmem(), vmem()),
        scratch_shapes=[sem((n_seq - 1,))] * 2
        + [
            pltpu.VMEM(buffer, packed.dtype),
            pltpu.VMEM((n_seq - 1, rows, width), packed.dtype),
        ]
        + [sem((n_seq - 1,))] * 2
        + reduce_rows_scratch(n_row // 2, parts, buffer, packed.dtype),
        compiler_params=remote_params(collective, 32),
        name="swap_and_reduce",
    )(blocks, packed, *after)


def swap_seq(blocks, collective):
    n_seq = lax.axis_size("seq")
    return pl.pallas_call(
        functools.partial(swap_seq_kernel, n_seq),
        out_shape=jax.ShapeDtypeStruct(blocks.shape, blocks.dtype),
        in_specs=[vmem()],
        out_specs=vmem(),
        scratch_shapes=[pltpu.SemaphoreType.DMA((n_seq - 1,))] * 2,
        compiler_params=remote_params(collective, 32),
        name="swap_seq",
    )(blocks)


def gather_input_kernel(
    parts, x_ref, out_ref, local_sem, own_sem, send_y, recv_y, send_f, recv_f, send_x, recv_x, send_g, recv_g
):
    row, seq = lax.axis_index("row"), lax.axis_index("seq")
    y, core = row // 2, lax.rem(row, 2)
    z, x = seq // 2, lax.rem(seq, 2)
    rows = x_ref.shape[0]
    half = rows // 2
    piece = half // parts
    sibling = (y * 2 + 1 - core, seq)
    over_y = ((1 - y) * 2 + core, seq)
    over_x = (row, z * 2 + 1 - x)
    greet([sibling, over_y, over_x])
    origin = (1 - y) * 2 + core
    first = []
    for c in range(parts):
        copy = send(
            x_ref.at[span(x * half + c * piece, piece)],
            out_ref.at[span(row * rows + x * half + c * piece, piece)],
            send_y.at[c],
            recv_y.at[c],
            over_y,
        )
        copy.start()
        first.append(copy)
    own = send(x_ref, out_ref.at[span(row * rows, rows)], own_sem.at[0], own_sem.at[1], sibling)
    own.start()
    local = pltpu.make_async_copy(x_ref, out_ref.at[span(row * rows, rows)], local_sem)
    local.start()
    rest = []
    side = []
    for c in range(parts):
        first[c].wait_recv()
        where = out_ref.at[span(origin * rows + x * half + c * piece, piece)]
        copy = send(where, where, send_x.at[c], recv_x.at[c], over_x)
        copy.start()
        side.append(copy)
        copy = send(where, where, send_f.at[c], recv_f.at[c], sibling)
        copy.start()
        rest.append(copy)
    for c in range(parts):
        side[c].wait_recv()
        where = out_ref.at[span(origin * rows + (1 - x) * half + c * piece, piece)]
        copy = send(where, where, send_g.at[c], recv_g.at[c], sibling)
        copy.start()
        rest.append(copy)
    local.wait()
    own.wait()
    for copy in first + side:
        copy.wait_send()
    for copy in rest:
        copy.wait()


def gather_input(shard, collective):
    n_row, n_seq = lax.axis_size("row"), lax.axis_size("seq")
    if n_row != 4 or n_seq != 2 * GROUPS:
        return lax.all_gather(shard, "row", axis=0, tiled=True)
    parts = 4
    sem = pltpu.SemaphoreType.DMA
    return pl.pallas_call(
        functools.partial(gather_input_kernel, parts),
        out_shape=jax.ShapeDtypeStruct((n_row * shard.shape[0], shard.shape[1]), shard.dtype),
        in_specs=[pl.BlockSpec(memory_space=pltpu.HBM)],
        out_specs=pl.BlockSpec(memory_space=pltpu.HBM),
        scratch_shapes=[sem, sem((2,))] + [sem((parts,))] * 8,
        compiler_params=remote_params(collective, 16),
        name="gather_input",
    )(shard)


def grad_blocks_kernel(up_rows, down_rows, d_ref, x_ref, h_ref, u_ref, *refs):
    out_ref = refs[-1]
    both = up_rows + down_rows
    out_ref[:up_rows, :] = left_trans(d_ref[...], x_ref[...]).astype(out_ref.dtype)
    out_ref[up_rows:both, :] = left_trans(h_ref[...], u_ref[...]).astype(out_ref.dtype)
    if len(refs) > 1:
        out_ref[both:, :] = refs[0][0]


def grad_blocks(d_gate_up, spread, hidden, upstream, extra=()):
    n_seq = lax.axis_size("seq")
    n_x = n_seq // GROUPS
    tokens, width = spread.shape
    up_rows, down_rows = d_gate_up.shape[1] // n_seq, hidden.shape[1] // n_seq
    rows = up_rows + down_rows + sum(part.shape[1] for part in extra)
    whole = pl.BlockSpec((tokens, width), lambda k: (0, 0))
    return pl.pallas_call(
        functools.partial(grad_blocks_kernel, up_rows, down_rows),
        out_shape=jax.ShapeDtypeStruct((n_seq * rows, width), jnp.bfloat16),
        grid=(n_seq,),
        in_specs=[
            pl.BlockSpec((tokens, up_rows), lambda k: (0, ring_member(k, n_x))),
            whole,
            pl.BlockSpec((tokens, down_rows), lambda k: (0, ring_member(k, n_x))),
            whole,
        ]
        + [
            pl.BlockSpec((1,) + part.shape[1:], lambda k: (ring_member(k, n_x), 0, 0))
            for part in extra
        ],
        out_specs=pl.BlockSpec((rows, width), lambda k: (k, 0)),
        compiler_params=pltpu.CompilerParams(vmem_limit_bytes=44 << 20),
        name="grad_blocks",
    )(d_gate_up, spread, hidden, upstream, *extra)


UNITS = 256
COLUMNS = 512


def mlp_kernel(mode, number, n_row, parts, pieces, *refs):
    forward, both = mode == "forward", mode == "both"
    refs = list(refs)

    def take(count):
        taken = refs[:count]
        del refs[:count]
        return taken

    block_ref, down_ref = take(2)
    up_refs = take(pieces)
    if both:
        (back_ref,) = take(1)
    elif not forward:
        gate_in, raise_in = take(2)
    all_ref, sum_ref = take(2)
    results = take(3 if forward or both else 1)
    if not forward and not both:
        back_ref = all_ref
    up, down, local_sem, part, near, stage, far, values_t, back_t, unit_t = take(10)
    send_c, recv_c, send_t, recv_t = take(4)
    gather_scratch = take(5)
    send_y, recv_y, send_f, recv_f, _ = gather_scratch
    (store_sem,) = take(1)
    if forward:
        hidden_ref, gate_ref, raise_ref = held = take(3)
    elif both:
        hidden_ref, slope_ref, out_ref = held = take(3)
    else:
        slope_ref, gate_ref, raise_ref = take(3)
        held = [slope_ref]
    stores = [
        pltpu.make_async_copy(held[i], results[i], store_sem.at[i]) for i in range(len(held))
    ]

    row, seq = lax.axis_index("row"), lax.axis_index("seq")
    y, core = row // 2, lax.rem(row, 2)
    n_y = n_row // 2
    rows = block_ref.shape[0]
    piece = rows // parts
    width = block_ref.shape[1]
    units = down.shape[0]
    sibling, across = row_peers(n_row)
    beside = y * 2 + 1 - core
    greet([sibling] + across)
    loads = [pltpu.make_async_copy(down_ref.at[number], down, local_sem.at[1])]
    depth = width // pieces
    for turn in range(pieces):
        origin = lax.rem(row + turn, n_row) if pieces > 1 else 0
        where = up.at[span(origin * depth, depth)]
        loads.append(pltpu.make_async_copy(up_refs[turn], where, local_sem.at[4 + turn]))
    if not forward and not both:
        loads.append(pltpu.make_async_copy(gate_in, gate_ref, local_sem.at[2]))
        loads.append(pltpu.make_async_copy(raise_in, raise_ref, local_sem.at[3]))
    for load in loads:
        load.start()
    started = start_gather_rows(n_row, parts, block_ref, all_ref, *gather_scratch)
    pending, own = started[5], started[6]
    for load in loads:
        load.wait()

    def work(offsets, size):
        spans = [span(offset, size) for offset in offsets]
        many = len(offsets) * size
        used = pl.ds(0, many)

        def joined(ref, cols):
            return jnp.concatenate([ref[here, cols] for here in spans], axis=0)

        def divided(ref, cols, value):
            for i, here in enumerate(spans):
                ref[here, cols] = value[i * size : (i + 1) * size]

        for i, here in enumerate(spans):
            values_t[pl.ds(i * size, size), :] = all_ref[here, :]
            if both:
                back_t[pl.ds(i * size, size), :] = back_ref[here, :]
        back = back_t if both else values_t

        def unit(j, _):
            at = pl.multiple_of(j * UNITS, UNITS)
            low = pl.ds(at, UNITS)
            gate_cols = pl.ds(pl.multiple_of(core * units + at, UNITS), UNITS)
            up_cols = pl.ds(pl.multiple_of((1 - core) * units + at, UNITS), UNITS)
            if forward or both:
                gate = product(values_t[used, :], up[:, gate_cols])
                raised = product(values_t[used, :], up[:, up_cols])
            else:
                gate, raised = joined(gate_ref, low), joined(raise_ref, low)
            share = 1.0 / (1.0 + jnp.exp(-gate))
            active = gate * share
            if forward or both:
                hidden = (active * raised).astype(hidden_ref.dtype)
                divided(hidden_ref, low, hidden)
            if forward:
                unit_t[used, low] = hidden
                divided(gate_ref, low, gate)
                divided(raise_ref, low, raised)
            else:
                d_hidden = right_trans(back[used, :], down[low, :])
                d_gate = d_hidden * raised * share * (1.0 + gate * (1.0 - share))
                d_gate = d_gate.astype(slope_ref.dtype)
                d_raised = (d_hidden * active).astype(slope_ref.dtype)
                unit_t[used, gate_cols] = d_gate
                unit_t[used, up_cols] = d_raised
                divided(slope_ref, gate_cols, d_gate)
                divided(slope_ref, up_cols, d_raised)
            return 0

        lax.fori_loop(0, units // UNITS, unit, 0)

        def column(j, _):
            cols = pl.ds(pl.multiple_of(j * COLUMNS, COLUMNS), COLUMNS)
            if forward:
                total = product(unit_t[used, :], down[:, cols])
            else:
                total = right_trans(unit_t[used, :], up[cols, :])
            divided(part, cols, total.astype(part.dtype))
            return 0

        lax.fori_loop(0, width // COLUMNS, column, 0)

    def to_sibling(d, block, c):
        return send(
            part.at[span(block * rows + c * piece, piece)],
            near.at[d, span(c * piece, piece)],
            send_c.at[d, c],
            recv_c.at[d, c],
            sibling,
        )

    def to_far(d, c):
        where = span(c * piece, piece)
        return send(
            stage.at[d - 1, where],
            far.at[d - 1, where],
            send_t.at[d - 1, c],
            recv_t.at[d - 1, c],
            across[d - 1],
        )

    def forwarded(d, block, c):
        where = all_ref.at[span(block * rows + c * piece, piece)]
        return send(where, where, send_f.at[d, c], recv_f.at[d, c], sibling)

    def arriving(d, c):
        return send(
            block_ref.at[span(c * piece, piece)],
            all_ref.at[span(row * rows + c * piece, piece)],
            send_y.at[d, c],
            recv_y.at[d, c],
            across[d],
        )

    own.wait_recv()
    work([row * rows, beside * rows], rows)
    for c in range(parts):
        to_sibling(0, beside, c).start()
    for d in range(n_y - 1):
        shift = n_y - 1 - d
        there = lax.rem(y + shift, n_y) * 2

        def far_step(c, _, d=d, shift=shift, there=there):
            arriving(d, c).wait_recv()
            forwarded(d, there + core, c).start()
            forwarded(d, there + core, c).wait_recv()
            work([(there + core) * rows + c * piece, (there + 1 - core) * rows + c * piece], piece)
            to_sibling(shift, there + 1 - core, c).start()
            to_sibling(shift, there + 1 - core, c).wait_recv()
            where = span(c * piece, piece)
            total = part[span((there + core) * rows + c * piece, piece), :].astype(
                jnp.float32
            ) + near[shift, where, :].astype(jnp.float32)
            stage[shift - 1, where, :] = total.astype(stage.dtype)
            to_far(shift, c).start()
            return 0

        lax.fori_loop(0, parts, far_step, 0)

    for store in stores[: 2 if both else 3]:
        store.start()
    if both:

        def result(i, _):
            here = span(i * rows, rows)

            def column(j, _):
                cols = pl.ds(pl.multiple_of(j * COLUMNS, COLUMNS), COLUMNS)
                out_ref[here, cols] = product(hidden_ref[here, :], down[:, cols]).astype(
                    out_ref.dtype
                )
                return 0

            lax.fori_loop(0, width // COLUMNS, column, 0)
            return 0

        lax.fori_loop(0, n_row, result, 0)
        stores[2].start()

    def last(c, _):
        where = span(c * piece, piece)
        to_sibling(0, beside, c).wait()
        total = part[span(row * rows + c * piece, piece), :].astype(jnp.float32) + near[
            0, where, :
        ].astype(jnp.float32)
        for d in range(n_y - 1):
            to_far(d + 1, c).wait()
            total = total + far[d, where, :].astype(jnp.float32)
        sum_ref[where, :] = total
        for d in range(n_y - 1):
            shift = n_y - 1 - d
            there = lax.rem(y + shift, n_y) * 2
            to_sibling(shift, there + 1 - core, c).wait_send()
            forwarded(d, there + core, c).wait_send()
            arriving(d, c).wait_send()
        return 0

    lax.fori_loop(0, parts, last, 0)
    own.wait_send()
    for store in stores:
        store.wait()


def mlp_fused(mode, number, block, ups, downs, extra, collective):
    n_row = lax.axis_size("row")
    n_y = n_row // 2
    rows, width = block.shape
    units = downs.shape[1]
    parts = 2
    total = n_row * rows
    low, high = jnp.bfloat16, jnp.float32
    shapes = [((total, width), low), ((rows, width), high)]
    if mode == "forward":
        shapes += [((total, units), low), ((total, units), high), ((total, units), high)]
    elif mode == "both":
        shapes += [((total, units), low), ((total, 2 * units), low), ((total, width), low)]
    else:
        shapes += [((total, 2 * units), low)]
    kept = shapes[2:] + [(part.shape, part.dtype) for part in extra if mode == "backward"]
    sem = pltpu.SemaphoreType.DMA
    buffer = (rows, width)
    return pl.pallas_call(
        functools.partial(
            mlp_kernel, mode, number, n_row, parts, len(ups)
        ),
        out_shape=tuple(jax.ShapeDtypeStruct(*shape) for shape in shapes),
        in_specs=[vmem(), anywhere()]
        + [anywhere()] * len(ups)
        + [vmem() if mode == "both" else anywhere()] * len(extra),
        out_specs=(vmem(),) * 2 + (anywhere(),) * (len(shapes) - 2),
        scratch_shapes=[
            pltpu.VMEM((width, 2 * units), low),
            pltpu.VMEM((units, width), low),
            sem((4 + len(ups),)),
            pltpu.VMEM((total, width), low),
            pltpu.VMEM((n_y,) + buffer, low),
            pltpu.VMEM((n_y - 1,) + buffer, low),
            pltpu.VMEM((n_y - 1,) + buffer, low),
            pltpu.VMEM((2 * rows, width), low),
            pltpu.VMEM((2 * rows, width) if mode == "both" else (16, LANES), low),
            pltpu.VMEM((2 * rows, units if mode == "forward" else 2 * units), low),
        ]
        + [sem((n_y, parts))] * 2
        + [sem((n_y - 1, parts))] * 2
        + gather_rows_scratch(n_y, parts)
        + [sem((3,))]
        + [pltpu.VMEM(*shape) for shape in kept],
        compiler_params=remote_params(collective, 56),
        name="mlp_" + mode,
    )(block, downs, *ups, *extra)


def owner_kernel(a_ref, b_ref, out_ref):
    first, second = a_ref[...], b_ref[...]
    half = first.shape[1] // 2
    out_ref[0] = jnp.concatenate([first[:, :half], second[:, :half]], axis=1)
    out_ref[1] = jnp.concatenate([first[:, half:], second[:, half:]], axis=1)


def conv_kernel(x_ref, top_ref, taps_ref, bias_ref, masks_ref, pre_ref, act_ref):
    values, top = x_ref[...], top_ref[...]
    edge = lax.broadcasted_iota(jnp.int32, top.shape, 0)
    total = bias_ref[...] + jnp.zeros_like(values)
    for tap in range(CONV):
        shift = CONV - 1 - tap
        moved = values
        if shift:
            moved = pltpu.roll(values, shift, 0)
            head = jnp.where(edge < shift, pltpu.roll(top, shift, 0), moved[:8])
            moved = jnp.concatenate([head, moved[8:]], axis=0)
        total = total + taps_ref[tap : tap + 1, :] * moved * masks_ref[:, tap : tap + 1]
    pre_ref[...] = total
    act_ref[...] = (total / (1.0 + jnp.exp(-total))).astype(act_ref.dtype)


def conv_forward(mixed, halo, taps, bias, masks):
    rows = mixed.shape[0]
    inner = taps.shape[1]
    cols = 512
    top = jnp.concatenate([jnp.zeros((8 - halo.shape[0], inner), halo.dtype), halo], axis=0)
    return pl.pallas_call(
        conv_kernel,
        out_shape=(
            jax.ShapeDtypeStruct((rows, inner), jnp.float32),
            jax.ShapeDtypeStruct((rows, inner), jnp.bfloat16),
        ),
        grid=(inner // cols,),
        in_specs=[
            pl.BlockSpec((rows, cols), lambda j: (0, j)),
            pl.BlockSpec((8, cols), lambda j: (0, j)),
            pl.BlockSpec((CONV, cols), lambda j: (0, j)),
            pl.BlockSpec((1, cols), lambda j: (0, j)),
            pl.BlockSpec((rows, CONV), lambda j: (0, 0)),
        ],
        out_specs=(
            pl.BlockSpec((rows, cols), lambda j: (0, j)),
            pl.BlockSpec((rows, cols), lambda j: (0, j)),
        ),
        compiler_params=pltpu.CompilerParams(vmem_limit_bytes=24 << 20),
        name="conv_forward",
    )(mixed, top, taps, bias[None], masks.T)


def cycle(depth, breadth):
    order = [(z, 0) for z in range(depth)]
    for turn in range(depth):
        across = range(1, breadth) if turn % 2 == 0 else range(breadth - 1, 0, -1)
        order += [(depth - 1 - turn, x) for x in across]
    return order


def seq_order():
    n_x = lax.axis_size("seq") // GROUPS
    return [z * n_x + x for z, x in cycle(GROUPS, n_x)]


def plane_order():
    n_x = lax.axis_size("seq") // GROUPS
    order = []
    for y, x in cycle(lax.axis_size("row") // 2, n_x):
        cores = (0, 1) if len(order) // 2 % 2 == 0 else (1, 0)
        order += [(2 * y + core, x) for core in cores]
    return order


def plane_groups():
    n_seq = lax.axis_size("seq")
    n_x = n_seq // GROUPS
    return [[r * n_seq + z * n_x + x for r, x in plane_order()] for z in range(GROUPS)]


def owner_blocks(half):
    n_row, n_seq = lax.axis_size("row"), lax.axis_size("seq")
    rows, columns = half.shape
    owned = columns // (n_row // 2 * n_seq)
    if n_row == 4 and owned % LANES == LANES // 2:
        pairs = n_seq // 2
        return pl.pallas_call(
            owner_kernel,
            out_shape=jax.ShapeDtypeStruct((n_seq, rows, 2 * owned), half.dtype),
            grid=(pairs,),
            in_specs=[
                pl.BlockSpec((rows, 2 * owned), lambda i: (0, i)),
                pl.BlockSpec((rows, 2 * owned), lambda i: (0, pairs + i)),
            ],
            out_specs=pl.BlockSpec((2, rows, 2 * owned), lambda i: (i, 0, 0)),
            name="owner_blocks",
        )(half, half)
    shaped = half.reshape(rows, n_row // 2, n_seq, owned).transpose(2, 0, 1, 3)
    return shaped.reshape(n_seq, rows, n_row // 2 * owned)


def input_term(spread, gathered):
    flat = spread.reshape(-1, spread.shape[2])
    return left_trans(flat, gathered).astype(jnp.bfloat16)


def norm_apply(values, gain_row):
    factor = lax.rsqrt(jnp.mean(values * values, axis=-1, keepdims=True) + eps)
    return (values * factor * gain_row, factor)


def norm_back(values, factor, gain_row, upstream):
    normed = values * factor
    weighted = upstream * gain_row
    gain_grad = jnp.sum(upstream * normed, axis=0)
    value_grad = factor * (weighted - normed * jnp.mean(weighted * normed, axis=-1, keepdims=True))
    return (value_grad, gain_grad)


def doc_index(positions, lengths):
    ends_at = jnp.cumsum(lengths)
    return jnp.sum((positions[:, None] >= ends_at[None, :]).astype(jnp.int32), axis=1)


def first_allowed(positions, lengths):
    ends_at = jnp.cumsum(lengths)
    begins = jnp.max(jnp.where(positions[:, None] >= ends_at[None, :], ends_at[None, :], 0), axis=1)
    return jnp.maximum(begins, positions - (WINDOW - 1)).astype(jnp.int32)


def conv_masks(positions, lengths):
    own_doc = doc_index(positions, lengths)
    rows_out = []
    for tap_index in range(CONV):
        earlier = positions - (CONV - 1) + tap_index
        rows_out.append(
            ((earlier >= 0) & (doc_index(earlier, lengths) == own_doc)).astype(jnp.float32)
        )
    return jnp.stack(rows_out, axis=0)


def rotary_tables(positions):
    half_dim = HEAD_DIM // 2
    frequency = jnp.power(rope_base, -2.0 * jnp.arange(half_dim).astype(jnp.float32) / HEAD_DIM)
    angles = positions.astype(jnp.float32)[:, None] * frequency[None, :]
    cosine, sine_tab = (jnp.cos(angles), jnp.sin(angles))
    return (
        jnp.concatenate([cosine, cosine], axis=1),
        jnp.concatenate([-sine_tab, sine_tab], axis=1),
    )


def own_up_columns(up_local, number):
    n_row = lax.axis_size("row")
    row = lax.axis_index("row")
    depth, both = up_local.shape[1:]
    ff_dim = both // 2
    ff_row = ff_dim // n_row

    def slab(dest):
        odd = dest % 2
        halves = [
            lax.dynamic_slice(
                up_local, (number, 0, half * ff_dim + dest * ff_row), (1, depth, ff_row)
            )[0]
            for half in (odd, 1 - odd)
        ]
        return jnp.concatenate(halves, axis=1)

    pieces = [slab(row)]
    for turn in range(1, n_row):
        pieces.append(
            lax.ppermute(
                slab((row + n_row - turn) % n_row),
                "row",
                [(i, (i - turn) % n_row) for i in range(n_row)],
            )
        )
    return pieces


def place_up_grad(grad):
    n_row = lax.axis_size("row")
    n_seq = lax.axis_size("seq")
    holders = [(r, s) for r in range(n_row) for s in range(n_seq)]
    pairs = []
    for r, s in holders:
        owner = owner_of_python(r, s, n_row, n_seq)
        pairs.append((r * n_seq + s, owner[0] * n_seq + owner[1]))
    return lax.ppermute(grad, ("row", "seq"), pairs)


def owner_of_python(r, s, n_row, n_seq):
    half = n_seq // 2
    if s // half == r % 2:
        return (r // 2, s)
    return (n_row // 2 + r // 2, (r % 2) * half + s % half)


def mlp_gradients(spread, hidden, d_gate_up, upstream_all, extra=(), before=()):
    n_seq = lax.axis_size("seq")
    width = spread.shape[1]
    up_rows = d_gate_up.shape[1] // n_seq
    if extra:
        extra = [part.astype(jnp.bfloat16).reshape(n_seq, -1, width) for part in extra]
        extra = [jnp.concatenate(extra, axis=1)]
    if up_rows % (2 * LANES) or (extra and extra[0].shape[1] % 16):
        parts = [left_trans(d_gate_up, spread), left_trans(hidden, upstream_all)]
        parts = [part.astype(jnp.bfloat16).reshape(n_seq, -1, width) for part in parts]
        merged = jnp.concatenate(parts + list(extra), axis=1)[jnp.array(seq_order())]
        merged = merged.reshape(-1, width)
    else:
        merged = grad_blocks(d_gate_up, spread, hidden, upstream_all, extra)
    merged = lax.optimization_barrier((merged,) + before)[0]
    summed = lax.psum_scatter(
        merged, "seq", scatter_dimension=0, tiled=True, axis_index_groups=[seq_order()]
    )
    down_end = up_rows + up_rows // 2
    return (merged, summed[:up_rows], summed[up_rows:down_end], summed[down_end:])


def matchings(edges, size):
    rounds = []
    left = list(range(len(edges)))
    while left:
        taken = {}

        def assign(source, seen):
            for e in left:
                if edges[e][0] == source and edges[e][1] not in seen:
                    seen.add(edges[e][1])
                    if edges[e][1] not in taken or assign(edges[taken[edges[e][1]]][0], seen):
                        taken[edges[e][1]] = e
                        return True
            return False

        for source in range(size):
            assign(source, set())
        chosen = sorted(taken.values())
        rounds.append(chosen)
        left = [e for e in left if e not in chosen]
    return rounds


def place_attn_grad(piece, width):
    n_row = lax.axis_size("row")
    n_seq = lax.axis_size("seq")
    n_x = n_seq // GROUPS
    size = n_row * n_seq
    me = lax.axis_index("row") * n_seq + lax.axis_index("seq")
    group_cols = width // GROUPS
    owned = piece.shape[0]
    unit = math.gcd(owned, group_cols)
    count = owned // unit
    edges, slots = [], []
    for member, (r, x) in enumerate(plane_order()):
        for z in range(GROUPS):
            for u in range(count):
                local = member * owned + u * unit
                column = (local // group_cols) * width + z * group_cols + local % group_cols
                edges.append((r * n_seq + z * n_x + x, column // owned))
                slots.append((u, column % owned // unit))
    result = jnp.zeros_like(piece)
    for chosen in matchings(edges, size):
        send_slot = [0] * size
        recv_slot = [0] * size
        for e in chosen:
            send_slot[edges[e][0]] = slots[e][0]
            recv_slot[edges[e][1]] = slots[e][1]
        taken = lax.dynamic_slice(
            piece, (jnp.array(send_slot, jnp.int32)[me] * unit, 0), (unit, piece.shape[1])
        )
        moved = lax.ppermute(taken, ("row", "seq"), [edges[e] for e in chosen])
        result = lax.dynamic_update_slice(
            result, moved, (jnp.array(recv_slot, jnp.int32)[me] * unit, 0)
        )
    return result


def per_device(
    tokens,
    norm_gain,
    input_weight,
    conv_weight,
    conv_bias,
    select_weight,
    step_weight,
    step_bias,
    decay_log,
    skip_scale,
    output_weight,
    attn_gain,
    attn_weight,
    attn_output,
    mlp_gain,
    mlp_up_weight,
    mlp_down_weight,
    doc_lengths,
    cotangent,
):
    n_row = lax.axis_size("row")
    n_seq = lax.axis_size("seq")
    n_x = n_seq // GROUPS
    rows_here = tokens.shape[1]
    width = tokens.shape[2]
    inner_dim = skip_scale.shape[0]
    rank_dim = step_weight.shape[0]
    state_dim = decay_log.shape[1]
    head_count = HEADS // GROUPS
    group_cols = head_count * HEAD_DIM
    lengths = doc_lengths[0]
    seq_index = lax.axis_index("seq")
    z_index = seq_index // n_x
    x_index = seq_index % n_x
    positions = seq_index * rows_here + jnp.arange(rows_here, dtype=jnp.int32)
    gain_in = norm_gain.astype(jnp.float32)
    gain_attn = attn_gain.astype(jnp.float32)
    gains_mlp = mlp_gain.astype(jnp.float32)
    conv_taps = conv_weight.astype(jnp.float32)
    skip_row = skip_scale.astype(jnp.float32)
    decays = -jnp.exp(decay_log.astype(jnp.float32)).T
    decay_planes = decays.reshape(state_dim, inner_dim // LANES, LANES)
    source = tokens[0].astype(jnp.float32)
    own_doc = doc_index(positions, lengths)
    keep_flag = ((positions > 0) & (own_doc == doc_index(positions - 1, lengths))).astype(
        jnp.float32
    )
    keep_lanes = jnp.broadcast_to(keep_flag[:, None], (rows_here, LANES))
    tap_masks = conv_masks(positions, lengths)
    whole_in = gather_input(input_weight, 10)
    up_local = lax.optimization_barrier((mlp_up_weight, whole_in))[0]
    up_first = own_up_columns(up_local, 0)
    normed_in, factor_in = norm_apply(source, gain_in)
    low_in = normed_in.astype(jnp.bfloat16)
    low_sent, grad_sent = lax.optimization_barrier((low_in, cotangent[0], whole_in))[:2]
    gathered_in = lax.all_gather(
        low_sent, "seq", axis=0, tiled=True, axis_index_groups=[seq_order()]
    )
    gathered_grad = lax.all_gather(grad_sent, "row", axis=0, tiled=True)
    mixed_in = product(low_in, whole_in)
    conv_input = mixed_in[:, :inner_dim]
    gate_input = mixed_in[:, inner_dim:]
    halo_rows = from_behind(
        conv_input[rows_here - (CONV - 1) :].astype(jnp.bfloat16), "seq", 1
    ).astype(jnp.float32)
    padded = jnp.concatenate([halo_rows, conv_input], axis=0)
    conv_pre, activated_low = conv_forward(
        mixed_in, halo_rows, conv_taps, conv_bias.astype(jnp.float32), tap_masks
    )
    activated = activated_low.astype(jnp.float32)
    picked = product(activated_low, select_weight)
    step_low = picked[:, :rank_dim].astype(jnp.bfloat16)
    step_pre = product(step_low, step_weight) + step_bias
    step_size = jax.nn.softplus(step_pre)
    in_flat = picked[:, rank_dim : rank_dim + state_dim].reshape(-1)
    read_flat = picked[:, rank_dim + state_dim :].reshape(-1)
    local_end = scan_end(step_size, activated_low, keep_lanes, in_flat, decay_planes)
    summed_steps = jnp.where(
        jnp.min(keep_flag) > 0, jnp.sum(step_size, axis=0), RESET
    ).reshape(-1, LANES)
    start_hidden = exchange_states(
        summed_steps, local_end, decay_planes, 5
    )
    scanned, marks = scan_out(
        start_hidden, step_size, activated_low, keep_lanes, in_flat, read_flat, decay_planes
    )
    mamba_out = scanned + skip_row * activated
    gate_act = jax.nn.silu(gate_input)
    gated = (mamba_out * gate_act).astype(jnp.bfloat16)
    first_out = source + product(gated, output_weight)
    normed_first, factor_first = norm_apply(first_out, gains_mlp[0])
    spread_first, second_sum, hidden_first, gate_first, raise_first = mlp_fused(
        "forward", 0, normed_first.astype(jnp.bfloat16), up_first, mlp_down_weight, (), 1
    )
    second_out = first_out + second_sum
    normed_attn, factor_attn = norm_apply(second_out, gain_attn)
    length = rows_here * n_seq
    cosine, sine_tab = rotary_tables(jnp.arange(length, dtype=jnp.int32))
    block_starts = (jnp.arange(GROUPS, dtype=jnp.int32) * n_x + x_index) * rows_here
    query_pos = (
        block_starts[:, None] + jnp.arange(rows_here, dtype=jnp.int32)[None, :]
    ).reshape(-1)
    first_key = first_allowed(query_pos, lengths)
    lows = jnp.min(first_key.reshape(GROUPS, rows_here), axis=1)
    x_array = x_index.reshape(1).astype(jnp.int32)
    context, triple, up_last = gather_seq(
        normed_attn.astype(jnp.bfloat16),
        mlp_up_weight,
        attn_weight,
        cosine,
        sine_tab,
        2 * group_cols,
        (gathered_in,),
    )
    attended, log_total = attend(
        x_array, lows, triple, first_key[:, None], n_x, head_count, rows_here
    )
    attended_low, gated_rows = swap_heads(attended, gated, True, 7)
    third_out = second_out + product(attended_low, attn_output)
    normed_last, factor_last = norm_apply(third_out, gains_mlp[1])
    spread_last, d_normed_last, hidden_last, slope_last, final_partial = mlp_fused(
        "both", 1, normed_last.astype(jnp.bfloat16), [up_last], mlp_down_weight, (gathered_grad,), 2
    )
    d_norm_last, g_gain_last = norm_back(third_out, factor_last, gains_mlp[1], d_normed_last)
    d_third = cotangent[0].astype(jnp.float32) + d_norm_last
    d_third_low = d_third.astype(jnp.bfloat16)
    d_attended, attended_rows, final_sum = swap_heads(
        right_trans(d_third_low, attn_output).astype(jnp.bfloat16),
        attended_low,
        False,
        8,
        final_partial,
    )
    output = (third_out + final_sum).astype(jnp.bfloat16)
    d_query, d_keys, d_values = attend_back(
        x_array,
        lows,
        triple,
        attended,
        d_attended,
        log_total,
        first_key[:, None],
        cosine,
        sine_tab,
        n_x,
        head_count,
        rows_here,
    )
    own_x = (jnp.arange(n_x) == x_index)[None, :, None, None]
    d_query_full = jnp.where(
        own_x, d_query.reshape(GROUPS, 1, rows_here, group_cols), jnp.bfloat16(0)
    ).reshape(length, group_cols)
    d_triple = jnp.concatenate([d_query_full, d_keys, d_values], axis=1)
    d_attn_normed, d_third_rows = reduce_seq(d_triple, attn_weight, d_third_low)
    summed_last = mlp_gradients(
        spread_last, hidden_last, slope_last, gathered_grad, (), (d_attn_normed,)
    )[1:3]
    g_down_last = summed_last[1].astype(jnp.float32)
    g_attn_local = left_trans(d_triple, context).astype(jnp.bfloat16)
    g_attn_local = lax.optimization_barrier((g_attn_local, d_attn_normed))[0]
    g_attn_weight = lax.psum_scatter(
        g_attn_local,
        ("row", "seq"),
        scatter_dimension=0,
        tiled=True,
        axis_index_groups=plane_groups(),
    )
    d_attn_norm, g_attn_gain = norm_back(
        second_out, factor_attn, gain_attn, d_attn_normed
    )
    d_second = d_third + d_attn_norm
    second_rows, d_normed_first, slope_first = mlp_fused(
        "backward",
        0,
        d_second.astype(jnp.bfloat16),
        up_first,
        mlp_down_weight,
        (gate_first, raise_first),
        3,
    )
    d_norm_first, g_gain_first = norm_back(first_out, factor_first, gains_mlp[0], d_normed_first)
    d_first = d_second + d_norm_first
    d_first_low = d_first.astype(jnp.bfloat16)
    d_gated = right_trans(d_first_low, output_weight)
    d_scanned = d_gated * gate_act
    gate_sig = jax.nn.sigmoid(gate_input)
    d_gate = d_gated * mamba_out * gate_sig * (1.0 + gate_input * (1.0 - gate_sig))
    d_gate_low = d_gate.astype(jnp.bfloat16)
    g_skip_scale = jnp.sum(d_scanned * activated, axis=0)
    back_end = adjoint_end(
        step_size, d_scanned, keep_lanes, read_flat, decay_planes
    )
    end_grad, gate_spread, d_first_rows = exchange_states(
        summed_steps, back_end, decay_planes, 6, owner_blocks(d_gate_low), d_first_low
    )
    merged_first, up_first_sum, g_down_first, tail_sum = mlp_gradients(
        spread_first,
        hidden_first,
        slope_first,
        second_rows,
        (left_trans(gated_rows, d_first_rows), left_trans(attended_rows, d_third_rows)),
        (g_attn_weight, end_grad),
    )
    g_step, g_activated, in_lanes, read_lanes, g_decays = adjoint_full(
        end_grad,
        marks,
        step_size,
        activated_low,
        d_scanned,
        keep_lanes,
        in_flat,
        read_flat,
        decay_planes,
        (merged_first,),
    )
    g_attn_weight, up_late = lax.optimization_barrier((g_attn_weight, summed_last[0], end_grad))[:2]
    attn_placed = place_attn_grad(g_attn_weight, width)
    up_placed = place_up_grad(up_late)
    g_up_last = up_placed.astype(jnp.float32).T
    g_attn_weight = attn_placed.astype(jnp.float32).T
    g_down_first = g_down_first.astype(jnp.float32)
    output_rows = inner_dim // (n_row * n_seq)
    g_output_weight = tail_sum[:output_rows].astype(jnp.float32)
    g_attn_output = tail_sum[output_rows:].astype(jnp.float32)
    g_input_map = jnp.sum(in_lanes.reshape(rows_here, state_dim, LANES), axis=2)
    g_read_map = jnp.sum(read_lanes.reshape(rows_here, state_dim, LANES), axis=2)
    g_decay_log = g_decays.reshape(state_dim, inner_dim) * decays
    d_step_pre = g_step * jax.nn.sigmoid(step_pre)
    g_step_bias = jnp.sum(d_step_pre, axis=0)
    d_step_low = d_step_pre.astype(jnp.bfloat16)
    d_picked = jnp.concatenate(
        [right_trans(d_step_low, step_weight), g_input_map, g_read_map], axis=1
    ).astype(jnp.bfloat16)
    g_select_weight = left_trans(activated_low, d_picked)
    d_activated = d_scanned * skip_row + g_activated + right_trans(d_picked, select_weight)
    pre_sig = jax.nn.sigmoid(conv_pre)
    d_conv_pre = d_activated * pre_sig * (1.0 + conv_pre * (1.0 - pre_sig))
    g_conv_bias = jnp.sum(d_conv_pre, axis=0)
    edge = CONV - 1
    d_edge = jnp.zeros((edge, inner_dim), jnp.float32)
    for tap_index in range(edge):
        kept_rows = (
            d_conv_pre[: edge - tap_index]
            * tap_masks[tap_index][: edge - tap_index, None]
            * conv_taps[tap_index]
        )
        d_edge = d_edge + jnp.pad(kept_rows, ((tap_index, 0), (0, 0)))
    back_rows = from_behind(d_edge.astype(jnp.bfloat16), "seq", -1)
    tap_grads = []
    d_padded = jnp.zeros((rows_here + CONV - 1, inner_dim), jnp.float32)
    for tap_index in range(CONV):
        masked = d_conv_pre * tap_masks[tap_index][:, None]
        tap_grads.append(jnp.sum(masked * padded[tap_index : tap_index + rows_here], axis=0))
        d_padded = d_padded + jnp.pad(
            masked * conv_taps[tap_index], ((tap_index, CONV - 1 - tap_index), (0, 0))
        )
    g_conv_weight = jnp.stack(tap_grads, axis=0)
    d_conv_input = d_padded[CONV - 1 :] + jnp.pad(back_rows, ((rows_here - (CONV - 1), 0), (0, 0)))
    d_conv_low = d_conv_input.astype(jnp.bfloat16)
    d_mixed = jnp.concatenate([d_conv_low, d_gate_low], axis=1)
    d_normed_in = right_trans(d_mixed, whole_in)
    d_source, g_norm_gain = norm_back(source, factor_in, gain_in, d_normed_in)
    tokens_grad = (d_first + d_source).astype(jnp.bfloat16)

    owners = n_row * n_seq
    gains = jnp.stack([g_norm_gain, g_attn_gain, g_gain_first, g_gain_last], axis=0)
    gain_rows = gains.size // inner_dim
    lines = [
        g_decay_log,
        g_conv_weight,
        g_conv_bias[None],
        g_step_bias[None],
        g_skip_scale[None],
        gains.reshape(gain_rows, -1, owners, width // owners)
        .transpose(0, 2, 1, 3)
        .reshape(gain_rows, inner_dim),
    ]
    used = sum(part.shape[0] for part in lines)
    columns = [g_select_weight, left_trans(d_step_low, step_low)]
    spare = -(used + sum(part.shape[1] for part in columns)) % LANES
    lines.append(jnp.zeros((spare, inner_dim), jnp.float32))
    packed = jnp.concatenate(columns + [jnp.concatenate(lines, axis=0).T], axis=1)
    conv_spread, summed = swap_and_reduce(
        owner_blocks(d_conv_low), packed.astype(jnp.bfloat16), 11, (attn_placed, up_placed)
    )
    g_input_weight, first_placed = reduce_rows(
        jnp.concatenate(
            [input_term(conv_spread, gathered_in), input_term(gate_spread, gathered_in)], axis=0
        ),
        up_first_sum,
        13,
    )
    g_input_weight = g_input_weight.T
    g_up_first = first_placed.astype(jnp.float32).T
    at = columns[0].shape[1]
    small_select = summed[:, :at]
    small_step = summed[:, at : at + rank_dim].T
    tail = summed[:, at + rank_dim :]
    small_lines = tail.T
    small = []
    at = 0
    for part in lines[:-1]:
        small.append(small_lines[at : at + part.shape[0]])
        at += part.shape[0]
    gain_sums = (
        small[5].reshape(gain_rows, -1, width // owners).reshape(4, width // owners)
    )
    return (
        output[None],
        tokens_grad[None],
        gain_sums[0],
        g_input_weight,
        small[1],
        small[2][0],
        small_select,
        small_step,
        small[3][0],
        tail[:, :state_dim],
        small[4][0],
        g_output_weight,
        gain_sums[1],
        g_attn_weight,
        g_attn_output,
        gain_sums[2:],
        jnp.stack([g_up_first, g_up_last], axis=0),
        jnp.stack([g_down_first, g_down_last], axis=0),
    )


def solution(mesh):
    return jax.shard_map(
        per_device,
        mesh=mesh,
        in_specs=(
            P("row", "seq", None),
            P(),
            P("row", None),
            P(),
            P(),
            P(),
            P(),
            P(),
            P(),
            P(),
            P(),
            P(),
            P(),
            P(),
            P(),
            P(None, "row", None),
            P(None, "row", None),
            P("row", None),
            P("row", "seq", None),
        ),
        out_specs=(
            P("row", "seq", None),
            P("row", "seq", None),
            P(("row", "seq")),
            P(None, ("row", "seq")),
            P(None, ("row", "seq")),
            P(("row", "seq")),
            P(("row", "seq"), None),
            P(None, ("row", "seq")),
            P(("row", "seq")),
            P(("row", "seq"), None),
            P(("row", "seq")),
            P(("row", "seq"), None),
            P(("row", "seq")),
            P(None, ("row", "seq")),
            P(("row", "seq"), None),
            P(None, ("row", "seq")),
            P(None, None, ("row", "seq")),
            P(None, ("row", "seq"), None),
        ),
        check_vma=False,
    )
```
